32 devices in a mesh: seq: 8 (over z, x), row: 4 (over y, core).
Axes of the slice: x: 2, y: 2, z: 4, core: 2. Of those that a mesh axis runs over, the one named last changes fastest.
Arguments:
- tokens: bfloat16 [4, 4096, 2048], P('row', 'seq'), may hold values from -6 to 6
- resets: int32 [4, 4096], P('row', 'seq'), may hold values from 0 to 1, as said below
- cotangent: bfloat16 [4, 4096, 2048], P('row', 'seq'), may hold values from -6 to 6
- weight: bfloat16 [2, 2048, 6144], P(None, ('seq', 'row')), may hold values from -0.125 to 0.125
- norm_gain: bfloat16 [2, 2048], P(None, ('seq', 'row')), may hold values from 0.5 to 1.5
- norm_bias: bfloat16 [2, 2048], P(None, ('seq', 'row')), may hold values from -1 to 1
- forget_peep: bfloat16 [2, 2048], P(None, ('seq', 'row')), may hold values from -1 to 1
- reset_peep: bfloat16 [2, 2048], P(None, ('seq', 'row')), may hold values from -2 to 2
- forget_bias: bfloat16 [2, 2048], P(None, ('seq', 'row')), may hold values from 3.5 to 10.5
- reset_bias: bfloat16 [2, 2048], P(None, ('seq', 'row')), may hold values from -1 to 1
Outputs:
- result: bfloat16 [4, 4096, 2048], P('row', 'seq')
- input_grad: bfloat16 [4, 4096, 2048], P('row', 'seq')
- weight_grad: float32 [2, 2048, 6144], P(None, ('seq', 'row'))
- norm_gain_grad: float32 [2, 2048], P(None, ('seq', 'row'))
- norm_bias_grad: float32 [2, 2048], P(None, ('seq', 'row'))
- forget_peep_grad: float32 [2, 2048], P(None, ('seq', 'row'))
- reset_peep_grad: float32 [2, 2048], P(None, ('seq', 'row'))
- forget_bias_grad: float32 [2, 2048], P(None, ('seq', 'row'))
- reset_bias_grad: float32 [2, 2048], P(None, ('seq', 'row'))
The draws below stay inside these ranges and needn't reach their ends.
Inputs may be any that keep to these rules, and one draw needn't show every extreme that they name: `resets`: position 0 of every row is 1. In each row one sentence starts within the first 512 positions and runs into the last 512 positions.
All inputs are finite; a program needn't handle non-finite values.
Results may differ from the reference program's by a relative error of at most 0.0045.
Values may be sent and summed in bfloat16 or wider, within the bound.
A program may use at most 256 MiB of HBM per device.

```python
import math
import jax
import jax.numpy as jnp
from jax import lax

D = 2048
LAYERS = 2
GROUP = 512
ROWS = 4
LENGTH = 4096


def sentence_flags(key):
    first_key, last_key, mark_key = jax.random.split(jax.random.fold_in(key, 5), 3)
    position = jnp.arange(LENGTH, dtype=jnp.int32)[None, :]
    first = jax.random.randint(first_key, (ROWS, 1), 1, GROUP)
    last = LENGTH - jax.random.randint(last_key, (ROWS, 1), 1, GROUP)
    marks = jax.random.randint(mark_key, (ROWS, LENGTH), 0, 32) == 0
    outside = (position < first) | (position > last)
    flags = outside & marks | (position == 0) | (position == first) | (position == last)
    return flags.astype(jnp.int32)


def draw_resets(key, part):
    return sentence_flags(key)


def draw_tokens(key, part):
    flags = sentence_flags(key)
    key = jax.random.fold_in(key, 7)
    noise_key, table_key = jax.random.split(key)
    sentence = jnp.cumsum(flags, axis=1).astype(jnp.int32) - 1
    slot = sentence % 32
    table = jax.random.normal(table_key, (ROWS, 32, D), jnp.float32)
    direction = table[jnp.arange(ROWS, dtype=jnp.int32)[:, None], slot]
    noise = jax.random.normal(noise_key, (ROWS, LENGTH, D), jnp.float32)
    return jnp.clip(0.8 * noise + 0.6 * direction, -6.0, 6.0).astype(jnp.bfloat16)


def draw_forget_bias(key, part):
    key = jax.random.fold_in(key, 11)
    pick_key, fast_key, slow_key = jax.random.split(key, 3)
    share = 0.3
    picked = jax.random.uniform(pick_key, (LAYERS, D), jnp.float32) < share
    fast_value = jax.random.uniform(fast_key, (LAYERS, D), jnp.float32, 3.5, 5.0)
    slow_value = math.log(LENGTH) + jax.random.uniform(slow_key, (LAYERS, D), jnp.float32, 0.0, 1.5)
    return jnp.where(picked, fast_value, slow_value).astype(jnp.bfloat16)


def shard_levels(stream_key, dims, cuts, least, top_value):
    level = 1.0
    for axis_at, parts in cuts:
        steps = jax.random.uniform(jax.random.fold_in(jax.random.fold_in(stream_key, 6), axis_at), (parts,), jnp.float32, least / len(cuts), top_value / len(cuts))
        level = level * jnp.repeat(jnp.exp(steps), dims[axis_at] // parts).reshape((-1,) + (1,) * (len(dims) - 1 - axis_at))
    return level


def centred(own_key, dims, scale, limit, shards=(), held_as=jnp.bfloat16):
    drawn = jax.random.normal(own_key, dims, jnp.float32) * scale
    if len(shards) > 0:
        drawn = shard_levels(own_key, dims, shards, -0.22, 0.18) * drawn
    return jnp.clip(drawn, min=-limit, max=limit).astype(held_as)


def setup_inputs(seed: int = 0) -> dict:
    seeds = jax.random.split(jax.random.key(seed), 11)
    tokens = draw_tokens(jax.random.fold_in(seeds[10], 71), 0)
    resets = draw_resets(jax.random.fold_in(seeds[10], 71), 0)
    cotangent = centred(seeds[2], (ROWS, LENGTH, D), 1.0, 6.0, ((0, 4), (1, 8)))
    weight = centred(seeds[3], (LAYERS, D, 3 * D), D ** -0.5, 0.125, ((1, 32),))
    norm_gain = jnp.clip(1.0 + 0.1 * jax.random.normal(seeds[4], (LAYERS, D), jnp.float32), 0.5, 1.5).astype(jnp.bfloat16)
    norm_bias = jnp.clip(jax.random.uniform(seeds[5], (LAYERS, D), jnp.float32, -1.0, 1.0) * shard_levels(seeds[5], (LAYERS, D), ((1, 32),), -0.4, 0.0), -1.0, 1.0).astype(jnp.bfloat16)
    forget_peep = jnp.clip(jax.random.uniform(seeds[6], (LAYERS, D), jnp.float32, -1.0, 1.0) * shard_levels(seeds[6], (LAYERS, D), ((1, 32),), -0.4, 0.0), -1.0, 1.0).astype(jnp.bfloat16)
    reset_peep = jnp.clip(jax.random.uniform(seeds[7], (LAYERS, D), jnp.float32, -2.0, 2.0) * shard_levels(seeds[7], (LAYERS, D), ((1, 32),), -0.4, 0.0), -2.0, 2.0).astype(jnp.bfloat16)
    forget_bias = draw_forget_bias(jax.random.fold_in(seeds[10], 71), 0)
    reset_bias = jnp.clip(jax.random.uniform(seeds[9], (LAYERS, D), jnp.float32, -1.0, 1.0) * shard_levels(seeds[9], (LAYERS, D), ((1, 32),), -0.4, 0.0), -1.0, 1.0).astype(jnp.bfloat16)
    return dict(tokens=tokens, resets=resets, cotangent=cotangent, weight=weight, norm_gain=norm_gain, norm_bias=norm_bias, forget_peep=forget_peep, reset_peep=reset_peep, forget_bias=forget_bias, reset_bias=reset_bias)


epsilon = 1e-05

@jax.custom_vjp
def low(v):
    return lax.optimization_barrier(v.astype(jnp.bfloat16)).astype(jnp.float32)

@jax.custom_vjp
def low_back(v):
    return v

def low_keep(v):
    return (low(v), None)

def low_pass(kept, grad):
    return (grad,)

def back_keep(v):
    return (v, None)

def back_low(kept, grad):
    return (low(grad),)
low.defvjp(low_keep, low_pass)
low_back.defvjp(back_keep, back_low)

def norm_layer(values, gain_row, shift_row):
    center = values - lax.optimization_barrier(jnp.mean(values, axis=-1, keepdims=True))
    variance = lax.optimization_barrier(jnp.mean(center * center, axis=-1, keepdims=True))
    return center * lax.rsqrt(variance + epsilon) * gain_row + shift_row

def recurrent_layer(inputs, keep_row, matrix, gain_row, shift_row, peep_forget, peep_reset, bias_forget, bias_reset):
    model_width = inputs.shape[-1]
    features = norm_layer(inputs, gain_row, shift_row)
    projected = low_back(jnp.dot(low(features), matrix, precision=lax.Precision.HIGHEST, preferred_element_type=jnp.float32))
    candidate = projected[:, :model_width]
    forget_pre = projected[:, model_width:2 * model_width]
    reset_pre = projected[:, 2 * model_width:]
    forget_logit = forget_pre + peep_forget * features + bias_forget
    forget = jax.nn.sigmoid(forget_logit)
    complement = jax.nn.sigmoid(-forget_logit)
    decay_rate = forget * keep_row

    def advance(running, pieces):
        decay_now, added_now, keep_now = pieces
        new_state = decay_now * running + added_now
        return (new_state, (new_state, keep_now * running))
    start = jnp.zeros((model_width,), jnp.float32)
    final_state, outputs = lax.scan(advance, start, (decay_rate, complement * candidate, keep_row))
    states, previous = outputs
    reset_gate = jax.nn.sigmoid(reset_pre + peep_reset * previous + bias_reset)
    return reset_gate * states + (1.0 - reset_gate) * inputs

def reference(tokens, resets, cotangent, weight, norm_gain, norm_bias, forget_peep, reset_peep, forget_bias, reset_bias):
    keep_all = (1 - resets).astype(jnp.float32)[:, :, None]
    primals = tuple((member.astype(jnp.float32) for member in (tokens, weight, norm_gain, norm_bias, forget_peep, reset_peep, forget_bias, reset_bias)))

    def forward(token_rows, matrices, gains, shifts, peeps_forget, peeps_reset, biases_forget, biases_reset):

        def row_pass(carry_value, row_items):
            values, keep_row = row_items
            for depth_index in range(LAYERS):
                values = recurrent_layer(values, keep_row, matrices[depth_index], gains[depth_index], shifts[depth_index], peeps_forget[depth_index], peeps_reset[depth_index], biases_forget[depth_index], biases_reset[depth_index])
            return (carry_value, values)
        final_carry, outputs = lax.scan(jax.checkpoint(row_pass), jnp.zeros((), jnp.float32), (token_rows, keep_all))
        return outputs
    outputs, pullback = jax.vjp(forward, primals[0], primals[1], primals[2], primals[3], primals[4], primals[5], primals[6], primals[7])
    grads = pullback(cotangent.astype(jnp.float32))
    return (outputs.astype(jnp.bfloat16), grads[0].astype(jnp.bfloat16), grads[1], grads[2], grads[3], grads[4], grads[5], grads[6], grads[7])
```

```python
import jax
import jax.numpy as jnp
from jax import lax
from jax.experimental import pallas as pl
from jax.experimental.pallas import tpu as pltpu
from jax.sharding import PartitionSpec as P

epsilon = 1e-05
SUB = 8
WIDE = 256
F32 = jnp.float32
BF16 = jnp.bfloat16
GAIN, SHIFT, FPEEP, RPEEP, FBIAS, RBIAS = range(6)


def params(limit=60 << 20):
    return pltpu.CompilerParams(
        dimension_semantics=("arbitrary",), vmem_limit_bytes=limit
    )


def both_sigmoids(z):
    tail = jnp.exp(-jnp.abs(z))
    big = 1.0 / (1.0 + tail)
    small = tail * big
    up = z >= 0
    return jnp.where(up, big, small), jnp.where(up, small, big)


def lanes(value, width):
    return jnp.concatenate([value] * (width // value.shape[-1]), axis=-1)


def row_of(vec, k):
    return jnp.broadcast_to(vec[k : k + 1, :], (SUB, vec.shape[-1]))


def norm_rows(u, vec, n, low, mean, inv):
    steps, _, d = u.shape
    gain, shift = vec[GAIN : GAIN + 1, :], vec[SHIFT : SHIFT + 1, :]
    piece = 8

    def one(k, _):
        at = pl.ds(k * piece, piece)
        x = u[at].reshape(piece * SUB, d)
        mu = jnp.mean(x, axis=-1, keepdims=True)
        x = x - mu
        rstd = lax.rsqrt(jnp.mean(x * x, axis=-1, keepdims=True) + epsilon)
        y = x * rstd * gain + shift
        n[at] = y.reshape(piece, SUB, d)
        low[pl.ds(pl.multiple_of(k * piece * SUB, piece * SUB), piece * SUB), :] = y.astype(BF16)
        mean[at] = jnp.broadcast_to(mu, (piece * SUB, 128)).reshape(piece, SUB, 128)
        inv[at] = jnp.broadcast_to(rstd, (piece * SUB, 128)).reshape(piece, SUB, 128)
        return 0

    lax.fori_loop(0, steps // piece, one, 0)


def forward_gates(u, keep, vec, w, low, mean, inv, f, g, cand, rpre, ends, n, proj):
    j = pl.program_id(0)
    steps, width = f.shape[0], f.shape[-1]

    @pl.when(j == 0)
    def _():
        norm_rows(u, vec, n, low, mean, inv)

    at = pl.ds(pl.multiple_of(j * width, width), width)
    proj[...] = jnp.dot(low[...], w[0], preferred_element_type=F32).reshape(steps, SUB, 3 * width)
    peep, bias, rbias = (row_of(vec[:, at], k) for k in (FPEEP, FBIAS, RBIAS))

    def one(i, carry):
        scale, state = carry
        c = proj[i, :, :width]
        z = proj[i, :, width : 2 * width] + peep * n[i, :, at] + bias
        up, down = both_sigmoids(z)
        f[i] = up
        g[i] = down
        cand[i] = c
        rpre[i] = proj[i, :, 2 * width :] + rbias
        a = up * lanes(keep[i], width)
        return scale * a, a * state + down * c

    start = jnp.ones((SUB, width), F32), jnp.zeros((SUB, width), F32)
    scale, state = lax.fori_loop(0, steps, one, start, unroll=8)
    ends[0] = scale
    ends[1] = state


def forward_states(f, g, cand, rpre, u, keep, vec, first, p, r, out):
    steps, width = f.shape[0], f.shape[-1]
    peep = row_of(vec, RPEEP)

    def one(i, c):
        before = lanes(keep[i], width) * c
        c = f[i] * before + g[i] * cand[i]
        gate = jax.nn.sigmoid(rpre[i] + peep * before)
        p[i] = before
        r[i] = gate
        out[i] = gate * c + (1.0 - gate) * u[i]
        return c

    lax.fori_loop(0, steps, one, first[...], unroll=8)


def step_terms(i, dh, f, g, cand, p, r, u, keep, peep):
    width = f.shape[-1]
    before, gate, up = p[i], r[i], f[i]
    c = up * before + g[i] * cand[i]
    top = dh[i]
    dz_r = top * (c - u[i]) * gate * (1.0 - gate)
    direct = top * gate
    kept = lanes(keep[i], width)
    decay = up * kept
    return before, up, dz_r, direct, decay, kept * peep * dz_r + decay * direct


def backward_ends(dh, f, g, cand, p, r, u, keep, vec, ends):
    steps, width = f.shape[0], f.shape[-1]
    peep = row_of(vec, RPEEP)

    def one(t, carry):
        scale, q = carry
        i = steps - 1 - t
        _, _, _, _, decay, term = step_terms(i, dh, f, g, cand, p, r, u, keep, peep)
        return scale * decay, decay * q + term

    start = jnp.ones((SUB, width), F32), jnp.zeros((SUB, width), F32)
    scale, q = lax.fori_loop(0, steps, one, start, unroll=8)
    ends[0] = scale
    ends[1] = q


def backward_states(
    dh, f, g, cand, p, r, u, keep, vec, mean, inv, first, du, dzf, sums, low
):
    steps, width = f.shape[0], f.shape[-1]
    peep, gain, shift = (row_of(vec, k) for k in (RPEEP, GAIN, SHIFT))

    def one(t, carry):
        q, s0, s1, s2, s3 = carry
        i = steps - 1 - t
        before, up, dz_r, direct, decay, term = step_terms(
            i, dh, f, g, cand, p, r, u, keep, peep
        )
        e = direct + q
        down = g[i]
        dz_f = e * (up * down) * (before - cand[i])
        n = (u[i] - lanes(mean[i], width)) * lanes(inv[i], width) * gain + shift
        low[0, i] = e * down
        low[1, i] = dz_f
        low[2, i] = dz_r
        dzf[i] = dz_f
        return (
            decay * q + term,
            s0 + dz_f * n,
            s1 + dz_r * before,
            s2 + dz_f,
            s3 + dz_r,
        )

    zero = jnp.zeros((SUB, width), F32)
    carry = lax.fori_loop(0, steps, one, (first[...], zero, zero, zero, zero), unroll=4)
    for k in range(4):
        sums[k] = carry[k + 1]
    for k in range(3):
        du[0, :, k * width : (k + 1) * width] = low[k].reshape(steps * SUB, width).astype(BF16)


def input_side(du, w, dzf, u, dh, r, mean, inv, vec, out, sums, acc):
    j = pl.program_id(0)
    steps, _, d = u.shape
    part = lax.dot_general(du[0], w[0], (((1,), (1,)), ((), ())), preferred_element_type=F32)

    @pl.when(j == 0)
    def _():
        acc[...] = part.reshape(steps, SUB, d)

    @pl.when(j > 0)
    def _():
        acc[...] += part.reshape(steps, SUB, d)

    @pl.when(j == pl.num_programs(0) - 1)
    def _():
        sums[...] = jnp.zeros_like(sums)
        peep, gain = row_of(vec, FPEEP), row_of(vec, GAIN)

        def one(i, _):
            dn = acc[i] + dzf[i] * peep
            rstd = lanes(inv[i], d)
            xhat = (u[i] - lanes(mean[i], d)) * rstd
            sums[0] += dn * xhat
            sums[1] += dn
            scaled = dn * gain
            m0 = jnp.mean(scaled, axis=-1, keepdims=True)
            m1 = jnp.mean(scaled * xhat, axis=-1, keepdims=True)
            out[i] = dh[i] * (1.0 - r[i]) + rstd * (scaled - m0 - xhat * m1)
            return 0

        lax.fori_loop(0, steps, one, 0, unroll=2)


def weight_side(low_t, du, out):
    out[0] = jnp.dot(low_t[...], du[0], preferred_element_type=F32)


def columns(steps, width):
    return pl.BlockSpec((steps, SUB, width), lambda j: (0, 0, j))


def whole(*shape):
    return pl.BlockSpec(shape, lambda j: (0,) * len(shape))


def vectors(width):
    return pl.BlockSpec((8, width), lambda j: (0, j))


def arr(*shape, dtype=F32):
    return jax.ShapeDtypeStruct(shape, dtype)


def chain(ends, axis, backward):
    everyone = lax.all_gather(ends, axis)
    count, mine = lax.axis_size(axis), lax.axis_index(axis)
    segments, d = ends.shape[1:]
    total = count * segments
    scale = everyone[:, 0].reshape(total, d)
    state = everyone[:, 1].reshape(total, d)
    if backward:
        scale, state = scale[::-1], state[::-1]
    value = jnp.zeros((d,), F32)
    entering = []
    for k in range(total):
        entering.append(value)
        value = scale[k] * value + state[k]
    entering = jnp.stack(entering)
    if backward:
        entering = entering[::-1]
    return lax.dynamic_slice_in_dim(entering, mine * segments, segments, 0)


def body(tokens, resets, cotangent, weight, *rows):
    _, t, d = tokens.shape
    layers = weight.shape[0]
    steps = t // SUB
    parts = d // WIDE
    axes = ("seq", "row")

    def permuted(x):
        return x.reshape(SUB, steps, -1).transpose(1, 0, 2)

    def restored(x):
        return x.reshape(steps, SUB, d).transpose(1, 0, 2).reshape(1, t, d)

    keep = permuted((1 - resets[0]).astype(F32)[:, None])
    keep = jnp.broadcast_to(keep, (steps, SUB, 128))
    packed = jnp.stack(rows + (jnp.zeros_like(rows[0]),) * 2, axis=1)
    every = lax.all_gather(packed, axes, axis=2, tiled=True).astype(F32)
    local = weight.reshape(layers, -1, 3, parts, WIDE).transpose(0, 3, 1, 2, 4)
    local = local.reshape(layers, parts, -1, 3 * WIDE)
    full = [lax.all_gather(local[l], axes, axis=1, tiled=True) for l in range(layers)]

    u = permuted(tokens).astype(F32)
    stored = []
    col = columns(steps, WIDE)
    keep_spec = whole(steps, SUB, 128)
    w_spec = pl.BlockSpec((1, d, 3 * WIDE), lambda j: (j, 0, 0))
    du_spec = pl.BlockSpec((1, t, 3 * WIDE), lambda j: (j, 0, 0))
    act = arr(steps, SUB, d)
    stat = arr(steps, SUB, 128)
    for l in range(layers):
        vec = every[l]
        low, mean, inv, f, g, cand, rpre, ends = pl.pallas_call(
            forward_gates,
            grid=(parts,),
            in_specs=[whole(steps, SUB, d), keep_spec, whole(8, d), w_spec],
            out_specs=[
                whole(t, d), keep_spec, keep_spec, col, col, col, col,
                pl.BlockSpec((2, SUB, WIDE), lambda j: (0, 0, j)),
            ],
            out_shape=[arr(t, d, dtype=BF16), stat, stat, act, act, act, act, arr(2, SUB, d)],
            scratch_shapes=[
                pltpu.VMEM((steps, SUB, d), F32), pltpu.VMEM((steps, SUB, 3 * WIDE), F32)
            ],
            compiler_params=params(),
            name="forward_gates",
        )(u, keep, vec, full[l])
        first = chain(ends, "seq", False)
        p, r, out = pl.pallas_call(
            forward_states,
            grid=(parts,),
            in_specs=[col] * 5 + [keep_spec, vectors(WIDE), vectors(WIDE)],
            out_specs=[col] * 3,
            out_shape=[act] * 3,
            compiler_params=params(),
            name="forward_states",
        )(f, g, cand, rpre, u, keep, vec, first)
        stored.append((u, low, mean, inv, f, g, cand, p, r))
        u = out
    result = restored(u.astype(BF16))

    dh = permuted(cotangent).astype(F32)
    weight_grads, vector_grads = [None] * layers, [None] * layers
    for l in reversed(range(layers)):
        vec = every[l]
        u, low, mean, inv, f, g, cand, p, r = stored[l]
        ends = pl.pallas_call(
            backward_ends,
            grid=(parts,),
            in_specs=[col] * 7 + [keep_spec, vectors(WIDE)],
            out_specs=pl.BlockSpec((2, SUB, WIDE), lambda j: (0, 0, j)),
            out_shape=arr(2, SUB, d),
            compiler_params=params(),
            name="backward_ends",
        )(dh, f, g, cand, p, r, u, keep, vec)
        first = chain(ends, "seq", True)
        du, dzf, sums = pl.pallas_call(
            backward_states,
            grid=(parts,),
            in_specs=[col] * 7 + [keep_spec, vectors(WIDE), keep_spec, keep_spec, vectors(WIDE)],
            out_specs=[du_spec, col, pl.BlockSpec((4, SUB, WIDE), lambda j: (0, 0, j))],
            out_shape=[arr(parts, t, 3 * WIDE, dtype=BF16), act, arr(4, SUB, d)],
            scratch_shapes=[pltpu.VMEM((3, steps, SUB, WIDE), F32)],
            compiler_params=params(),
            name="backward_states",
        )(dh, f, g, cand, p, r, u, keep, vec, mean, inv, first)
        grad = pl.pallas_call(
            weight_side,
            grid=(parts,),
            in_specs=[whole(d, t), du_spec],
            out_specs=w_spec,
            out_shape=arr(parts, d, 3 * WIDE),
            compiler_params=params(),
            name="weight_side",
        )(low.T, du)
        dh, more = pl.pallas_call(
            input_side,
            grid=(parts,),
            in_specs=[du_spec, w_spec]
            + [whole(steps, SUB, d)] * 4
            + [keep_spec, keep_spec, whole(8, d)],
            out_specs=[whole(steps, SUB, d), whole(2, SUB, d)],
            out_shape=[act, arr(2, SUB, d)],
            scratch_shapes=[pltpu.VMEM((steps, SUB, d), F32)],
            compiler_params=params(),
            name="input_side",
        )(du, full[l], dzf, u, dh, r, mean, inv, vec)
        grad = lax.psum_scatter(grad, axes, scatter_dimension=1, tiled=True)
        weight_grads[l] = (
            grad.reshape(parts, -1, 3, WIDE).transpose(1, 2, 0, 3).reshape(-1, 3 * d)
        )
        vector_grads[l] = jnp.concatenate([more.sum(1), sums.sum(1)])
    input_grad = restored(dh.astype(BF16))
    vector_out = lax.psum_scatter(
        jnp.stack(vector_grads), axes, scatter_dimension=2, tiled=True
    )
    return (result, input_grad, jnp.stack(weight_grads)) + tuple(
        vector_out[:, k] for k in range(6)
    )


def solution(mesh):
    tokens = P("row", "seq", None)
    rows = P(None, ("seq", "row"))
    weight = P(None, ("seq", "row"), None)
    return jax.shard_map(
        body,
        mesh=mesh,
        in_specs=(tokens, P("row", "seq"), tokens, weight) + (rows,) * 6,
        out_specs=(tokens, tokens, weight) + (rows,) * 6,
        check_vma=False,
    )
```

```python
import jax
import jax.numpy as jnp
from jax import lax
from jax.experimental import pallas as pl
from jax.experimental.pallas import tpu as pltpu
from jax.sharding import PartitionSpec as P

epsilon = 1e-05
SUB = 8
WIDE = 256
F32 = jnp.float32
BF16 = jnp.bfloat16
GAIN, SHIFT, FPEEP, RPEEP, FBIAS, RBIAS = range(6)


def params(limit=60 << 20):
    return pltpu.CompilerParams(
        dimension_semantics=("arbitrary",), vmem_limit_bytes=limit
    )


def both_sigmoids(z):
    tail = jnp.exp(-jnp.abs(z))
    big = 1.0 / (1.0 + tail)
    small = tail * big
    up = z >= 0
    return jnp.where(up, big, small), jnp.where(up, small, big)


def lanes(value, width):
    return jnp.concatenate([value] * (width // value.shape[-1]), axis=-1)


def row_of(vec, k):
    return jnp.broadcast_to(vec[k : k + 1, :], (SUB, vec.shape[-1]))


def norm_rows(u, vec, n, low, mean, inv):
    steps, _, d = u.shape
    gain, shift = vec[GAIN : GAIN + 1, :], vec[SHIFT : SHIFT + 1, :]
    piece = 8

    def one(k, _):
        at = pl.ds(k * piece, piece)
        x = u[at].reshape(piece * SUB, d)
        mu = jnp.mean(x, axis=-1, keepdims=True)
        x = x - mu
        rstd = lax.rsqrt(jnp.mean(x * x, axis=-1, keepdims=True) + epsilon)
        y = x * rstd * gain + shift
        n[at] = y.reshape(piece, SUB, d)
        low[pl.ds(pl.multiple_of(k * piece * SUB, piece * SUB), piece * SUB), :] = y.astype(BF16)
        mean[at] = jnp.broadcast_to(mu, (piece * SUB, 128)).reshape(piece, SUB, 128)
        inv[at] = jnp.broadcast_to(rstd, (piece * SUB, 128)).reshape(piece, SUB, 128)
        return 0

    lax.fori_loop(0, steps // piece, one, 0)


def forward_states(f, g, cand, rpre, u, keep, vec, first, p, r, out):
    steps, width = f.shape[0], f.shape[-1]
    peep = row_of(vec, RPEEP)

    def one(i, c):
        before = lanes(keep[i], width) * c
        c = f[i] * before + g[i] * cand[i]
        gate = jax.nn.sigmoid(rpre[i] + peep * before)
        p[i] = before
        r[i] = gate
        out[i] = gate * c + (1.0 - gate) * u[i]
        return c

    lax.fori_loop(0, steps, one, first[...], unroll=8)


def step_terms(i, dh, f, g, cand, p, r, u, keep, peep):
    width = f.shape[-1]
    before, gate, up = p[i], r[i], f[i]
    c = up * before + g[i] * cand[i]
    top = dh[i]
    dz_r = top * (c - u[i]) * gate * (1.0 - gate)
    direct = top * gate
    kept = lanes(keep[i], width)
    decay = up * kept
    return before, up, dz_r, direct, decay, kept * peep * dz_r + decay * direct


def backward_ends(dh, f, g, cand, p, r, u, keep, vec, ends):
    steps, width = f.shape[0], f.shape[-1]
    peep = row_of(vec, RPEEP)

    def one(t, carry):
        scale, q = carry
        i = steps - 1 - t
        _, _, _, _, decay, term = step_terms(i, dh, f, g, cand, p, r, u, keep, peep)
        return scale * decay, decay * q + term

    start = jnp.ones((SUB, width), F32), jnp.zeros((SUB, width), F32)
    scale, q = lax.fori_loop(0, steps, one, start, unroll=8)
    ends[0] = scale
    ends[1] = q


def backward_states(
    dh, f, g, cand, p, r, u, keep, vec, mean, inv, first, du, dzf, sums, low
):
    steps, width = f.shape[0], f.shape[-1]
    peep, gain, shift = (row_of(vec, k) for k in (RPEEP, GAIN, SHIFT))

    def one(t, carry):
        q, s0, s1, s2, s3 = carry
        i = steps - 1 - t
        before, up, dz_r, direct, decay, term = step_terms(
            i, dh, f, g, cand, p, r, u, keep, peep
        )
        e = direct + q
        down = g[i]
        dz_f = e * (up * down) * (before - cand[i])
        n = (u[i] - lanes(mean[i], width)) * lanes(inv[i], width) * gain + shift
        low[0, i] = e * down
        low[1, i] = dz_f
        low[2, i] = dz_r
        dzf[i] = dz_f
        return (
            decay * q + term,
            s0 + dz_f * n,
            s1 + dz_r * before,
            s2 + dz_f,
            s3 + dz_r,
        )

    zero = jnp.zeros((SUB, width), F32)
    carry = lax.fori_loop(0, steps, one, (first[...], zero, zero, zero, zero), unroll=4)
    for k in range(4):
        sums[k] = carry[k + 1]
    for h in range(2):
        for k in range(3):
            v = low[k, :, :, h * LANE : (h + 1) * LANE].reshape(steps * SUB, LANE)
            du[0, h, :, k * LANE : (k + 1) * LANE] = v.astype(BF16)


def input_side(du, w, dzf, u, dh, r, mean, inv, vec, out, sums, acc):
    j = pl.program_id(0)
    steps, _, d = u.shape
    across = (((1,), (1,)), ((), ()))
    part = lax.dot_general(du[0, 0], w[0, 0], across, preferred_element_type=F32)
    part = part + lax.dot_general(du[0, 1], w[0, 1], across, preferred_element_type=F32)

    @pl.when(j == 0)
    def _():
        acc[...] = part.reshape(steps, SUB, d)

    @pl.when(j > 0)
    def _():
        acc[...] += part.reshape(steps, SUB, d)

    @pl.when(j == pl.num_programs(0) - 1)
    def _():
        sums[...] = jnp.zeros_like(sums)
        peep, gain = row_of(vec, FPEEP), row_of(vec, GAIN)

        def one(i, _):
            dn = acc[i] + dzf[i] * peep
            rstd = lanes(inv[i], d)
            xhat = (u[i] - lanes(mean[i], d)) * rstd
            sums[0] += dn * xhat
            sums[1] += dn
            scaled = dn * gain
            m0 = jnp.mean(scaled, axis=-1, keepdims=True)
            m1 = jnp.mean(scaled * xhat, axis=-1, keepdims=True)
            out[i] = dh[i] * (1.0 - r[i]) + rstd * (scaled - m0 - xhat * m1)
            return 0

        lax.fori_loop(0, steps, one, 0, unroll=2)


MESH = pl.DeviceIdType.MESH
HALF = 384
LANE = 128


class Place:
    def __init__(self, seq, row):
        self.Y = row // 2
        self.X = self.Y
        self.Z = seq // self.X
        self.C = 2
        self.sizes = dict(z=self.Z, x=self.X, y=self.Y, c=self.C)
        s, r = lax.axis_index("seq"), lax.axis_index("row")
        self.at = dict(z=s // self.X, x=s % self.X, y=r // 2, c=r % 2)

    def moved(self, axis, k):
        size = self.sizes[axis]
        return dict(self.at, **{axis: lax.rem(self.at[axis] + k, size)})

    def device(self, at):
        return {"seq": at["z"] * self.X + at["x"], "row": at["y"] * 2 + at["c"]}

    def others(self, axis):
        return range(1, self.sizes[axis])

    def barrier(self, seq):
        sem = pltpu.get_barrier_semaphore()
        count = 0
        s, r = lax.axis_index("seq"), lax.axis_index("row")
        for k in range(1, seq):
            pl.semaphore_signal(
                sem, inc=1, device_id={"seq": lax.rem(s + k, seq), "row": r}, device_id_type=MESH
            )
            count += 1
        for axis in ("y", "c"):
            for k in self.others(axis):
                pl.semaphore_signal(
                    sem, inc=1, device_id=self.device(self.moved(axis, k)), device_id_type=MESH
                )
                count += 1
        pl.semaphore_wait(sem, count)


def remote(src, dst, send, recv, to):
    return pltpu.make_async_remote_copy(
        src_ref=src, dst_ref=dst, send_sem=send, recv_sem=recv, device_id=to, device_id_type=MESH
    )


def share_ends(table, own, send, recv, seq):
    s, r = lax.axis_index("seq"), lax.axis_index("row")
    table[s] = own

    def copy(k, where, to):
        return remote(table.at[where], table.at[where], send.at[k], recv.at[k], {"seq": to, "row": r})

    for k in range(1, seq):
        copy(k, s, lax.rem(s + k, seq)).start()
    for k in range(1, seq):
        back = lax.rem(s + seq - k, seq)
        copy(k, back, back).wait_recv()
    for k in range(1, seq):
        copy(k, s, lax.rem(s + k, seq)).wait_send()


def total_of(scale, state, backward):
    order = range(SUB - 1, -1, -1) if backward else range(SUB)
    whole_scale, whole_state = None, None
    for k in order:
        a, b = scale[k : k + 1], state[k : k + 1]
        if whole_scale is None:
            whole_scale, whole_state = a, b
        else:
            whole_scale, whole_state = a * whole_scale, a * whole_state + b
    return jnp.concatenate([whole_scale, whole_state], axis=0)


def entering(table, scale, state, seq, backward):
    s = lax.axis_index("seq")
    value = jnp.zeros_like(scale[:1])
    for k in range(seq - 1):
        if backward:
            k = seq - 1 - k
        longer = table[k, 0:1] * value + table[k, 1:2]
        value = jnp.where(k > s if backward else k < s, longer, value)
    out = [None] * SUB
    for k in range(SUB - 1, -1, -1) if backward else range(SUB):
        out[k] = value
        value = scale[k : k + 1] * value + state[k : k + 1]
    return jnp.concatenate(out, axis=0)


def gather_gates(
    seq, row, tag, u, keep, vin, w_own, *refs
):
    if tag == 0:
        (w_all, vec_out, low, mean, inv, f_out, g_out, cand_out, rpre_out, first,
         table, ends, n, proj, wbuf, f, g, cand, rpre, vall,
         snd, rcv, loc, outs, xsnd, xrcv, vsnd, vrcv) = refs
    else:
        (w_all, low, mean, inv, f_out, g_out, cand_out, rpre_out, first,
         table, ends, n, proj, wbuf, f, g, cand, rpre,
         snd, rcv, loc, outs, xsnd, xrcv) = refs
    pos = Place(seq, row)
    at = pos.at
    z, x, y, c = (at[k] for k in "zxyc")
    steps, _, d = u.shape
    parts = w_own.shape[0]
    pos.barrier(seq)
    every = slice(None)

    def region(ref, head, stage, h, who):
        first_axis = ("y", "x")[h]
        spot = [who["z"], who["x"], who["y"], who["c"]]
        if stage >= 1:
            spot[0] = every
        if stage >= 2:
            spot[2 if first_axis == "y" else 1] = every
        if stage >= 3:
            spot[1] = spot[2] = every
        return ref.at[head + tuple(spot)]

    def axis_of(stage, h):
        return ("z", ("y", "x")[h], ("x", "y")[h], "c")[stage]

    base = (0, pos.Z - 1, pos.Z - 1 + pos.X - 1, pos.Z - 1 + pos.X - 1 + pos.Y - 1)

    def copies(m, stage, h, arriving):
        axis = axis_of(stage, h)
        size = pos.sizes[axis]
        for k in pos.others(axis):
            k_sem = base[stage] + k - 1
            to = pos.moved(axis, k)
            who = pos.moved(axis, size - k) if arriving else at
            mine = region(w_all, (m, h), stage, h, who)
            src = w_own.at[m, h] if stage == 0 and not arriving else mine
            yield remote(src, mine, snd.at[h, m, k_sem], rcv.at[h, m, k_sem], pos.device(to))

    def local(m, h):
        return pltpu.make_async_copy(
            w_own.at[m, h], w_all.at[m, h, z, x, y, c], loc.at[h, m]
        )

    def begin(m):
        for h in range(2):
            local(m, h).start()
            for copy in copies(m, 0, h, False):
                copy.start()

    def advance(m, stage):
        for h in range(2):
            if stage == 1:
                local(m, h).wait()
            for copy in copies(m, stage - 1, h, True):
                copy.wait_recv()
            if stage < 4:
                for copy in copies(m, stage, h, False):
                    copy.start()

    def load(m, h):
        return pltpu.make_async_copy(
            w_all.at[m, h],
            wbuf.at[lax.rem(m, 2), :, :, :, :, :, pl.ds(h * HALF, HALF)],
            loc.at[h, parts + lax.rem(m, 2)],
        )

    def vcopies(stage, arriving):
        axis = axis_of(stage, 0)
        size = pos.sizes[axis]
        for k in pos.others(axis):
            k_sem = base[stage] + k - 1
            to = pos.moved(axis, k)
            who = pos.moved(axis, size - k) if arriving else at
            mine = region(vall, (), stage, 0, who)
            yield remote(mine, mine, vsnd.at[k_sem], vrcv.at[k_sem], pos.device(to))

    if tag == 0:
        vall[z, x, y, c] = vin[...]
        for copy in vcopies(0, False):
            copy.start()
    begin(0)
    begin(1)
    if tag == 0:
        for stage in range(1, 5):
            for copy in vcopies(stage - 1, True):
                copy.wait_recv()
            if stage < 4:
                for copy in vcopies(stage, False):
                    copy.start()
        per = d // (seq * row)
        rows = []
        for q in range(d // LANE):
            pieces = []
            for e in range(LANE // per):
                i = q * (LANE // per) + e
                spot = (i // (2 * pos.Y * pos.X), i // (2 * pos.Y) % pos.X, i // 2 % pos.Y, i % 2)
                pieces.append(vall[spot][:, :per].astype(F32))
            rows.append(jnp.concatenate(pieces, axis=-1))
        for q, value in enumerate(rows):
            for l in range(2):
                vec_out[l, :, q * LANE : (q + 1) * LANE] = value[l * 8 : l * 8 + 8]
        vec = vec_out.at[0]
    else:
        vec = vin
    norm_rows(u, vec, n, low, mean, inv)

    def gates(m):
        for h in range(2):
            load(m, h).wait()
        w = wbuf[lax.rem(m, 2)].reshape(d, 2 * HALF)
        proj[...] = jnp.dot(low[...], w, preferred_element_type=F32).reshape(steps, SUB, 2 * HALF)
        for h in range(2):
            cols = pl.ds(pl.multiple_of(m * 2 * LANE + h * LANE, LANE), LANE)
            peep, bias, rbias = (
                jnp.broadcast_to(vec[k : k + 1, cols], (SUB, LANE)) for k in (FPEEP, FBIAS, RBIAS)
            )
            off = h * HALF

            def one(i, carry):
                scale, state = carry
                cd = proj[i, :, off : off + LANE]
                zf = proj[i, :, off + LANE : off + 2 * LANE] + peep * n[i, :, cols] + bias
                up, down = both_sigmoids(zf)
                f[i, :, cols] = up
                g[i, :, cols] = down
                cand[i, :, cols] = cd
                rpre[i, :, cols] = proj[i, :, off + 2 * LANE : off + 3 * LANE] + rbias
                a = up * keep[i]
                return scale * a, a * state + down * cd

            start = jnp.ones((SUB, LANE), F32), jnp.zeros((SUB, LANE), F32)
            scale, state = lax.fori_loop(0, steps, one, start, unroll=8)
            ends[0, :, cols] = scale
            ends[1, :, cols] = state
        for copy in stash(m):
            copy.start()

    def stash(m):
        cols = pl.ds(pl.multiple_of(m * 2 * LANE, 2 * LANE), 2 * LANE)
        for k, (src, dst) in enumerate(
            ((f, f_out), (g, g_out), (cand, cand_out), (rpre, rpre_out))
        ):
            yield pltpu.make_async_copy(src.at[:, :, cols], dst.at[:, :, cols], outs.at[k, m])

    def turn(i, _):
        @pl.when(i + 2 < parts)
        def _():
            begin(i + 2)

        for stage in range(1, 5):
            m = i - (stage - 1)

            @pl.when((m >= 0) & (m < parts))
            def _():
                advance(m, stage)
                if stage == 4:
                    for h in range(2):
                        load(m, h).start()

        @pl.when(i >= 4)
        def _():
            gates(i - 4)

        return 0

    lax.fori_loop(0, parts + 4, turn, 0)

    scale, state = ends[0], ends[1]
    share_ends(table, total_of(scale, state, False), xsnd, xrcv, seq)
    first[...] = entering(table, scale, state, seq, False)

    def finish(m, _):
        for h in range(2):
            for stage in range(4):
                for copy in copies(m, stage, h, False):
                    copy.wait_send()
        for copy in stash(m):
            copy.wait()
        return 0

    lax.fori_loop(0, parts, finish, 0)
    if tag == 0:
        for stage in range(4):
            for copy in vcopies(stage, False):
                copy.wait_send()


def call_gather(seq, row, tag, u, keep, vin, w_own):
    steps, _, d = u.shape
    parts, _, per, _ = w_own.shape
    Y = row // 2
    X = Y
    Z = seq // X
    act, stat = arr(steps, SUB, d), arr(steps, SUB, LANE)
    vmem = pl.BlockSpec(memory_space=pltpu.VMEM)
    hbm = pl.BlockSpec(memory_space=pl.ANY)
    count = Z + X + Y - 2
    dma = pltpu.SemaphoreType.DMA
    big = pltpu.VMEM((steps, SUB, d), F32)
    return pl.pallas_call(
        lambda *refs: gather_gates(seq, row, tag, *refs),
        in_specs=[vmem, vmem, vmem, hbm],
        out_specs=[hbm] + [vmem] * (tag == 0) + [vmem] * 3 + [hbm] * 4 + [vmem],
        out_shape=[arr(parts, 2, Z, X, Y, 2, per, HALF, dtype=BF16)]
        + [arr(2, 8, d)] * (tag == 0)
        + [arr(steps * SUB, d, dtype=BF16), stat, stat]
        + [act] * 4
        + [arr(SUB, d)],
        scratch_shapes=[
            pltpu.VMEM((seq, 2, d), F32),
            pltpu.VMEM((2, SUB, d), F32),
            big,
            pltpu.VMEM((steps, SUB, 2 * HALF), F32),
            pltpu.VMEM((2, Z, X, Y, 2, per, 2 * HALF), BF16),
            big, big, big, big,
        ]
        + [pltpu.VMEM((Z, X, Y, 2, 16, LANE), BF16)] * (tag == 0)
        + [
            dma((2, parts, count)),
            dma((2, parts, count)),
            dma((2, parts + 2)),
            dma((4, parts)),
            dma((seq,)),
            dma((seq,)),
        ]
        + [dma((count,)), dma((count,))] * (tag == 0),
        compiler_params=pltpu.CompilerParams(
            collective_id=tag, has_side_effects=True, vmem_limit_bytes=60 << 20
        ),
        name="gather_gates" + str(tag),
    )(u, keep, vin, w_own)


SLOTS = 4


def scatter_weight(
    seq, row, low_t, du, out, send0, recv0, keep1, send1, recv1, keep2, send2, recv2, keep3,
    send3, recv3, done, snd, rcv, outs
):
    pos = Place(seq, row)
    at = pos.at
    parts = du.shape[0]
    _, Z, X, Y, per, t = low_t.shape
    pos.barrier(seq)
    every = slice(None)
    base = (0, 1, 1 + max(X, Y) - 1, 1 + 2 * (max(X, Y) - 1))

    def axis_of(stage, h):
        return ("c", ("x", "y")[h], ("y", "x")[h], "z")[stage]

    bufs = ((send0, recv0), (send1, recv1), (send2, recv2), (send3, recv3))

    def copy(m, stage, h, k):
        slot = lax.rem(m, SLOTS)
        send, recv = bufs[stage]
        sem = base[stage] + k - 1
        to = pos.device(pos.moved(axis_of(stage, h), k))
        return remote(
            send.at[slot, h, k - 1], recv.at[slot, h, k - 1],
            snd.at[slot, h, sem], rcv.at[slot, h, sem], to,
        )

    def ready(m, stage, h):
        for k in pos.others(axis_of(stage, h)):
            @pl.when(m >= SLOTS)
            def _():
                copy(m, stage, h, k).wait_send()

    def start(m, stage, h):
        for k in pos.others(axis_of(stage, h)):
            copy(m, stage, h, k).start()

    def arrive(m, stage, h):
        for k in pos.others(axis_of(stage, h)):
            copy(m, stage, h, k).wait_recv()

    def stage0(m):
        slot = lax.rem(m, SLOTS)
        rows = low_t[1 - at["c"]].reshape(-1, t)
        for h in range(2):
            ready(m, 0, h)
            v = jnp.dot(rows, du[m, h], preferred_element_type=F32).astype(BF16)
            send0[slot, h, 0] = v.reshape(Z, X, Y, per, HALF)
            start(m, 0, h)

    def stage1(m):
        slot = lax.rem(m, SLOTS)
        for h in range(2):
            axis = axis_of(1, h)
            arrive(m, 0, h)
            ready(m, 1, h)
            for k in range(pos.sizes[axis]):
                p = pos.moved(axis, k)[axis]
                where = (every, p) if h == 0 else (every, every, p)
                rows = low_t[(at["c"],) + where].reshape(-1, t)
                v = jnp.dot(rows, du[m, h], preferred_element_type=F32)
                got = recv0[(slot, h, 0) + where]
                v = v.reshape(got.shape) + got.astype(F32)
                if k == 0:
                    keep1[slot, h] = v
                else:
                    send1[slot, h, k - 1] = v.astype(BF16)
            start(m, 1, h)

    def stage2(m):
        slot = lax.rem(m, SLOTS)
        for h in range(2):
            axis = axis_of(2, h)
            arrive(m, 1, h)
            ready(m, 2, h)
            for k in range(pos.sizes[axis]):
                p = pos.moved(axis, k)[axis]
                v = keep1[slot, h, :, p]
                for e in pos.others(axis_of(1, h)):
                    v = v + recv1[slot, h, e - 1, :, p].astype(F32)
                if k == 0:
                    keep2[slot, h] = v
                else:
                    send2[slot, h, k - 1] = v.astype(BF16)
            start(m, 2, h)

    def stage3(m):
        slot = lax.rem(m, SLOTS)
        for h in range(2):
            arrive(m, 2, h)
            ready(m, 3, h)
            for k in range(Z):
                p = pos.moved("z", k)["z"]
                v = keep2[slot, h, p]
                for e in pos.others(axis_of(2, h)):
                    v = v + recv2[slot, h, e - 1, p].astype(F32)
                if k == 0:
                    keep3[slot, h] = v
                else:
                    send3[slot, h, k - 1] = v.astype(BF16)
            start(m, 3, h)

    def result(m, h, e):
        d = out.shape[-1] // 3
        cols = pl.ds(pl.multiple_of(e * d + (2 * m + h) * LANE, LANE), LANE)
        return pltpu.make_async_copy(
            done.at[m, h, :, e * LANE : (e + 1) * LANE], out.at[:, cols], outs.at[m, h, e]
        )

    def stage4(m):
        slot = lax.rem(m, SLOTS)
        for h in range(2):
            arrive(m, 3, h)
            v = keep3[slot, h]
            for k in range(1, Z):
                v = v + recv3[slot, h, k - 1].astype(F32)
            done[m, h] = v
            for e in range(3):
                result(m, h, e).start()

    def turn(i, _):
        for stage, act in enumerate((stage0, stage1, stage2, stage3, stage4)):
            m = i - stage

            @pl.when((m >= 0) & (m < parts))
            def _():
                act(m)

        return 0

    lax.fori_loop(0, parts + 4, turn, 0)

    def finish(m, _):
        for stage in range(4):
            for h in range(2):
                for k in pos.others(axis_of(stage, h)):
                    copy(m, stage, h, k).wait_send()
        return 0

    lax.fori_loop(max(parts - SLOTS, 0), parts, finish, 0)

    def written(m, _):
        for h in range(2):
            for e in range(3):
                result(m, h, e).wait()
        return 0

    lax.fori_loop(0, parts, written, 0)


def call_scatter(seq, row, tag, low_t, du, d):
    parts, _, t, _ = du.shape
    _, Z, X, Y, per, _ = low_t.shape
    vmem = pl.BlockSpec(memory_space=pltpu.VMEM)
    count = 1 + 2 * (X - 1) + Z - 1
    dma = pltpu.SemaphoreType.DMA

    def buf(*shape, dtype=BF16):
        return pltpu.VMEM((SLOTS, 2) + shape, dtype)

    one, two, three = (Z, Y, per, HALF), (Z, per, HALF), (per, HALF)
    return pl.pallas_call(
        lambda *refs: scatter_weight(seq, row, *refs),
        in_specs=[vmem, vmem],
        out_specs=pl.BlockSpec(memory_space=pl.ANY),
        out_shape=arr(per, 3 * d),
        scratch_shapes=[
            buf(1, Z, X, Y, per, HALF), buf(1, Z, X, Y, per, HALF),
            buf(*one, dtype=F32), buf(X - 1, *one), buf(X - 1, *one),
            buf(*two, dtype=F32), buf(Y - 1, *two), buf(Y - 1, *two),
            buf(*three, dtype=F32), buf(Z - 1, *three), buf(Z - 1, *three),
            pltpu.VMEM((parts, 2, per, HALF), F32),
            dma((SLOTS, 2, count)), dma((SLOTS, 2, count)), dma((parts, 2, 3)),
        ],
        compiler_params=pltpu.CompilerParams(
            collective_id=tag, has_side_effects=True, vmem_limit_bytes=60 << 20
        ),
        name="scatter_weight" + str(tag),
    )(low_t, du)


def columns(steps, width):
    return pl.BlockSpec((steps, SUB, width), lambda j: (0, 0, j))


def whole(*shape):
    return pl.BlockSpec(shape, lambda j: (0,) * len(shape))


def vectors(width):
    return pl.BlockSpec((8, width), lambda j: (0, j))


def arr(*shape, dtype=F32):
    return jax.ShapeDtypeStruct(shape, dtype)


def chain(ends, axis, backward):
    everyone = lax.all_gather(ends, axis)
    count, mine = lax.axis_size(axis), lax.axis_index(axis)
    segments, d = ends.shape[1:]
    total = count * segments
    scale = everyone[:, 0].reshape(total, d)
    state = everyone[:, 1].reshape(total, d)
    if backward:
        scale, state = scale[::-1], state[::-1]
    value = jnp.zeros((d,), F32)
    entering = []
    for k in range(total):
        entering.append(value)
        value = scale[k] * value + state[k]
    entering = jnp.stack(entering)
    if backward:
        entering = entering[::-1]
    return lax.dynamic_slice_in_dim(entering, mine * segments, segments, 0)


def body(tokens, resets, cotangent, weight, *rows):
    _, t, d = tokens.shape
    layers = weight.shape[0]
    steps = t // SUB
    parts = d // WIDE
    axes = ("seq", "row")
    seq, row = lax.axis_size("seq"), lax.axis_size("row")
    Y = row // 2
    X = Y
    Z = seq // X

    def permuted(x):
        return x.reshape(SUB, steps, -1).transpose(1, 0, 2)

    def restored(x):
        return x.reshape(steps, SUB, d).transpose(1, 0, 2).reshape(1, t, d)

    keep = permuted((1 - resets[0]).astype(F32)[:, None])
    keep = jnp.broadcast_to(keep, (steps, SUB, LANE))
    per = rows[0].shape[-1]
    packed = jnp.stack(rows + (jnp.zeros_like(rows[0]),) * 2, axis=1).reshape(2 * 8, per)
    packed = jnp.pad(packed, ((0, 0), (0, LANE - per)))
    local = weight.reshape(layers, -1, 3, parts, 2, LANE).transpose(0, 3, 4, 1, 2, 5)
    local = local.reshape(layers, parts, 2, -1, HALF)

    u = permuted(tokens).astype(F32)
    stored = []
    col = columns(steps, WIDE)
    keep_spec = whole(steps, SUB, 128)
    w_spec = pl.BlockSpec((1, 2, d, HALF), lambda j: (j, 0, 0, 0))
    du_spec = pl.BlockSpec((1, 2, t, HALF), lambda j: (j, 0, 0, 0))
    act = arr(steps, SUB, d)
    for l in range(layers):
        if l == 0:
            full, every, low, mean, inv, f, g, cand, rpre, first = call_gather(
                seq, row, 0, u, keep, packed, local[0]
            )
        else:
            full, low, mean, inv, f, g, cand, rpre, first = call_gather(
                seq, row, 1, u, keep, every[1], local[1]
            )
        vec = every[l]
        p, r, out = pl.pallas_call(
            forward_states,
            grid=(parts,),
            in_specs=[col] * 5 + [keep_spec, vectors(WIDE), vectors(WIDE)],
            out_specs=[col] * 3,
            out_shape=[act] * 3,
            compiler_params=params(),
            name="forward_states",
        )(f, g, cand, rpre, u, keep, vec, first)
        stored.append((u, low, mean, inv, f, g, cand, p, r, full.reshape(parts, 2, d, HALF)))
        u = out
    result = restored(u.astype(BF16))

    dh = permuted(cotangent).astype(F32)
    weight_grads, vector_grads = [None] * layers, [None] * layers
    for l in reversed(range(layers)):
        vec = every[l]
        u, low, mean, inv, f, g, cand, p, r, full = stored[l]
        ends = pl.pallas_call(
            backward_ends,
            grid=(parts,),
            in_specs=[col] * 7 + [keep_spec, vectors(WIDE)],
            out_specs=pl.BlockSpec((2, SUB, WIDE), lambda j: (0, 0, j)),
            out_shape=arr(2, SUB, d),
            compiler_params=params(),
            name="backward_ends",
        )(dh, f, g, cand, p, r, u, keep, vec)
        first = chain(ends, "seq", True)
        du, dzf, sums = pl.pallas_call(
            backward_states,
            grid=(parts,),
            in_specs=[col] * 7 + [keep_spec, vectors(WIDE), keep_spec, keep_spec, vectors(WIDE)],
            out_specs=[du_spec, col, pl.BlockSpec((4, SUB, WIDE), lambda j: (0, 0, j))],
            out_shape=[arr(parts, 2, t, HALF, dtype=BF16), act, arr(4, SUB, d)],
            scratch_shapes=[pltpu.VMEM((3, steps, SUB, WIDE), F32)],
            compiler_params=params(),
            name="backward_states",
        )(dh, f, g, cand, p, r, u, keep, vec, mean, inv, first)
        low_t = low.T.reshape(Z, X, Y, 2, per, t).transpose(3, 0, 1, 2, 4, 5)
        weight_grads[l] = call_scatter(seq, row, 2 + l, low_t, du, d)
        dh, more = pl.pallas_call(
            input_side,
            grid=(parts,),
            in_specs=[du_spec, w_spec]
            + [whole(steps, SUB, d)] * 4
            + [keep_spec, keep_spec, whole(8, d)],
            out_specs=[whole(steps, SUB, d), whole(2, SUB, d)],
            out_shape=[act, arr(2, SUB, d)],
            scratch_shapes=[pltpu.VMEM((steps, SUB, d), F32)],
            compiler_params=params(),
            name="input_side",
        )(du, full, dzf, u, dh, r, mean, inv, vec)
        vector_grads[l] = jnp.concatenate([more.sum(1), sums.sum(1)])
    input_grad = restored(dh.astype(BF16))
    vector_out = lax.psum_scatter(
        jnp.stack(vector_grads), axes, scatter_dimension=2, tiled=True
    )
    return (result, input_grad, jnp.stack(weight_grads)) + tuple(
        vector_out[:, k] for k in range(6)
    )


def solution(mesh):
    tokens = P("row", "seq", None)
    rows = P(None, ("seq", "row"))
    weight = P(None, ("seq", "row"), None)
    return jax.shard_map(
        body,
        mesh=mesh,
        in_specs=(tokens, P("row", "seq"), tokens, weight) + (rows,) * 6,
        out_specs=(tokens, tokens, weight) + (rows,) * 6,
        check_vma=False,
    )
```

```python
import jax
import jax.numpy as jnp
from jax import lax
from jax.experimental import pallas as pl
from jax.experimental.pallas import tpu as pltpu
from jax.sharding import PartitionSpec as P

epsilon = 1e-05
SUB = 8
WIDE = 256
F32 = jnp.float32
BF16 = jnp.bfloat16
GAIN, SHIFT, FPEEP, RPEEP, FBIAS, RBIAS = range(6)


def both_sigmoids(z):
    tail = jnp.exp(-jnp.abs(z))
    big = 1.0 / (1.0 + tail)
    small = tail * big
    up = z >= 0
    return jnp.where(up, big, small), jnp.where(up, small, big)


def lanes(value, width):
    return jnp.concatenate([value] * (width // value.shape[-1]), axis=-1)


def arr(*shape, dtype=F32):
    return jax.ShapeDtypeStruct(shape, dtype)


MESH = pl.DeviceIdType.MESH
HALF = 384
LANE = 128


class Place:
    def __init__(self, seq, row):
        self.Y = row // 2
        self.X = self.Y
        self.Z = seq // self.X
        self.C = 2
        self.sizes = dict(z=self.Z, x=self.X, y=self.Y, c=self.C)
        s, r = lax.axis_index("seq"), lax.axis_index("row")
        self.at = dict(z=s // self.X, x=s % self.X, y=r // 2, c=r % 2)
        self.zl = lax.rem(self.at["z"], 2)

    def moved(self, axis, k):
        size = self.sizes[axis]
        return dict(self.at, **{axis: lax.rem(self.at[axis] + k, size)})

    def device(self, at):
        return {"seq": at["z"] * self.X + at["x"], "row": at["y"] * 2 + at["c"]}

    def others(self, axis):
        return range(1, self.sizes[axis])

    def barrier(self, seq):
        sem = pltpu.get_barrier_semaphore()
        count = 0
        s, r = lax.axis_index("seq"), lax.axis_index("row")
        for k in range(1, seq):
            pl.semaphore_signal(
                sem, inc=1, device_id={"seq": lax.rem(s + k, seq), "row": r}, device_id_type=MESH
            )
            count += 1
        for axis in ("y", "c"):
            for k in self.others(axis):
                pl.semaphore_signal(
                    sem, inc=1, device_id=self.device(self.moved(axis, k)), device_id_type=MESH
                )
                count += 1
        pl.semaphore_wait(sem, count)


def remote(src, dst, send, recv, to):
    return pltpu.make_async_remote_copy(
        src_ref=src, dst_ref=dst, send_sem=send, recv_sem=recv, device_id=to, device_id_type=MESH
    )


def total_of(scale, state, backward):
    order = range(SUB - 1, -1, -1) if backward else range(SUB)
    whole_scale, whole_state = None, None
    for k in order:
        a, b = scale[k : k + 1], state[k : k + 1]
        if whole_scale is None:
            whole_scale, whole_state = a, b
        else:
            whole_scale, whole_state = a * whole_scale, a * whole_state + b
    return jnp.concatenate([whole_scale, whole_state], axis=0)


class Gather:
    def __init__(self, pos, parts, w_own, w_all, snd, rcv, loc):
        self.pos, self.parts = pos, parts
        self.w_own, self.w_all, self.snd, self.rcv, self.loc = w_own, w_all, snd, rcv, loc
        z, x, y = pos.Z - 1, pos.X - 1, pos.Y - 1
        self.base = (0, z, z + max(x, y), z + 2 * max(x, y))

    def axis(self, stage, h):
        return ("z", ("y", "x")[h], ("x", "y")[h], "c")[stage]

    def region(self, ref, head, stage, h, who):
        every = slice(None)
        spot = [who["z"], who["x"], who["y"], who["c"]]
        if stage >= 1:
            spot[0] = every
        if stage >= 2:
            spot[2 if h == 0 else 1] = every
        if stage >= 3:
            spot[1] = spot[2] = every
        return ref.at[head + tuple(spot)]

    def copies(self, g, stage, h, arriving):
        pos, axis = self.pos, self.axis(stage, h)
        l, m = g // self.parts, lax.rem(g, self.parts)
        size = pos.sizes[axis]
        for k in pos.others(axis):
            sem = self.base[stage] + k - 1
            to = pos.moved(axis, k)
            who = pos.moved(axis, size - k) if arriving else pos.at
            mine = self.region(self.w_all, (l, m, h), stage, h, who)
            src = mine
            if stage == 0 and not arriving:
                src = self.w_own.at[l, lax.rem(to["z"], 2), m, h]
            yield remote(src, mine, self.snd.at[h, g, sem], self.rcv.at[h, g, sem], pos.device(to))

    def local(self, g, h):
        at = self.pos.at
        l, m = g // self.parts, lax.rem(g, self.parts)
        return pltpu.make_async_copy(
            self.w_own.at[l, self.pos.zl, m, h],
            self.w_all.at[l, m, h, at["z"], at["x"], at["y"], at["c"]],
            self.loc.at[h, g],
        )

    def begin(self, g):
        for h in range(2):
            self.local(g, h).start()
            for copy in self.copies(g, 0, h, False):
                copy.start()

    def advance(self, g, stage):
        for h in range(2):
            if stage == 1:
                self.local(g, h).wait()
            for copy in self.copies(g, stage - 1, h, True):
                copy.wait_recv()
            if stage < 4:
                for copy in self.copies(g, stage, h, False):
                    copy.start()

    def turn(self, i):
        total = 2 * self.parts

        @pl.when(i + 2 < total)
        def _():
            self.begin(i + 2)

        for stage in range(1, 5):
            g = i - (stage - 1)

            @pl.when((g >= 0) & (g < total))
            def _():
                self.advance(g, stage)

    def finish(self):
        def one(g, _):
            for h in range(2):
                for stage in range(4):
                    for copy in self.copies(g, stage, h, False):
                        copy.wait_send()
            return 0

        lax.fori_loop(0, 2 * self.parts, one, 0)


class Chain:
    def __init__(self, pos, table, snd, rcv):
        self.pos, self.table, self.snd, self.rcv = pos, table, snd, rcv

    def run(self, ends, first, backward):
        pos, table = self.pos, self.table
        zh, x = pos.at["z"] // 2, pos.at["x"]
        r = lax.axis_index("row")
        for b in range(2):
            table[zh, x, b] = total_of(ends[b, 0], ends[b, 1], backward)
        moves = [(i, j) for i in range(pos.Z // 2) for j in range(pos.X) if i or j]

        def copy(k, sign):
            i, j = moves[k]
            there = lax.rem(zh + i, pos.Z // 2), lax.rem(x + j, pos.X)
            back = lax.rem(zh + pos.Z // 2 - i, pos.Z // 2), lax.rem(x + pos.X - j, pos.X)
            spot = (zh, x) if sign > 0 else back
            to = {"seq": (2 * there[0] + pos.zl) * pos.X + there[1], "row": r}
            return remote(table.at[spot], table.at[spot], self.snd.at[k], self.rcv.at[k], to)

        for k in range(len(moves)):
            copy(k, 1).start()
        for k in range(len(moves)):
            copy(k, -1).wait_recv()
        for k in range(len(moves)):
            copy(k, 1).wait_send()
        blocks = [(i, b, j) for i in range(pos.Z // 2) for b in range(2) for j in range(pos.X)]
        if backward:
            blocks = blocks[::-1]
        value = jnp.zeros_like(table[0, 0, 0, 0:1])
        mine = [value, value]
        for i, b, j in blocks:
            here = (i == zh) & (j == x)
            mine[b] = jnp.where(here, value, mine[b])
            value = table[i, j, b, 0:1] * value + table[i, j, b, 1:2]
        for b in range(2):
            value = mine[b]
            for k in range(SUB - 1, -1, -1) if backward else range(SUB):
                first[b, k : k + 1] = value
                value = ends[b, 0, k : k + 1] * value + ends[b, 1, k : k + 1]


def diagonal():
    return lax.broadcasted_iota(jnp.int32, (LANE, LANE), 0) == lax.broadcasted_iota(
        jnp.int32, (LANE, LANE), 1
    )


def to_row(column):
    spread = jnp.broadcast_to(column, (LANE, LANE))
    return jnp.sum(jnp.where(diagonal(), spread, 0.0), axis=0, keepdims=True)


def to_column(line):
    spread = jnp.broadcast_to(line, (LANE, LANE))
    return jnp.sum(jnp.where(diagonal(), spread, 0.0), axis=1, keepdims=True)


def spread_rows(column):
    return jnp.broadcast_to(column, (LANE, LANE)).reshape(LANE // SUB, SUB, LANE)


def lane_tile(m, width):
    return pl.ds(pl.multiple_of(m * width, width), width)


def forward_all(
    seq, row, tok, cot, keep_in, vin, w_own,
    w_all, vec, keep, stats, f0, g0, cand0, p0, r0, u0, low0, low1, u1, dhr1, dn1, du1, result,
    sums, tokbuf, cotbuf, keepc, vall, u, np_, f, g, cand, rpre, low, wbuf, proj, du, resbuf, top_of, ends,
    first, tables, st_own, st_got, st_fin,
    gsnd, grcv, gloc, vsnd, vrcv, wsem, psnd, prcv, csnd, crcv, outs,
):
    pos = Place(seq, row)
    at, zl = pos.at, pos.zl
    z, x, y, c = (at[k] for k in "zxyc")
    _, t, d = tokbuf.shape
    steps, H = u.shape[1], u.shape[3]
    parts = w_own.shape[2]
    partner = pos.device(dict(at, z=z + 1 - 2 * zl))
    own = pl.ds(pl.multiple_of(zl * H, H), H)
    other = pl.ds(pl.multiple_of((1 - zl) * H, H), H)
    rows_of = lambda b: pl.ds(pl.multiple_of(b * t, t), t)
    pos.barrier(seq)

    gather = Gather(pos, parts, w_own, w_all, gsnd, grcv, gloc)
    chains = [Chain(pos, tables.at[k], csnd.at[k], crcv.at[k]) for k in range(3)]

    def pair(k, src, dst):
        return remote(src, dst, psnd.at[k], prcv.at[k], partner)

    def tokens(b):
        return pair(0, tok, tokbuf.at[b])

    def cotangents(b):
        return pair(1, cot.at[:, other], cotbuf.at[b])

    def keeps(b):
        return pair(2, keepc.at[b], keepc.at[b])

    def statistics(b, to):
        return pair(3 + b, st_own.at[b], to.at[b])

    def lows(b, cols):
        return pair(5 + b, low.at[rows_of(b), cols], low.at[rows_of(b), cols])

    def results(cols):
        return pair(7, resbuf.at[1 - zl], result.at[:, cols])

    def vcopies(stage, arriving):
        axis = gather.axis(stage, 0)
        size = pos.sizes[axis]
        for k in pos.others(axis):
            sem = gather.base[stage] + k - 1
            to = pos.moved(axis, k)
            who = pos.moved(axis, size - k) if arriving else at
            mine = gather.region(vall, (), stage, 0, who)
            yield remote(mine, mine, vsnd.at[sem], vrcv.at[sem], pos.device(to))

    def vadvance(stage):
        for copy in vcopies(stage - 1, True):
            copy.wait_recv()
        if stage < 4:
            for copy in vcopies(stage, False):
                copy.start()

    own_tokens = pltpu.make_async_copy(tok, tokbuf.at[zl], outs.at[0])
    own_cot = pltpu.make_async_copy(cot.at[:, own], cotbuf.at[zl], outs.at[1])
    vall[z, x, y, c] = vin[...]
    keepc[zl] = keep_in[...]
    own_tokens.start()
    own_cot.start()
    for copy in vcopies(0, False):
        copy.start()
    keeps(zl).start()
    gather.begin(0)
    gather.begin(1)
    tokens(zl).start()
    vadvance(1)
    gather.turn(0)
    vadvance(2)
    vadvance(3)
    gather.turn(1)
    vadvance(4)

    per = d // (seq * row)
    for q in range(d // LANE):
        pieces = []
        for e in range(LANE // per):
            i = q * (LANE // per) + e
            spot = (i // (2 * pos.Y * pos.X), i // (2 * pos.Y) % pos.X, i // 2 % pos.Y, i % 2)
            pieces.append(vall[spot][:, :per].astype(F32))
        value = jnp.concatenate(pieces, axis=-1)
        for l in range(2):
            vec[l, :, q * LANE : (q + 1) * LANE] = value[l * 8 : l * 8 + 8]
    keeps(1 - zl).wait_recv()
    for b in range(2):
        for q in range(t // LANE):
            piece = spread_rows(to_column(keepc[b, q : q + 1, :]))
            keep[b, q * (LANE // SUB) : (q + 1) * (LANE // SUB)] = piece

    def norm0(b):
        piece = 8

        def one(k, _):
            rows = pl.ds(pl.multiple_of(k * piece * SUB, piece * SUB), piece * SUB)
            spot = pl.ds(k * piece, piece)
            v = tokbuf[b, rows, :].astype(F32)
            mu = jnp.mean(v, axis=-1, keepdims=True)
            v = v - mu
            rstd = lax.rsqrt(jnp.mean(v * v, axis=-1, keepdims=True) + epsilon)
            v = v * rstd * vec[0, GAIN : GAIN + 1, :] + vec[0, SHIFT : SHIFT + 1, :]
            at_rows = pl.ds(pl.multiple_of(b * t + k * piece * SUB, piece * SUB), piece * SUB)
            low[at_rows, :] = v.astype(BF16)
            v = tokbuf[b, rows, own].astype(F32)
            u[b, spot] = v.reshape(piece, SUB, H)
            v = (v - mu) * rstd * vec[0, GAIN : GAIN + 1, own] + vec[0, SHIFT : SHIFT + 1, own]
            np_[b, spot] = v.reshape(piece, SUB, H)
            stats[0, 0, b, spot] = jnp.broadcast_to(mu, (piece * SUB, LANE)).reshape(piece, SUB, LANE)
            stats[0, 1, b, spot] = jnp.broadcast_to(rstd, (piece * SUB, LANE)).reshape(
                piece, SUB, LANE
            )
            return 0

        lax.fori_loop(0, steps // piece, one, 0)

    def load(l, m, h):
        slot = lax.rem(m, 2)
        return pltpu.make_async_copy(
            w_all.at[l, m, h],
            wbuf.at[slot, :, :, :, :, :, pl.ds(h * HALF, HALF)],
            wsem.at[slot, h],
        )

    def start_load(l, m):
        for h in range(2):
            load(l, m, h).start()

    def gates(l, m, b):
        for h in range(2):
            load(l, m, h).wait()
        w = wbuf[lax.rem(m, 2)].reshape(d, 2 * HALF)
        v = jnp.dot(low[rows_of(b), :], w, preferred_element_type=F32)
        proj[...] = v.reshape(steps, SUB, 2 * HALF)
        cols = lane_tile(m, 2 * LANE)
        wide = pl.ds(pl.multiple_of(zl * H + m * 2 * LANE, 2 * LANE), 2 * LANE)
        peep, bias, rbias = (
            jnp.broadcast_to(vec[l, k : k + 1, wide], (SUB, 2 * LANE)) for k in (FPEEP, FBIAS, RBIAS)
        )

        def both(i, off):
            return jnp.concatenate(
                [proj[i, :, h * HALF + off : h * HALF + off + LANE] for h in range(2)], axis=-1
            )

        def one(i, carry):
            scale, state = carry
            cd = both(i, 0)
            up, down = both_sigmoids(both(i, LANE) + peep * np_[b, i, :, cols] + bias)
            f[b, i, :, cols] = up
            g[b, i, :, cols] = down
            cand[b, i, :, cols] = cd
            rpre[b, i, :, cols] = both(i, 2 * LANE) + rbias
            a = up * lanes(keep[b, i], 2 * LANE)
            return scale * a, a * state + down * cd

        start = jnp.ones((SUB, 2 * LANE), F32), jnp.zeros((SUB, 2 * LANE), F32)
        scale, state = lax.fori_loop(0, steps, one, start, unroll=8)
        ends[b, 0, :, cols] = scale
        ends[b, 1, :, cols] = state

    def pass_gates(l, b):
        start_load(l, 0)

        def one(m, _):
            @pl.when(m + 1 < parts)
            def _():
                start_load(l, m + 1)

            gates(l, m, b)
            return 0

        lax.fori_loop(0, parts, one, 0)

    def stash(k, src, dst):
        return pltpu.make_async_copy(src, dst, outs.at[k])

    own_tokens.wait()
    norm0(zl)

    def turn(i, _):
        gather.turn(i)

        @pl.when((i >= 3) & (i - 3 < parts))
        def _():
            start_load(0, i - 3)

        @pl.when(i >= 4)
        def _():
            gates(0, i - 4, zl)

        return 0

    lax.fori_loop(2, parts + 4, turn, 0)
    tokens(1 - zl).wait_recv()
    cotangents(zl).start()
    gather.turn(parts + 4)
    norm0(1 - zl)
    keep_u0, keep_low0 = stash(2, u, u0), stash(3, low, low0)
    keep_u0.start()
    keep_low0.start()
    pass_gates(0, 1 - zl)
    gates0 = [stash(4, f, f0), stash(5, g, g0), stash(6, cand, cand0)]
    for copy in gates0:
        copy.start()
    gather.turn(parts + 5)
    chains[0].run(ends, first, False)
    keep_u0.wait()
    keep_low0.wait()

    def states0(b):
        def tile(m, _):
            cols = lane_tile(m, 2 * LANE)
            wide = pl.ds(pl.multiple_of(zl * H + m * 2 * LANE, 2 * LANE), 2 * LANE)
            peep = jnp.broadcast_to(vec[0, RPEEP : RPEEP + 1, wide], (SUB, 2 * LANE))

            def one(i, cell):
                before = lanes(keep[b, i], 2 * LANE) * cell
                cell = f[b, i, :, cols] * before + g[b, i, :, cols] * cand[b, i, :, cols]
                gate = jax.nn.sigmoid(rpre[b, i, :, cols] + peep * before)
                np_[b, i, :, cols] = before
                rpre[b, i, :, cols] = gate
                u[b, i, :, cols] = gate * cell + (1.0 - gate) * u[b, i, :, cols]
                return cell

            lax.fori_loop(0, steps, one, first[b, :, cols], unroll=8)
            return 0

        lax.fori_loop(0, parts, tile, 0)

    def local_stats(b):
        def one(q, _):
            v = u[b, pl.ds(q * (LANE // SUB), LANE // SUB)].reshape(LANE, H)
            mu = jnp.mean(v, axis=-1, keepdims=True)
            v = v - mu
            square = jnp.sum(v * v, axis=-1, keepdims=True)
            st_own[b, pl.ds(q, 1), :] = to_row(mu)
            st_own[b, pl.ds(q + t // LANE, 1), :] = to_row(square)
            return 0

        lax.fori_loop(0, t // LANE, one, 0)
        statistics(b, st_got).start()

    def norm1(b):
        half = t // LANE
        statistics(b, st_got).wait_recv()
        m0, m1 = st_own[b, :half], st_got[b, :half]
        gap = m0 - m1
        square = st_own[b, half:] + st_got[b, half:] + gap * gap * (H / 2)
        st_fin[b, :half] = (m0 + m1) * 0.5
        st_fin[b, half:] = lax.rsqrt(square / (2 * H) + epsilon)

        def one(q, _):
            spot = pl.ds(q * (LANE // SUB), LANE // SUB)
            mu = to_column(st_fin[b, pl.ds(q, 1), :])
            rstd = to_column(st_fin[b, pl.ds(q + half, 1), :])
            v = u[b, spot].reshape(LANE, H)
            v = (v - mu) * rstd * vec[1, GAIN : GAIN + 1, own] + vec[1, SHIFT : SHIFT + 1, own]
            np_[b, spot] = v.reshape(LANE // SUB, SUB, H)
            low[pl.ds(pl.multiple_of(b * t + q * LANE, LANE), LANE), own] = v.astype(BF16)
            stats[1, 0, b, spot] = spread_rows(mu)
            stats[1, 1, b, spot] = spread_rows(rstd)
            return 0

        lax.fori_loop(0, half, one, 0)
        lows(b, own).start()

    states0(0)
    local_stats(0)
    gather.turn(parts + 6)
    states0(1)
    local_stats(1)
    later = [stash(7, np_, p0), stash(8, rpre, r0)]
    for copy in later:
        copy.start()
    for copy in later + gates0:
        copy.wait()
    norm1(0)
    norm1(1)
    for b in range(2):
        lows(b, other).wait_recv()
        pass_gates(1, b)
    keep_low1 = stash(2, low, low1)
    keep_low1.start()
    chains[1].run(ends, first, False)
    own_cot.wait()
    cotangents(1 - zl).wait_recv()

    def step_back(b, i, cols, top, peep):
        before, gate, up = np_[b, i, :, cols], rpre[b, i, :, cols], f[b, i, :, cols]
        cell = up * before + g[b, i, :, cols] * cand[b, i, :, cols]
        dz_r = top * (cell - u[b, i, :, cols]) * gate * (1.0 - gate)
        direct = top * gate
        kept = lanes(keep[b, i], 2 * LANE)
        decay = up * kept
        return before, gate, up, dz_r, direct, decay, kept * peep * dz_r + decay * direct

    def turn_round(b):
        def tile(m, _):
            cols = lane_tile(m, 2 * LANE)
            wide = pl.ds(pl.multiple_of(zl * H + m * 2 * LANE, 2 * LANE), 2 * LANE)
            peep = jnp.broadcast_to(vec[1, RPEEP : RPEEP + 1, wide], (SUB, 2 * LANE))
            top = cotbuf[b, :, cols].astype(F32).reshape(steps, SUB, 2 * LANE)
            proj[:, :, 2 * LANE : 4 * LANE] = top

            def one(i, cell):
                before = lanes(keep[b, i], 2 * LANE) * cell
                cell = f[b, i, :, cols] * before + g[b, i, :, cols] * cand[b, i, :, cols]
                gate = jax.nn.sigmoid(rpre[b, i, :, cols] + peep * before)
                np_[b, i, :, cols] = before
                rpre[b, i, :, cols] = gate
                proj[i, :, : 2 * LANE] = gate * cell + (1.0 - gate) * u[b, i, :, cols]
                return cell

            lax.fori_loop(0, steps, one, first[b, :, cols], unroll=8)
            v = proj[:, :, : 2 * LANE].reshape(t, 2 * LANE)
            resbuf[b, :, cols] = v.astype(BF16)

            def back(k, carry):
                scale, q = carry
                i = steps - 1 - k
                _, _, _, _, _, decay, term = step_back(
                    b, i, cols, proj[i, :, 2 * LANE : 4 * LANE], peep
                )
                return scale * decay, decay * q + term

            start = jnp.ones((SUB, 2 * LANE), F32), jnp.zeros((SUB, 2 * LANE), F32)
            scale, q = lax.fori_loop(0, steps, back, start, unroll=8)
            ends[b, 0, :, cols] = scale
            ends[b, 1, :, cols] = q
            return 0

        lax.fori_loop(0, parts, tile, 0)

    turn_round(0)
    turn_round(1)
    results(own).start()
    own_result = stash(9, resbuf.at[zl], result.at[:, own])
    own_result.start()
    chains[2].run(ends, first, True)

    def down(b):
        def tile(m, _):
            cols = lane_tile(m, 2 * LANE)
            wide = pl.ds(pl.multiple_of(zl * H + m * 2 * LANE, 2 * LANE), 2 * LANE)
            fpeep, rpeep, gain, shift = (
                jnp.broadcast_to(vec[1, k : k + 1, wide], (SUB, 2 * LANE))
                for k in (FPEEP, RPEEP, GAIN, SHIFT)
            )

            def one(k, carry):
                q, s0, s1, s2, s3 = carry
                i = steps - 1 - k
                top = top_of[i]
                before, gate, up, dz_r, direct, decay, term = step_back(b, i, cols, top, rpeep)
                e = direct + q
                low_f = g[b, i, :, cols]
                dz_f = e * (up * low_f) * (before - cand[b, i, :, cols])
                n = (u[b, i, :, cols] - lanes(stats[1, 0, b, i], 2 * LANE)) * lanes(
                    stats[1, 1, b, i], 2 * LANE
                ) * gain + shift
                proj[i, :, : 2 * LANE] = e * low_f
                proj[i, :, 2 * LANE : 4 * LANE] = dz_f
                proj[i, :, 4 * LANE :] = dz_r
                cand[b, i, :, cols] = dz_f * fpeep
                rpre[b, i, :, cols] = top * (1.0 - gate)
                return (
                    decay * q + term,
                    s0 + dz_f * n,
                    s1 + dz_r * before,
                    s2 + dz_f,
                    s3 + dz_r,
                )

            top_of[...] = cotbuf[b, :, cols].astype(F32).reshape(steps, SUB, 2 * LANE)
            zero = jnp.zeros((SUB, 2 * LANE), F32)
            carry = lax.fori_loop(0, steps, one, (first[b, :, cols], zero, zero, zero, zero), unroll=4)
            for k in range(4):
                sums[b, k, :, cols] = carry[k + 1]
            for h in range(2):
                for k in range(3):
                    v = proj[:, :, k * 2 * LANE + h * LANE : k * 2 * LANE + (h + 1) * LANE]
                    to = pl.ds(pl.multiple_of((2 * m + h) * HALF + k * LANE, LANE), LANE)
                    du[rows_of(b), to] = v.reshape(t, LANE).astype(BF16)
            return 0

        lax.fori_loop(0, parts, tile, 0)

    down(0)
    down(1)
    last = [
        stash(3, du, du1), stash(4, cand, dn1), stash(5, rpre, dhr1), stash(6, u, u1),
    ]
    for copy in last:
        copy.start()
    for copy in last + [keep_low1, own_result]:
        copy.wait()
    results(other).wait_recv()
    gather.finish()
    for stage in range(4):
        for copy in vcopies(stage, False):
            copy.wait_send()
    tokens(zl).wait_send()
    cotangents(zl).wait_send()
    keeps(zl).wait_send()
    for b in range(2):
        statistics(b, st_got).wait_send()
        lows(b, own).wait_send()
    results(own).wait_send()


def call_forward(seq, row, tok, cot, keep, vin, w_own):
    t, d = tok.shape
    layers, _, parts, _, per, _ = w_own.shape
    Y = row // 2
    X = Y
    Z = seq // X
    H = d // 2
    steps = t // SUB
    act, stat = arr(2, steps, SUB, H), arr(2, steps, SUB, LANE)
    half = arr(2 * t, d, dtype=BF16)
    vmem = pl.BlockSpec(memory_space=pltpu.VMEM)
    hbm = pl.BlockSpec(memory_space=pl.ANY)
    count = Z + 2 * X - 2
    dma = pltpu.SemaphoreType.DMA
    big = pltpu.VMEM((2, steps, SUB, H), F32)
    st = pltpu.VMEM((2, 8, LANE), F32)
    return pl.pallas_call(
        lambda *refs: forward_all(seq, row, *refs),
        in_specs=[hbm, hbm, vmem, vmem, hbm],
        out_specs=[hbm, vmem, vmem, vmem] + [hbm] * 13 + [vmem],
        out_shape=[
            arr(layers, parts, 2, Z, X, Y, 2, per, HALF, dtype=BF16),
            arr(2, 8, d),
            stat,
            arr(2, 2, 2, steps, SUB, LANE),
        ]
        + [act] * 6
        + [half, half, act, act, act, arr(2 * t, 3 * H, dtype=BF16), arr(t, d, dtype=BF16)]
        + [arr(2, 4, SUB, H)],
        scratch_shapes=[
            pltpu.VMEM((2, t, d), BF16),
            pltpu.VMEM((2, t, H), BF16),
            pltpu.VMEM((2, 8, LANE), F32),
            pltpu.VMEM((Z, X, Y, 2, 16, LANE), BF16),
            big, big, big, big, big, big,
            pltpu.VMEM((2 * t, d), BF16),
            pltpu.VMEM((2, Z, X, Y, 2, per, 2 * HALF), BF16),
            pltpu.VMEM((steps, SUB, 2 * HALF), F32),
            pltpu.VMEM((2 * t, 3 * H), BF16),
            pltpu.VMEM((2, t, H), BF16),
            pltpu.VMEM((steps, SUB, 2 * LANE), F32),
            pltpu.VMEM((2, 2, SUB, H), F32),
            pltpu.VMEM((2, SUB, H), F32),
            pltpu.VMEM((3, Z // 2, X, 2, 2, H), F32),
            st, st, st,
            dma((2, 2 * parts, count)),
            dma((2, 2 * parts, count)),
            dma((2, 2 * parts)),
            dma((count,)),
            dma((count,)),
            dma((2, 2)),
            dma((8,)),
            dma((8,)),
            dma((3, Z // 2 * X)),
            dma((3, Z // 2 * X)),
            dma((10,)),
        ],
        compiler_params=pltpu.CompilerParams(
            collective_id=0, has_side_effects=True, vmem_limit_bytes=62 << 20
        ),
        name="forward_all",
    )(tok, cot, keep, vin, w_own)


def wrap(a, b):
    return a % b if isinstance(a, int) else lax.rem(a, b)


class Scatter:
    slots = (2, 4, 4, 4)

    def __init__(self, pos, count, low, du, out, keep, send, recv, done, snd, rcv, outs):
        self.pos, self.count, self.low, self.du, self.out = pos, count, low, du, out
        self.keep, self.send, self.recv, self.done = keep, send, recv, done
        self.snd, self.rcv, self.outs = snd, rcv, outs
        n = pos.X - 1
        self.base = (0, 1, 1 + n, 1 + 2 * n)

    def axis(self, stage, h):
        return ("c", ("x", "y")[h], ("y", "x")[h], "z")[stage]

    def copy(self, g, stage, h, k):
        slot = wrap(g, self.slots[stage])
        sem = self.base[stage] + k - 1
        to = self.pos.device(self.pos.moved(self.axis(stage, h), k))
        return remote(
            self.send[stage].at[slot, k - 1], self.recv[stage].at[slot, k - 1],
            self.snd.at[slot, sem], self.rcv.at[slot, sem], to,
        )

    def each(self, stage, h):
        return self.pos.others(self.axis(stage, h))

    def ready(self, g, stage, h):
        def wait():
            for k in self.each(stage, h):
                self.copy(g, stage, h, k).wait_send()

        if isinstance(g, int):
            if g >= self.slots[stage]:
                wait()
        else:
            pl.when(g >= self.slots[stage])(wait)

    def start(self, g, stage, h):
        for k in self.each(stage, h):
            self.copy(g, stage, h, k).start()

    def arrive(self, g, stage, h):
        for k in self.each(stage, h):
            self.copy(g, stage, h, k).wait_recv()

    def stage0(self, g, h):
        pos, low, t = self.pos, self.low, self.low.shape[0]
        rows = low.shape[1] // pos.Z
        slot = wrap(g, 2)
        q = wrap(g, self.count)
        cols = pl.ds(q * HALF if isinstance(q, int) else pl.multiple_of(q * HALF, LANE), HALF)
        self.ready(g, 0, h)
        first = pos.at["c"] == 0

        def one(z, _):
            lhs = low[:, pl.ds(pl.multiple_of(z * rows, LANE), rows)]
            v = lax.dot_general(
                lhs, self.du[:, cols], (((0,), (0,)), ((), ())), preferred_element_type=F32
            )
            v = v.reshape(pos.X, pos.Y, 2, -1, HALF)
            even, odd = v[:, :, 0], v[:, :, 1]
            self.keep[0][z] = jnp.where(first, even, odd)
            self.send[0][slot, 0, z] = jnp.where(first, odd, even).astype(BF16)
            return 0

        lax.fori_loop(0, pos.Z, one, 0)
        self.start(g, 0, h)

    def stage1(self, g, h):
        pos, axis = self.pos, self.axis(1, h)
        slot = wrap(g, 4)
        got = wrap(g, 2)
        self.arrive(g, 0, h)
        self.ready(g, 1, h)
        for k in range(pos.sizes[axis]):
            p = pos.moved(axis, k)[axis]

            def one(z, _):
                where = (z, p) if h == 0 else (z, slice(None), p)
                v = self.keep[0][where] + self.recv[0][(got, 0) + where].astype(F32)
                if k == 0:
                    self.keep[1][got, z] = v
                else:
                    self.send[1][slot, k - 1, z] = v.astype(BF16)
                return 0

            lax.fori_loop(0, pos.Z, one, 0)
        self.start(g, 1, h)

    def stage2(self, g, h):
        pos, axis = self.pos, self.axis(2, h)
        slot, mine = wrap(g, 4), wrap(g, 2)
        self.arrive(g, 1, h)
        self.ready(g, 2, h)
        for k in range(pos.sizes[axis]):
            p = pos.moved(axis, k)[axis]
            v = self.keep[1][mine, :, p]
            for e in self.each(1, h):
                v = v + self.recv[1][slot, e - 1, :, p].astype(F32)
            if k == 0:
                self.keep[2][mine] = v
            else:
                self.send[2][slot, k - 1] = v.astype(BF16)
        self.start(g, 2, h)

    def stage3(self, g, h):
        pos = self.pos
        slot, mine = wrap(g, 4), wrap(g, 2)
        self.arrive(g, 2, h)
        self.ready(g, 3, h)
        for k in range(pos.Z):
            p = pos.moved("z", k)["z"]
            v = self.keep[2][mine, p]
            for e in self.each(2, h):
                v = v + self.recv[2][slot, e - 1, p].astype(F32)
            if k == 0:
                self.keep[3][mine] = v
            else:
                self.send[3][slot, k - 1] = v.astype(BF16)
        self.start(g, 3, h)

    def result(self, l, q, half, e):
        d = self.out.shape[-1] // 3
        at = e * d + half * (d // 2) + q * LANE
        return pltpu.make_async_copy(
            self.done.at[half, q, :, e * LANE : (e + 1) * LANE],
            self.out.at[l, :, pl.ds(pl.multiple_of(at, LANE), LANE)],
            self.outs.at[half, q, e],
        )

    def stage4(self, g, h, l):
        pos = self.pos
        slot, mine, q = wrap(g, 4), wrap(g, 2), wrap(g, self.count)
        self.arrive(g, 3, h)
        own, other = self.keep[3][mine], None
        for k in range(1, pos.Z):
            v = self.recv[3][slot, k - 1].astype(F32)
            if k % 2 == 0:
                own = own + v
            else:
                other = v if other is None else other + v
        self.done[pos.zl, q] = own
        self.done[1 - pos.zl, q] = other
        for half in (pos.zl, 1 - pos.zl):
            for e in range(3):
                self.result(l, q, half, e).start()

    def turn(self, run, l, pair, e, enters=True):
        first = run * self.count

        def stage(s, f):
            g = first + 2 * pair + e - s
            h = (e - s) % 2
            if isinstance(g, int):
                if first <= g < first + self.count:
                    f(g, h)
            elif s:
                pl.when(g >= first)(lambda: f(g, h))
            else:
                f(g, h)

        stage(1, self.stage1)
        if enters:
            stage(0, self.stage0)
        stage(2, self.stage2)
        stage(3, self.stage3)
        stage(4, lambda g, h: self.stage4(g, h, l))

    def written(self, l):
        def one(q, _):
            for half in (self.pos.zl, 1 - self.pos.zl):
                for e in range(3):
                    self.result(l, q, half, e).wait()
            return 0

        lax.fori_loop(0, self.count, one, 0)

    def finish(self, total):
        for stage in range(4):
            for g in range(total - self.slots[stage], total):
                for k in self.each(stage, g % 2):
                    self.copy(g, stage, g % 2, k).wait_send()


def backward_all(
    seq, row, w_all, vec, keep, stats, f0, g0, cand0, p0, r0, u0, low0, low1, u1, dhr1, dn1, du1,
    sums1,
    grad, input_grad, vout,
    wbuf, du, low, dn, dnsend, dnrecv, u, dhr, stream, proj, top_of,
    keep0, send0, recv0, keep1, send1, recv1, keep2, send2, recv2, keep3, send3, recv3, done,
    ends, first, table, b_own, b_got, b_fin, sums, vbuf, vr0, vr1, vr2, vr3,
    snd, rcv, gouts, psnd, prcv, csnd, crcv, vsnd, vrcv, ins, ssem, wsem,
):
    pos = Place(seq, row)
    at, zl = pos.at, pos.zl
    z, x, y, c = (at[k] for k in "zxyc")
    t2, H3 = du.shape
    t, H = t2 // 2, H3 // 3
    d = 2 * H
    steps = t // SUB
    parts = H // WIDE
    partner = pos.device(dict(at, z=z + 1 - 2 * zl))
    own = pl.ds(pl.multiple_of(zl * H, H), H)
    other = pl.ds(pl.multiple_of((1 - zl) * H, H), H)
    rows_of = lambda b: pl.ds(pl.multiple_of(b * t, t), t)
    pos.barrier(seq)

    def load(k, src, dst):
        return pltpu.make_async_copy(src, dst, ins.at[k])

    def weights(l, half):
        zs = pl.ds(half * (pos.Z // 2), pos.Z // 2)
        for m in range(parts):
            for h in range(2):
                q = 2 * m + h
                yield pltpu.make_async_copy(
                    w_all.at[l, m, h, zs],
                    wbuf.at[:, :, :, :, :, q * HALF : (q + 1) * HALF],
                    wsem.at[q],
                )

    def begin(copies):
        for copy in copies:
            copy.start()

    def end(copies):
        for copy in copies:
            copy.wait()

    get_du, get_low, get_dn = load(0, du1, du), load(1, low1, low), load(2, dn1, dn)
    get_u, get_dhr = load(3, u1, u), load(4, dhr1, dhr)
    begin(weights(1, 1 - zl))
    begin([get_du, get_low, get_dn, get_u, get_dhr])
    scatter = Scatter(
        pos, 2 * parts, low, du, grad, (keep0, keep1, keep2, keep3), (send0, send1, send2, send3),
        (recv0, recv1, recv2, recv3), done, snd, rcv, gouts,
    )
    chain = Chain(pos, table, csnd, crcv)

    def pair(k, src, dst):
        return remote(src, dst, psnd.at[k], prcv.at[k], partner)

    def partial_sums(b):
        return pair(b, dnsend.at[b], dnrecv.at[b])

    def statistics(b):
        return pair(2 + b, b_own.at[b], b_got.at[b])

    def outputs(b, cols):
        return pair(4, dnsend.at[b], input_grad.at[:, cols])

    across = (((1,), (1,)), ((), ()))

    def theirs(b, _):
        v = lax.dot_general(
            du[rows_of(b), :], wbuf[...].reshape(H, H3), across, preferred_element_type=F32
        )
        dnsend[b] = v.astype(BF16)
        partial_sums(b).start()
        return 0

    def ours(k):
        n = t2 // parts
        rows = pl.ds(pl.multiple_of(k * n, n), n)
        v = lax.dot_general(
            du[rows, :], wbuf[...].reshape(H, H3), across, preferred_element_type=F32
        )
        blocks = t // n
        spot = pl.ds(pl.multiple_of(lax.rem(k, blocks) * (n // SUB), n // SUB), n // SUB)
        dn[k // blocks, spot] += v.reshape(n // SUB, SUB, H)

    half = t // LANE

    def norm_sums(l, b):
        partial_sums(b).wait_recv()

        def one(q, _):
            spot = pl.ds(q * (LANE // SUB), LANE // SUB)
            rows = pl.ds(pl.multiple_of(q * LANE, LANE), LANE)
            v = dn[b, spot].reshape(LANE, H) + dnrecv[b, rows, :].astype(F32)
            dn[b, spot] = v.reshape(LANE // SUB, SUB, H)
            xhat = hat(l, b, spot)
            sums[l, 0] += jnp.sum((v * xhat).reshape(LANE // SUB, SUB, H), axis=0)
            sums[l, 1] += jnp.sum(v.reshape(LANE // SUB, SUB, H), axis=0)
            v = v * vec[l, GAIN : GAIN + 1, own]
            b_own[b, pl.ds(q, 1), :] = to_row(jnp.sum(v, axis=-1, keepdims=True))
            b_own[b, pl.ds(q + half, 1), :] = to_row(jnp.sum(v * xhat, axis=-1, keepdims=True))
            return 0

        lax.fori_loop(0, half, one, 0)
        statistics(b).start()

    def hat(l, b, spot):
        mu = stats[l, 0, b, spot].reshape(LANE, LANE)[:, :1]
        rstd = stats[l, 1, b, spot].reshape(LANE, LANE)[:, :1]
        return (u[b, spot].reshape(LANE, H) - mu) * rstd

    def norm_back(l, b):
        statistics(b).wait_recv()
        b_fin[...] = (b_own[b] + b_got[b]) * (1.0 / d)

        def one(q, _):
            spot = pl.ds(q * (LANE // SUB), LANE // SUB)
            xhat = hat(l, b, spot)
            rstd = stats[l, 1, b, spot].reshape(LANE, LANE)[:, :1]
            m0 = to_column(b_fin[pl.ds(q, 1), :])
            m1 = to_column(b_fin[pl.ds(q + half, 1), :])
            v = dn[b, spot].reshape(LANE, H) * vec[l, GAIN : GAIN + 1, own]
            v = dhr[b, spot].reshape(LANE, H) + rstd * (v - m0 - xhat * m1)
            if l == 1:
                dhr[b, spot] = v.reshape(LANE // SUB, SUB, H)
            else:
                dnsend[b, pl.ds(pl.multiple_of(q * LANE, LANE), LANE), :] = v.astype(BF16)
            return 0

        lax.fori_loop(0, half, one, 0)

    units = 2 * parts
    sources = (f0, g0, cand0, p0, r0)

    def fetch(k):
        slot = lax.rem(k, 2)
        b, m = k // parts, lax.rem(k, parts)
        for j, src in enumerate(sources):
            yield pltpu.make_async_copy(
                src.at[b, :, :, lane_tile(m, WIDE)], stream.at[slot, j], ssem.at[slot, j]
            )

    def tiles(work):
        begin(fetch(0))

        def one(k, _):
            @pl.when(k + 1 < units)
            def _():
                begin(fetch(k + 1))

            end(fetch(k))
            b, m = k // parts, lax.rem(k, parts)
            cols = lane_tile(m, WIDE)
            wide = pl.ds(pl.multiple_of(zl * H + m * WIDE, WIDE), WIDE)
            work(lax.rem(k, 2), b, m, cols, wide)
            return 0

        lax.fori_loop(0, units, one, 0)

    def step_back(slot, b, i, cols, peep):
        up, down, cd, before, gate = (stream[slot, j, i] for j in range(5))
        cell = up * before + down * cd
        top = dhr[b, i, :, cols]
        dz_r = top * (cell - u[b, i, :, cols]) * gate * (1.0 - gate)
        direct = top * gate
        kept = lanes(keep[b, i], WIDE)
        decay = up * kept
        term = kept * peep * dz_r + decay * direct
        return up, down, cd, before, gate, top, dz_r, direct, decay, term

    def row_wide(l, k, wide):
        return jnp.broadcast_to(vec[l, k : k + 1, wide], (SUB, WIDE))

    def ends_work(slot, b, m, cols, wide):
        peep = row_wide(0, RPEEP, wide)

        def one(k, carry):
            scale, q = carry
            decay, term = step_back(slot, b, steps - 1 - k, cols, peep)[-2:]
            return scale * decay, decay * q + term

        start = jnp.ones((SUB, WIDE), F32), jnp.zeros((SUB, WIDE), F32)
        scale, q = lax.fori_loop(0, steps, one, start, unroll=8)
        ends[b, 0, :, cols] = scale
        ends[b, 1, :, cols] = q

    def down_work(slot, b, m, cols, wide):
        fpeep, rpeep, gain, shift = (row_wide(0, k, wide) for k in (FPEEP, RPEEP, GAIN, SHIFT))

        def one(k, carry):
            q, s0, s1, s2, s3 = carry
            i = steps - 1 - k
            up, low_f, cd, before, gate, top, dz_r, direct, decay, term = step_back(
                slot, b, i, cols, rpeep
            )
            e = direct + q
            dz_f = e * (up * low_f) * (before - cd)
            n = (u[b, i, :, cols] - lanes(stats[0, 0, b, i], WIDE)) * lanes(
                stats[0, 1, b, i], WIDE
            ) * gain + shift
            proj[i, :, :WIDE] = e * low_f
            proj[i, :, WIDE : 2 * WIDE] = dz_f
            proj[i, :, 2 * WIDE :] = dz_r
            dn[b, i, :, cols] = dz_f * fpeep
            dhr[b, i, :, cols] = top * (1.0 - gate)
            return (
                decay * q + term,
                s0 + dz_f * n,
                s1 + dz_r * before,
                s2 + dz_f,
                s3 + dz_r,
            )

        zero = jnp.zeros((SUB, WIDE), F32)
        carry = lax.fori_loop(0, steps, one, (first[b, :, cols], zero, zero, zero, zero), unroll=4)
        for k in range(4):
            sums[0, 2 + k, :, cols] += carry[k + 1]
        for h in range(2):
            for k in range(3):
                v = proj[:, :, k * WIDE + h * LANE : k * WIDE + (h + 1) * LANE]
                to = pl.ds(pl.multiple_of((2 * m + h) * HALF + k * LANE, LANE), LANE)
                du[rows_of(b), to] = v.reshape(t, LANE).astype(BF16)

    def layer(run, l):
        end(weights(l, 1 - zl))
        lax.fori_loop(0, 2, theirs, 0)
        begin(weights(l, zl))

        def one(k, _):
            scatter.turn(run, l, k, 0)

            @pl.when(k == 0)
            def _():
                end(weights(l, zl))

            ours(k)
            scatter.turn(run, l, k, 1)
            return 0

        lax.fori_loop(0, parts, one, 0)

    sums[...] = jnp.zeros_like(sums)
    sums[1, 2:6] = sums1[0] + sums1[1]
    get_du.wait()
    get_low.wait()
    get_dn.wait()
    layer(0, 1)
    get_low = load(1, low0, low)
    get_low.start()
    get_u.wait()
    get_dhr.wait()
    begin(weights(0, 1 - zl))
    norm_sums(1, 0)
    norm_sums(1, 1)
    scatter.turn(0, 1, parts, 0, False)
    norm_back(1, 0)
    norm_back(1, 1)
    get_u = load(3, u0, u)
    get_u.start()
    scatter.turn(0, 1, parts, 1, False)
    get_u.wait()
    tiles(ends_work)
    scatter.turn(0, 1, parts + 1, 0, False)
    chain.run(ends, first, True)
    scatter.turn(0, 1, parts + 1, 1, False)
    tiles(down_work)
    for b in range(2):
        partial_sums(b).wait_send()
        statistics(b).wait_send()
    scatter.written(1)
    get_low.wait()
    layer(1, 0)
    norm_sums(0, 0)
    norm_sums(0, 1)
    scatter.turn(1, 0, parts, 0, False)
    for b in range(2):
        partial_sums(b).wait_send()
    norm_back(0, 0)
    norm_back(0, 1)
    outputs(1 - zl, own).start()
    own_out = load(0, dnsend.at[zl], input_grad.at[:, own])
    own_out.start()
    scatter.turn(1, 0, parts, 1, False)

    vbuf[...] = jnp.zeros_like(vbuf)
    per = d // (seq * row)
    total = [jnp.sum(sums[l], axis=1) for l in range(2)]
    blank = jnp.zeros((6, LANE - per), F32) if per < LANE else None
    for i in range(H // per):
        spot = (zl * (pos.Z // 2) + i // (2 * pos.Y * pos.X), i // (2 * pos.Y) % pos.X, i // 2 % pos.Y, i % 2)
        for l in range(2):
            piece = total[l][:, i * per : (i + 1) * per]
            vbuf[spot + (slice(l * 8, l * 8 + 6),)] = jnp.concatenate([piece, blank], axis=-1)
    every = slice(None)

    def vspot(stage, who):
        if stage == 0:
            return (every, every, every, who["c"])
        if stage == 1:
            return (every, who["x"], every, c)
        if stage == 2:
            return (every, x, who["y"], c)
        return (who["z"], x, y, c)

    vrecv = (vr0, vr1, vr2, vr3)

    def vcopy(stage, k):
        axis = "cxyz"[stage]
        to = pos.moved(axis, k)
        sem = scatter.base[stage] + k - 1
        return remote(
            vbuf.at[vspot(stage, to)], vrecv[stage].at[k - 1], vsnd.at[sem], vrcv.at[sem],
            pos.device(to),
        )

    def vstart(stage):
        for k in pos.others("cxyz"[stage]):
            vcopy(stage, k).start()

    def vtake(stage):
        for k in pos.others("cxyz"[stage]):
            vcopy(stage, k).wait_recv()
            vbuf[vspot(stage, at)] += vrecv[stage][k - 1]

    vstart(0)
    scatter.turn(1, 0, parts + 1, 0, False)
    vtake(0)
    vstart(1)
    scatter.turn(1, 0, parts + 1, 1, False)
    vtake(1)
    vstart(2)
    vtake(2)
    vstart(3)
    vtake(3)
    vout[...] = vbuf[z, x, y, c]
    for stage in range(4):
        for k in pos.others("cxyz"[stage]):
            vcopy(stage, k).wait_send()
    scatter.written(0)
    scatter.finish(2 * scatter.count)
    for b in range(2):
        statistics(b).wait_send()
    own_out.wait()
    outputs(1 - zl, own).wait_send()
    outputs(1 - zl, other).wait_recv()


def call_backward(seq, row, t, d, given):
    w_all = given[0]
    layers, parts, _, Z, X, Y, _, per, _ = w_all.shape
    H = d // 2
    steps = t // SUB
    vmem = pl.BlockSpec(memory_space=pltpu.VMEM)
    hbm = pl.BlockSpec(memory_space=pl.ANY)
    dma = pltpu.SemaphoreType.DMA
    big = pltpu.VMEM((2, steps, SUB, H), F32)
    half = pltpu.VMEM((2, t, H), BF16)
    st = pltpu.VMEM((2, 8, LANE), F32)
    count = 1 + 2 * (X - 1) + Z - 1
    chunk = (Z, X, Y, per, HALF)

    def buf(*shape, dtype=BF16):
        return pltpu.VMEM(shape, dtype)

    return pl.pallas_call(
        lambda *refs: backward_all(seq, row, *refs),
        in_specs=[hbm, vmem, vmem, vmem] + [hbm] * 12 + [vmem],
        out_specs=[hbm, hbm, vmem],
        out_shape=[arr(layers, per, 3 * d), arr(t, d, dtype=BF16), arr(16, LANE)],
        scratch_shapes=[
            buf(Z // 2, X, Y, 2, per, 3 * H),
            buf(2 * t, 3 * H),
            buf(2 * t, d),
            big, half, half, big, big,
            buf(2, 5, steps, SUB, WIDE, dtype=F32),
            buf(steps, SUB, 3 * WIDE, dtype=F32),
            buf(8, LANE, dtype=F32),
            buf(*chunk, dtype=F32), buf(2, 1, *chunk), buf(2, 1, *chunk),
            buf(2, Z, Y, per, HALF, dtype=F32), buf(4, X - 1, Z, Y, per, HALF),
            buf(4, X - 1, Z, Y, per, HALF),
            buf(2, Z, per, HALF, dtype=F32), buf(4, Y - 1, Z, per, HALF),
            buf(4, Y - 1, Z, per, HALF),
            buf(2, per, HALF, dtype=F32), buf(4, Z - 1, per, HALF), buf(4, Z - 1, per, HALF),
            buf(2, 2 * parts, per, HALF, dtype=F32),
            buf(2, 2, SUB, H, dtype=F32),
            buf(2, SUB, H, dtype=F32),
            buf(Z // 2, X, 2, 2, H, dtype=F32),
            st, st, buf(8, LANE, dtype=F32),
            buf(2, 6, SUB, H, dtype=F32),
            buf(Z, X, Y, 2, 16, LANE, dtype=F32),
            buf(1, Z, X, Y, 16, LANE, dtype=F32),
            buf(X - 1, Z, Y, 16, LANE, dtype=F32),
            buf(Y - 1, Z, 16, LANE, dtype=F32),
            buf(Z - 1, 16, LANE, dtype=F32),
            dma((4, count)), dma((4, count)),
            dma((2, 2 * parts, 3)),
            dma((5,)), dma((5,)),
            dma((Z // 2 * X,)), dma((Z // 2 * X,)),
            dma((count,)), dma((count,)),
            dma((5,)),
            dma((2, 5)),
            dma((2 * parts,)),
        ],
        compiler_params=pltpu.CompilerParams(
            collective_id=1, has_side_effects=True, vmem_limit_bytes=62 << 20
        ),
        name="backward_all",
    )(*given)


def body(tokens, resets, cotangent, weight, *rows):
    _, t, d = tokens.shape
    layers = weight.shape[0]
    steps = t // SUB
    seq, row = lax.axis_size("seq"), lax.axis_size("row")
    H = d // 2
    parts = H // WIDE

    def permuted(v):
        return v.reshape(SUB, steps, -1).transpose(1, 0, 2).reshape(t, -1)

    def restored(v):
        return v.reshape(steps, SUB, d).transpose(1, 0, 2).reshape(1, t, d)

    keep = permuted((1 - resets[0]).astype(F32)[:, None]).reshape(t // LANE, LANE)
    keep = jnp.pad(keep, ((0, 8 - t // LANE), (0, 0)))
    per = rows[0].shape[-1]
    packed = jnp.stack(rows + (jnp.zeros_like(rows[0]),) * 2, axis=1).reshape(2 * 8, per)
    packed = jnp.pad(packed, ((0, 0), (0, LANE - per)))
    local = weight.reshape(layers, per, 3, 2, parts, 2, LANE).transpose(0, 3, 4, 5, 1, 2, 6)
    local = local.reshape(layers, 2, parts, 2, per, HALF)
    out = call_forward(
        seq, row, permuted(tokens[0]), permuted(cotangent[0]), keep, packed, local
    )
    result, sums = out[-2:]
    grad, input_grad, vectors = call_backward(seq, row, t, d, tuple(out[:-2]) + (sums,))
    return (restored(result), restored(input_grad), grad) + tuple(
        jnp.stack([vectors[l * 8 + k, :per] for l in range(layers)]) for k in range(6)
    )


def solution(mesh):
    tokens = P("row", "seq", None)
    rows = P(None, ("seq", "row"))
    weight = P(None, ("seq", "row"), None)
    return jax.shard_map(
        body,
        mesh=mesh,
        in_specs=(tokens, P("row", "seq"), tokens, weight) + (rows,) * 6,
        out_specs=(tokens, tokens, weight) + (rows,) * 6,
        check_vma=False,
    )
```

```python
import jax
import jax.numpy as jnp
from jax import lax
from jax.experimental import pallas as pl
from jax.experimental.pallas import tpu as pltpu
from jax.sharding import PartitionSpec as P

epsilon = 1e-05
SUB = 8
WIDE = 256
F32 = jnp.float32
BF16 = jnp.bfloat16
GAIN, SHIFT, FPEEP, RPEEP, FBIAS, RBIAS = range(6)


def both_sigmoids(z):
    tail = jnp.exp(-jnp.abs(z))
    big = 1.0 / (1.0 + tail)
    small = tail * big
    up = z >= 0
    return jnp.where(up, big, small), jnp.where(up, small, big)


def lanes(value, width):
    return jnp.concatenate([value] * (width // value.shape[-1]), axis=-1)


def arr(*shape, dtype=F32):
    return jax.ShapeDtypeStruct(shape, dtype)


MESH = pl.DeviceIdType.MESH
HALF = 384
LANE = 128


class Place:
    def __init__(self, seq, row):
        self.Y = row // 2
        self.X = self.Y
        self.Z = seq // self.X
        self.C = 2
        self.sizes = dict(z=self.Z, x=self.X, y=self.Y, c=self.C)
        s, r = lax.axis_index("seq"), lax.axis_index("row")
        self.at = dict(z=s // self.X, x=s % self.X, y=r // 2, c=r % 2)
        self.zl = lax.rem(self.at["z"], 2)

    def moved(self, axis, k):
        size = self.sizes[axis]
        return dict(self.at, **{axis: lax.rem(self.at[axis] + k, size)})

    def device(self, at):
        return {"seq": at["z"] * self.X + at["x"], "row": at["y"] * 2 + at["c"]}

    def others(self, axis):
        return range(1, self.sizes[axis])

    def barrier(self, seq):
        sem = pltpu.get_barrier_semaphore()
        count = 0
        s, r = lax.axis_index("seq"), lax.axis_index("row")
        for k in range(1, seq):
            pl.semaphore_signal(
                sem, inc=1, device_id={"seq": lax.rem(s + k, seq), "row": r}, device_id_type=MESH
            )
            count += 1
        for axis in ("y", "c"):
            for k in self.others(axis):
                pl.semaphore_signal(
                    sem, inc=1, device_id=self.device(self.moved(axis, k)), device_id_type=MESH
                )
                count += 1
        pl.semaphore_wait(sem, count)


def remote(src, dst, send, recv, to):
    return pltpu.make_async_remote_copy(
        src_ref=src, dst_ref=dst, send_sem=send, recv_sem=recv, device_id=to, device_id_type=MESH
    )


def total_of(scale, state, backward):
    order = range(SUB - 1, -1, -1) if backward else range(SUB)
    whole_scale, whole_state = None, None
    for k in order:
        a, b = scale[k : k + 1], state[k : k + 1]
        if whole_scale is None:
            whole_scale, whole_state = a, b
        else:
            whole_scale, whole_state = a * whole_scale, a * whole_state + b
    return jnp.concatenate([whole_scale, whole_state], axis=0)


class Gather:
    def __init__(self, pos, parts, w_own, w_all, snd, rcv, loc):
        self.pos, self.parts = pos, parts
        self.w_own, self.w_all, self.snd, self.rcv, self.loc = w_own, w_all, snd, rcv, loc
        z, x, y = pos.Z - 1, pos.X - 1, pos.Y - 1
        self.base = (0, z, z + max(x, y), z + 2 * max(x, y))

    def axis(self, stage, h):
        return ("z", ("y", "x")[h], ("x", "y")[h], "c")[stage]

    def region(self, ref, head, stage, h, who):
        every = slice(None)
        spot = [who["z"], who["x"], who["y"], who["c"]]
        if stage >= 1:
            spot[0] = every
        if stage >= 2:
            spot[2 if h == 0 else 1] = every
        if stage >= 3:
            spot[1] = spot[2] = every
        return ref.at[head + tuple(spot)]

    def copies(self, g, stage, h, arriving):
        pos, axis = self.pos, self.axis(stage, h)
        l, m = g // self.parts, lax.rem(g, self.parts)
        size = pos.sizes[axis]
        for k in pos.others(axis):
            sem = self.base[stage] + k - 1
            to = pos.moved(axis, k)
            who = pos.moved(axis, size - k) if arriving else pos.at
            mine = self.region(self.w_all, (l, m, h), stage, h, who)
            src = mine
            if stage == 0 and not arriving:
                src = self.w_own.at[l, lax.rem(to["z"], 2), m, h]
            yield remote(src, mine, self.snd.at[h, g, sem], self.rcv.at[h, g, sem], pos.device(to))

    def local(self, g, h):
        at = self.pos.at
        l, m = g // self.parts, lax.rem(g, self.parts)
        return pltpu.make_async_copy(
            self.w_own.at[l, self.pos.zl, m, h],
            self.w_all.at[l, m, h, at["z"], at["x"], at["y"], at["c"]],
            self.loc.at[h, g],
        )

    def begin(self, g):
        for h in range(2):
            self.local(g, h).start()
            for copy in self.copies(g, 0, h, False):
                copy.start()

    def advance(self, g, stage):
        for h in range(2):
            if stage == 1:
                self.local(g, h).wait()
            for copy in self.copies(g, stage - 1, h, True):
                copy.wait_recv()
            if stage < 4:
                for copy in self.copies(g, stage, h, False):
                    copy.start()

    def turn(self, i):
        total = 2 * self.parts

        @pl.when(i + 4 < total)
        def _():
            self.begin(i + 4)

        for stage in range(1, 5):
            g = i - (stage - 1)

            @pl.when((g >= 0) & (g < total))
            def _():
                self.advance(g, stage)

    def finish(self):
        def one(g, _):
            for h in range(2):
                for stage in range(4):
                    for copy in self.copies(g, stage, h, False):
                        copy.wait_send()
            return 0

        lax.fori_loop(0, 2 * self.parts, one, 0)


class Chain:
    def __init__(self, pos, table, snd, rcv):
        self.pos, self.table, self.snd, self.rcv = pos, table, snd, rcv

    def run(self, ends, first, backward):
        pos, table = self.pos, self.table
        zh, x = pos.at["z"] // 2, pos.at["x"]
        r = lax.axis_index("row")
        for b in range(2):
            table[zh, x, b] = total_of(ends[b, 0], ends[b, 1], backward)
        moves = [(i, j) for i in range(pos.Z // 2) for j in range(pos.X) if i or j]

        def copy(k, sign):
            i, j = moves[k]
            there = lax.rem(zh + i, pos.Z // 2), lax.rem(x + j, pos.X)
            back = lax.rem(zh + pos.Z // 2 - i, pos.Z // 2), lax.rem(x + pos.X - j, pos.X)
            spot = (zh, x) if sign > 0 else back
            to = {"seq": (2 * there[0] + pos.zl) * pos.X + there[1], "row": r}
            return remote(table.at[spot], table.at[spot], self.snd.at[k], self.rcv.at[k], to)

        for k in range(len(moves)):
            copy(k, 1).start()
        for k in range(len(moves)):
            copy(k, -1).wait_recv()
        for k in range(len(moves)):
            copy(k, 1).wait_send()
        blocks = [(i, b, j) for i in range(pos.Z // 2) for b in range(2) for j in range(pos.X)]
        if backward:
            blocks = blocks[::-1]
        value = jnp.zeros_like(table[0, 0, 0, 0:1])
        mine = [value, value]
        for i, b, j in blocks:
            here = (i == zh) & (j == x)
            mine[b] = jnp.where(here, value, mine[b])
            value = table[i, j, b, 0:1] * value + table[i, j, b, 1:2]
        for b in range(2):
            value = mine[b]
            for k in range(SUB - 1, -1, -1) if backward else range(SUB):
                first[b, k : k + 1] = value
                value = ends[b, 0, k : k + 1] * value + ends[b, 1, k : k + 1]


def diagonal():
    return lax.broadcasted_iota(jnp.int32, (LANE, LANE), 0) == lax.broadcasted_iota(
        jnp.int32, (LANE, LANE), 1
    )


def to_row(column):
    spread = jnp.broadcast_to(column, (LANE, LANE))
    return jnp.sum(jnp.where(diagonal(), spread, 0.0), axis=0, keepdims=True)


def to_column(line):
    spread = jnp.broadcast_to(line, (LANE, LANE))
    return jnp.sum(jnp.where(diagonal(), spread, 0.0), axis=1, keepdims=True)


def spread_rows(column):
    return jnp.broadcast_to(column, (LANE, LANE)).reshape(LANE // SUB, SUB, LANE)


def lane_tile(m, width):
    return pl.ds(pl.multiple_of(m * width, width), width)


def forward_all(
    seq, row, tok, cot, keep_in, vin, w_own,
    w_all, vec, keep, stats, f0, g0, cand0, p0, r0, u0, low0, low1, u1, dhr1, dn1, du1, res1,
    sums, tokbuf, cotbuf, keepc, vall, u, np_, f, g, cand, rpre, low, wbuf, proj, du, resbuf, top_of, ends,
    first, tables, st_own, st_got, st_fin,
    gsnd, grcv, gloc, vsnd, vrcv, wsem, psnd, prcv, csnd, crcv, outs,
):
    pos = Place(seq, row)
    at, zl = pos.at, pos.zl
    z, x, y, c = (at[k] for k in "zxyc")
    _, t, d = tokbuf.shape
    steps, H = u.shape[1], u.shape[3]
    parts = w_own.shape[2]
    partner = pos.device(dict(at, z=z + 1 - 2 * zl))
    own = pl.ds(pl.multiple_of(zl * H, H), H)
    other = pl.ds(pl.multiple_of((1 - zl) * H, H), H)
    rows_of = lambda b: pl.ds(pl.multiple_of(b * t, t), t)
    pos.barrier(seq)

    gather = Gather(pos, parts, w_own, w_all, gsnd, grcv, gloc)
    chains = [Chain(pos, tables.at[k], csnd.at[k], crcv.at[k]) for k in range(3)]

    def pair(k, src, dst):
        return remote(src, dst, psnd.at[k], prcv.at[k], partner)

    def tokens(b):
        return pair(0, tok, tokbuf.at[b])

    def cotangents(b):
        return pair(1, cot.at[:, other], cotbuf.at[b])

    def keeps(b):
        return pair(2, keepc.at[b], keepc.at[b])

    def statistics(b, to):
        return pair(3 + b, st_own.at[b], to.at[b])

    def lows(b, cols):
        return pair(5 + b, low.at[rows_of(b), cols], low.at[rows_of(b), cols])

    def vcopies(stage, arriving):
        axis = gather.axis(stage, 0)
        size = pos.sizes[axis]
        for k in pos.others(axis):
            sem = gather.base[stage] + k - 1
            to = pos.moved(axis, k)
            who = pos.moved(axis, size - k) if arriving else at
            mine = gather.region(vall, (), stage, 0, who)
            yield remote(mine, mine, vsnd.at[sem], vrcv.at[sem], pos.device(to))

    def vadvance(stage):
        for copy in vcopies(stage - 1, True):
            copy.wait_recv()
        if stage < 4:
            for copy in vcopies(stage, False):
                copy.start()

    own_tokens = pltpu.make_async_copy(tok, tokbuf.at[zl], outs.at[0])
    own_cot = pltpu.make_async_copy(cot.at[:, own], cotbuf.at[zl], outs.at[1])
    vall[z, x, y, c] = vin[...]
    keepc[zl] = keep_in[...]
    own_tokens.start()
    own_cot.start()
    for copy in vcopies(0, False):
        copy.start()
    keeps(zl).start()
    gather.begin(0)
    gather.begin(1)
    gather.begin(2)
    gather.begin(3)
    vadvance(1)
    gather.turn(0)
    vadvance(2)
    vadvance(3)
    gather.turn(1)
    tokens(zl).start()
    vadvance(4)

    per = d // (seq * row)
    for q in range(d // LANE):
        pieces = []
        for e in range(LANE // per):
            i = q * (LANE // per) + e
            spot = (i // (2 * pos.Y * pos.X), i // (2 * pos.Y) % pos.X, i // 2 % pos.Y, i % 2)
            pieces.append(vall[spot][:, :per].astype(F32))
        value = jnp.concatenate(pieces, axis=-1)
        for l in range(2):
            vec[l, :, q * LANE : (q + 1) * LANE] = value[l * 8 : l * 8 + 8]
    keeps(1 - zl).wait_recv()
    for b in range(2):
        for q in range(t // LANE):
            piece = spread_rows(to_column(keepc[b, q : q + 1, :]))
            keep[b, q * (LANE // SUB) : (q + 1) * (LANE // SUB)] = piece

    def norm0(b):
        piece = 8

        def one(k, _):
            rows = pl.ds(pl.multiple_of(k * piece * SUB, piece * SUB), piece * SUB)
            spot = pl.ds(k * piece, piece)
            v = tokbuf[b, rows, :].astype(F32)
            mu = jnp.mean(v, axis=-1, keepdims=True)
            v = v - mu
            rstd = lax.rsqrt(jnp.mean(v * v, axis=-1, keepdims=True) + epsilon)
            v = v * rstd * vec[0, GAIN : GAIN + 1, :] + vec[0, SHIFT : SHIFT + 1, :]
            at_rows = pl.ds(pl.multiple_of(b * t + k * piece * SUB, piece * SUB), piece * SUB)
            low[at_rows, :] = v.astype(BF16)
            u[b, spot] = tokbuf[b, rows, own].astype(F32).reshape(piece, SUB, H)
            stats[0, 0, b, spot] = jnp.broadcast_to(mu, (piece * SUB, LANE)).reshape(piece, SUB, LANE)
            stats[0, 1, b, spot] = jnp.broadcast_to(rstd, (piece * SUB, LANE)).reshape(
                piece, SUB, LANE
            )
            return 0

        lax.fori_loop(0, steps // piece, one, 0)

    def load(l, m, h):
        slot = lax.rem(m, 2)
        return pltpu.make_async_copy(
            w_all.at[l, m, h],
            wbuf.at[slot, :, :, :, :, :, pl.ds(h * HALF, HALF)],
            wsem.at[slot, h],
        )

    def start_load(l, m):
        for h in range(2):
            load(l, m, h).start()

    def end_load(l, m):
        for h in range(2):
            load(l, m, h).wait()

    def gates(l, m, b):
        w = wbuf[lax.rem(m, 2)].reshape(d, 2 * HALF)
        v = jnp.dot(low[rows_of(b), :], w, preferred_element_type=F32)
        proj[...] = v.reshape(steps, SUB, 2 * HALF)
        cols = lane_tile(m, 2 * LANE)
        wide = pl.ds(pl.multiple_of(zl * H + m * 2 * LANE, 2 * LANE), 2 * LANE)
        peep, bias, rbias, gain, shift = (
            jnp.broadcast_to(vec[l, k : k + 1, wide], (SUB, 2 * LANE))
            for k in (FPEEP, FBIAS, RBIAS, GAIN, SHIFT)
        )

        def both(i, off):
            return jnp.concatenate(
                [proj[i, :, h * HALF + off : h * HALF + off + LANE] for h in range(2)], axis=-1
            )

        def one(i, carry):
            scale, state = carry
            cd = both(i, 0)
            n = (u[b, i, :, cols] - lanes(stats[l, 0, b, i], 2 * LANE)) * lanes(
                stats[l, 1, b, i], 2 * LANE
            ) * gain + shift
            up, down = both_sigmoids(both(i, LANE) + peep * n + bias)
            f[b, i, :, cols] = up
            g[b, i, :, cols] = down
            cand[b, i, :, cols] = cd
            rpre[b, i, :, cols] = both(i, 2 * LANE) + rbias
            a = up * lanes(keep[b, i], 2 * LANE)
            return scale * a, a * state + down * cd

        start = jnp.ones((SUB, 2 * LANE), F32), jnp.zeros((SUB, 2 * LANE), F32)
        scale, state = lax.fori_loop(0, steps, one, start, unroll=8)
        ends[b, 0, :, cols] = scale
        ends[b, 1, :, cols] = state

    def stash(k, src, dst):
        return pltpu.make_async_copy(src, dst, outs.at[k])

    own_tokens.wait()
    norm0(zl)

    def turn(i, _):
        gather.turn(i)

        @pl.when(i >= 3)
        def _():
            @pl.when(i < parts + 1)
            def _():
                start_load(0, i - 3)

        @pl.when((i >= 4) & (i < parts + 2))
        def _():
            end_load(0, i - 4)
            gates(0, i - 4, zl)

        @pl.when(i == parts + 1)
        def _():
            tokens(1 - zl).wait_recv()
            norm0(1 - zl)

        @pl.when(i > parts)
        def _():
            last = i == parts + 2

            def job(k, _):
                m = jnp.where(last, parts - 2 + k // 2, k)
                b = jnp.where(last & (lax.rem(k, 2) == 0), zl, 1 - zl)

                @pl.when(last & (lax.rem(k, 2) == 0))
                def _():
                    end_load(0, m)

                gates(0, m, b)

                @pl.when(jnp.logical_not(last) & (k == 0))
                def _():
                    start_load(0, parts - 2)

                return 0

            @pl.when(last)
            def _():
                start_load(0, parts - 1)

            lax.fori_loop(0, jnp.where(last, 4, parts - 2), job, 0)

        return 0

    lax.fori_loop(2, parts + 3, turn, 0)
    keep_u0, keep_low0 = stash(2, u, u0), stash(3, low, low0)
    gates0 = [stash(4, f, f0), stash(5, g, g0), stash(6, cand, cand0)]
    for copy in [keep_u0, keep_low0] + gates0:
        copy.start()
    chains[0].run(ends, first, False)
    gather.turn(parts + 3)
    keep_u0.wait()
    keep_low0.wait()

    def states0(b):
        def tile(m, _):
            cols = lane_tile(m, 2 * LANE)
            wide = pl.ds(pl.multiple_of(zl * H + m * 2 * LANE, 2 * LANE), 2 * LANE)
            peep = jnp.broadcast_to(vec[0, RPEEP : RPEEP + 1, wide], (SUB, 2 * LANE))

            def one(i, cell):
                before = lanes(keep[b, i], 2 * LANE) * cell
                cell = f[b, i, :, cols] * before + g[b, i, :, cols] * cand[b, i, :, cols]
                gate = jax.nn.sigmoid(rpre[b, i, :, cols] + peep * before)
                np_[b, i, :, cols] = before
                rpre[b, i, :, cols] = gate
                u[b, i, :, cols] = gate * cell + (1.0 - gate) * u[b, i, :, cols]
                return cell

            lax.fori_loop(0, steps, one, first[b, :, cols], unroll=8)
            return 0

        lax.fori_loop(0, parts, tile, 0)

    def local_stats(b):
        def one(q, _):
            v = u[b, pl.ds(q * (LANE // SUB), LANE // SUB)].reshape(LANE, H)
            mu = jnp.mean(v, axis=-1, keepdims=True)
            v = v - mu
            square = jnp.sum(v * v, axis=-1, keepdims=True)
            st_own[b, pl.ds(q, 1), :] = to_row(mu)
            st_own[b, pl.ds(q + t // LANE, 1), :] = to_row(square)
            return 0

        lax.fori_loop(0, t // LANE, one, 0)
        statistics(b, st_got).start()

    def norm1(b):
        half = t // LANE
        statistics(b, st_got).wait_recv()
        m0, m1 = st_own[b, :half], st_got[b, :half]
        gap = m0 - m1
        square = st_own[b, half:] + st_got[b, half:] + gap * gap * (H / 2)
        st_fin[b, :half] = (m0 + m1) * 0.5
        st_fin[b, half:] = lax.rsqrt(square / (2 * H) + epsilon)

        def one(q, _):
            spot = pl.ds(q * (LANE // SUB), LANE // SUB)
            mu = to_column(st_fin[b, pl.ds(q, 1), :])
            rstd = to_column(st_fin[b, pl.ds(q + half, 1), :])
            v = u[b, spot].reshape(LANE, H)
            v = (v - mu) * rstd * vec[1, GAIN : GAIN + 1, own] + vec[1, SHIFT : SHIFT + 1, own]
            low[pl.ds(pl.multiple_of(b * t + q * LANE, LANE), LANE), own] = v.astype(BF16)
            stats[1, 0, b, spot] = spread_rows(mu)
            stats[1, 1, b, spot] = spread_rows(rstd)
            return 0

        lax.fori_loop(0, half, one, 0)
        lows(b, own).start()

    states0(0)
    local_stats(0)
    states0(1)
    keep_p0, keep_r0 = stash(7, np_, p0), stash(8, rpre, r0)
    keep_p0.start()
    keep_r0.start()
    norm1(0)
    local_stats(1)
    gather.turn(parts + 4)
    norm1(1)
    gather.turn(parts + 5)
    gather.turn(parts + 6)
    start_load(1, 0)
    keep_u1 = stash(2, u, u1)
    keep_u1.start()
    for copy in gates0 + [keep_r0]:
        copy.wait()

    def job1(k, _):
        b, m = k // parts, lax.rem(k, parts)

        @pl.when(m == 0)
        def _():
            lows(b, other).wait_recv()

        @pl.when(k == parts)
        def _():
            cotangents(zl).start()

        @pl.when(k + 1 < 2 * parts)
        def _():
            start_load(1, lax.rem(k + 1, parts))

        end_load(1, m)
        gates(1, m, b)
        return 0

    lax.fori_loop(0, 2 * parts, job1, 0)
    keep_low1 = stash(3, low, low1)
    keep_low1.start()
    chains[1].run(ends, first, False)
    keep_p0.wait()
    own_cot.wait()

    def step_back(b, i, cols, top, peep):
        before, gate, up = np_[b, i, :, cols], rpre[b, i, :, cols], f[b, i, :, cols]
        cell = up * before + g[b, i, :, cols] * cand[b, i, :, cols]
        dz_r = top * (cell - u[b, i, :, cols]) * gate * (1.0 - gate)
        direct = top * gate
        kept = lanes(keep[b, i], 2 * LANE)
        decay = up * kept
        return before, gate, up, dz_r, direct, decay, kept * peep * dz_r + decay * direct

    def turn_round(b):
        def tile(m, _):
            cols = lane_tile(m, 2 * LANE)
            wide = pl.ds(pl.multiple_of(zl * H + m * 2 * LANE, 2 * LANE), 2 * LANE)
            peep = jnp.broadcast_to(vec[1, RPEEP : RPEEP + 1, wide], (SUB, 2 * LANE))
            top = cotbuf[b, :, cols].astype(F32).reshape(steps, SUB, 2 * LANE)
            proj[:, :, 2 * LANE : 4 * LANE] = top

            def one(i, cell):
                before = lanes(keep[b, i], 2 * LANE) * cell
                cell = f[b, i, :, cols] * before + g[b, i, :, cols] * cand[b, i, :, cols]
                gate = jax.nn.sigmoid(rpre[b, i, :, cols] + peep * before)
                np_[b, i, :, cols] = before
                rpre[b, i, :, cols] = gate
                proj[i, :, : 2 * LANE] = gate * cell + (1.0 - gate) * u[b, i, :, cols]
                return cell

            lax.fori_loop(0, steps, one, first[b, :, cols], unroll=8)
            v = proj[:, :, : 2 * LANE].reshape(t, 2 * LANE)
            resbuf[b, :, cols] = v.astype(BF16)

            def back(k, carry):
                scale, q = carry
                i = steps - 1 - k
                _, _, _, _, _, decay, term = step_back(
                    b, i, cols, proj[i, :, 2 * LANE : 4 * LANE], peep
                )
                return scale * decay, decay * q + term

            start = jnp.ones((SUB, 2 * LANE), F32), jnp.zeros((SUB, 2 * LANE), F32)
            scale, q = lax.fori_loop(0, steps, back, start, unroll=8)
            ends[b, 0, :, cols] = scale
            ends[b, 1, :, cols] = q
            return 0

        lax.fori_loop(0, parts, tile, 0)

    def blocks(k, _):
        @pl.when(k == 1)
        def _():
            cotangents(1 - zl).wait_recv()

        turn_round(jnp.where(k == 0, zl, 1 - zl))
        return 0

    lax.fori_loop(0, 2, blocks, 0)
    keep_res = stash(9, resbuf, res1)
    keep_res.start()
    chains[2].run(ends, first, True)

    def down(b):
        def tile(m, _):
            cols = lane_tile(m, 2 * LANE)
            wide = pl.ds(pl.multiple_of(zl * H + m * 2 * LANE, 2 * LANE), 2 * LANE)
            fpeep, rpeep, gain, shift = (
                jnp.broadcast_to(vec[1, k : k + 1, wide], (SUB, 2 * LANE))
                for k in (FPEEP, RPEEP, GAIN, SHIFT)
            )

            def one(k, carry):
                q, s0, s1, s2, s3 = carry
                i = steps - 1 - k
                top = top_of[i]
                before, gate, up, dz_r, direct, decay, term = step_back(b, i, cols, top, rpeep)
                e = direct + q
                low_f = g[b, i, :, cols]
                dz_f = e * (up * low_f) * (before - cand[b, i, :, cols])
                n = (u[b, i, :, cols] - lanes(stats[1, 0, b, i], 2 * LANE)) * lanes(
                    stats[1, 1, b, i], 2 * LANE
                ) * gain + shift
                proj[i, :, : 2 * LANE] = e * low_f
                proj[i, :, 2 * LANE : 4 * LANE] = dz_f
                proj[i, :, 4 * LANE :] = dz_r
                cand[b, i, :, cols] = dz_f * fpeep
                rpre[b, i, :, cols] = top * (1.0 - gate)
                return (
                    decay * q + term,
                    s0 + dz_f * n,
                    s1 + dz_r * before,
                    s2 + dz_f,
                    s3 + dz_r,
                )

            top_of[...] = cotbuf[b, :, cols].astype(F32).reshape(steps, SUB, 2 * LANE)
            zero = jnp.zeros((SUB, 2 * LANE), F32)
            carry = lax.fori_loop(0, steps, one, (first[b, :, cols], zero, zero, zero, zero), unroll=4)
            for k in range(4):
                sums[b, k, :, cols] = carry[k + 1]
            for h in range(2):
                for k in range(3):
                    v = proj[:, :, k * 2 * LANE + h * LANE : k * 2 * LANE + (h + 1) * LANE]
                    to = pl.ds(pl.multiple_of((2 * m + h) * HALF + k * LANE, LANE), LANE)
                    du[rows_of(b), to] = v.reshape(t, LANE).astype(BF16)
            return 0

        lax.fori_loop(0, parts, tile, 0)

    keep_low1.wait()

    def last(b):
        yield stash(3, du.at[rows_of(b)], du1.at[rows_of(b)])
        yield stash(4, cand.at[b], dn1.at[b])
        yield stash(5, rpre.at[b], dhr1.at[b])

    down(0)
    for copy in last(0):
        copy.start()
    down(1)
    for copy in last(0):
        copy.wait()
    for copy in last(1):
        copy.start()
    gather.finish()
    for stage in range(4):
        for copy in vcopies(stage, False):
            copy.wait_send()
    for copy in list(last(1)) + [keep_u1, keep_res]:
        copy.wait()
    tokens(zl).wait_send()
    cotangents(zl).wait_send()
    keeps(zl).wait_send()
    for b in range(2):
        statistics(b, st_got).wait_send()
        lows(b, own).wait_send()


def call_forward(seq, row, tok, cot, keep, vin, w_own):
    t, d = tok.shape
    layers, _, parts, _, per, _ = w_own.shape
    Y = row // 2
    X = Y
    Z = seq // X
    H = d // 2
    steps = t // SUB
    act, stat = arr(2, steps, SUB, H), arr(2, steps, SUB, LANE)
    half = arr(2 * t, d, dtype=BF16)
    vmem = pl.BlockSpec(memory_space=pltpu.VMEM)
    hbm = pl.BlockSpec(memory_space=pl.ANY)
    count = Z + 2 * X - 2
    dma = pltpu.SemaphoreType.DMA
    big = pltpu.VMEM((2, steps, SUB, H), F32)
    st = pltpu.VMEM((2, 8, LANE), F32)
    return pl.pallas_call(
        lambda *refs: forward_all(seq, row, *refs),
        in_specs=[hbm, hbm, vmem, vmem, hbm],
        out_specs=[hbm, vmem, vmem, vmem] + [hbm] * 13 + [vmem],
        out_shape=[
            arr(layers, parts, 2, Z, X, Y, 2, per, HALF, dtype=BF16),
            arr(2, 8, d),
            stat,
            arr(2, 2, 2, steps, SUB, LANE),
        ]
        + [act] * 6
        + [half, half, act, act, act, arr(2 * t, 3 * H, dtype=BF16), arr(2, t, H, dtype=BF16)]
        + [arr(2, 4, SUB, H)],
        scratch_shapes=[
            pltpu.VMEM((2, t, d), BF16),
            pltpu.VMEM((2, t, H), BF16),
            pltpu.VMEM((2, 8, LANE), F32),
            pltpu.VMEM((Z, X, Y, 2, 16, LANE), BF16),
            big, big, big, big, big, big,
            pltpu.VMEM((2 * t, d), BF16),
            pltpu.VMEM((2, Z, X, Y, 2, per, 2 * HALF), BF16),
            pltpu.VMEM((steps, SUB, 2 * HALF), F32),
            pltpu.VMEM((2 * t, 3 * H), BF16),
            pltpu.VMEM((2, t, H), BF16),
            pltpu.VMEM((steps, SUB, 2 * LANE), F32),
            pltpu.VMEM((2, 2, SUB, H), F32),
            pltpu.VMEM((2, SUB, H), F32),
            pltpu.VMEM((3, Z // 2, X, 2, 2, H), F32),
            st, st, st,
            dma((2, 2 * parts, count)),
            dma((2, 2 * parts, count)),
            dma((2, 2 * parts)),
            dma((count,)),
            dma((count,)),
            dma((2, 2)),
            dma((7,)),
            dma((7,)),
            dma((3, Z // 2 * X)),
            dma((3, Z // 2 * X)),
            dma((10,)),
        ],
        compiler_params=pltpu.CompilerParams(
            collective_id=0, has_side_effects=True, vmem_limit_bytes=62 << 20
        ),
        name="forward_all",
    )(tok, cot, keep, vin, w_own)


def wrap(a, b):
    return a % b if isinstance(a, int) else lax.rem(a, b)


class Scatter:
    slots = (2, 4, 4, 4)

    def __init__(self, pos, count, low, du, out, keep, send, recv, done, snd, rcv, outs):
        self.pos, self.count, self.low, self.du, self.out = pos, count, low, du, out
        self.keep, self.send, self.recv, self.done = keep, send, recv, done
        self.snd, self.rcv, self.outs = snd, rcv, outs
        n = pos.X - 1
        self.base = (0, 1, 1 + n, 1 + 2 * n)

    def axis(self, stage, h):
        return ("c", ("x", "y")[h], ("y", "x")[h], "z")[stage]

    def copy(self, g, stage, h, k):
        slot = wrap(g, self.slots[stage])
        sem = self.base[stage] + k - 1
        to = self.pos.device(self.pos.moved(self.axis(stage, h), k))
        return remote(
            self.send[stage].at[slot, k - 1], self.recv[stage].at[slot, k - 1],
            self.snd.at[slot, sem], self.rcv.at[slot, sem], to,
        )

    def each(self, stage, h):
        return self.pos.others(self.axis(stage, h))

    def ready(self, g, stage, h):
        def wait():
            for k in self.each(stage, h):
                self.copy(g, stage, h, k).wait_send()

        if isinstance(g, int):
            if g >= self.slots[stage]:
                wait()
        else:
            pl.when(g >= self.slots[stage])(wait)

    def start(self, g, stage, h):
        for k in self.each(stage, h):
            self.copy(g, stage, h, k).start()

    def arrive(self, g, stage, h):
        for k in self.each(stage, h):
            self.copy(g, stage, h, k).wait_recv()

    def stage0(self, g, h):
        pos, low, t = self.pos, self.low, self.low.shape[0]
        rows = low.shape[1] // pos.Z
        slot = wrap(g, 2)
        q = wrap(g, self.count)
        cols = pl.ds(q * HALF if isinstance(q, int) else pl.multiple_of(q * HALF, LANE), HALF)
        self.ready(g, 0, h)
        first = pos.at["c"] == 0

        def one(z, _):
            lhs = low[:, pl.ds(pl.multiple_of(z * rows, LANE), rows)]
            v = lax.dot_general(
                lhs, self.du[:, cols], (((0,), (0,)), ((), ())), preferred_element_type=F32
            )
            v = v.reshape(pos.X, pos.Y, 2, -1, HALF)
            even, odd = v[:, :, 0], v[:, :, 1]
            self.keep[0][z] = jnp.where(first, even, odd)
            self.send[0][slot, 0, z] = jnp.where(first, odd, even).astype(BF16)
            return 0

        lax.fori_loop(0, pos.Z, one, 0)
        self.start(g, 0, h)

    def stage1(self, g, h):
        pos, axis = self.pos, self.axis(1, h)
        slot = wrap(g, 4)
        got = wrap(g, 2)
        self.arrive(g, 0, h)
        self.ready(g, 1, h)
        for k in range(pos.sizes[axis]):
            p = pos.moved(axis, k)[axis]

            def one(z, _):
                where = (z, p) if h == 0 else (z, slice(None), p)
                v = self.keep[0][where] + self.recv[0][(got, 0) + where].astype(F32)
                if k == 0:
                    self.keep[1][got, z] = v
                else:
                    self.send[1][slot, k - 1, z] = v.astype(BF16)
                return 0

            lax.fori_loop(0, pos.Z, one, 0)
        self.start(g, 1, h)

    def stage2(self, g, h):
        pos, axis = self.pos, self.axis(2, h)
        slot, mine = wrap(g, 4), wrap(g, 2)
        self.arrive(g, 1, h)
        self.ready(g, 2, h)
        for k in range(pos.sizes[axis]):
            p = pos.moved(axis, k)[axis]
            v = self.keep[1][mine, :, p]
            for e in self.each(1, h):
                v = v + self.recv[1][slot, e - 1, :, p].astype(F32)
            if k == 0:
                self.keep[2][mine] = v
            else:
                self.send[2][slot, k - 1] = v.astype(BF16)
        self.start(g, 2, h)

    def stage3(self, g, h):
        pos = self.pos
        slot, mine = wrap(g, 4), wrap(g, 2)
        self.arrive(g, 2, h)
        self.ready(g, 3, h)
        for k in range(pos.Z):
            p = pos.moved("z", k)["z"]
            v = self.keep[2][mine, p]
            for e in self.each(2, h):
                v = v + self.recv[2][slot, e - 1, p].astype(F32)
            if k == 0:
                self.keep[3][mine] = v
            else:
                self.send[3][slot, k - 1] = v.astype(BF16)
        self.start(g, 3, h)

    def result(self, l, q, half, e):
        d = self.out.shape[-1] // 3
        at = e * d + half * (d // 2) + q * LANE
        return pltpu.make_async_copy(
            self.done.at[half, q, :, e * LANE : (e + 1) * LANE],
            self.out.at[l, :, pl.ds(pl.multiple_of(at, LANE), LANE)],
            self.outs.at[half, q, e],
        )

    def stage4(self, g, h, l):
        pos = self.pos
        slot, mine, q = wrap(g, 4), wrap(g, 2), wrap(g, self.count)
        self.arrive(g, 3, h)
        own, other = self.keep[3][mine], None
        for k in range(1, pos.Z):
            v = self.recv[3][slot, k - 1].astype(F32)
            if k % 2 == 0:
                own = own + v
            else:
                other = v if other is None else other + v
        self.done[pos.zl, q] = own
        self.done[1 - pos.zl, q] = other
        for half in (pos.zl, 1 - pos.zl):
            for e in range(3):
                self.result(l, q, half, e).start()

    def turn(self, run, l, pair, e, enters=True):
        first = run * self.count

        def stage(s, f):
            g = first + 2 * pair + e - s
            h = (e - s) % 2
            if isinstance(g, int):
                if first <= g < first + self.count:
                    f(g, h)
            elif s:
                pl.when(g >= first)(lambda: f(g, h))
            else:
                f(g, h)

        stage(1, self.stage1)
        if enters:
            stage(0, self.stage0)
        stage(2, self.stage2)
        stage(3, self.stage3)
        stage(4, lambda g, h: self.stage4(g, h, l))

    def written(self, l):
        def one(q, _):
            for half in (self.pos.zl, 1 - self.pos.zl):
                for e in range(3):
                    self.result(l, q, half, e).wait()
            return 0

        lax.fori_loop(0, self.count, one, 0)

    def finish(self, total):
        for stage in range(4):
            for g in range(total - self.slots[stage], total):
                for k in self.each(stage, g % 2):
                    self.copy(g, stage, g % 2, k).wait_send()


def backward_all(
    seq, row, w_all, vec, keep, stats, f0, g0, cand0, p0, r0, u0, low0, low1, u1, dhr1, dn1, du1,
    res1, sums1,
    grad, input_grad, result, vout,
    wbuf, du, low, dn, dnsend, dnrecv, u, dhr, stream, proj, top_of,
    keep0, send0, recv0, keep1, send1, recv1, keep2, send2, recv2, keep3, send3, recv3, done,
    ends, first, table, b_own, b_got, b_fin, sums, vbuf, vr0, vr1, vr2, vr3,
    snd, rcv, gouts, psnd, prcv, csnd, crcv, vsnd, vrcv, ins, ssem, wsem,
):
    pos = Place(seq, row)
    at, zl = pos.at, pos.zl
    z, x, y, c = (at[k] for k in "zxyc")
    t2, H3 = du.shape
    t, H = t2 // 2, H3 // 3
    d = 2 * H
    steps = t // SUB
    parts = H // WIDE
    partner = pos.device(dict(at, z=z + 1 - 2 * zl))
    own = pl.ds(pl.multiple_of(zl * H, H), H)
    other = pl.ds(pl.multiple_of((1 - zl) * H, H), H)
    rows_of = lambda b: pl.ds(pl.multiple_of(b * t, t), t)
    pos.barrier(seq)

    def load(k, src, dst):
        return pltpu.make_async_copy(src, dst, ins.at[k])

    def weights(l, half):
        zs = pl.ds(half * (pos.Z // 2), pos.Z // 2)
        for m in range(parts):
            for h in range(2):
                q = 2 * m + h
                yield pltpu.make_async_copy(
                    w_all.at[l, m, h, zs],
                    wbuf.at[:, :, :, :, :, q * HALF : (q + 1) * HALF],
                    wsem.at[q],
                )

    def begin(copies):
        for copy in copies:
            copy.start()

    def end(copies):
        for copy in copies:
            copy.wait()

    get_du, get_low, get_dn = load(0, du1, du), load(1, low1, low), load(2, dn1, dn)
    get_u, get_dhr = load(3, u1, u), load(4, dhr1, dhr)
    begin(weights(1, 1 - zl))
    begin([get_du, get_low, get_dn, get_u, get_dhr])
    scatter = Scatter(
        pos, 2 * parts, low, du, grad, (keep0, keep1, keep2, keep3), (send0, send1, send2, send3),
        (recv0, recv1, recv2, recv3), done, snd, rcv, gouts,
    )
    chain = Chain(pos, table, csnd, crcv)

    def pair(k, src, dst):
        return remote(src, dst, psnd.at[k], prcv.at[k], partner)

    def partial_sums(b):
        return pair(b, dnsend.at[b], dnrecv.at[b])

    def statistics(b):
        return pair(2 + b, b_own.at[b], b_got.at[b])

    def outputs(b, cols):
        return pair(4, dnsend.at[b], input_grad.at[:, cols])

    def results(cols):
        return pair(5, res1.at[1 - zl], result.at[:, cols])

    own_result = load(5, res1.at[zl], result.at[:, own])
    own_result.start()
    results(own).start()
    across = (((1,), (1,)), ((), ()))

    def theirs(b, _):
        v = lax.dot_general(
            du[rows_of(b), :], wbuf[...].reshape(H, H3), across, preferred_element_type=F32
        )
        dnsend[b] = v.astype(BF16)
        partial_sums(b).start()
        return 0

    def ours(k):
        n = t2 // parts
        rows = pl.ds(pl.multiple_of(k * n, n), n)
        v = lax.dot_general(
            du[rows, :], wbuf[...].reshape(H, H3), across, preferred_element_type=F32
        )
        blocks = t // n
        spot = pl.ds(pl.multiple_of(lax.rem(k, blocks) * (n // SUB), n // SUB), n // SUB)
        dn[k // blocks, spot] += v.reshape(n // SUB, SUB, H)

    half = t // LANE

    def norm_sums(l, b):
        partial_sums(b).wait_recv()

        def one(q, _):
            spot = pl.ds(q * (LANE // SUB), LANE // SUB)
            rows = pl.ds(pl.multiple_of(q * LANE, LANE), LANE)
            v = dn[b, spot].reshape(LANE, H) + dnrecv[b, rows, :].astype(F32)
            dn[b, spot] = v.reshape(LANE // SUB, SUB, H)
            xhat = hat(l, b, spot)
            sums[l, 0] += jnp.sum((v * xhat).reshape(LANE // SUB, SUB, H), axis=0)
            sums[l, 1] += jnp.sum(v.reshape(LANE // SUB, SUB, H), axis=0)
            v = v * vec[l, GAIN : GAIN + 1, own]
            b_own[b, pl.ds(q, 1), :] = to_row(jnp.sum(v, axis=-1, keepdims=True))
            b_own[b, pl.ds(q + half, 1), :] = to_row(jnp.sum(v * xhat, axis=-1, keepdims=True))
            return 0

        lax.fori_loop(0, half, one, 0)
        statistics(b).start()

    def hat(l, b, spot):
        mu = stats[l, 0, b, spot].reshape(LANE, LANE)[:, :1]
        rstd = stats[l, 1, b, spot].reshape(LANE, LANE)[:, :1]
        return (u[b, spot].reshape(LANE, H) - mu) * rstd

    def norm_back(l, b):
        statistics(b).wait_recv()
        b_fin[...] = (b_own[b] + b_got[b]) * (1.0 / d)

        def one(q, _):
            spot = pl.ds(q * (LANE // SUB), LANE // SUB)
            xhat = hat(l, b, spot)
            rstd = stats[l, 1, b, spot].reshape(LANE, LANE)[:, :1]
            m0 = to_column(b_fin[pl.ds(q, 1), :])
            m1 = to_column(b_fin[pl.ds(q + half, 1), :])
            v = dn[b, spot].reshape(LANE, H) * vec[l, GAIN : GAIN + 1, own]
            v = dhr[b, spot].reshape(LANE, H) + rstd * (v - m0 - xhat * m1)
            if l == 1:
                dhr[b, spot] = v.reshape(LANE // SUB, SUB, H)
            else:
                dnsend[b, pl.ds(pl.multiple_of(q * LANE, LANE), LANE), :] = v.astype(BF16)
            return 0

        lax.fori_loop(0, half, one, 0)

    units = 2 * parts
    sources = (f0, g0, cand0, p0, r0)

    def fetch(k):
        slot = lax.rem(k, 2)
        b, m = k // parts, lax.rem(k, parts)
        for j, src in enumerate(sources):
            yield pltpu.make_async_copy(
                src.at[b, :, :, lane_tile(m, WIDE)], stream.at[slot, j], ssem.at[slot, j]
            )

    def tiles(work):
        begin(fetch(0))

        def one(k, _):
            @pl.when(k + 1 < units)
            def _():
                begin(fetch(k + 1))

            end(fetch(k))
            b, m = k // parts, lax.rem(k, parts)
            cols = lane_tile(m, WIDE)
            wide = pl.ds(pl.multiple_of(zl * H + m * WIDE, WIDE), WIDE)
            work(lax.rem(k, 2), b, m, cols, wide)
            return 0

        lax.fori_loop(0, units, one, 0)

    def step_back(slot, b, i, cols, peep):
        up, down, cd, before, gate = (stream[slot, j, i] for j in range(5))
        cell = up * before + down * cd
        top = dhr[b, i, :, cols]
        dz_r = top * (cell - u[b, i, :, cols]) * gate * (1.0 - gate)
        direct = top * gate
        kept = lanes(keep[b, i], WIDE)
        decay = up * kept
        term = kept * peep * dz_r + decay * direct
        return up, down, cd, before, gate, top, dz_r, direct, decay, term

    def row_wide(l, k, wide):
        return jnp.broadcast_to(vec[l, k : k + 1, wide], (SUB, WIDE))

    def ends_work(slot, b, m, cols, wide):
        peep = row_wide(0, RPEEP, wide)

        def one(k, carry):
            scale, q = carry
            decay, term = step_back(slot, b, steps - 1 - k, cols, peep)[-2:]
            return scale * decay, decay * q + term

        start = jnp.ones((SUB, WIDE), F32), jnp.zeros((SUB, WIDE), F32)
        scale, q = lax.fori_loop(0, steps, one, start, unroll=8)
        ends[b, 0, :, cols] = scale
        ends[b, 1, :, cols] = q

    def down_work(slot, b, m, cols, wide):
        fpeep, rpeep, gain, shift = (row_wide(0, k, wide) for k in (FPEEP, RPEEP, GAIN, SHIFT))

        def one(k, carry):
            q, s0, s1, s2, s3 = carry
            i = steps - 1 - k
            up, low_f, cd, before, gate, top, dz_r, direct, decay, term = step_back(
                slot, b, i, cols, rpeep
            )
            e = direct + q
            dz_f = e * (up * low_f) * (before - cd)
            n = (u[b, i, :, cols] - lanes(stats[0, 0, b, i], WIDE)) * lanes(
                stats[0, 1, b, i], WIDE
            ) * gain + shift
            proj[i, :, :WIDE] = e * low_f
            proj[i, :, WIDE : 2 * WIDE] = dz_f
            proj[i, :, 2 * WIDE :] = dz_r
            dn[b, i, :, cols] = dz_f * fpeep
            dhr[b, i, :, cols] = top * (1.0 - gate)
            return (
                decay * q + term,
                s0 + dz_f * n,
                s1 + dz_r * before,
                s2 + dz_f,
                s3 + dz_r,
            )

        zero = jnp.zeros((SUB, WIDE), F32)
        carry = lax.fori_loop(0, steps, one, (first[b, :, cols], zero, zero, zero, zero), unroll=4)
        for k in range(4):
            sums[0, 2 + k, :, cols] += carry[k + 1]
        for h in range(2):
            for k in range(3):
                v = proj[:, :, k * WIDE + h * LANE : k * WIDE + (h + 1) * LANE]
                to = pl.ds(pl.multiple_of((2 * m + h) * HALF + k * LANE, LANE), LANE)
                du[rows_of(b), to] = v.reshape(t, LANE).astype(BF16)

    def layer(run, l):
        end(weights(l, 1 - zl))
        lax.fori_loop(0, 2, theirs, 0)
        begin(weights(l, zl))

        def one(k, _):
            scatter.turn(run, l, k, 0)

            @pl.when(k == 0)
            def _():
                end(weights(l, zl))

            ours(k)
            scatter.turn(run, l, k, 1)
            return 0

        lax.fori_loop(0, parts, one, 0)

    sums[...] = jnp.zeros_like(sums)
    sums[1, 2:6] = sums1[0] + sums1[1]
    get_du.wait()
    get_low.wait()
    get_dn.wait()
    layer(0, 1)
    get_low = load(1, low0, low)
    get_low.start()
    get_u.wait()
    get_dhr.wait()
    begin(weights(0, 1 - zl))
    norm_sums(1, 0)
    norm_sums(1, 1)
    scatter.turn(0, 1, parts, 0, False)
    norm_back(1, 0)
    norm_back(1, 1)
    get_u = load(3, u0, u)
    get_u.start()
    scatter.turn(0, 1, parts, 1, False)
    get_u.wait()
    tiles(ends_work)
    scatter.turn(0, 1, parts + 1, 0, False)
    chain.run(ends, first, True)
    scatter.turn(0, 1, parts + 1, 1, False)
    tiles(down_work)
    for b in range(2):
        partial_sums(b).wait_send()
        statistics(b).wait_send()
    scatter.written(1)
    get_low.wait()
    layer(1, 0)
    norm_sums(0, 0)
    norm_sums(0, 1)
    scatter.turn(1, 0, parts, 0, False)
    for b in range(2):
        partial_sums(b).wait_send()
    norm_back(0, 0)
    norm_back(0, 1)
    outputs(1 - zl, own).start()
    own_out = load(0, dnsend.at[zl], input_grad.at[:, own])
    own_out.start()
    scatter.turn(1, 0, parts, 1, False)

    vbuf[...] = jnp.zeros_like(vbuf)
    per = d // (seq * row)
    total = [jnp.sum(sums[l], axis=1) for l in range(2)]
    blank = jnp.zeros((6, LANE - per), F32) if per < LANE else None
    for i in range(H // per):
        spot = (zl * (pos.Z // 2) + i // (2 * pos.Y * pos.X), i // (2 * pos.Y) % pos.X, i // 2 % pos.Y, i % 2)
        for l in range(2):
            piece = total[l][:, i * per : (i + 1) * per]
            vbuf[spot + (slice(l * 8, l * 8 + 6),)] = jnp.concatenate([piece, blank], axis=-1)
    every = slice(None)

    def vspot(stage, who):
        if stage == 0:
            return (every, every, every, who["c"])
        if stage == 1:
            return (every, who["x"], every, c)
        if stage == 2:
            return (every, x, who["y"], c)
        return (who["z"], x, y, c)

    vrecv = (vr0, vr1, vr2, vr3)

    def vcopy(stage, k):
        axis = "cxyz"[stage]
        to = pos.moved(axis, k)
        sem = scatter.base[stage] + k - 1
        return remote(
            vbuf.at[vspot(stage, to)], vrecv[stage].at[k - 1], vsnd.at[sem], vrcv.at[sem],
            pos.device(to),
        )

    def vstart(stage):
        for k in pos.others("cxyz"[stage]):
            vcopy(stage, k).start()

    def vtake(stage):
        for k in pos.others("cxyz"[stage]):
            vcopy(stage, k).wait_recv()
            vbuf[vspot(stage, at)] += vrecv[stage][k - 1]

    vstart(0)
    scatter.turn(1, 0, parts + 1, 0, False)
    vtake(0)
    vstart(1)
    scatter.turn(1, 0, parts + 1, 1, False)
    vtake(1)
    vstart(2)
    vtake(2)
    vstart(3)
    vtake(3)
    vout[...] = vbuf[z, x, y, c]
    for stage in range(4):
        for k in pos.others("cxyz"[stage]):
            vcopy(stage, k).wait_send()
    scatter.written(0)
    scatter.finish(2 * scatter.count)
    for b in range(2):
        statistics(b).wait_send()
    own_out.wait()
    own_result.wait()
    results(own).wait_send()
    results(other).wait_recv()
    outputs(1 - zl, own).wait_send()
    outputs(1 - zl, other).wait_recv()


def call_backward(seq, row, t, d, given):
    w_all = given[0]
    layers, parts, _, Z, X, Y, _, per, _ = w_all.shape
    H = d // 2
    steps = t // SUB
    vmem = pl.BlockSpec(memory_space=pltpu.VMEM)
    hbm = pl.BlockSpec(memory_space=pl.ANY)
    dma = pltpu.SemaphoreType.DMA
    big = pltpu.VMEM((2, steps, SUB, H), F32)
    half = pltpu.VMEM((2, t, H), BF16)
    st = pltpu.VMEM((2, 8, LANE), F32)
    count = 1 + 2 * (X - 1) + Z - 1
    chunk = (Z, X, Y, per, HALF)

    def buf(*shape, dtype=BF16):
        return pltpu.VMEM(shape, dtype)

    return pl.pallas_call(
        lambda *refs: backward_all(seq, row, *refs),
        in_specs=[hbm, vmem, vmem, vmem] + [hbm] * 13 + [vmem],
        out_specs=[hbm, hbm, hbm, vmem],
        out_shape=[arr(layers, per, 3 * d)] + [arr(t, d, dtype=BF16)] * 2 + [arr(16, LANE)],
        scratch_shapes=[
            buf(Z // 2, X, Y, 2, per, 3 * H),
            buf(2 * t, 3 * H),
            buf(2 * t, d),
            big, half, half, big, big,
            buf(2, 5, steps, SUB, WIDE, dtype=F32),
            buf(steps, SUB, 3 * WIDE, dtype=F32),
            buf(8, LANE, dtype=F32),
            buf(*chunk, dtype=F32), buf(2, 1, *chunk), buf(2, 1, *chunk),
            buf(2, Z, Y, per, HALF, dtype=F32), buf(4, X - 1, Z, Y, per, HALF),
            buf(4, X - 1, Z, Y, per, HALF),
            buf(2, Z, per, HALF, dtype=F32), buf(4, Y - 1, Z, per, HALF),
            buf(4, Y - 1, Z, per, HALF),
            buf(2, per, HALF, dtype=F32), buf(4, Z - 1, per, HALF), buf(4, Z - 1, per, HALF),
            buf(2, 2 * parts, per, HALF, dtype=F32),
            buf(2, 2, SUB, H, dtype=F32),
            buf(2, SUB, H, dtype=F32),
            buf(Z // 2, X, 2, 2, H, dtype=F32),
            st, st, buf(8, LANE, dtype=F32),
            buf(2, 6, SUB, H, dtype=F32),
            buf(Z, X, Y, 2, 16, LANE, dtype=F32),
            buf(1, Z, X, Y, 16, LANE, dtype=F32),
            buf(X - 1, Z, Y, 16, LANE, dtype=F32),
            buf(Y - 1, Z, 16, LANE, dtype=F32),
            buf(Z - 1, 16, LANE, dtype=F32),
            dma((4, count)), dma((4, count)),
            dma((2, 2 * parts, 3)),
            dma((6,)), dma((6,)),
            dma((Z // 2 * X,)), dma((Z // 2 * X,)),
            dma((count,)), dma((count,)),
            dma((6,)),
            dma((2, 5)),
            dma((2 * parts,)),
        ],
        compiler_params=pltpu.CompilerParams(
            collective_id=1, has_side_effects=True, vmem_limit_bytes=62 << 20
        ),
        name="backward_all",
    )(*given)


def body(tokens, resets, cotangent, weight, *rows):
    _, t, d = tokens.shape
    layers = weight.shape[0]
    steps = t // SUB
    seq, row = lax.axis_size("seq"), lax.axis_size("row")
    H = d // 2
    parts = H // WIDE

    def permuted(v):
        return v.reshape(SUB, steps, -1).transpose(1, 0, 2).reshape(t, -1)

    def restored(v):
        return v.reshape(steps, SUB, d).transpose(1, 0, 2).reshape(1, t, d)

    keep = permuted((1 - resets[0]).astype(F32)[:, None]).reshape(t // LANE, LANE)
    keep = jnp.pad(keep, ((0, 8 - t // LANE), (0, 0)))
    per = rows[0].shape[-1]
    packed = jnp.stack(rows + (jnp.zeros_like(rows[0]),) * 2, axis=1).reshape(2 * 8, per)
    packed = jnp.pad(packed, ((0, 0), (0, LANE - per)))
    local = weight.reshape(layers, per, 3, 2, parts, 2, LANE).transpose(0, 3, 4, 5, 1, 2, 6)
    local = local.reshape(layers, 2, parts, 2, per, HALF)
    out = call_forward(
        seq, row, permuted(tokens[0]), permuted(cotangent[0]), keep, packed, local
    )
    grad, input_grad, result, vectors = call_backward(seq, row, t, d, out)
    return (restored(result), restored(input_grad), grad) + tuple(
        jnp.stack([vectors[l * 8 + k, :per] for l in range(layers)]) for k in range(6)
    )


def solution(mesh):
    tokens = P("row", "seq", None)
    rows = P(None, ("seq", "row"))
    weight = P(None, ("seq", "row"), None)
    return jax.shard_map(
        body,
        mesh=mesh,
        in_specs=(tokens, P("row", "seq"), tokens, weight) + (rows,) * 6,
        out_specs=(tokens, tokens, weight) + (rows,) * 6,
        check_vma=False,
    )
```

```python
import jax
import jax.numpy as jnp
from jax import lax
from jax.experimental import pallas as pl
from jax.experimental.pallas import tpu as pltpu
from jax.sharding import PartitionSpec as P

epsilon = 1e-05
SUB = 8
WIDE = 256
F32 = jnp.float32
BF16 = jnp.bfloat16
GAIN, SHIFT, FPEEP, RPEEP, FBIAS, RBIAS = range(6)


def both_sigmoids(z):
    tail = jnp.exp(-jnp.abs(z))
    big = 1.0 / (1.0 + tail)
    small = tail * big
    up = z >= 0
    return jnp.where(up, big, small), jnp.where(up, small, big)


def lanes(value, width):
    return jnp.concatenate([value] * (width // value.shape[-1]), axis=-1)


def arr(*shape, dtype=F32):
    return jax.ShapeDtypeStruct(shape, dtype)


MESH = pl.DeviceIdType.MESH
HALF = 384
LANE = 128


class Place:
    def __init__(self, seq, row):
        self.Y = row // 2
        self.X = self.Y
        self.Z = seq // self.X
        self.C = 2
        self.sizes = dict(z=self.Z, x=self.X, y=self.Y, c=self.C)
        s, r = lax.axis_index("seq"), lax.axis_index("row")
        self.at = dict(z=s // self.X, x=s % self.X, y=r // 2, c=r % 2)
        self.zl = lax.rem(self.at["z"], 2)

    def moved(self, axis, k):
        size = self.sizes[axis]
        return dict(self.at, **{axis: lax.rem(self.at[axis] + k, size)})

    def device(self, at):
        return {"seq": at["z"] * self.X + at["x"], "row": at["y"] * 2 + at["c"]}

    def others(self, axis):
        return range(1, self.sizes[axis])

    def barrier(self, seq):
        sem = pltpu.get_barrier_semaphore()
        count = 0
        s, r = lax.axis_index("seq"), lax.axis_index("row")
        for k in range(1, seq):
            pl.semaphore_signal(
                sem, inc=1, device_id={"seq": lax.rem(s + k, seq), "row": r}, device_id_type=MESH
            )
            count += 1
        for axis in ("y", "c"):
            for k in self.others(axis):
                pl.semaphore_signal(
                    sem, inc=1, device_id=self.device(self.moved(axis, k)), device_id_type=MESH
                )
                count += 1
        pl.semaphore_wait(sem, count)


def remote(src, dst, send, recv, to):
    return pltpu.make_async_remote_copy(
        src_ref=src, dst_ref=dst, send_sem=send, recv_sem=recv, device_id=to, device_id_type=MESH
    )


def total_of(scale, state, backward):
    order = range(SUB - 1, -1, -1) if backward else range(SUB)
    whole_scale, whole_state = None, None
    for k in order:
        a, b = scale[k : k + 1], state[k : k + 1]
        if whole_scale is None:
            whole_scale, whole_state = a, b
        else:
            whole_scale, whole_state = a * whole_scale, a * whole_state + b
    return jnp.concatenate([whole_scale, whole_state], axis=0)


class Gather:
    def __init__(self, pos, parts, w_own, w_all, snd, rcv, loc):
        self.pos, self.parts = pos, parts
        self.w_own, self.w_all, self.snd, self.rcv, self.loc = w_own, w_all, snd, rcv, loc
        z, x, y = pos.Z - 1, pos.X - 1, pos.Y - 1
        self.base = (0, z, z + max(x, y), z + 2 * max(x, y))

    def axis(self, stage, h):
        return ("z", ("y", "x")[h], ("x", "y")[h], "c")[stage]

    def region(self, ref, head, stage, h, who):
        every = slice(None)
        spot = [who["z"], who["x"], who["y"], who["c"]]
        if stage >= 1:
            spot[0] = every
        if stage >= 2:
            spot[2 if h == 0 else 1] = every
        if stage >= 3:
            spot[1] = spot[2] = every
        return ref.at[head + tuple(spot)]

    def copies(self, g, stage, h, arriving):
        pos, axis = self.pos, self.axis(stage, h)
        l, m = g // self.parts, lax.rem(g, self.parts)
        size = pos.sizes[axis]
        for k in pos.others(axis):
            sem = self.base[stage] + k - 1
            to = pos.moved(axis, k)
            who = pos.moved(axis, size - k) if arriving else pos.at
            mine = self.region(self.w_all, (l, m, h), stage, h, who)
            src = mine
            if stage == 0 and not arriving:
                src = self.w_own.at[l, lax.rem(to["z"], 2), m, h]
            yield remote(src, mine, self.snd.at[h, g, sem], self.rcv.at[h, g, sem], pos.device(to))

    def local(self, g, h):
        at = self.pos.at
        l, m = g // self.parts, lax.rem(g, self.parts)
        return pltpu.make_async_copy(
            self.w_own.at[l, self.pos.zl, m, h],
            self.w_all.at[l, m, h, at["z"], at["x"], at["y"], at["c"]],
            self.loc.at[h, g],
        )

    def begin(self, g):
        for h in range(2):
            self.local(g, h).start()
            for copy in self.copies(g, 0, h, False):
                copy.start()

    def advance(self, g, stage):
        for h in range(2):
            if stage == 1:
                self.local(g, h).wait()
            for copy in self.copies(g, stage - 1, h, True):
                copy.wait_recv()
            if stage < 4:
                for copy in self.copies(g, stage, h, False):
                    copy.start()

    def turn(self, i):
        total = 2 * self.parts

        @pl.when(i + 4 < total)
        def _():
            self.begin(i + 4)

        for stage in range(1, 5):
            g = i - (stage - 1)

            @pl.when((g >= 0) & (g < total))
            def _():
                self.advance(g, stage)

    def finish(self):
        def one(g, _):
            for h in range(2):
                for stage in range(4):
                    for copy in self.copies(g, stage, h, False):
                        copy.wait_send()
            return 0

        lax.fori_loop(0, 2 * self.parts, one, 0)


class Chain:
    def __init__(self, pos, table, snd, rcv):
        self.pos, self.table, self.snd, self.rcv = pos, table, snd, rcv

    def run(self, ends, first, backward):
        pos, table = self.pos, self.table
        zh, x = pos.at["z"] // 2, pos.at["x"]
        r = lax.axis_index("row")
        for b in range(2):
            table[zh, x, b] = total_of(ends[b, 0], ends[b, 1], backward)
        moves = [(i, j) for i in range(pos.Z // 2) for j in range(pos.X) if i or j]

        def copy(k, sign):
            i, j = moves[k]
            there = lax.rem(zh + i, pos.Z // 2), lax.rem(x + j, pos.X)
            back = lax.rem(zh + pos.Z // 2 - i, pos.Z // 2), lax.rem(x + pos.X - j, pos.X)
            spot = (zh, x) if sign > 0 else back
            to = {"seq": (2 * there[0] + pos.zl) * pos.X + there[1], "row": r}
            return remote(table.at[spot], table.at[spot], self.snd.at[k], self.rcv.at[k], to)

        for k in range(len(moves)):
            copy(k, 1).start()
        for k in range(len(moves)):
            copy(k, -1).wait_recv()
        for k in range(len(moves)):
            copy(k, 1).wait_send()
        blocks = [(i, b, j) for i in range(pos.Z // 2) for b in range(2) for j in range(pos.X)]
        if backward:
            blocks = blocks[::-1]
        value = jnp.zeros_like(table[0, 0, 0, 0:1])
        mine = [value, value]
        for i, b, j in blocks:
            here = (i == zh) & (j == x)
            mine[b] = jnp.where(here, value, mine[b])
            value = table[i, j, b, 0:1] * value + table[i, j, b, 1:2]
        for b in range(2):
            value = mine[b]
            for k in range(SUB - 1, -1, -1) if backward else range(SUB):
                first[b, k : k + 1] = value
                value = ends[b, 0, k : k + 1] * value + ends[b, 1, k : k + 1]


def diagonal():
    return lax.broadcasted_iota(jnp.int32, (LANE, LANE), 0) == lax.broadcasted_iota(
        jnp.int32, (LANE, LANE), 1
    )


def to_row(column):
    spread = jnp.broadcast_to(column, (LANE, LANE))
    return jnp.sum(jnp.where(diagonal(), spread, 0.0), axis=0, keepdims=True)


def to_column(line):
    spread = jnp.broadcast_to(line, (LANE, LANE))
    return jnp.sum(jnp.where(diagonal(), spread, 0.0), axis=1, keepdims=True)


def spread_rows(column):
    return jnp.broadcast_to(column, (LANE, LANE)).reshape(LANE // SUB, SUB, LANE)


def lane_tile(m, width):
    return pl.ds(pl.multiple_of(m * width, width), width)


def forward_all(
    seq, row, tok, cot, keep_in, vin, w_own,
    w_all, vec, keep, stats, f0, g0, cand0, p0, r0, u0, low0, low1, u1, dhr1, dn1, du1, res1,
    sums, tokbuf, cotbuf, keepc, vall, u, np_, f, g, cand, rpre, low, wbuf, proj, du, resbuf, top_of, ends,
    first, tables, st_own, st_got, st_fin,
    gsnd, grcv, gloc, vsnd, vrcv, wsem, psnd, prcv, csnd, crcv, outs,
):
    pos = Place(seq, row)
    at, zl = pos.at, pos.zl
    z, x, y, c = (at[k] for k in "zxyc")
    _, t, d = tokbuf.shape
    steps, H = u.shape[1], u.shape[3]
    parts = w_own.shape[2]
    partner = pos.device(dict(at, z=z + 1 - 2 * zl))
    own = pl.ds(pl.multiple_of(zl * H, H), H)
    other = pl.ds(pl.multiple_of((1 - zl) * H, H), H)
    rows_of = lambda b: pl.ds(pl.multiple_of(b * t, t), t)
    pos.barrier(seq)

    gather = Gather(pos, parts, w_own, w_all, gsnd, grcv, gloc)
    chains = [Chain(pos, tables.at[k], csnd.at[k], crcv.at[k]) for k in range(3)]

    def pair(k, src, dst):
        return remote(src, dst, psnd.at[k], prcv.at[k], partner)

    def tokens(b):
        return pair(0, tok, tokbuf.at[b])

    def cotangents(b):
        return pair(1, cot.at[:, other], cotbuf.at[b])

    def keeps(b):
        return pair(2, keepc.at[b], keepc.at[b])

    def statistics(b, to):
        return pair(3 + b, st_own.at[b], to.at[b])

    def lows(b, cols):
        return pair(5 + b, low.at[rows_of(b), cols], low.at[rows_of(b), cols])

    def vcopies(stage, arriving):
        axis = gather.axis(stage, 0)
        size = pos.sizes[axis]
        for k in pos.others(axis):
            sem = gather.base[stage] + k - 1
            to = pos.moved(axis, k)
            who = pos.moved(axis, size - k) if arriving else at
            mine = gather.region(vall, (), stage, 0, who)
            yield remote(mine, mine, vsnd.at[sem], vrcv.at[sem], pos.device(to))

    def vadvance(stage):
        for copy in vcopies(stage - 1, True):
            copy.wait_recv()
        if stage < 4:
            for copy in vcopies(stage, False):
                copy.start()

    own_tokens = pltpu.make_async_copy(tok, tokbuf.at[zl], outs.at[0])
    own_cot = pltpu.make_async_copy(cot.at[:, own], cotbuf.at[zl], outs.at[1])
    vall[z, x, y, c] = vin[...]
    keepc[zl] = keep_in[...]
    own_tokens.start()
    own_cot.start()
    for copy in vcopies(0, False):
        copy.start()
    keeps(zl).start()
    gather.begin(0)
    gather.begin(1)
    gather.begin(2)
    gather.begin(3)
    vadvance(1)
    gather.turn(0)
    vadvance(2)
    vadvance(3)
    gather.turn(1)
    tokens(zl).start()
    vadvance(4)

    per = d // (seq * row)
    for q in range(d // LANE):
        pieces = []
        for e in range(LANE // per):
            i = q * (LANE // per) + e
            spot = (i // (2 * pos.Y * pos.X), i // (2 * pos.Y) % pos.X, i // 2 % pos.Y, i % 2)
            pieces.append(vall[spot][:, :per].astype(F32))
        value = jnp.concatenate(pieces, axis=-1)
        for l in range(2):
            vec[l, :, q * LANE : (q + 1) * LANE] = value[l * 8 : l * 8 + 8]
    keeps(1 - zl).wait_recv()
    for b in range(2):
        for q in range(t // LANE):
            piece = spread_rows(to_column(keepc[b, q : q + 1, :]))
            keep[b, q * (LANE // SUB) : (q + 1) * (LANE // SUB)] = piece

    def norm0(b):
        piece = 8

        def one(k, _):
            rows = pl.ds(pl.multiple_of(k * piece * SUB, piece * SUB), piece * SUB)
            spot = pl.ds(k * piece, piece)
            v = tokbuf[b, rows, :].astype(F32)
            mu = jnp.mean(v, axis=-1, keepdims=True)
            v = v - mu
            rstd = lax.rsqrt(jnp.mean(v * v, axis=-1, keepdims=True) + epsilon)
            v = v * rstd * vec[0, GAIN : GAIN + 1, :] + vec[0, SHIFT : SHIFT + 1, :]
            at_rows = pl.ds(pl.multiple_of(b * t + k * piece * SUB, piece * SUB), piece * SUB)
            low[at_rows, :] = v.astype(BF16)
            u[b, spot] = tokbuf[b, rows, own].astype(F32).reshape(piece, SUB, H)
            stats[0, 0, b, spot] = jnp.broadcast_to(mu, (piece * SUB, LANE)).reshape(piece, SUB, LANE)
            stats[0, 1, b, spot] = jnp.broadcast_to(rstd, (piece * SUB, LANE)).reshape(
                piece, SUB, LANE
            )
            return 0

        lax.fori_loop(0, steps // piece, one, 0)

    def load(l, m, h):
        slot = lax.rem(m, 2)
        return pltpu.make_async_copy(
            w_all.at[l, m, h],
            wbuf.at[slot, :, :, :, :, :, pl.ds(h * HALF, HALF)],
            wsem.at[slot, h],
        )

    def start_load(l, m):
        for h in range(2):
            load(l, m, h).start()

    def end_load(l, m):
        for h in range(2):
            load(l, m, h).wait()

    def gates(l, m, b):
        w = wbuf[lax.rem(m, 2)].reshape(d, 2 * HALF)
        v = jnp.dot(low[rows_of(b), :], w, preferred_element_type=F32)
        proj[...] = v.reshape(steps, SUB, 2 * HALF)
        cols = lane_tile(m, 2 * LANE)
        wide = pl.ds(pl.multiple_of(zl * H + m * 2 * LANE, 2 * LANE), 2 * LANE)
        peep, bias, rbias, gain, shift = (
            jnp.broadcast_to(vec[l, k : k + 1, wide], (SUB, 2 * LANE))
            for k in (FPEEP, FBIAS, RBIAS, GAIN, SHIFT)
        )

        def both(i, off):
            return jnp.concatenate(
                [proj[i, :, h * HALF + off : h * HALF + off + LANE] for h in range(2)], axis=-1
            )

        def one(i, carry):
            scale, state = carry
            cd = both(i, 0)
            n = (u[b, i, :, cols] - lanes(stats[l, 0, b, i], 2 * LANE)) * lanes(
                stats[l, 1, b, i], 2 * LANE
            ) * gain + shift
            up, down = both_sigmoids(both(i, LANE) + peep * n + bias)
            f[b, i, :, cols] = up
            g[b, i, :, cols] = down
            cand[b, i, :, cols] = cd
            rpre[b, i, :, cols] = both(i, 2 * LANE) + rbias
            a = up * lanes(keep[b, i], 2 * LANE)
            return scale * a, a * state + down * cd

        start = jnp.ones((SUB, 2 * LANE), F32), jnp.zeros((SUB, 2 * LANE), F32)
        scale, state = lax.fori_loop(0, steps, one, start, unroll=8)
        ends[b, 0, :, cols] = scale
        ends[b, 1, :, cols] = state

    def stash(k, src, dst):
        return pltpu.make_async_copy(src, dst, outs.at[k])

    own_tokens.wait()
    norm0(zl)

    def turn(i, _):
        gather.turn(i)

        @pl.when(i >= 3)
        def _():
            @pl.when(i < parts + 1)
            def _():
                start_load(0, i - 3)

        @pl.when((i >= 4) & (i < parts + 2))
        def _():
            end_load(0, i - 4)
            gates(0, i - 4, zl)

        @pl.when(i == parts + 1)
        def _():
            tokens(1 - zl).wait_recv()
            norm0(1 - zl)

        @pl.when(i > parts)
        def _():
            last = i == parts + 2

            def job(k, _):
                m = jnp.where(last, parts - 2 + k // 2, k)
                b = jnp.where(last & (lax.rem(k, 2) == 0), zl, 1 - zl)

                @pl.when(last & (lax.rem(k, 2) == 0))
                def _():
                    end_load(0, m)

                gates(0, m, b)

                @pl.when(jnp.logical_not(last) & (k == 0))
                def _():
                    start_load(0, parts - 2)

                return 0

            @pl.when(last)
            def _():
                start_load(0, parts - 1)

            lax.fori_loop(0, jnp.where(last, 4, parts - 2), job, 0)

        return 0

    lax.fori_loop(2, parts + 3, turn, 0)
    keep_u0, keep_low0 = stash(2, u, u0), stash(3, low, low0)
    gates0 = [stash(4, f, f0), stash(5, g, g0), stash(6, cand, cand0)]
    for copy in [keep_u0, keep_low0] + gates0:
        copy.start()
    chains[0].run(ends, first, False)
    gather.turn(parts + 3)
    keep_u0.wait()
    keep_low0.wait()

    def states0(b):
        def tile(m, _):
            cols = lane_tile(m, 2 * LANE)
            wide = pl.ds(pl.multiple_of(zl * H + m * 2 * LANE, 2 * LANE), 2 * LANE)
            peep = jnp.broadcast_to(vec[0, RPEEP : RPEEP + 1, wide], (SUB, 2 * LANE))

            def one(i, cell):
                before = lanes(keep[b, i], 2 * LANE) * cell
                cell = f[b, i, :, cols] * before + g[b, i, :, cols] * cand[b, i, :, cols]
                gate = jax.nn.sigmoid(rpre[b, i, :, cols] + peep * before)
                np_[b, i, :, cols] = before
                rpre[b, i, :, cols] = gate
                u[b, i, :, cols] = gate * cell + (1.0 - gate) * u[b, i, :, cols]
                return cell

            lax.fori_loop(0, steps, one, first[b, :, cols], unroll=8)
            return 0

        lax.fori_loop(0, parts, tile, 0)

    def local_stats(b):
        def one(q, _):
            v = u[b, pl.ds(q * (LANE // SUB), LANE // SUB)].reshape(LANE, H)
            mu = jnp.mean(v, axis=-1, keepdims=True)
            v = v - mu
            square = jnp.sum(v * v, axis=-1, keepdims=True)
            st_own[b, pl.ds(q, 1), :] = to_row(mu)
            st_own[b, pl.ds(q + t // LANE, 1), :] = to_row(square)
            return 0

        lax.fori_loop(0, t // LANE, one, 0)
        statistics(b, st_got).start()

    def norm1(b):
        half = t // LANE
        statistics(b, st_got).wait_recv()
        m0, m1 = st_own[b, :half], st_got[b, :half]
        gap = m0 - m1
        square = st_own[b, half:] + st_got[b, half:] + gap * gap * (H / 2)
        st_fin[b, :half] = (m0 + m1) * 0.5
        st_fin[b, half:] = lax.rsqrt(square / (2 * H) + epsilon)

        def one(q, _):
            spot = pl.ds(q * (LANE // SUB), LANE // SUB)
            mu = to_column(st_fin[b, pl.ds(q, 1), :])
            rstd = to_column(st_fin[b, pl.ds(q + half, 1), :])
            v = u[b, spot].reshape(LANE, H)
            v = (v - mu) * rstd * vec[1, GAIN : GAIN + 1, own] + vec[1, SHIFT : SHIFT + 1, own]
            low[pl.ds(pl.multiple_of(b * t + q * LANE, LANE), LANE), own] = v.astype(BF16)
            stats[1, 0, b, spot] = spread_rows(mu)
            stats[1, 1, b, spot] = spread_rows(rstd)
            return 0

        lax.fori_loop(0, half, one, 0)
        lows(b, own).start()

    states0(0)
    local_stats(0)
    states0(1)
    keep_p0, keep_r0 = stash(7, np_, p0), stash(8, rpre, r0)
    keep_p0.start()
    keep_r0.start()
    norm1(0)
    local_stats(1)
    gather.turn(parts + 4)
    norm1(1)
    gather.turn(parts + 5)
    gather.turn(parts + 6)
    start_load(1, 0)
    keep_u1 = stash(2, u, u1)
    keep_u1.start()
    for copy in gates0 + [keep_r0]:
        copy.wait()

    def job1(k, _):
        b, m = k // parts, lax.rem(k, parts)

        @pl.when(m == 0)
        def _():
            lows(b, other).wait_recv()

        @pl.when(k == parts)
        def _():
            cotangents(zl).start()

        @pl.when(k + 1 < 2 * parts)
        def _():
            start_load(1, lax.rem(k + 1, parts))

        end_load(1, m)
        gates(1, m, b)
        return 0

    lax.fori_loop(0, 2 * parts, job1, 0)
    keep_low1 = stash(3, low, low1)
    keep_low1.start()
    chains[1].run(ends, first, False)
    keep_p0.wait()
    own_cot.wait()

    def step_back(b, i, cols, top, peep):
        before, gate, up = np_[b, i, :, cols], rpre[b, i, :, cols], f[b, i, :, cols]
        cell = up * before + g[b, i, :, cols] * cand[b, i, :, cols]
        dz_r = top * (cell - u[b, i, :, cols]) * gate * (1.0 - gate)
        direct = top * gate
        kept = lanes(keep[b, i], 2 * LANE)
        decay = up * kept
        return before, gate, up, dz_r, direct, decay, kept * peep * dz_r + decay * direct

    def turn_round(b):
        def tile(m, _):
            cols = lane_tile(m, 2 * LANE)
            wide = pl.ds(pl.multiple_of(zl * H + m * 2 * LANE, 2 * LANE), 2 * LANE)
            peep = jnp.broadcast_to(vec[1, RPEEP : RPEEP + 1, wide], (SUB, 2 * LANE))
            top = cotbuf[b, :, cols].astype(F32).reshape(steps, SUB, 2 * LANE)
            proj[:, :, 2 * LANE : 4 * LANE] = top

            def one(i, cell):
                before = lanes(keep[b, i], 2 * LANE) * cell
                cell = f[b, i, :, cols] * before + g[b, i, :, cols] * cand[b, i, :, cols]
                gate = jax.nn.sigmoid(rpre[b, i, :, cols] + peep * before)
                np_[b, i, :, cols] = before
                rpre[b, i, :, cols] = gate
                proj[i, :, : 2 * LANE] = gate * cell + (1.0 - gate) * u[b, i, :, cols]
                return cell

            lax.fori_loop(0, steps, one, first[b, :, cols], unroll=8)
            v = proj[:, :, : 2 * LANE].reshape(t, 2 * LANE)
            resbuf[b, :, cols] = v.astype(BF16)

            def back(k, carry):
                scale, q = carry
                i = steps - 1 - k
                _, _, _, _, _, decay, term = step_back(
                    b, i, cols, proj[i, :, 2 * LANE : 4 * LANE], peep
                )
                return scale * decay, decay * q + term

            start = jnp.ones((SUB, 2 * LANE), F32), jnp.zeros((SUB, 2 * LANE), F32)
            scale, q = lax.fori_loop(0, steps, back, start, unroll=8)
            ends[b, 0, :, cols] = scale
            ends[b, 1, :, cols] = q
            return 0

        lax.fori_loop(0, parts, tile, 0)

    def blocks(k, _):
        @pl.when(k == 1)
        def _():
            cotangents(1 - zl).wait_recv()

        turn_round(jnp.where(k == 0, zl, 1 - zl))
        return 0

    lax.fori_loop(0, 2, blocks, 0)
    keep_res = stash(9, resbuf, res1)
    keep_res.start()
    chains[2].run(ends, first, True)

    def down(b):
        def tile(m, _):
            cols = lane_tile(m, 2 * LANE)
            wide = pl.ds(pl.multiple_of(zl * H + m * 2 * LANE, 2 * LANE), 2 * LANE)
            fpeep, rpeep, gain, shift = (
                jnp.broadcast_to(vec[1, k : k + 1, wide], (SUB, 2 * LANE))
                for k in (FPEEP, RPEEP, GAIN, SHIFT)
            )

            def one(k, carry):
                q, s0, s1, s2, s3 = carry
                i = steps - 1 - k
                top = top_of[i]
                before, gate, up, dz_r, direct, decay, term = step_back(b, i, cols, top, rpeep)
                e = direct + q
                low_f = g[b, i, :, cols]
                dz_f = e * (up * low_f) * (before - cand[b, i, :, cols])
                n = (u[b, i, :, cols] - lanes(stats[1, 0, b, i], 2 * LANE)) * lanes(
                    stats[1, 1, b, i], 2 * LANE
                ) * gain + shift
                proj[i, :, : 2 * LANE] = e * low_f
                proj[i, :, 2 * LANE : 4 * LANE] = dz_f
                proj[i, :, 4 * LANE :] = dz_r
                cand[b, i, :, cols] = dz_f * fpeep
                rpre[b, i, :, cols] = top * (1.0 - gate)
                return (
                    decay * q + term,
                    s0 + dz_f * n,
                    s1 + dz_r * before,
                    s2 + dz_f,
                    s3 + dz_r,
                )

            top_of[...] = cotbuf[b, :, cols].astype(F32).reshape(steps, SUB, 2 * LANE)
            zero = jnp.zeros((SUB, 2 * LANE), F32)
            carry = lax.fori_loop(0, steps, one, (first[b, :, cols], zero, zero, zero, zero), unroll=4)
            for k in range(4):
                sums[b, k, :, cols] = carry[k + 1]
            for h in range(2):
                for k in range(3):
                    v = proj[:, :, k * 2 * LANE + h * LANE : k * 2 * LANE + (h + 1) * LANE]
                    to = pl.ds(pl.multiple_of((2 * m + h) * HALF + k * LANE, LANE), LANE)
                    du[rows_of(b), to] = v.reshape(t, LANE).astype(BF16)
            return 0

        lax.fori_loop(0, parts, tile, 0)

    keep_low1.wait()

    def last(b):
        yield stash(3, du.at[rows_of(b)], du1.at[rows_of(b)])
        yield stash(4, cand.at[b], dn1.at[b])
        yield stash(5, rpre.at[b], dhr1.at[b])

    down(0)
    for copy in last(0):
        copy.start()
    down(1)
    for copy in last(0):
        copy.wait()
    for copy in last(1):
        copy.start()
    gather.finish()
    for stage in range(4):
        for copy in vcopies(stage, False):
            copy.wait_send()
    for copy in list(last(1)) + [keep_u1, keep_res]:
        copy.wait()
    tokens(zl).wait_send()
    cotangents(zl).wait_send()
    keeps(zl).wait_send()
    for b in range(2):
        statistics(b, st_got).wait_send()
        lows(b, own).wait_send()


def call_forward(seq, row, tok, cot, keep, vin, w_own):
    t, d = tok.shape
    layers, _, parts, _, per, _ = w_own.shape
    Y = row // 2
    X = Y
    Z = seq // X
    H = d // 2
    steps = t // SUB
    act, stat = arr(2, steps, SUB, H), arr(2, steps, SUB, LANE)
    half = arr(2 * t, d, dtype=BF16)
    vmem = pl.BlockSpec(memory_space=pltpu.VMEM)
    hbm = pl.BlockSpec(memory_space=pl.ANY)
    count = Z + 2 * X - 2
    dma = pltpu.SemaphoreType.DMA
    big = pltpu.VMEM((2, steps, SUB, H), F32)
    st = pltpu.VMEM((2, 8, LANE), F32)
    return pl.pallas_call(
        lambda *refs: forward_all(seq, row, *refs),
        in_specs=[hbm, hbm, vmem, vmem, hbm],
        out_specs=[hbm, vmem, vmem, vmem] + [hbm] * 13 + [vmem],
        out_shape=[
            arr(layers, parts, 2, Z, X, Y, 2, per, HALF, dtype=BF16),
            arr(2, 8, d),
            stat,
            arr(2, 2, 2, steps, SUB, LANE),
        ]
        + [act] * 6
        + [half, half, act, act, act, arr(2 * t, 3 * H, dtype=BF16), arr(2, t, H, dtype=BF16)]
        + [arr(2, 4, SUB, H)],
        scratch_shapes=[
            pltpu.VMEM((2, t, d), BF16),
            pltpu.VMEM((2, t, H), BF16),
            pltpu.VMEM((2, 8, LANE), F32),
            pltpu.VMEM((Z, X, Y, 2, 16, LANE), BF16),
            big, big, big, big, big, big,
            pltpu.VMEM((2 * t, d), BF16),
            pltpu.VMEM((2, Z, X, Y, 2, per, 2 * HALF), BF16),
            pltpu.VMEM((steps, SUB, 2 * HALF), F32),
            pltpu.VMEM((2 * t, 3 * H), BF16),
            pltpu.VMEM((2, t, H), BF16),
            pltpu.VMEM((steps, SUB, 2 * LANE), F32),
            pltpu.VMEM((2, 2, SUB, H), F32),
            pltpu.VMEM((2, SUB, H), F32),
            pltpu.VMEM((3, Z // 2, X, 2, 2, H), F32),
            st, st, st,
            dma((2, 2 * parts, count)),
            dma((2, 2 * parts, count)),
            dma((2, 2 * parts)),
            dma((count,)),
            dma((count,)),
            dma((2, 2)),
            dma((7,)),
            dma((7,)),
            dma((3, Z // 2 * X)),
            dma((3, Z // 2 * X)),
            dma((10,)),
        ],
        compiler_params=pltpu.CompilerParams(
            collective_id=0, has_side_effects=True, vmem_limit_bytes=62 << 20
        ),
        name="forward_all",
    )(tok, cot, keep, vin, w_own)


def wrap(a, b):
    return a % b if isinstance(a, int) else lax.rem(a, b)


class Scatter:
    lag = (0, 1, 3, 5, 7)
    sends = (2, 4, 4, 4)
    slots = (2, 6, 6, 6)
    kept = (1, 3, 3, 3)

    def __init__(self, pos, count, low, du, out, keep, send, recv, done, snd, rcv, outs):
        self.pos, self.count, self.low, self.du, self.out = pos, count, low, du, out
        self.keep, self.send, self.recv, self.done = keep, send, recv, done
        self.snd, self.rcv, self.outs = snd, rcv, outs
        n = pos.X - 1
        self.base = (0, 1, 1 + n, 1 + 2 * n)

    def axis(self, stage, h):
        return ("c", ("x", "y")[h], ("y", "x")[h], "z")[stage]

    def copy(self, g, stage, h, k):
        mine, slot = wrap(g, self.sends[stage]), wrap(g, self.slots[stage])
        sem = self.base[stage] + k - 1
        to = self.pos.device(self.pos.moved(self.axis(stage, h), k))
        return remote(
            self.send[stage].at[mine, k - 1], self.recv[stage].at[slot, k - 1],
            self.snd.at[mine, sem], self.rcv.at[slot, sem], to,
        )

    def each(self, stage, h):
        return self.pos.others(self.axis(stage, h))

    def ready(self, g, stage, h):
        def wait():
            for k in self.each(stage, h):
                self.copy(g, stage, h, k).wait_send()

        if isinstance(g, int):
            if g >= self.sends[stage]:
                wait()
        else:
            pl.when(g >= self.sends[stage])(wait)

    def start(self, g, stage, h):
        for k in self.each(stage, h):
            self.copy(g, stage, h, k).start()

    def arrive(self, g, stage, h):
        for k in self.each(stage, h):
            self.copy(g, stage, h, k).wait_recv()

    def stage0(self, g, h):
        pos, low, t = self.pos, self.low, self.low.shape[0]
        rows = low.shape[1] // pos.Z
        slot = wrap(g, 2)
        q = wrap(g, self.count)
        cols = pl.ds(q * HALF if isinstance(q, int) else pl.multiple_of(q * HALF, LANE), HALF)
        self.ready(g, 0, h)
        first = pos.at["c"] == 0

        def one(z, _):
            lhs = low[:, pl.ds(pl.multiple_of(z * rows, LANE), rows)]
            v = lax.dot_general(
                lhs, self.du[:, cols], (((0,), (0,)), ((), ())), preferred_element_type=F32
            )
            v = v.reshape(pos.X, pos.Y, 2, -1, HALF)
            even, odd = v[:, :, 0], v[:, :, 1]
            self.keep[0][z] = jnp.where(first, even, odd)
            self.send[0][slot, 0, z] = jnp.where(first, odd, even).astype(BF16)
            return 0

        lax.fori_loop(0, pos.Z, one, 0)
        self.start(g, 0, h)

    def stage1(self, g, h):
        pos, axis = self.pos, self.axis(1, h)
        slot, got, mine = wrap(g, 4), wrap(g, 2), wrap(g, 3)
        self.arrive(g, 0, h)
        self.ready(g, 1, h)
        for k in range(pos.sizes[axis]):
            p = pos.moved(axis, k)[axis]

            def one(z, _):
                where = (z, p) if h == 0 else (z, slice(None), p)
                v = self.keep[0][where] + self.recv[0][(got, 0) + where].astype(F32)
                if k == 0:
                    self.keep[1][mine, z] = v
                else:
                    self.send[1][slot, k - 1, z] = v.astype(BF16)
                return 0

            lax.fori_loop(0, pos.Z, one, 0)
        self.start(g, 1, h)

    def stage2(self, g, h):
        pos, axis = self.pos, self.axis(2, h)
        slot, got, mine = wrap(g, 4), wrap(g, 6), wrap(g, 3)
        self.arrive(g, 1, h)
        self.ready(g, 2, h)
        for k in range(pos.sizes[axis]):
            p = pos.moved(axis, k)[axis]
            v = self.keep[1][mine, :, p]
            for e in self.each(1, h):
                v = v + self.recv[1][got, e - 1, :, p].astype(F32)
            if k == 0:
                self.keep[2][mine] = v
            else:
                self.send[2][slot, k - 1] = v.astype(BF16)
        self.start(g, 2, h)

    def stage3(self, g, h):
        pos = self.pos
        slot, got, mine = wrap(g, 4), wrap(g, 6), wrap(g, 3)
        self.arrive(g, 2, h)
        self.ready(g, 3, h)
        for k in range(pos.Z):
            p = pos.moved("z", k)["z"]
            v = self.keep[2][mine, p]
            for e in self.each(2, h):
                v = v + self.recv[2][got, e - 1, p].astype(F32)
            if k == 0:
                self.keep[3][mine] = v
            else:
                self.send[3][slot, k - 1] = v.astype(BF16)
        self.start(g, 3, h)

    def result(self, l, q, half, e):
        d = self.out.shape[-1] // 3
        at = e * d + half * (d // 2) + q * LANE
        return pltpu.make_async_copy(
            self.done.at[half, wrap(q, 4), :, e * LANE : (e + 1) * LANE],
            self.out.at[l, :, pl.ds(pl.multiple_of(at, LANE), LANE)],
            self.outs.at[half, wrap(q, 4), e],
        )

    def stage4(self, g, h, l):
        pos = self.pos
        got, mine, q = wrap(g, 6), wrap(g, 3), wrap(g, self.count)
        self.arrive(g, 3, h)
        own, other = self.keep[3][mine], None
        for k in range(1, pos.Z):
            v = self.recv[3][got, k - 1].astype(F32)
            if k % 2 == 0:
                own = own + v
            else:
                other = v if other is None else other + v
        if isinstance(q, int):
            if q >= 4:
                self.stored(l, q - 4)
        else:
            pl.when(q >= 4)(lambda: self.stored(l, q - 4))
        self.done[pos.zl, wrap(q, 4)] = own
        self.done[1 - pos.zl, wrap(q, 4)] = other
        for half in (pos.zl, 1 - pos.zl):
            for e in range(3):
                self.result(l, q, half, e).start()

    def stored(self, l, q):
        for half in (self.pos.zl, 1 - self.pos.zl):
            for e in range(3):
                self.result(l, q, half, e).wait()

    def turn(self, run, l, pair, e, enters=True):
        first = run * self.count

        def stage(s, f):
            g = first + 2 * pair + e - self.lag[s]
            h = (e - self.lag[s]) % 2
            if isinstance(g, int):
                if first <= g < first + self.count:
                    f(g, h)
            elif s:
                pl.when(g >= first)(lambda: f(g, h))
            else:
                f(g, h)

        stage(1, self.stage1)
        if enters:
            stage(0, self.stage0)
        stage(2, self.stage2)
        stage(3, self.stage3)
        stage(4, lambda g, h: self.stage4(g, h, l))

    def written(self, l):
        for q in range(self.count - 4, self.count):
            self.stored(l, q)

    def finish(self, total):
        for stage in range(4):
            for g in range(total - self.sends[stage], total):
                for k in self.each(stage, g % 2):
                    self.copy(g, stage, g % 2, k).wait_send()


def backward_all(
    seq, row, w_all, vec, keep, stats_all, f0, g0, cand0, p0, r0, u0, low0, low1, u1, dhr1, dn1, du1,
    res1, sums1, tok,
    grad, input_grad, result, vout,
    stats, wbuf, du, low, dn, dnsend, dnrecv, hsend, hrecv, tokx, u, dhr, stream, proj,
    keep0, send0, recv0, keep1, send1, recv1, keep2, send2, recv2, keep3, send3, recv3, done,
    ends, first, table, b_own, b_got, b_fin, sums, sumsx, vbuf, vr0, vr1, vr2, vr3,
    snd, rcv, gouts, psnd, prcv, csnd, crcv, vsnd, vrcv, ins, ssem, wsem,
):
    pos = Place(seq, row)
    at, zl = pos.at, pos.zl
    z, x, y, c = (at[k] for k in "zxyc")
    t2, H3 = du.shape
    t, H = t2 // 2, H3 // 3
    d = 2 * H
    steps = t // SUB
    parts = H // WIDE
    partner = pos.device(dict(at, z=z + 1 - 2 * zl))
    own = pl.ds(pl.multiple_of(zl * H, H), H)
    other = pl.ds(pl.multiple_of((1 - zl) * H, H), H)
    rows_of = lambda b: pl.ds(pl.multiple_of(b * t, t), t)
    pos.barrier(seq)

    def load(k, src, dst):
        return pltpu.make_async_copy(src, dst, ins.at[k])

    def weights(l, half):
        zs = pl.ds(half * (pos.Z // 2), pos.Z // 2)
        for m in range(parts):
            for h in range(2):
                q = 2 * m + h
                yield pltpu.make_async_copy(
                    w_all.at[l, m, h, zs],
                    wbuf.at[:, :, :, :, :, q * HALF : (q + 1) * HALF],
                    wsem.at[q],
                )

    def begin(copies):
        for copy in copies:
            copy.start()

    def end(copies):
        for copy in copies:
            copy.wait()

    get_du, get_low, get_dn = load(0, du1, du), load(1, low1, low), load(2, dn1, dn)
    get_u, get_dhr = load(3, u1, u), load(4, dhr1, dhr)
    begin(weights(1, 1 - zl))
    get_stats = load(6, stats_all.at[1], stats)
    begin([get_du, get_low, get_dn, get_u, get_dhr, get_stats])
    scatter = Scatter(
        pos, 2 * parts, low, du, grad, (keep0, keep1, keep2, keep3), (send0, send1, send2, send3),
        (recv0, recv1, recv2, recv3), done, snd, rcv, gouts,
    )
    chain = Chain(pos, table, csnd, crcv)

    def pair(k, src, dst):
        return remote(src, dst, psnd.at[k], prcv.at[k], partner)

    def partial_sums(b):
        return pair(b, dnsend.at[b], dnrecv.at[b])

    def statistics(b):
        return pair(2 + b, b_own.at[b], b_got.at[b])

    def carried():
        return pair(4, hsend, hrecv)

    def results(cols):
        return pair(5, res1.at[1 - zl], result.at[:, cols])

    own_result = load(5, res1.at[zl], result.at[:, own])
    own_result.start()
    results(own).start()
    across = (((1,), (1,)), ((), ()))

    n = t2 // parts
    blocks = t // n

    def product(b, k):
        rows = pl.ds(pl.multiple_of(b * t + k * n, n), n)
        return lax.dot_general(
            du[rows, :], wbuf[...].reshape(H, H3), across, preferred_element_type=F32
        )

    def of_block(k):
        return pl.ds(pl.multiple_of(k * (n // SUB), n // SUB), n // SUB)

    def theirs(q, b, more=None):
        def one(k, _):
            v = product(b, k)
            if more is not None:
                v = v + more[of_block(k)].reshape(n, H)
            dnsend[q, pl.ds(pl.multiple_of(k * n, n), n), :] = v.astype(BF16)
            return 0

        lax.fori_loop(0, blocks, one, 0)
        partial_sums(q).start()

    def ours(to, b, k, fresh=False):
        v = product(b, k).reshape(n // SUB, SUB, H)
        if fresh:
            dn[to, of_block(k)] = v
        else:
            dn[to, of_block(k)] += v

    half = t // LANE

    def norm_sums(l, b):
        partial_sums(b).wait_recv()

        def one(q, _):
            spot = pl.ds(q * (LANE // SUB), LANE // SUB)
            rows = pl.ds(pl.multiple_of(q * LANE, LANE), LANE)
            v = dn[b, spot].reshape(LANE, H) + dnrecv[b, rows, :].astype(F32)
            dn[b, spot] = v.reshape(LANE // SUB, SUB, H)
            xhat = hat(l, b, spot)
            sums[l, 0] += jnp.sum((v * xhat).reshape(LANE // SUB, SUB, H), axis=0)
            sums[l, 1] += jnp.sum(v.reshape(LANE // SUB, SUB, H), axis=0)
            v = v * vec[l, GAIN : GAIN + 1, own]
            b_own[b, pl.ds(q, 1), :] = to_row(jnp.sum(v, axis=-1, keepdims=True))
            b_own[b, pl.ds(q + half, 1), :] = to_row(jnp.sum(v * xhat, axis=-1, keepdims=True))
            return 0

        lax.fori_loop(0, half, one, 0)
        statistics(b).start()

    def hat(l, b, spot):
        mu = stats[0, b, spot].reshape(LANE, LANE)[:, :1]
        rstd = stats[1, b, spot].reshape(LANE, LANE)[:, :1]
        return (u[b, spot].reshape(LANE, H) - mu) * rstd

    def norm_back(l, b):
        statistics(b).wait_recv()
        b_fin[...] = (b_own[b] + b_got[b]) * (1.0 / d)

        def one(q, _):
            spot = pl.ds(q * (LANE // SUB), LANE // SUB)
            xhat = hat(l, b, spot)
            rstd = stats[1, b, spot].reshape(LANE, LANE)[:, :1]
            m0 = to_column(b_fin[pl.ds(q, 1), :])
            m1 = to_column(b_fin[pl.ds(q + half, 1), :])
            v = dn[b, spot].reshape(LANE, H) * vec[l, GAIN : GAIN + 1, own]
            v = dhr[b, spot].reshape(LANE, H) + rstd * (v - m0 - xhat * m1)
            dhr[b, spot] = v.reshape(LANE // SUB, SUB, H)
            return 0

        lax.fori_loop(0, half, one, 0)

    def norm_last():
        for q in range(2):
            partial_sums(q).wait_recv()
        carried().wait_recv()
        get_tok.wait()
        piece = 4
        n = piece * SUB

        def one(k, _):
            spot = pl.ds(k * piece, piece)
            rows = pl.ds(pl.multiple_of(k * n, n), n)
            mu = stats[0, zl, spot].reshape(n, LANE)[:, :1]
            rstd = stats[1, zl, spot].reshape(n, LANE)[:, :1]
            scaled, hats = [], []
            m0 = m1 = 0.0
            for q, part in enumerate((zl, 1 - zl)):
                x = u[zl, spot].reshape(n, H) if q == 0 else tokx[rows, :].astype(F32)
                xhat = (x - mu) * rstd
                v = dn[part, spot].reshape(n, H) + dnrecv[q, rows, :].astype(F32)
                total = sums.at[0] if q == 0 else sumsx
                total[0] += jnp.sum((v * xhat).reshape(piece, SUB, H), axis=0)
                total[1] += jnp.sum(v.reshape(piece, SUB, H), axis=0)
                v = v * vec[0, GAIN : GAIN + 1, own if q == 0 else other]
                m0 += jnp.sum(v, axis=-1, keepdims=True)
                m1 += jnp.sum(v * xhat, axis=-1, keepdims=True)
                scaled.append(v)
                hats.append(xhat)
            m0, m1 = m0 * (1.0 / d), m1 * (1.0 / d)
            for q in range(2):
                v = rstd * (scaled[q] - m0 - hats[q] * m1)
                if q == 0:
                    v = v + dhr[zl, spot].reshape(n, H)
                else:
                    v = v + hrecv[rows, :].astype(F32)
                dnsend[q, rows, :] = v.astype(BF16)
            return 0

        lax.fori_loop(0, steps // piece, one, 0)

    units = 2 * parts
    sources = (f0, g0, cand0, p0, r0)

    def fetch(k):
        slot = lax.rem(k, 2)
        b, m = jnp.where(k < parts, 1 - zl, zl), lax.rem(k, parts)
        for j, src in enumerate(sources):
            yield pltpu.make_async_copy(
                src.at[b, :, :, lane_tile(m, WIDE)], stream.at[slot, j], ssem.at[slot, j]
            )

    def tiles(work, between=None):
        begin(fetch(0))

        def one(k, _):
            @pl.when(k + 1 < units)
            def _():
                begin(fetch(k + 1))

            end(fetch(k))
            b, m = jnp.where(k < parts, 1 - zl, zl), lax.rem(k, parts)
            cols = lane_tile(m, WIDE)
            wide = pl.ds(pl.multiple_of(zl * H + m * WIDE, WIDE), WIDE)
            work(lax.rem(k, 2), b, m, cols, wide)
            if between is not None:
                between(k)
            return 0

        lax.fori_loop(0, units, one, 0)

    def step_back(slot, b, i, cols, peep):
        up, down, cd, before, gate = (stream[slot, j, i] for j in range(5))
        cell = up * before + down * cd
        top = dhr[b, i, :, cols]
        dz_r = top * (cell - u[b, i, :, cols]) * gate * (1.0 - gate)
        direct = top * gate
        kept = lanes(keep[b, i], WIDE)
        decay = up * kept
        term = kept * peep * dz_r + decay * direct
        return up, down, cd, before, gate, top, dz_r, direct, decay, term

    def row_wide(l, k, wide):
        return jnp.broadcast_to(vec[l, k : k + 1, wide], (SUB, WIDE))

    def ends_work(slot, b, m, cols, wide):
        peep = row_wide(0, RPEEP, wide)

        def one(k, carry):
            scale, q = carry
            i = steps - 1 - k
            terms = step_back(slot, b, i, cols, peep)
            gate, top, decay, term = terms[4], terms[5], terms[-2], terms[-1]
            proj[i, :, :WIDE] = top * (1.0 - gate)
            return scale * decay, decay * q + term

        start = jnp.ones((SUB, WIDE), F32), jnp.zeros((SUB, WIDE), F32)
        scale, q = lax.fori_loop(0, steps, one, start, unroll=8)
        ends[b, 0, :, cols] = scale
        ends[b, 1, :, cols] = q

        @pl.when(b != zl)
        def _():
            hsend[:, cols] = proj[:, :, :WIDE].reshape(t, WIDE).astype(BF16)

    def send_carried(k):
        pl.when(k == parts - 1)(lambda: carried().start())

    def down_work(slot, b, m, cols, wide):
        fpeep, rpeep, gain, shift = (row_wide(0, k, wide) for k in (FPEEP, RPEEP, GAIN, SHIFT))

        def one(k, carry):
            q, s0, s1, s2, s3 = carry
            i = steps - 1 - k
            up, low_f, cd, before, gate, top, dz_r, direct, decay, term = step_back(
                slot, b, i, cols, rpeep
            )
            e = direct + q
            dz_f = e * (up * low_f) * (before - cd)
            n = (u[b, i, :, cols] - lanes(stats[0, b, i], WIDE)) * lanes(
                stats[1, b, i], WIDE
            ) * gain + shift
            proj[i, :, :WIDE] = e * low_f
            proj[i, :, WIDE : 2 * WIDE] = dz_f
            proj[i, :, 2 * WIDE :] = dz_r
            dn[b, i, :, cols] = dz_f * fpeep
            dhr[b, i, :, cols] = top * (1.0 - gate)
            return (
                decay * q + term,
                s0 + dz_f * n,
                s1 + dz_r * before,
                s2 + dz_f,
                s3 + dz_r,
            )

        zero = jnp.zeros((SUB, WIDE), F32)
        carry = lax.fori_loop(0, steps, one, (first[b, :, cols], zero, zero, zero, zero), unroll=4)
        for k in range(4):
            sums[0, 2 + k, :, cols] += carry[k + 1]
        for h in range(2):
            for k in range(3):
                v = proj[:, :, k * WIDE + h * LANE : k * WIDE + (h + 1) * LANE]
                to = pl.ds(pl.multiple_of((2 * m + h) * HALF + k * LANE, LANE), LANE)
                du[rows_of(b), to] = v.reshape(t, LANE).astype(BF16)

    def late(run, l, k):
        scatter.turn(run, l, parts + k // 2, k % 2, False)

    sums[...] = jnp.zeros_like(sums)
    sumsx[...] = jnp.zeros_like(sumsx)
    sums[1, 2:6] = sums1[0] + sums1[1]
    get_du.wait()
    end(weights(1, 1 - zl))
    for b in range(2):
        theirs(b, b)
    begin(weights(1, zl))
    get_low.wait()
    get_dn.wait()

    def last_layer(k, _):
        scatter.turn(0, 1, k, 0)

        @pl.when(k == 0)
        def _():
            end(weights(1, zl))

        ours(k // blocks, k // blocks, lax.rem(k, blocks))
        scatter.turn(0, 1, k, 1)
        return 0

    lax.fori_loop(0, parts, last_layer, 0)
    get_low = load(1, low0, low)
    get_low.start()
    get_u.wait()
    get_dhr.wait()
    get_stats.wait()
    begin(weights(0, 1 - zl))
    norm_sums(1, 0)
    norm_sums(1, 1)
    late(0, 1, 0)
    norm_back(1, 0)
    norm_back(1, 1)
    get_u, get_stats = load(3, u0, u), load(6, stats_all.at[0], stats)
    get_tok = load(7, tok.at[:, other], tokx)
    begin([get_u, get_stats, get_tok])
    late(0, 1, 1)
    get_u.wait()
    get_stats.wait()
    late(0, 1, 2)
    tiles(ends_work, send_carried)
    late(0, 1, 3)
    chain.run(ends, first, True)
    for k in range(4, 7):
        late(0, 1, k)
    for b in range(2):
        partial_sums(b).wait_send()
        statistics(b).wait_send()
    end(weights(0, 1 - zl))

    def between(k):
        @pl.when(k == parts - 1)
        def _():
            theirs(0, 1 - zl)
            begin(weights(0, zl))

    tiles(down_work, between)
    end(weights(0, zl))
    theirs(1, 1 - zl, dn.at[1 - zl])
    scatter.written(1)
    get_low.wait()

    def first_layer(k, _):
        scatter.turn(1, 0, k, 0)

        @pl.when(k < blocks)
        def _():
            ours(zl, zl, k)

        @pl.when(k == blocks - 1)
        def _():
            begin(weights(0, 1 - zl))

        @pl.when(k == blocks)
        def _():
            end(weights(0, 1 - zl))

        @pl.when(k >= blocks)
        def _():
            ours(1 - zl, zl, k - blocks, True)

        scatter.turn(1, 0, k, 1)
        return 0

    lax.fori_loop(0, parts, first_layer, 0)
    late(1, 0, 0)
    late(1, 0, 1)
    for b in range(2):
        partial_sums(b).wait_send()
    norm_last()
    out_own = load(0, dnsend.at[0], input_grad.at[:, own])
    out_other = load(1, dnsend.at[1], input_grad.at[:, other])
    begin([out_own, out_other])
    late(1, 0, 2)
    late(1, 0, 3)

    vbuf[...] = jnp.zeros_like(vbuf)
    per = d // (seq * row)
    total = [jnp.sum(sums[l], axis=1) for l in range(2)]
    totalx = jnp.sum(sumsx[...], axis=1)
    blank = jnp.zeros((6, LANE - per), F32) if per < LANE else None
    for i in range(H // per):
        spot = (zl * (pos.Z // 2) + i // (2 * pos.Y * pos.X), i // (2 * pos.Y) % pos.X, i // 2 % pos.Y, i % 2)
        for l in range(2):
            piece = total[l][:, i * per : (i + 1) * per]
            vbuf[spot + (slice(l * 8, l * 8 + 6),)] = jnp.concatenate([piece, blank], axis=-1)
        away = (lax.rem(spot[0] + pos.Z // 2, pos.Z),) + spot[1:]
        piece = totalx[:, i * per : (i + 1) * per]
        vbuf[away + (slice(0, 2),)] = jnp.concatenate([piece, blank[:2]], axis=-1)
    every = slice(None)

    def vspot(stage, who):
        if stage == 0:
            return (every, every, every, who["c"])
        if stage == 1:
            return (every, who["x"], every, c)
        if stage == 2:
            return (every, x, who["y"], c)
        return (who["z"], x, y, c)

    vrecv = (vr0, vr1, vr2, vr3)

    def vcopy(stage, k):
        axis = "cxyz"[stage]
        to = pos.moved(axis, k)
        sem = scatter.base[stage] + k - 1
        return remote(
            vbuf.at[vspot(stage, to)], vrecv[stage].at[k - 1], vsnd.at[sem], vrcv.at[sem],
            pos.device(to),
        )

    def vstart(stage):
        for k in pos.others("cxyz"[stage]):
            vcopy(stage, k).start()

    def vtake(stage):
        for k in pos.others("cxyz"[stage]):
            vcopy(stage, k).wait_recv()
            vbuf[vspot(stage, at)] += vrecv[stage][k - 1]

    vstart(0)
    late(1, 0, 4)
    vtake(0)
    vstart(1)
    late(1, 0, 5)
    vtake(1)
    vstart(2)
    late(1, 0, 6)
    vtake(2)
    vstart(3)
    vtake(3)
    vout[...] = vbuf[z, x, y, c]
    for stage in range(4):
        for k in pos.others("cxyz"[stage]):
            vcopy(stage, k).wait_send()
    scatter.written(0)
    scatter.finish(2 * scatter.count)
    carried().wait_send()
    end([out_own, out_other])
    own_result.wait()
    results(own).wait_send()
    results(other).wait_recv()


def call_backward(seq, row, t, d, given):
    w_all = given[0]
    layers, parts, _, Z, X, Y, _, per, _ = w_all.shape
    H = d // 2
    steps = t // SUB
    vmem = pl.BlockSpec(memory_space=pltpu.VMEM)
    hbm = pl.BlockSpec(memory_space=pl.ANY)
    dma = pltpu.SemaphoreType.DMA
    big = pltpu.VMEM((2, steps, SUB, H), F32)
    half, quarter = pltpu.VMEM((2, t, H), BF16), pltpu.VMEM((t, H), BF16)
    st = pltpu.VMEM((2, 8, LANE), F32)
    count = 1 + 2 * (X - 1) + Z - 1
    chunk = (Z, X, Y, per, HALF)

    def buf(*shape, dtype=BF16):
        return pltpu.VMEM(shape, dtype)

    return pl.pallas_call(
        lambda *refs: backward_all(seq, row, *refs),
        in_specs=[hbm, vmem, vmem] + [hbm] * 14 + [vmem, hbm],
        out_specs=[hbm, hbm, hbm, vmem],
        out_shape=[arr(layers, per, 3 * d)] + [arr(t, d, dtype=BF16)] * 2 + [arr(16, LANE)],
        scratch_shapes=[
            buf(2, 2, steps, SUB, LANE, dtype=F32),
            buf(Z // 2, X, Y, 2, per, 3 * H),
            buf(2 * t, 3 * H),
            buf(2 * t, d),
            big, half, half, quarter, quarter, quarter, big, big,
            buf(2, 5, steps, SUB, WIDE, dtype=F32),
            buf(steps, SUB, 3 * WIDE, dtype=F32),
            buf(*chunk, dtype=F32), buf(2, 1, *chunk), buf(2, 1, *chunk),
            buf(3, Z, Y, per, HALF, dtype=F32), buf(4, X - 1, Z, Y, per, HALF),
            buf(6, X - 1, Z, Y, per, HALF),
            buf(3, Z, per, HALF, dtype=F32), buf(4, Y - 1, Z, per, HALF),
            buf(6, Y - 1, Z, per, HALF),
            buf(3, per, HALF, dtype=F32), buf(4, Z - 1, per, HALF), buf(6, Z - 1, per, HALF),
            buf(2, 4, per, HALF, dtype=F32),
            buf(2, 2, SUB, H, dtype=F32),
            buf(2, SUB, H, dtype=F32),
            buf(Z // 2, X, 2, 2, H, dtype=F32),
            st, st, buf(8, LANE, dtype=F32),
            buf(2, 6, SUB, H, dtype=F32),
            buf(2, SUB, H, dtype=F32),
            buf(Z, X, Y, 2, 16, LANE, dtype=F32),
            buf(1, Z, X, Y, 16, LANE, dtype=F32),
            buf(X - 1, Z, Y, 16, LANE, dtype=F32),
            buf(Y - 1, Z, 16, LANE, dtype=F32),
            buf(Z - 1, 16, LANE, dtype=F32),
            dma((4, count)), dma((6, count)),
            dma((2, 4, 3)),
            dma((6,)), dma((6,)),
            dma((Z // 2 * X,)), dma((Z // 2 * X,)),
            dma((count,)), dma((count,)),
            dma((8,)),
            dma((2, 5)),
            dma((2 * parts,)),
        ],
        compiler_params=pltpu.CompilerParams(
            collective_id=1, has_side_effects=True, vmem_limit_bytes=63 << 20
        ),
        name="backward_all",
    )(*given)


def body(tokens, resets, cotangent, weight, *rows):
    _, t, d = tokens.shape
    layers = weight.shape[0]
    steps = t // SUB
    seq, row = lax.axis_size("seq"), lax.axis_size("row")
    H = d // 2
    parts = H // WIDE

    def permuted(v):
        return v.reshape(SUB, steps, -1).transpose(1, 0, 2).reshape(t, -1)

    def restored(v):
        return v.reshape(steps, SUB, d).transpose(1, 0, 2).reshape(1, t, d)

    keep = permuted((1 - resets[0]).astype(F32)[:, None]).reshape(t // LANE, LANE)
    keep = jnp.pad(keep, ((0, 8 - t // LANE), (0, 0)))
    per = rows[0].shape[-1]
    packed = jnp.stack(rows + (jnp.zeros_like(rows[0]),) * 2, axis=1).reshape(2 * 8, per)
    packed = jnp.pad(packed, ((0, 0), (0, LANE - per)))
    local = weight.reshape(layers, per, 3, 2, parts, 2, LANE).transpose(0, 3, 4, 5, 1, 2, 6)
    local = local.reshape(layers, 2, parts, 2, per, HALF)
    out = call_forward(
        seq, row, permuted(tokens[0]), permuted(cotangent[0]), keep, packed, local
    )
    grad, input_grad, result, vectors = call_backward(seq, row, t, d, tuple(out) + (permuted(tokens[0]),))
    return (restored(result), restored(input_grad), grad) + tuple(
        jnp.stack([vectors[l * 8 + k, :per] for l in range(layers)]) for k in range(6)
    )


def solution(mesh):
    tokens = P("row", "seq", None)
    rows = P(None, ("seq", "row"))
    weight = P(None, ("seq", "row"), None)
    return jax.shard_map(
        body,
        mesh=mesh,
        in_specs=(tokens, P("row", "seq"), tokens, weight) + (rows,) * 6,
        out_specs=(tokens, tokens, weight) + (rows,) * 6,
        check_vma=False,
    )
```

```python
import jax
import jax.numpy as jnp
from jax import lax
from jax.experimental import pallas as pl
from jax.experimental.pallas import tpu as pltpu
from jax.sharding import PartitionSpec as P

epsilon = 1e-05
SUB = 8
WIDE = 256
F32 = jnp.float32
BF16 = jnp.bfloat16
GAIN, SHIFT, FPEEP, RPEEP, FBIAS, RBIAS = range(6)


def both_sigmoids(z):
    tail = jnp.exp(-jnp.abs(z))
    big = 1.0 / (1.0 + tail)
    small = tail * big
    up = z >= 0
    return jnp.where(up, big, small), jnp.where(up, small, big)


def lanes(value, width):
    return jnp.concatenate([value] * (width // value.shape[-1]), axis=-1)


def arr(*shape, dtype=F32):
    return jax.ShapeDtypeStruct(shape, dtype)


MESH = pl.DeviceIdType.MESH
HALF = 384
LANE = 128


class Place:
    def __init__(self, seq, row):
        self.Y = row // 2
        self.X = self.Y
        self.Z = seq // self.X
        self.C = 2
        self.sizes = dict(z=self.Z, x=self.X, y=self.Y, c=self.C)
        s, r = lax.axis_index("seq"), lax.axis_index("row")
        self.at = dict(z=s // self.X, x=s % self.X, y=r // 2, c=r % 2)
        self.zl = lax.rem(self.at["z"], 2)

    def moved(self, axis, k):
        size = self.sizes[axis]
        return dict(self.at, **{axis: lax.rem(self.at[axis] + k, size)})

    def device(self, at):
        return {"seq": at["z"] * self.X + at["x"], "row": at["y"] * 2 + at["c"]}

    def others(self, axis):
        return range(1, self.sizes[axis])

    def barrier(self, seq):
        sem = pltpu.get_barrier_semaphore()
        count = 0
        s, r = lax.axis_index("seq"), lax.axis_index("row")
        for k in range(1, seq):
            pl.semaphore_signal(
                sem, inc=1, device_id={"seq": lax.rem(s + k, seq), "row": r}, device_id_type=MESH
            )
            count += 1
        for axis in ("y", "c"):
            for k in self.others(axis):
                pl.semaphore_signal(
                    sem, inc=1, device_id=self.device(self.moved(axis, k)), device_id_type=MESH
                )
                count += 1
        pl.semaphore_wait(sem, count)


def remote(src, dst, send, recv, to):
    return pltpu.make_async_remote_copy(
        src_ref=src, dst_ref=dst, send_sem=send, recv_sem=recv, device_id=to, device_id_type=MESH
    )


def total_of(scale, state, backward):
    order = range(SUB - 1, -1, -1) if backward else range(SUB)
    whole_scale, whole_state = None, None
    for k in order:
        a, b = scale[k : k + 1], state[k : k + 1]
        if whole_scale is None:
            whole_scale, whole_state = a, b
        else:
            whole_scale, whole_state = a * whole_scale, a * whole_state + b
    return jnp.concatenate([whole_scale, whole_state], axis=0)


class Gather:
    def __init__(self, pos, parts, w_own, w_all, snd, rcv, loc):
        self.pos, self.parts = pos, parts
        self.w_own, self.w_all, self.snd, self.rcv, self.loc = w_own, w_all, snd, rcv, loc
        z, x, y = pos.Z - 1, pos.X - 1, pos.Y - 1
        self.base = (0, z, z + max(x, y), z + 2 * max(x, y))

    def axis(self, stage, h):
        return ("z", ("y", "x")[h], ("x", "y")[h], "c")[stage]

    def region(self, ref, head, stage, h, who):
        every = slice(None)
        spot = [who["z"], who["x"], who["y"], who["c"]]
        if stage >= 1:
            spot[0] = every
        if stage >= 2:
            spot[2 if h == 0 else 1] = every
        if stage >= 3:
            spot[1] = spot[2] = every
        return ref.at[head + tuple(spot)]

    def copies(self, g, stage, h, arriving):
        pos, axis = self.pos, self.axis(stage, h)
        l, m = g // self.parts, lax.rem(g, self.parts)
        size = pos.sizes[axis]
        for k in pos.others(axis):
            sem = self.base[stage] + k - 1
            to = pos.moved(axis, k)
            who = pos.moved(axis, size - k) if arriving else pos.at
            mine = self.region(self.w_all, (l, m, h), stage, h, who)
            src = mine
            if stage == 0 and not arriving:
                src = self.w_own.at[l, lax.rem(to["z"], 2), m, h]
            yield remote(src, mine, self.snd.at[h, g, sem], self.rcv.at[h, g, sem], pos.device(to))

    def local(self, g, h):
        at = self.pos.at
        l, m = g // self.parts, lax.rem(g, self.parts)
        return pltpu.make_async_copy(
            self.w_own.at[l, self.pos.zl, m, h],
            self.w_all.at[l, m, h, at["z"], at["x"], at["y"], at["c"]],
            self.loc.at[h, g],
        )

    def begin(self, g):
        for h in range(2):
            self.local(g, h).start()
            for copy in self.copies(g, 0, h, False):
                copy.start()

    def advance(self, g, stage):
        for h in range(2):
            if stage == 1:
                self.local(g, h).wait()
            for copy in self.copies(g, stage - 1, h, True):
                copy.wait_recv()
            if stage < 4:
                for copy in self.copies(g, stage, h, False):
                    copy.start()

    def turn(self, i):
        total = 2 * self.parts

        @pl.when(i < 2)
        def _():
            self.begin(i + 4)

        for stage in range(1, 5):
            g = i - (stage - 1)

            @pl.when((g >= 0) & (g < total))
            def _():
                self.advance(g, stage)

    def finish(self):
        def one(g, _):
            for h in range(2):
                for stage in range(4):
                    for copy in self.copies(g, stage, h, False):
                        copy.wait_send()
            return 0

        lax.fori_loop(0, 2 * self.parts, one, 0)


class Chain:
    def __init__(self, pos, table, snd, rcv):
        self.pos, self.table, self.snd, self.rcv = pos, table, snd, rcv

    def run(self, ends, first, backward):
        pos, table = self.pos, self.table
        zh, x = pos.at["z"] // 2, pos.at["x"]
        r = lax.axis_index("row")
        for b in range(2):
            table[zh, x, b] = total_of(ends[b, 0], ends[b, 1], backward)
        moves = [(i, j) for i in range(pos.Z // 2) for j in range(pos.X) if i or j]

        def copy(k, sign):
            i, j = moves[k]
            there = lax.rem(zh + i, pos.Z // 2), lax.rem(x + j, pos.X)
            back = lax.rem(zh + pos.Z // 2 - i, pos.Z // 2), lax.rem(x + pos.X - j, pos.X)
            spot = (zh, x) if sign > 0 else back
            to = {"seq": (2 * there[0] + pos.zl) * pos.X + there[1], "row": r}
            return remote(table.at[spot], table.at[spot], self.snd.at[k], self.rcv.at[k], to)

        for k in range(len(moves)):
            copy(k, 1).start()
        for k in range(len(moves)):
            copy(k, -1).wait_recv()
        for k in range(len(moves)):
            copy(k, 1).wait_send()
        blocks = [(i, b, j) for i in range(pos.Z // 2) for b in range(2) for j in range(pos.X)]
        if backward:
            blocks = blocks[::-1]
        value = jnp.zeros_like(table[0, 0, 0, 0:1])
        mine = [value, value]
        for i, b, j in blocks:
            here = (i == zh) & (j == x)
            mine[b] = jnp.where(here, value, mine[b])
            value = table[i, j, b, 0:1] * value + table[i, j, b, 1:2]
        for b in range(2):
            value = mine[b]
            for k in range(SUB - 1, -1, -1) if backward else range(SUB):
                first[b, k : k + 1] = value
                value = ends[b, 0, k : k + 1] * value + ends[b, 1, k : k + 1]


def diagonal():
    return lax.broadcasted_iota(jnp.int32, (LANE, LANE), 0) == lax.broadcasted_iota(
        jnp.int32, (LANE, LANE), 1
    )


def to_row(column):
    spread = jnp.broadcast_to(column, (LANE, LANE))
    return jnp.sum(jnp.where(diagonal(), spread, 0.0), axis=0, keepdims=True)


def to_column(line):
    spread = jnp.broadcast_to(line, (LANE, LANE))
    return jnp.sum(jnp.where(diagonal(), spread, 0.0), axis=1, keepdims=True)


def spread_rows(column):
    return jnp.broadcast_to(column, (LANE, LANE)).reshape(LANE // SUB, SUB, LANE)


def lane_tile(m, width):
    return pl.ds(pl.multiple_of(m * width, width), width)


def forward_all(
    seq, row, tok, cot, keep_in, vin, weight,
    w_all, vec, keep, stats, f0, g0, cand0, p0, r0, u0, low0, low1, u1, dhr1, dn1, du1, res1, resx,
    sums, w_nat, w_own, tokbuf, cotbuf, keepc, vall, u, np_, f, g, cand, rpre, low, wbuf, proj, du, resbuf, top_of, ends,
    first, tables, st_own, st_got, st_fin,
    gsnd, grcv, gloc, vsnd, vrcv, wsem, psnd, prcv, csnd, crcv, outs,
):
    pos = Place(seq, row)
    at, zl = pos.at, pos.zl
    z, x, y, c = (at[k] for k in "zxyc")
    _, t, d = tokbuf.shape
    steps, H = u.shape[1], u.shape[3]
    parts = w_own.shape[2]
    partner = pos.device(dict(at, z=z + 1 - 2 * zl))
    own = pl.ds(pl.multiple_of(zl * H, H), H)
    other = pl.ds(pl.multiple_of((1 - zl) * H, H), H)
    rows_of = lambda b: pl.ds(pl.multiple_of(b * t, t), t)
    get_weight = pltpu.make_async_copy(weight, w_nat, outs.at[10])
    get_weight.start()
    pos.barrier(seq)
    get_weight.wait()
    for l in range(2):
        for p in range(2):
            for m in range(parts):
                for h in range(2):
                    for e in range(3):
                        start = e * d + p * H + (2 * m + h) * LANE
                        w_own[l, p, m, h, :, e * LANE : (e + 1) * LANE] = w_nat[
                            l, :, start : start + LANE
                        ]

    gather = Gather(pos, parts, w_own, w_all, gsnd, grcv, gloc)
    chains = [Chain(pos, tables.at[k], csnd.at[k], crcv.at[k]) for k in range(3)]

    def pair(k, src, dst):
        return remote(src, dst, psnd.at[k], prcv.at[k], partner)

    def tokens(b):
        return pair(0, tok, tokbuf.at[b])

    def cotangents(b):
        return pair(1, cot.at[:, other], cotbuf.at[b])

    def keeps(b):
        return pair(2, keepc.at[b], keepc.at[b])

    def statistics(b, to):
        return pair(3 + b, st_own.at[b], to.at[b])

    def lows(b, cols):
        return pair(5 + b, low.at[rows_of(b), cols], low.at[rows_of(b), cols])

    def results():
        return pair(7, resbuf.at[1 - zl, pl.ds(0, t // 2)], resx)

    def vcopies(stage, arriving):
        axis = gather.axis(stage, 0)
        size = pos.sizes[axis]
        for k in pos.others(axis):
            sem = gather.base[stage] + k - 1
            to = pos.moved(axis, k)
            who = pos.moved(axis, size - k) if arriving else at
            mine = gather.region(vall, (), stage, 0, who)
            yield remote(mine, mine, vsnd.at[sem], vrcv.at[sem], pos.device(to))

    def vadvance(stage):
        for copy in vcopies(stage - 1, True):
            copy.wait_recv()
        if stage < 4:
            for copy in vcopies(stage, False):
                copy.start()

    own_tokens = pltpu.make_async_copy(tok, tokbuf.at[zl], outs.at[0])
    own_cot = pltpu.make_async_copy(cot.at[:, own], cotbuf.at[zl], outs.at[1])
    vall[z, x, y, c] = vin[...]
    keepc[zl] = keep_in[...]
    own_tokens.start()
    own_cot.start()
    for copy in vcopies(0, False):
        copy.start()
    keeps(zl).start()
    gather.begin(0)
    gather.begin(1)
    gather.begin(2)
    gather.begin(3)
    vadvance(1)
    gather.turn(0)
    vadvance(2)
    vadvance(3)
    gather.turn(1)
    tokens(zl).start()
    vadvance(4)

    per = d // (seq * row)
    for q in range(d // LANE):
        pieces = []
        for e in range(LANE // per):
            i = q * (LANE // per) + e
            spot = (i // (2 * pos.Y * pos.X), i // (2 * pos.Y) % pos.X, i // 2 % pos.Y, i % 2)
            pieces.append(vall[spot][:, :per].astype(F32))
        value = jnp.concatenate(pieces, axis=-1)
        for l in range(2):
            vec[l, :, q * LANE : (q + 1) * LANE] = value[l * 8 : l * 8 + 8]
    keeps(1 - zl).wait_recv()
    for b in range(2):
        for q in range(t // LANE):
            piece = spread_rows(to_column(keepc[b, q : q + 1, :]))
            keep[b, q * (LANE // SUB) : (q + 1) * (LANE // SUB)] = piece

    def norm0(b):
        piece = 8

        def one(k, _):
            rows = pl.ds(pl.multiple_of(k * piece * SUB, piece * SUB), piece * SUB)
            spot = pl.ds(k * piece, piece)
            v = tokbuf[b, rows, :].astype(F32)
            mu = jnp.mean(v, axis=-1, keepdims=True)
            v = v - mu
            rstd = lax.rsqrt(jnp.mean(v * v, axis=-1, keepdims=True) + epsilon)
            v = v * rstd * vec[0, GAIN : GAIN + 1, :] + vec[0, SHIFT : SHIFT + 1, :]
            at_rows = pl.ds(pl.multiple_of(b * t + k * piece * SUB, piece * SUB), piece * SUB)
            low[at_rows, :] = v.astype(BF16)
            u[b, spot] = tokbuf[b, rows, own].astype(F32).reshape(piece, SUB, H)
            stats[0, 0, b, spot] = jnp.broadcast_to(mu, (piece * SUB, LANE)).reshape(piece, SUB, LANE)
            stats[0, 1, b, spot] = jnp.broadcast_to(rstd, (piece * SUB, LANE)).reshape(
                piece, SUB, LANE
            )
            return 0

        lax.fori_loop(0, steps // piece, one, 0)

    def load(l, m, h):
        slot = lax.rem(m, 2)
        return pltpu.make_async_copy(
            w_all.at[l, m, h],
            wbuf.at[slot, :, :, :, :, :, pl.ds(h * HALF, HALF)],
            wsem.at[slot, h],
        )

    def start_load(l, m):
        for h in range(2):
            load(l, m, h).start()

    def end_load(l, m):
        for h in range(2):
            load(l, m, h).wait()

    def gates(l, m, b):
        w = wbuf[lax.rem(m, 2)].reshape(d, 2 * HALF)
        v = jnp.dot(low[rows_of(b), :], w, preferred_element_type=F32)
        proj[...] = v.reshape(steps, SUB, 2 * HALF)
        cols = lane_tile(m, 2 * LANE)
        wide = pl.ds(pl.multiple_of(zl * H + m * 2 * LANE, 2 * LANE), 2 * LANE)
        peep, bias, rbias, gain, shift = (
            jnp.broadcast_to(vec[l, k : k + 1, wide], (SUB, 2 * LANE))
            for k in (FPEEP, FBIAS, RBIAS, GAIN, SHIFT)
        )

        def both(i, off):
            return jnp.concatenate(
                [proj[i, :, h * HALF + off : h * HALF + off + LANE] for h in range(2)], axis=-1
            )

        def one(i, carry):
            scale, state = carry
            cd = both(i, 0)
            n = (u[b, i, :, cols] - lanes(stats[l, 0, b, i], 2 * LANE)) * lanes(
                stats[l, 1, b, i], 2 * LANE
            ) * gain + shift
            up, down = both_sigmoids(both(i, LANE) + peep * n + bias)
            f[b, i, :, cols] = up
            g[b, i, :, cols] = down
            cand[b, i, :, cols] = cd
            rpre[b, i, :, cols] = both(i, 2 * LANE) + rbias
            a = up * lanes(keep[b, i], 2 * LANE)
            return scale * a, a * state + down * cd

        start = jnp.ones((SUB, 2 * LANE), F32), jnp.zeros((SUB, 2 * LANE), F32)
        scale, state = lax.fori_loop(0, steps, one, start, unroll=16)
        ends[b, 0, :, cols] = scale
        ends[b, 1, :, cols] = state

    def stash(k, src, dst):
        return pltpu.make_async_copy(src, dst, outs.at[k])

    own_tokens.wait()
    norm0(zl)

    def turn(i, _):
        gather.turn(i)

        @pl.when(i >= 3)
        def _():
            @pl.when(i < parts + 1)
            def _():
                start_load(0, i - 3)

        @pl.when((i >= 4) & (i < parts + 2))
        def _():
            end_load(0, i - 4)
            gates(0, i - 4, zl)

        @pl.when(i == parts + 1)
        def _():
            tokens(1 - zl).wait_recv()
            for k in range(6, 2 * parts):
                gather.begin(k)
            norm0(1 - zl)

        @pl.when(i > parts)
        def _():
            last = i == parts + 2

            def job(k, _):
                m = jnp.where(last, parts - 2 + k // 2, k)
                b = jnp.where(last & (lax.rem(k, 2) == 0), zl, 1 - zl)

                @pl.when(last & (lax.rem(k, 2) == 0))
                def _():
                    end_load(0, m)

                gates(0, m, b)

                @pl.when(jnp.logical_not(last) & (k == 0))
                def _():
                    start_load(0, parts - 2)

                return 0

            @pl.when(last)
            def _():
                start_load(0, parts - 1)

            lax.fori_loop(0, jnp.where(last, 4, parts - 2), job, 0)

        return 0

    lax.fori_loop(2, parts + 3, turn, 0)
    keep_u0, keep_low0 = stash(2, u, u0), stash(3, low, low0)
    gates0 = [stash(4, f, f0), stash(5, g, g0), stash(6, cand, cand0)]
    for copy in [keep_u0, keep_low0] + gates0:
        copy.start()
    chains[0].run(ends, first, False)
    gather.turn(parts + 3)
    keep_u0.wait()
    keep_low0.wait()

    def states0(b):
        def tile(m, _):
            cols = lane_tile(m, 2 * LANE)
            wide = pl.ds(pl.multiple_of(zl * H + m * 2 * LANE, 2 * LANE), 2 * LANE)
            peep = jnp.broadcast_to(vec[0, RPEEP : RPEEP + 1, wide], (SUB, 2 * LANE))

            def one(i, cell):
                before = lanes(keep[b, i], 2 * LANE) * cell
                cell = f[b, i, :, cols] * before + g[b, i, :, cols] * cand[b, i, :, cols]
                gate = jax.nn.sigmoid(rpre[b, i, :, cols] + peep * before)
                np_[b, i, :, cols] = before
                rpre[b, i, :, cols] = gate
                u[b, i, :, cols] = gate * cell + (1.0 - gate) * u[b, i, :, cols]
                return cell

            lax.fori_loop(0, steps, one, first[b, :, cols], unroll=16)
            return 0

        lax.fori_loop(0, parts, tile, 0)

    def local_stats(b):
        def one(q, _):
            v = u[b, pl.ds(q * (LANE // SUB), LANE // SUB)].reshape(LANE, H)
            mu = jnp.mean(v, axis=-1, keepdims=True)
            v = v - mu
            square = jnp.sum(v * v, axis=-1, keepdims=True)
            st_own[b, pl.ds(q, 1), :] = to_row(mu)
            st_own[b, pl.ds(q + t // LANE, 1), :] = to_row(square)
            return 0

        lax.fori_loop(0, t // LANE, one, 0)
        statistics(b, st_got).start()

    def norm1(b):
        half = t // LANE
        statistics(b, st_got).wait_recv()
        m0, m1 = st_own[b, :half], st_got[b, :half]
        gap = m0 - m1
        square = st_own[b, half:] + st_got[b, half:] + gap * gap * (H / 2)
        st_fin[b, :half] = (m0 + m1) * 0.5
        st_fin[b, half:] = lax.rsqrt(square / (2 * H) + epsilon)

        def one(q, _):
            spot = pl.ds(q * (LANE // SUB), LANE // SUB)
            mu = to_column(st_fin[b, pl.ds(q, 1), :])
            rstd = to_column(st_fin[b, pl.ds(q + half, 1), :])
            v = u[b, spot].reshape(LANE, H)
            v = (v - mu) * rstd * vec[1, GAIN : GAIN + 1, own] + vec[1, SHIFT : SHIFT + 1, own]
            low[pl.ds(pl.multiple_of(b * t + q * LANE, LANE), LANE), own] = v.astype(BF16)
            stats[1, 0, b, spot] = spread_rows(mu)
            stats[1, 1, b, spot] = spread_rows(rstd)
            return 0

        lax.fori_loop(0, half, one, 0)
        lows(b, own).start()

    states0(0)
    local_stats(0)
    states0(1)
    keep_p0, keep_r0 = stash(7, np_, p0), stash(8, rpre, r0)
    keep_p0.start()
    keep_r0.start()
    norm1(0)
    local_stats(1)
    gather.turn(parts + 4)
    norm1(1)
    start_load(1, 0)
    keep_u1 = stash(2, u, u1)
    keep_u1.start()
    for copy in gates0 + [keep_r0]:
        copy.wait()

    def job1(k, _):
        b, m = k // parts, lax.rem(k, parts)

        @pl.when(m == 0)
        def _():
            lows(b, other).wait_recv()

        @pl.when(k == parts)
        def _():
            cotangents(zl).start()

        @pl.when((k == 1) | (k == 2))
        def _():
            gather.turn(parts + 4 + k)

        @pl.when(k + 1 < 2 * parts)
        def _():
            start_load(1, lax.rem(k + 1, parts))

        end_load(1, m)
        gates(1, m, b)
        return 0

    lax.fori_loop(0, 2 * parts, job1, 0)
    keep_low1 = stash(3, low, low1)
    keep_low1.start()
    chains[1].run(ends, first, False)
    keep_p0.wait()
    own_cot.wait()

    def step_back(b, i, cols, top, peep):
        before, gate, up = np_[b, i, :, cols], rpre[b, i, :, cols], f[b, i, :, cols]
        cell = up * before + g[b, i, :, cols] * cand[b, i, :, cols]
        dz_r = top * (cell - u[b, i, :, cols]) * gate * (1.0 - gate)
        direct = top * gate
        kept = lanes(keep[b, i], 2 * LANE)
        decay = up * kept
        return before, gate, up, dz_r, direct, decay, kept * peep * dz_r + decay * direct

    def turn_round(b):
        def tile(m, _):
            cols = lane_tile(m, 2 * LANE)
            wide = pl.ds(pl.multiple_of(zl * H + m * 2 * LANE, 2 * LANE), 2 * LANE)
            peep = jnp.broadcast_to(vec[1, RPEEP : RPEEP + 1, wide], (SUB, 2 * LANE))
            top = cotbuf[b, :, cols].astype(F32).reshape(steps, SUB, 2 * LANE)
            proj[:, :, 2 * LANE : 4 * LANE] = top

            def one(i, cell):
                before = lanes(keep[b, i], 2 * LANE) * cell
                cell = f[b, i, :, cols] * before + g[b, i, :, cols] * cand[b, i, :, cols]
                gate = jax.nn.sigmoid(rpre[b, i, :, cols] + peep * before)
                np_[b, i, :, cols] = before
                rpre[b, i, :, cols] = gate
                proj[i, :, : 2 * LANE] = gate * cell + (1.0 - gate) * u[b, i, :, cols]
                return cell

            lax.fori_loop(0, steps, one, first[b, :, cols], unroll=16)
            v = proj[:, :, : 2 * LANE].reshape(t, 2 * LANE)
            resbuf[b, :, cols] = v.astype(BF16)

            def back(k, carry):
                scale, q = carry
                i = steps - 1 - k
                _, _, _, _, _, decay, term = step_back(
                    b, i, cols, proj[i, :, 2 * LANE : 4 * LANE], peep
                )
                return scale * decay, decay * q + term

            start = jnp.ones((SUB, 2 * LANE), F32), jnp.zeros((SUB, 2 * LANE), F32)
            scale, q = lax.fori_loop(0, steps, back, start, unroll=16)
            ends[b, 0, :, cols] = scale
            ends[b, 1, :, cols] = q
            return 0

        lax.fori_loop(0, parts, tile, 0)

    def blocks(k, _):
        @pl.when(k == 1)
        def _():
            cotangents(1 - zl).wait_recv()

        turn_round(jnp.where(k == 0, zl, 1 - zl))
        return 0

    lax.fori_loop(0, 2, blocks, 0)
    results().start()
    keep_res = stash(9, resbuf, res1)
    keep_res.start()
    chains[2].run(ends, first, True)

    def down(b):
        def tile(m, _):
            cols = lane_tile(m, 2 * LANE)
            wide = pl.ds(pl.multiple_of(zl * H + m * 2 * LANE, 2 * LANE), 2 * LANE)
            fpeep, rpeep, gain, shift = (
                jnp.broadcast_to(vec[1, k : k + 1, wide], (SUB, 2 * LANE))
                for k in (FPEEP, RPEEP, GAIN, SHIFT)
            )

            def one(k, carry):
                q, s0, s1, s2, s3 = carry
                i = steps - 1 - k
                top = top_of[i]
                before, gate, up, dz_r, direct, decay, term = step_back(b, i, cols, top, rpeep)
                e = direct + q
                low_f = g[b, i, :, cols]
                dz_f = e * (up * low_f) * (before - cand[b, i, :, cols])
                n = (u[b, i, :, cols] - lanes(stats[1, 0, b, i], 2 * LANE)) * lanes(
                    stats[1, 1, b, i], 2 * LANE
                ) * gain + shift
                proj[i, :, : 2 * LANE] = e * low_f
                proj[i, :, 2 * LANE : 4 * LANE] = dz_f
                proj[i, :, 4 * LANE :] = dz_r
                cand[b, i, :, cols] = dz_f * fpeep
                rpre[b, i, :, cols] = top * (1.0 - gate)
                return (
                    decay * q + term,
                    s0 + dz_f * n,
                    s1 + dz_r * before,
                    s2 + dz_f,
                    s3 + dz_r,
                )

            top_of[...] = cotbuf[b, :, cols].astype(F32).reshape(steps, SUB, 2 * LANE)
            zero = jnp.zeros((SUB, 2 * LANE), F32)
            carry = lax.fori_loop(0, steps, one, (first[b, :, cols], zero, zero, zero, zero), unroll=16)
            for k in range(4):
                sums[b, k, :, cols] = carry[k + 1]
            for h in range(2):
                for k in range(3):
                    v = proj[:, :, k * 2 * LANE + h * LANE : k * 2 * LANE + (h + 1) * LANE]
                    to = pl.ds(pl.multiple_of((2 * m + h) * HALF + k * LANE, LANE), LANE)
                    du[rows_of(b), to] = v.reshape(t, LANE).astype(BF16)
            return 0

        lax.fori_loop(0, parts, tile, 0)

    keep_low1.wait()

    def last(b):
        yield stash(3, du.at[rows_of(b)], du1.at[rows_of(b)])
        yield stash(4, cand.at[b], dn1.at[b])
        yield stash(5, rpre.at[b], dhr1.at[b])

    down(0)
    for copy in last(0):
        copy.start()
    down(1)
    for copy in last(0):
        copy.wait()
    for copy in last(1):
        copy.start()
    gather.finish()
    for stage in range(4):
        for copy in vcopies(stage, False):
            copy.wait_send()
    for copy in list(last(1)) + [keep_u1, keep_res]:
        copy.wait()
    results().wait_recv()
    results().wait_send()
    tokens(zl).wait_send()
    cotangents(zl).wait_send()
    keeps(zl).wait_send()
    for b in range(2):
        statistics(b, st_got).wait_send()
        lows(b, own).wait_send()


def call_forward(seq, row, tok, cot, keep, vin, weight):
    t, d = tok.shape
    layers, per, _ = weight.shape
    Y = row // 2
    X = Y
    Z = seq // X
    H = d // 2
    parts = H // WIDE
    steps = t // SUB
    act, stat = arr(2, steps, SUB, H), arr(2, steps, SUB, LANE)
    half = arr(2 * t, d, dtype=BF16)
    vmem = pl.BlockSpec(memory_space=pltpu.VMEM)
    hbm = pl.BlockSpec(memory_space=pl.ANY)
    count = Z + 2 * X - 2
    dma = pltpu.SemaphoreType.DMA
    big = pltpu.VMEM((2, steps, SUB, H), F32)
    st = pltpu.VMEM((2, 8, LANE), F32)
    return pl.pallas_call(
        lambda *refs: forward_all(seq, row, *refs),
        in_specs=[hbm, hbm, vmem, vmem, hbm],
        out_specs=[hbm, vmem, vmem, vmem] + [hbm] * 14 + [vmem],
        out_shape=[
            arr(layers, parts, 2, Z, X, Y, 2, per, HALF, dtype=BF16),
            arr(2, 8, d),
            stat,
            arr(2, 2, 2, steps, SUB, LANE),
        ]
        + [act] * 6
        + [half, half, act, act, act, arr(2 * t, 3 * H, dtype=BF16), arr(2, t, H, dtype=BF16), arr(t // 2, H, dtype=BF16)]
        + [arr(2, 4, SUB, H)],
        scratch_shapes=[
            pltpu.VMEM((layers, per, 3 * d), BF16),
            pltpu.VMEM((layers, 2, parts, 2, per, HALF), BF16),
            pltpu.VMEM((2, t, d), BF16),
            pltpu.VMEM((2, t, H), BF16),
            pltpu.VMEM((2, 8, LANE), F32),
            pltpu.VMEM((Z, X, Y, 2, 16, LANE), BF16),
            big, big, big, big, big, big,
            pltpu.VMEM((2 * t, d), BF16),
            pltpu.VMEM((2, Z, X, Y, 2, per, 2 * HALF), BF16),
            pltpu.VMEM((steps, SUB, 2 * HALF), F32),
            pltpu.VMEM((2 * t, 3 * H), BF16),
            pltpu.VMEM((2, t, H), BF16),
            pltpu.VMEM((steps, SUB, 2 * LANE), F32),
            pltpu.VMEM((2, 2, SUB, H), F32),
            pltpu.VMEM((2, SUB, H), F32),
            pltpu.VMEM((3, Z // 2, X, 2, 2, H), F32),
            st, st, st,
            dma((2, 2 * parts, count)),
            dma((2, 2 * parts, count)),
            dma((2, 2 * parts)),
            dma((count,)),
            dma((count,)),
            dma((2, 2)),
            dma((8,)),
            dma((8,)),
            dma((3, Z // 2 * X)),
            dma((3, Z // 2 * X)),
            dma((11,)),
        ],
        compiler_params=pltpu.CompilerParams(
            collective_id=0, has_side_effects=True, vmem_limit_bytes=62 << 20
        ),
        name="forward_all",
    )(tok, cot, keep, vin, weight)


def wrap(a, b):
    return a % b if isinstance(a, int) else lax.rem(a, b)


class Scatter:
    lag = (0, 1, 3, 5, 7)
    sends = (2, 4, 4, 4)
    slots = (2, 6, 6, 6)
    kept = (1, 3, 3, 3)

    def __init__(self, pos, count, low, du, out, keep, send, recv, done, snd, rcv, outs):
        self.pos, self.count, self.low, self.du, self.out = pos, count, low, du, out
        self.keep, self.send, self.recv, self.done = keep, send, recv, done
        self.snd, self.rcv, self.outs = snd, rcv, outs
        n = pos.X - 1
        self.base = (0, 1, 1 + n, 1 + 2 * n)

    def axis(self, stage, h):
        return ("c", ("x", "y")[h], ("y", "x")[h], "z")[stage]

    def copy(self, g, stage, h, k):
        mine, slot = wrap(g, self.sends[stage]), wrap(g, self.slots[stage])
        sem = self.base[stage] + k - 1
        to = self.pos.device(self.pos.moved(self.axis(stage, h), k))
        return remote(
            self.send[stage].at[mine, k - 1], self.recv[stage].at[slot, k - 1],
            self.snd.at[mine, sem], self.rcv.at[slot, sem], to,
        )

    def each(self, stage, h):
        return self.pos.others(self.axis(stage, h))

    def ready(self, g, stage, h):
        def wait():
            for k in self.each(stage, h):
                self.copy(g, stage, h, k).wait_send()

        if isinstance(g, int):
            if g >= self.sends[stage]:
                wait()
        else:
            pl.when(g >= self.sends[stage])(wait)

    def start(self, g, stage, h):
        for k in self.each(stage, h):
            self.copy(g, stage, h, k).start()

    def arrive(self, g, stage, h):
        for k in self.each(stage, h):
            self.copy(g, stage, h, k).wait_recv()

    def stage0(self, g, h):
        pos, low, t = self.pos, self.low, self.low.shape[0]
        rows = low.shape[1] // pos.Z
        slot = wrap(g, 2)
        q = wrap(g, self.count)
        cols = pl.ds(q * HALF if isinstance(q, int) else pl.multiple_of(q * HALF, LANE), HALF)
        self.ready(g, 0, h)
        first = pos.at["c"] == 0

        def one(z, _):
            lhs = low[:, pl.ds(pl.multiple_of(z * rows, LANE), rows)]
            v = lax.dot_general(
                lhs, self.du[:, cols], (((0,), (0,)), ((), ())), preferred_element_type=F32
            )
            v = v.reshape(pos.X, pos.Y, 2, -1, HALF)
            even, odd = v[:, :, 0], v[:, :, 1]
            self.keep[0][z] = jnp.where(first, even, odd)
            self.send[0][slot, 0, z] = jnp.where(first, odd, even).astype(BF16)
            return 0

        lax.fori_loop(0, pos.Z, one, 0)
        self.start(g, 0, h)

    def stage1(self, g, h):
        pos, axis = self.pos, self.axis(1, h)
        slot, got, mine = wrap(g, 4), wrap(g, 2), wrap(g, 3)
        self.arrive(g, 0, h)
        self.ready(g, 1, h)
        for k in range(pos.sizes[axis]):
            p = pos.moved(axis, k)[axis]

            def one(z, _):
                where = (z, p) if h == 0 else (z, slice(None), p)
                v = self.keep[0][where] + self.recv[0][(got, 0) + where].astype(F32)
                if k == 0:
                    self.keep[1][mine, z] = v
                else:
                    self.send[1][slot, k - 1, z] = v.astype(BF16)
                return 0

            lax.fori_loop(0, pos.Z, one, 0)
        self.start(g, 1, h)

    def stage2(self, g, h):
        pos, axis = self.pos, self.axis(2, h)
        slot, got, mine = wrap(g, 4), wrap(g, 6), wrap(g, 3)
        self.arrive(g, 1, h)
        self.ready(g, 2, h)
        for k in range(pos.sizes[axis]):
            p = pos.moved(axis, k)[axis]
            v = self.keep[1][mine, :, p]
            for e in self.each(1, h):
                v = v + self.recv[1][got, e - 1, :, p].astype(F32)
            if k == 0:
                self.keep[2][mine] = v
            else:
                self.send[2][slot, k - 1] = v.astype(BF16)
        self.start(g, 2, h)

    def stage3(self, g, h):
        pos = self.pos
        slot, got, mine = wrap(g, 4), wrap(g, 6), wrap(g, 3)
        self.arrive(g, 2, h)
        self.ready(g, 3, h)
        for k in range(pos.Z):
            p = pos.moved("z", k)["z"]
            v = self.keep[2][mine, p]
            for e in self.each(2, h):
                v = v + self.recv[2][got, e - 1, p].astype(F32)
            if k == 0:
                self.keep[3][mine] = v
            else:
                self.send[3][slot, k - 1] = v.astype(BF16)
        self.start(g, 3, h)

    def result(self, l, q, half, e):
        d = self.out.shape[-1] // 3
        at = e * d + half * (d // 2) + q * LANE
        return pltpu.make_async_copy(
            self.done.at[half, wrap(q, 4), :, e * LANE : (e + 1) * LANE],
            self.out.at[l, :, pl.ds(pl.multiple_of(at, LANE), LANE)],
            self.outs.at[half, wrap(q, 4), e],
        )

    def stage4(self, g, h, l):
        pos = self.pos
        got, mine, q = wrap(g, 6), wrap(g, 3), wrap(g, self.count)
        self.arrive(g, 3, h)
        own, other = self.keep[3][mine], None
        for k in range(1, pos.Z):
            v = self.recv[3][got, k - 1].astype(F32)
            if k % 2 == 0:
                own = own + v
            else:
                other = v if other is None else other + v
        if isinstance(q, int):
            if q >= 4:
                self.stored(l, q - 4)
        else:
            pl.when(q >= 4)(lambda: self.stored(l, q - 4))
        self.done[pos.zl, wrap(q, 4)] = own
        self.done[1 - pos.zl, wrap(q, 4)] = other
        for half in (pos.zl, 1 - pos.zl):
            for e in range(3):
                self.result(l, q, half, e).start()

    def stored(self, l, q):
        for half in (self.pos.zl, 1 - self.pos.zl):
            for e in range(3):
                self.result(l, q, half, e).wait()

    def turn(self, run, l, pair, e, enters=True):
        first = run * self.count

        def stage(s, f):
            g = first + 2 * pair + e - self.lag[s]
            h = (e - self.lag[s]) % 2
            if isinstance(g, int):
                if first <= g < first + self.count:
                    f(g, h)
            elif s:
                pl.when(g >= first)(lambda: f(g, h))
            else:
                f(g, h)

        stage(1, self.stage1)
        if enters:
            stage(0, self.stage0)
        stage(2, self.stage2)
        stage(3, self.stage3)
        stage(4, lambda g, h: self.stage4(g, h, l))

    def written(self, l):
        for q in range(self.count - 4, self.count):
            self.stored(l, q)

    def finish(self, total):
        for stage in range(4):
            for g in range(total - self.sends[stage], total):
                for k in self.each(stage, g % 2):
                    self.copy(g, stage, g % 2, k).wait_send()


def backward_all(
    seq, row, w_all, vec, keep, stats_all, f0, g0, cand0, p0, r0, u0, low0, low1, u1, dhr1, dn1, du1,
    res1, resx, sums1, tok,
    grad, input_grad, result, vout,
    stats, wbuf, du, low, dn, dnsend, dnrecv, hsend, hrecv, tokx, u, dhr, stream, proj,
    keep0, send0, recv0, keep1, send1, recv1, keep2, send2, recv2, keep3, send3, recv3, done,
    ends, first, table, b_own, b_got, b_fin, sums, sumsx, vbuf, vr0, vr1, vr2, vr3,
    snd, rcv, gouts, psnd, prcv, csnd, crcv, vsnd, vrcv, ins, ssem, wsem,
):
    pos = Place(seq, row)
    at, zl = pos.at, pos.zl
    z, x, y, c = (at[k] for k in "zxyc")
    t2, H3 = du.shape
    t, H = t2 // 2, H3 // 3
    d = 2 * H
    steps = t // SUB
    parts = H // WIDE
    partner = pos.device(dict(at, z=z + 1 - 2 * zl))
    own = pl.ds(pl.multiple_of(zl * H, H), H)
    other = pl.ds(pl.multiple_of((1 - zl) * H, H), H)
    rows_of = lambda b: pl.ds(pl.multiple_of(b * t, t), t)
    pos.barrier(seq)

    def load(k, src, dst):
        return pltpu.make_async_copy(src, dst, ins.at[k])

    def weights(l, half):
        zs = pl.ds(half * (pos.Z // 2), pos.Z // 2)
        for m in range(parts):
            for h in range(2):
                q = 2 * m + h
                yield pltpu.make_async_copy(
                    w_all.at[l, m, h, zs],
                    wbuf.at[:, :, :, :, :, q * HALF : (q + 1) * HALF],
                    wsem.at[q],
                )

    def begin(copies):
        for copy in copies:
            copy.start()

    def end(copies):
        for copy in copies:
            copy.wait()

    get_du, get_low, get_dn = load(0, du1, du), load(1, low1, low), load(2, dn1, dn)
    get_u, get_dhr = load(3, u1, u), load(4, dhr1, dhr)
    begin(weights(1, 1 - zl))
    get_stats = load(6, stats_all.at[1], stats)
    begin([get_du, get_low, get_dn, get_u, get_dhr, get_stats])
    scatter = Scatter(
        pos, 2 * parts, low, du, grad, (keep0, keep1, keep2, keep3), (send0, send1, send2, send3),
        (recv0, recv1, recv2, recv3), done, snd, rcv, gouts,
    )
    chain = Chain(pos, table, csnd, crcv)

    def pair(k, src, dst):
        return remote(src, dst, psnd.at[k], prcv.at[k], partner)

    def partial_sums(b):
        return pair(b, dnsend.at[b], dnrecv.at[b])

    def statistics(b):
        return pair(2 + b, b_own.at[b], b_got.at[b])

    def carried():
        return pair(4, hsend, hrecv)

    def results(cols):
        rows = pl.ds(t // 2, t // 2)
        return pair(5, res1.at[1 - zl, rows], result.at[rows, cols])

    own_result = load(5, res1.at[zl], result.at[:, own])
    own_result.start()
    got_result = load(8, resx, result.at[pl.ds(0, t // 2), other])
    got_result.start()
    results(own).start()
    across = (((1,), (1,)), ((), ()))

    n = t2 // parts
    blocks = t // n

    def product(b, k):
        rows = pl.ds(pl.multiple_of(b * t + k * n, n), n)
        return lax.dot_general(
            du[rows, :], wbuf[...].reshape(H, H3), across, preferred_element_type=F32
        )

    def of_block(k):
        return pl.ds(pl.multiple_of(k * (n // SUB), n // SUB), n // SUB)

    def theirs(q, b, more=None):
        def one(k, _):
            v = product(b, k)
            if more is not None:
                v = v + more[of_block(k)].reshape(n, H)
            dnsend[q, pl.ds(pl.multiple_of(k * n, n), n), :] = v.astype(BF16)
            return 0

        lax.fori_loop(0, blocks, one, 0)
        partial_sums(q).start()

    def ours(to, b, k, fresh=False):
        v = product(b, k).reshape(n // SUB, SUB, H)
        if fresh:
            dn[to, of_block(k)] = v
        else:
            dn[to, of_block(k)] += v

    half = t // LANE

    def norm_sums(l, b):
        partial_sums(b).wait_recv()

        def one(q, _):
            spot = pl.ds(q * (LANE // SUB), LANE // SUB)
            rows = pl.ds(pl.multiple_of(q * LANE, LANE), LANE)
            v = dn[b, spot].reshape(LANE, H) + dnrecv[b, rows, :].astype(F32)
            dn[b, spot] = v.reshape(LANE // SUB, SUB, H)
            xhat = hat(l, b, spot)
            sums[l, 0] += jnp.sum((v * xhat).reshape(LANE // SUB, SUB, H), axis=0)
            sums[l, 1] += jnp.sum(v.reshape(LANE // SUB, SUB, H), axis=0)
            v = v * vec[l, GAIN : GAIN + 1, own]
            b_own[b, pl.ds(q, 1), :] = to_row(jnp.sum(v, axis=-1, keepdims=True))
            b_own[b, pl.ds(q + half, 1), :] = to_row(jnp.sum(v * xhat, axis=-1, keepdims=True))
            return 0

        lax.fori_loop(0, half, one, 0)
        statistics(b).start()

    def hat(l, b, spot):
        mu = stats[0, b, spot].reshape(LANE, LANE)[:, :1]
        rstd = stats[1, b, spot].reshape(LANE, LANE)[:, :1]
        return (u[b, spot].reshape(LANE, H) - mu) * rstd

    def norm_back(l, b):
        statistics(b).wait_recv()
        b_fin[...] = (b_own[b] + b_got[b]) * (1.0 / d)

        def one(q, _):
            spot = pl.ds(q * (LANE // SUB), LANE // SUB)
            xhat = hat(l, b, spot)
            rstd = stats[1, b, spot].reshape(LANE, LANE)[:, :1]
            m0 = to_column(b_fin[pl.ds(q, 1), :])
            m1 = to_column(b_fin[pl.ds(q + half, 1), :])
            v = dn[b, spot].reshape(LANE, H) * vec[l, GAIN : GAIN + 1, own]
            v = dhr[b, spot].reshape(LANE, H) + rstd * (v - m0 - xhat * m1)
            dhr[b, spot] = v.reshape(LANE // SUB, SUB, H)
            return 0

        lax.fori_loop(0, half, one, 0)

    def norm_last():
        for q in range(2):
            partial_sums(q).wait_recv()
        carried().wait_recv()
        get_tok.wait()
        piece = 4
        n = piece * SUB

        def one(k, _):
            spot = pl.ds(k * piece, piece)
            rows = pl.ds(pl.multiple_of(k * n, n), n)
            mu = stats[0, zl, spot].reshape(n, LANE)[:, :1]
            rstd = stats[1, zl, spot].reshape(n, LANE)[:, :1]
            scaled, hats = [], []
            m0 = m1 = 0.0
            for q, part in enumerate((zl, 1 - zl)):
                x = u[zl, spot].reshape(n, H) if q == 0 else tokx[rows, :].astype(F32)
                xhat = (x - mu) * rstd
                v = dn[part, spot].reshape(n, H) + dnrecv[q, rows, :].astype(F32)
                total = sums.at[0] if q == 0 else sumsx
                total[0] += jnp.sum((v * xhat).reshape(piece, SUB, H), axis=0)
                total[1] += jnp.sum(v.reshape(piece, SUB, H), axis=0)
                v = v * vec[0, GAIN : GAIN + 1, own if q == 0 else other]
                m0 += jnp.sum(v, axis=-1, keepdims=True)
                m1 += jnp.sum(v * xhat, axis=-1, keepdims=True)
                scaled.append(v)
                hats.append(xhat)
            m0, m1 = m0 * (1.0 / d), m1 * (1.0 / d)
            for q in range(2):
                v = rstd * (scaled[q] - m0 - hats[q] * m1)
                if q == 0:
                    v = v + dhr[zl, spot].reshape(n, H)
                else:
                    v = v + hrecv[rows, :].astype(F32)
                dnsend[q, rows, :] = v.astype(BF16)
            return 0

        lax.fori_loop(0, steps // piece, one, 0)

    units = 2 * parts
    sources = (f0, g0, cand0, p0, r0)

    def fetch(k):
        slot = lax.rem(k, 2)
        b, m = jnp.where(k < parts, 1 - zl, zl), lax.rem(k, parts)
        for j, src in enumerate(sources):
            yield pltpu.make_async_copy(
                src.at[b, :, :, lane_tile(m, WIDE)], stream.at[slot, j], ssem.at[slot, j]
            )

    def tiles(work, between=None):
        begin(fetch(0))

        def one(k, _):
            @pl.when(k + 1 < units)
            def _():
                begin(fetch(k + 1))

            end(fetch(k))
            b, m = jnp.where(k < parts, 1 - zl, zl), lax.rem(k, parts)
            cols = lane_tile(m, WIDE)
            wide = pl.ds(pl.multiple_of(zl * H + m * WIDE, WIDE), WIDE)
            work(lax.rem(k, 2), b, m, cols, wide)
            if between is not None:
                between(k)
            return 0

        lax.fori_loop(0, units, one, 0)

    def step_back(slot, b, i, cols, peep):
        up, down, cd, before, gate = (stream[slot, j, i] for j in range(5))
        cell = up * before + down * cd
        top = dhr[b, i, :, cols]
        dz_r = top * (cell - u[b, i, :, cols]) * gate * (1.0 - gate)
        direct = top * gate
        kept = lanes(keep[b, i], WIDE)
        decay = up * kept
        term = kept * peep * dz_r + decay * direct
        return up, down, cd, before, gate, top, dz_r, direct, decay, term

    def row_wide(l, k, wide):
        return jnp.broadcast_to(vec[l, k : k + 1, wide], (SUB, WIDE))

    def ends_work(slot, b, m, cols, wide):
        peep = row_wide(0, RPEEP, wide)

        def one(k, carry):
            scale, q = carry
            i = steps - 1 - k
            terms = step_back(slot, b, i, cols, peep)
            gate, top, decay, term = terms[4], terms[5], terms[-2], terms[-1]
            proj[i, :, :WIDE] = top * (1.0 - gate)
            return scale * decay, decay * q + term

        start = jnp.ones((SUB, WIDE), F32), jnp.zeros((SUB, WIDE), F32)
        scale, q = lax.fori_loop(0, steps, one, start, unroll=16)
        ends[b, 0, :, cols] = scale
        ends[b, 1, :, cols] = q

        @pl.when(b != zl)
        def _():
            hsend[:, cols] = proj[:, :, :WIDE].reshape(t, WIDE).astype(BF16)

    def send_carried(k):
        pl.when(k == parts - 1)(lambda: carried().start())

    def down_work(slot, b, m, cols, wide):
        fpeep, rpeep, gain, shift = (row_wide(0, k, wide) for k in (FPEEP, RPEEP, GAIN, SHIFT))

        def one(k, carry):
            q, s0, s1, s2, s3 = carry
            i = steps - 1 - k
            up, low_f, cd, before, gate, top, dz_r, direct, decay, term = step_back(
                slot, b, i, cols, rpeep
            )
            e = direct + q
            dz_f = e * (up * low_f) * (before - cd)
            n = (u[b, i, :, cols] - lanes(stats[0, b, i], WIDE)) * lanes(
                stats[1, b, i], WIDE
            ) * gain + shift
            proj[i, :, :WIDE] = e * low_f
            proj[i, :, WIDE : 2 * WIDE] = dz_f
            proj[i, :, 2 * WIDE :] = dz_r
            dn[b, i, :, cols] = dz_f * fpeep
            dhr[b, i, :, cols] = top * (1.0 - gate)
            return (
                decay * q + term,
                s0 + dz_f * n,
                s1 + dz_r * before,
                s2 + dz_f,
                s3 + dz_r,
            )

        zero = jnp.zeros((SUB, WIDE), F32)
        carry = lax.fori_loop(0, steps, one, (first[b, :, cols], zero, zero, zero, zero), unroll=16)
        for k in range(4):
            sums[0, 2 + k, :, cols] += carry[k + 1]
        for h in range(2):
            for k in range(3):
                v = proj[:, :, k * WIDE + h * LANE : k * WIDE + (h + 1) * LANE]
                to = pl.ds(pl.multiple_of((2 * m + h) * HALF + k * LANE, LANE), LANE)
                du[rows_of(b), to] = v.reshape(t, LANE).astype(BF16)

    def late(run, l, k):
        scatter.turn(run, l, parts + k // 2, k % 2, False)

    sums[...] = jnp.zeros_like(sums)
    sumsx[...] = jnp.zeros_like(sumsx)
    sums[1, 2:6] = sums1[0] + sums1[1]
    get_du.wait()
    end(weights(1, 1 - zl))
    for b in range(2):
        theirs(b, b)
    begin(weights(1, zl))
    get_low.wait()
    get_dn.wait()

    def last_layer(k, _):
        scatter.turn(0, 1, k, 0)

        @pl.when(k == 0)
        def _():
            end(weights(1, zl))

        ours(k // blocks, k // blocks, lax.rem(k, blocks))
        scatter.turn(0, 1, k, 1)
        return 0

    lax.fori_loop(0, parts, last_layer, 0)
    get_low = load(1, low0, low)
    get_low.start()
    get_u.wait()
    get_dhr.wait()
    get_stats.wait()
    begin(weights(0, 1 - zl))
    norm_sums(1, 0)
    norm_sums(1, 1)
    late(0, 1, 0)
    norm_back(1, 0)
    norm_back(1, 1)
    get_u, get_stats = load(3, u0, u), load(6, stats_all.at[0], stats)
    get_tok = load(7, tok.at[:, other], tokx)
    begin([get_u, get_stats, get_tok])
    late(0, 1, 1)
    get_u.wait()
    get_stats.wait()
    late(0, 1, 2)
    tiles(ends_work, send_carried)
    late(0, 1, 3)
    chain.run(ends, first, True)
    for k in range(4, 7):
        late(0, 1, k)
    for b in range(2):
        partial_sums(b).wait_send()
        statistics(b).wait_send()
    end(weights(0, 1 - zl))

    def between(k):
        @pl.when(k == parts - 1)
        def _():
            theirs(0, 1 - zl)
            begin(weights(0, zl))

        for e in range(2):
            pl.when(k == parts + e)(lambda: scatter.turn(1, 0, 0, e))

    scatter.written(1)
    get_low.wait()
    tiles(down_work, between)
    end(weights(0, zl))
    theirs(1, 1 - zl, dn.at[1 - zl])

    def first_layer(k, _):
        scatter.turn(1, 0, k, 0)

        @pl.when(k == 1)
        def _():
            ours(zl, zl, 0)
            ours(zl, zl, 1)
            begin(weights(0, 1 - zl))

        @pl.when(k == 2)
        def _():
            end(weights(0, 1 - zl))

        @pl.when(k > 1)
        def _():
            ours(1 - zl, zl, k - 2, True)

        scatter.turn(1, 0, k, 1)
        return 0

    lax.fori_loop(1, parts, first_layer, 0)
    late(1, 0, 0)
    late(1, 0, 1)
    for b in range(2):
        partial_sums(b).wait_send()
    norm_last()
    out_own = load(0, dnsend.at[0], input_grad.at[:, own])
    out_other = load(1, dnsend.at[1], input_grad.at[:, other])
    begin([out_own, out_other])
    late(1, 0, 2)
    late(1, 0, 3)

    vbuf[...] = jnp.zeros_like(vbuf)
    per = d // (seq * row)
    total = [jnp.sum(sums[l], axis=1) for l in range(2)]
    totalx = jnp.sum(sumsx[...], axis=1)
    blank = jnp.zeros((6, LANE - per), F32) if per < LANE else None
    for i in range(H // per):
        spot = (zl * (pos.Z // 2) + i // (2 * pos.Y * pos.X), i // (2 * pos.Y) % pos.X, i // 2 % pos.Y, i % 2)
        for l in range(2):
            piece = total[l][:, i * per : (i + 1) * per]
            vbuf[spot + (slice(l * 8, l * 8 + 6),)] = jnp.concatenate([piece, blank], axis=-1)
        away = (lax.rem(spot[0] + pos.Z // 2, pos.Z),) + spot[1:]
        piece = totalx[:, i * per : (i + 1) * per]
        vbuf[away + (slice(0, 2),)] = jnp.concatenate([piece, blank[:2]], axis=-1)
    every = slice(None)

    def vspot(stage, who):
        if stage == 0:
            return (every, every, every, who["c"])
        if stage == 1:
            return (every, who["x"], every, c)
        if stage == 2:
            return (every, x, who["y"], c)
        return (who["z"], x, y, c)

    vrecv = (vr0, vr1, vr2, vr3)

    def vcopy(stage, k):
        axis = "cxyz"[stage]
        to = pos.moved(axis, k)
        sem = scatter.base[stage] + k - 1
        return remote(
            vbuf.at[vspot(stage, to)], vrecv[stage].at[k - 1], vsnd.at[sem], vrcv.at[sem],
            pos.device(to),
        )

    def vstart(stage):
        for k in pos.others("cxyz"[stage]):
            vcopy(stage, k).start()

    def vtake(stage):
        for k in pos.others("cxyz"[stage]):
            vcopy(stage, k).wait_recv()
            vbuf[vspot(stage, at)] += vrecv[stage][k - 1]

    vstart(0)
    late(1, 0, 4)
    vtake(0)
    vstart(1)
    late(1, 0, 5)
    vtake(1)
    vstart(2)
    late(1, 0, 6)
    vtake(2)
    vstart(3)
    vtake(3)
    vout[...] = vbuf[z, x, y, c]
    for stage in range(4):
        for k in pos.others("cxyz"[stage]):
            vcopy(stage, k).wait_send()
    scatter.written(0)
    scatter.finish(2 * scatter.count)
    carried().wait_send()
    end([out_own, out_other])
    own_result.wait()
    got_result.wait()
    results(own).wait_send()
    results(other).wait_recv()


def call_backward(seq, row, t, d, given):
    w_all = given[0]
    layers, parts, _, Z, X, Y, _, per, _ = w_all.shape
    H = d // 2
    steps = t // SUB
    vmem = pl.BlockSpec(memory_space=pltpu.VMEM)
    hbm = pl.BlockSpec(memory_space=pl.ANY)
    dma = pltpu.SemaphoreType.DMA
    big = pltpu.VMEM((2, steps, SUB, H), F32)
    half, quarter = pltpu.VMEM((2, t, H), BF16), pltpu.VMEM((t, H), BF16)
    st = pltpu.VMEM((2, 8, LANE), F32)
    count = 1 + 2 * (X - 1) + Z - 1
    chunk = (Z, X, Y, per, HALF)

    def buf(*shape, dtype=BF16):
        return pltpu.VMEM(shape, dtype)

    return pl.pallas_call(
        lambda *refs: backward_all(seq, row, *refs),
        in_specs=[hbm, vmem, vmem] + [hbm] * 15 + [vmem, hbm],
        out_specs=[hbm, hbm, hbm, vmem],
        out_shape=[arr(layers, per, 3 * d)] + [arr(t, d, dtype=BF16)] * 2 + [arr(16, LANE)],
        scratch_shapes=[
            buf(2, 2, steps, SUB, LANE, dtype=F32),
            buf(Z // 2, X, Y, 2, per, 3 * H),
            buf(2 * t, 3 * H),
            buf(2 * t, d),
            big, half, half, quarter, quarter, quarter, big, big,
            buf(2, 5, steps, SUB, WIDE, dtype=F32),
            buf(steps, SUB, 3 * WIDE, dtype=F32),
            buf(*chunk, dtype=F32), buf(2, 1, *chunk), buf(2, 1, *chunk),
            buf(3, Z, Y, per, HALF, dtype=F32), buf(4, X - 1, Z, Y, per, HALF),
            buf(6, X - 1, Z, Y, per, HALF),
            buf(3, Z, per, HALF, dtype=F32), buf(4, Y - 1, Z, per, HALF),
            buf(6, Y - 1, Z, per, HALF),
            buf(3, per, HALF, dtype=F32), buf(4, Z - 1, per, HALF), buf(6, Z - 1, per, HALF),
            buf(2, 4, per, HALF, dtype=F32),
            buf(2, 2, SUB, H, dtype=F32),
            buf(2, SUB, H, dtype=F32),
            buf(Z // 2, X, 2, 2, H, dtype=F32),
            st, st, buf(8, LANE, dtype=F32),
            buf(2, 6, SUB, H, dtype=F32),
            buf(2, SUB, H, dtype=F32),
            buf(Z, X, Y, 2, 16, LANE, dtype=F32),
            buf(1, Z, X, Y, 16, LANE, dtype=F32),
            buf(X - 1, Z, Y, 16, LANE, dtype=F32),
            buf(Y - 1, Z, 16, LANE, dtype=F32),
            buf(Z - 1, 16, LANE, dtype=F32),
            dma((4, count)), dma((6, count)),
            dma((2, 4, 3)),
            dma((6,)), dma((6,)),
            dma((Z // 2 * X,)), dma((Z // 2 * X,)),
            dma((count,)), dma((count,)),
            dma((9,)),
            dma((2, 5)),
            dma((2 * parts,)),
        ],
        compiler_params=pltpu.CompilerParams(
            collective_id=1, has_side_effects=True, vmem_limit_bytes=63 << 20
        ),
        name="backward_all",
    )(*given)


def body(tokens, resets, cotangent, weight, *rows):
    _, t, d = tokens.shape
    layers = weight.shape[0]
    steps = t // SUB
    seq, row = lax.axis_size("seq"), lax.axis_size("row")

    def permuted(v):
        return v.reshape(SUB, steps, -1).transpose(1, 0, 2).reshape(t, -1)

    def restored(v):
        return v.reshape(steps, SUB, d).transpose(1, 0, 2).reshape(1, t, d)

    keep = permuted((1 - resets[0]).astype(F32)[:, None]).reshape(t // LANE, LANE)
    keep = jnp.pad(keep, ((0, 8 - t // LANE), (0, 0)))
    per = rows[0].shape[-1]
    blank = jnp.zeros((), BF16)
    packed = sum(
        lax.pad(v, blank, ((k, 7 - k, 7), (0, LANE - per, 0))) for k, v in enumerate(rows)
    )
    out = call_forward(
        seq, row, permuted(tokens[0]), permuted(cotangent[0]), keep, packed, weight
    )
    grad, input_grad, result, vectors = call_backward(seq, row, t, d, tuple(out) + (permuted(tokens[0]),))
    return (restored(result), restored(input_grad), grad) + tuple(
        jnp.stack([vectors[l * 8 + k, :per] for l in range(layers)]) for k in range(6)
    )


def solution(mesh):
    tokens = P("row", "seq", None)
    rows = P(None, ("seq", "row"))
    weight = P(None, ("seq", "row"), None)
    return jax.shard_map(
        body,
        mesh=mesh,
        in_specs=(tokens, P("row", "seq"), tokens, weight) + (rows,) * 6,
        out_specs=(tokens, tokens, weight) + (rows,) * 6,
        check_vma=False,
    )
```

```python
import jax
import jax.numpy as jnp
from jax import lax
from jax.experimental import pallas as pl
from jax.experimental.pallas import tpu as pltpu
from jax.sharding import PartitionSpec as P

epsilon = 1e-05
SUB = 8
WIDE = 256
F32 = jnp.float32
BF16 = jnp.bfloat16
GAIN, SHIFT, FPEEP, RPEEP, FBIAS, RBIAS = range(6)


def both_sigmoids(z):
    tail = jnp.exp(-jnp.abs(z))
    big = 1.0 / (1.0 + tail)
    small = tail * big
    up = z >= 0
    return jnp.where(up, big, small), jnp.where(up, small, big)


def lanes(value, width):
    return jnp.concatenate([value] * (width // value.shape[-1]), axis=-1)


def arr(*shape, dtype=F32):
    return jax.ShapeDtypeStruct(shape, dtype)


MESH = pl.DeviceIdType.MESH
HALF = 384
LANE = 128


class Place:
    def __init__(self, seq, row):
        self.Y = row // 2
        self.X = self.Y
        self.Z = seq // self.X
        self.C = 2
        self.sizes = dict(z=self.Z, x=self.X, y=self.Y, c=self.C)
        s, r = lax.axis_index("seq"), lax.axis_index("row")
        self.at = dict(z=s // self.X, x=s % self.X, y=r // 2, c=r % 2)
        self.zl = lax.rem(self.at["z"], 2)

    def moved(self, axis, k):
        size = self.sizes[axis]
        return dict(self.at, **{axis: lax.rem(self.at[axis] + k, size)})

    def device(self, at):
        return {"seq": at["z"] * self.X + at["x"], "row": at["y"] * 2 + at["c"]}

    def others(self, axis):
        return range(1, self.sizes[axis])

    def barrier(self, seq):
        sem = pltpu.get_barrier_semaphore()
        count = 0
        s, r = lax.axis_index("seq"), lax.axis_index("row")
        for k in range(1, seq):
            pl.semaphore_signal(
                sem, inc=1, device_id={"seq": lax.rem(s + k, seq), "row": r}, device_id_type=MESH
            )
            count += 1
        for axis in ("y", "c"):
            for k in self.others(axis):
                pl.semaphore_signal(
                    sem, inc=1, device_id=self.device(self.moved(axis, k)), device_id_type=MESH
                )
                count += 1
        pl.semaphore_wait(sem, count)


def remote(src, dst, send, recv, to):
    return pltpu.make_async_remote_copy(
        src_ref=src, dst_ref=dst, send_sem=send, recv_sem=recv, device_id=to, device_id_type=MESH
    )


def total_of(scale, state, backward):
    order = range(SUB - 1, -1, -1) if backward else range(SUB)
    whole_scale, whole_state = None, None
    for k in order:
        a, b = scale[k : k + 1], state[k : k + 1]
        if whole_scale is None:
            whole_scale, whole_state = a, b
        else:
            whole_scale, whole_state = a * whole_scale, a * whole_state + b
    return jnp.concatenate([whole_scale, whole_state], axis=0)


class Gather:
    def __init__(self, pos, parts, w_own, w_all, snd, rcv, loc):
        self.pos, self.parts = pos, parts
        self.w_own, self.w_all, self.snd, self.rcv, self.loc = w_own, w_all, snd, rcv, loc
        z, x, y = pos.Z - 1, pos.X - 1, pos.Y - 1
        self.base = (0, z, z + max(x, y), z + 2 * max(x, y))

    def axis(self, stage, h):
        return ("z", ("y", "x")[h], ("x", "y")[h], "c")[stage]

    def region(self, ref, head, stage, h, who):
        every = slice(None)
        spot = [who["z"], who["x"], who["y"], who["c"]]
        if stage >= 1:
            spot[0] = every
        if stage >= 2:
            spot[2 if h == 0 else 1] = every
        if stage >= 3:
            spot[1] = spot[2] = every
        return ref.at[head + tuple(spot)]

    def copies(self, g, stage, h, arriving):
        pos, axis = self.pos, self.axis(stage, h)
        l, m = g // self.parts, lax.rem(g, self.parts)
        size = pos.sizes[axis]
        for k in pos.others(axis):
            sem = self.base[stage] + k - 1
            to = pos.moved(axis, k)
            who = pos.moved(axis, size - k) if arriving else pos.at
            mine = self.region(self.w_all, (l, m, h), stage, h, who)
            src = mine
            if stage == 0 and not arriving:
                src = self.w_own.at[l, lax.rem(to["z"], 2), m, h]
            yield remote(src, mine, self.snd.at[h, g, sem], self.rcv.at[h, g, sem], pos.device(to))

    def local(self, g, h):
        at = self.pos.at
        l, m = g // self.parts, lax.rem(g, self.parts)
        return pltpu.make_async_copy(
            self.w_own.at[l, self.pos.zl, m, h],
            self.w_all.at[l, m, h, at["z"], at["x"], at["y"], at["c"]],
            self.loc.at[h, g],
        )

    def begin(self, g):
        for h in range(2):
            self.local(g, h).start()
            for copy in self.copies(g, 0, h, False):
                copy.start()

    def advance(self, g, stage):
        for h in range(2):
            if stage == 1:
                self.local(g, h).wait()
            for copy in self.copies(g, stage - 1, h, True):
                copy.wait_recv()
            if stage < 4:
                for copy in self.copies(g, stage, h, False):
                    copy.start()

    def turn(self, i):
        total = 2 * self.parts

        @pl.when(i < 2)
        def _():
            self.begin(i + 4)

        for stage in range(1, 5):
            g = i - (stage - 1)

            @pl.when((g >= 0) & (g < total))
            def _():
                self.advance(g, stage)

    def finish(self):
        def one(g, _):
            for h in range(2):
                for stage in range(4):
                    for copy in self.copies(g, stage, h, False):
                        copy.wait_send()
            return 0

        lax.fori_loop(0, 2 * self.parts, one, 0)


class Chain:
    def __init__(self, pos, table, snd, rcv):
        self.pos, self.table, self.snd, self.rcv = pos, table, snd, rcv

    def run(self, ends, first, backward):
        pos, table = self.pos, self.table
        zh, x = pos.at["z"] // 2, pos.at["x"]
        r = lax.axis_index("row")
        for b in range(2):
            table[zh, x, b] = total_of(ends[b, 0], ends[b, 1], backward)
        moves = [(i, j) for i in range(pos.Z // 2) for j in range(pos.X) if i or j]

        def copy(k, sign):
            i, j = moves[k]
            there = lax.rem(zh + i, pos.Z // 2), lax.rem(x + j, pos.X)
            back = lax.rem(zh + pos.Z // 2 - i, pos.Z // 2), lax.rem(x + pos.X - j, pos.X)
            spot = (zh, x) if sign > 0 else back
            to = {"seq": (2 * there[0] + pos.zl) * pos.X + there[1], "row": r}
            return remote(table.at[spot], table.at[spot], self.snd.at[k], self.rcv.at[k], to)

        for k in range(len(moves)):
            copy(k, 1).start()
        for k in range(len(moves)):
            copy(k, -1).wait_recv()
        for k in range(len(moves)):
            copy(k, 1).wait_send()
        blocks = [(i, b, j) for i in range(pos.Z // 2) for b in range(2) for j in range(pos.X)]
        if backward:
            blocks = blocks[::-1]
        value = jnp.zeros_like(table[0, 0, 0, 0:1])
        mine = [value, value]
        for i, b, j in blocks:
            here = (i == zh) & (j == x)
            mine[b] = jnp.where(here, value, mine[b])
            value = table[i, j, b, 0:1] * value + table[i, j, b, 1:2]
        for b in range(2):
            value = mine[b]
            for k in range(SUB - 1, -1, -1) if backward else range(SUB):
                first[b, k : k + 1] = value
                value = ends[b, 0, k : k + 1] * value + ends[b, 1, k : k + 1]


def diagonal():
    return lax.broadcasted_iota(jnp.int32, (LANE, LANE), 0) == lax.broadcasted_iota(
        jnp.int32, (LANE, LANE), 1
    )


def to_row(column):
    spread = jnp.broadcast_to(column, (LANE, LANE))
    return jnp.sum(jnp.where(diagonal(), spread, 0.0), axis=0, keepdims=True)


def to_column(line):
    spread = jnp.broadcast_to(line, (LANE, LANE))
    return jnp.sum(jnp.where(diagonal(), spread, 0.0), axis=1, keepdims=True)


def spread_rows(column):
    return jnp.broadcast_to(column, (LANE, LANE)).reshape(LANE // SUB, SUB, LANE)


def lane_tile(m, width):
    return pl.ds(pl.multiple_of(m * width, width), width)


def forward_all(
    seq, row, tok, cot, resets, gain_in, shift_in, fpeep_in, rpeep_in, fbias_in, rbias_in, weight,
    w_all, vec, keep, stats, f0, g0, cand0, p0, r0, u0, low0, low1, u1, dhr1, dn1, du1, res1, resx, tokx0,
    sums, nat, w_nat, w_own, tokbuf, cotbuf, keepc, vall, u, np_, f, g, cand, rpre, low, wbuf, proj, du, resbuf, top_of, ends,
    first, tables, st_own, st_got, st_fin,
    gsnd, grcv, gloc, vsnd, vrcv, wsem, psnd, prcv, csnd, crcv, outs,
):
    pos = Place(seq, row)
    at, zl = pos.at, pos.zl
    z, x, y, c = (at[k] for k in "zxyc")
    _, t, d = tokbuf.shape
    steps, H = u.shape[1], u.shape[3]
    parts = w_own.shape[2]
    partner = pos.device(dict(at, z=z + 1 - 2 * zl))
    own = pl.ds(pl.multiple_of(zl * H, H), H)
    other = pl.ds(pl.multiple_of((1 - zl) * H, H), H)
    rows_of = lambda b: pl.ds(pl.multiple_of(b * t, t), t)
    get_weight = pltpu.make_async_copy(weight, w_nat, outs.at[10])
    get_weight.start()
    pos.barrier(seq)
    get_weight.wait()
    for l in range(2):
        for p in range(2):
            for m in range(parts):
                for h in range(2):
                    for e in range(3):
                        start = e * d + p * H + (2 * m + h) * LANE
                        w_own[l, p, m, h, :, e * LANE : (e + 1) * LANE] = w_nat[
                            l, :, start : start + LANE
                        ]

    gather = Gather(pos, parts, w_own, w_all, gsnd, grcv, gloc)
    chains = [Chain(pos, tables.at[k], csnd.at[k], crcv.at[k]) for k in range(3)]

    def pair(k, src, dst):
        return remote(src, dst, psnd.at[k], prcv.at[k], partner)

    def tokens(b):
        return pair(0, tokbuf.at[b], tokbuf.at[b])

    def cotangents(b):
        return pair(1, du.at[t : 2 * t, d : d + H], cotbuf.at[b])

    def permute(src, store):
        group = nat.shape[0]
        for q in range(d // LANE // group):
            for k in range(group):
                at_lanes = (q * group + k) * LANE
                nat[k] = src[:, at_lanes : at_lanes + LANE].astype(F32)

            def one(k, _):
                rows = [
                    jnp.concatenate(
                        [nat[e, pl.ds(2 * k + j, SUB, stride=steps), :] for e in range(group)], axis=-1
                    )
                    for j in range(2)
                ]
                spot = pl.ds(pl.multiple_of(2 * SUB * k, 2 * SUB), 2 * SUB)
                store(spot, q, jnp.concatenate(rows, axis=0).astype(BF16))
                return 0

            lax.fori_loop(0, steps // 2, one, 0, unroll=4)

    def keeps(b):
        return pair(2, keepc.at[b], keepc.at[b])

    def statistics(b, to):
        return pair(3 + b, st_own.at[b], to.at[b])

    def lows(b, cols):
        return pair(5 + b, low.at[rows_of(b), cols], low.at[rows_of(b), cols])

    def results():
        return pair(7, resbuf.at[1 - zl, pl.ds(0, t // 2)], resx)

    def vcopies(stage, arriving):
        axis = gather.axis(stage, 0)
        size = pos.sizes[axis]
        for k in pos.others(axis):
            sem = gather.base[stage] + k - 1
            to = pos.moved(axis, k)
            who = pos.moved(axis, size - k) if arriving else at
            mine = gather.region(vall, (), stage, 0, who)
            yield remote(mine, mine, vsnd.at[sem], vrcv.at[sem], pos.device(to))

    def vadvance(stage):
        for copy in vcopies(stage - 1, True):
            copy.wait_recv()
        if stage < 4:
            for copy in vcopies(stage, False):
                copy.start()

    own_tokens = pltpu.make_async_copy(tok, du.at[0:t, 0:d], outs.at[0])
    own_cot = pltpu.make_async_copy(cot, du.at[t : 2 * t, 0:d], outs.at[1])
    given = [
        v[...].astype(F32) for v in (gain_in, shift_in, fpeep_in, rpeep_in, fbias_in, rbias_in)
    ]
    per = given[0].shape[-1]
    blank = jnp.zeros((2, per), F32)
    given = jnp.concatenate(
        [v[l : l + 1] for l in range(2) for v in given + [blank] * 2], axis=0
    )
    given = jnp.concatenate([given, jnp.zeros((16, LANE - per), F32)], axis=-1)
    vall[z, x, y, c] = given.astype(BF16)
    kept = 1.0 - resets[...].astype(F32)
    kept = jnp.concatenate([kept[:, k * steps : (k + 1) * steps] for k in range(SUB)], axis=0)
    keepc[zl] = jnp.concatenate([kept, jnp.zeros((SUB, LANE - steps), F32)], axis=-1)
    own_tokens.start()
    own_cot.start()
    for copy in vcopies(0, False):
        copy.start()
    keeps(zl).start()
    gather.begin(0)
    gather.begin(1)
    gather.begin(2)
    gather.begin(3)
    vadvance(1)
    own_tokens.wait()
    wide = nat.shape[0] * LANE

    def store_tokens(rows, q, v):
        tokbuf[zl, rows, q * wide : (q + 1) * wide] = v

    permute(du.at[0:t, 0:d], store_tokens)
    gather.turn(0)
    vadvance(2)
    vadvance(3)
    gather.turn(1)
    tokens(zl).start()
    vadvance(4)

    per = d // (seq * row)
    for q in range(d // LANE):
        pieces = []
        for e in range(LANE // per):
            i = q * (LANE // per) + e
            spot = (i // (2 * pos.Y * pos.X), i // (2 * pos.Y) % pos.X, i // 2 % pos.Y, i % 2)
            pieces.append(vall[spot][:, :per].astype(F32))
        value = jnp.concatenate(pieces, axis=-1)
        for l in range(2):
            vec[l, :, q * LANE : (q + 1) * LANE] = value[l * 8 : l * 8 + 8]
    keeps(1 - zl).wait_recv()
    for b in range(2):
        kept = keepc[b]
        for i in range(steps):
            keep[b, i] = jnp.broadcast_to(kept[:, i : i + 1], (SUB, LANE))

    def norm0(b):
        piece = 8

        def one(k, _):
            rows = pl.ds(pl.multiple_of(k * piece * SUB, piece * SUB), piece * SUB)
            spot = pl.ds(k * piece, piece)
            v = tokbuf[b, rows, :].astype(F32)
            mu = jnp.mean(v, axis=-1, keepdims=True)
            v = v - mu
            rstd = lax.rsqrt(jnp.mean(v * v, axis=-1, keepdims=True) + epsilon)
            v = v * rstd * vec[0, GAIN : GAIN + 1, :] + vec[0, SHIFT : SHIFT + 1, :]
            at_rows = pl.ds(pl.multiple_of(b * t + k * piece * SUB, piece * SUB), piece * SUB)
            low[at_rows, :] = v.astype(BF16)
            u[b, spot] = tokbuf[b, rows, own].astype(F32).reshape(piece, SUB, H)
            stats[0, 0, b, spot] = jnp.broadcast_to(mu, (piece * SUB, LANE)).reshape(piece, SUB, LANE)
            stats[0, 1, b, spot] = jnp.broadcast_to(rstd, (piece * SUB, LANE)).reshape(
                piece, SUB, LANE
            )
            return 0

        lax.fori_loop(0, steps // piece, one, 0)

    def load(l, m, h):
        slot = lax.rem(m, 2)
        return pltpu.make_async_copy(
            w_all.at[l, m, h],
            wbuf.at[slot, :, :, :, :, :, pl.ds(h * HALF, HALF)],
            wsem.at[slot, h],
        )

    def start_load(l, m):
        for h in range(2):
            load(l, m, h).start()

    def end_load(l, m):
        for h in range(2):
            load(l, m, h).wait()

    def gates(l, m, b):
        w = wbuf[lax.rem(m, 2)].reshape(d, 2 * HALF)
        v = jnp.dot(low[rows_of(b), :], w, preferred_element_type=F32)
        proj[...] = v.reshape(steps, SUB, 2 * HALF)
        cols = lane_tile(m, 2 * LANE)
        wide = pl.ds(pl.multiple_of(zl * H + m * 2 * LANE, 2 * LANE), 2 * LANE)
        peep, bias, rbias, gain, shift = (
            jnp.broadcast_to(vec[l, k : k + 1, wide], (SUB, 2 * LANE))
            for k in (FPEEP, FBIAS, RBIAS, GAIN, SHIFT)
        )

        def both(i, off):
            return jnp.concatenate(
                [proj[i, :, h * HALF + off : h * HALF + off + LANE] for h in range(2)], axis=-1
            )

        def one(i, carry):
            scale, state = carry
            cd = both(i, 0)
            n = (u[b, i, :, cols] - lanes(stats[l, 0, b, i], 2 * LANE)) * lanes(
                stats[l, 1, b, i], 2 * LANE
            ) * gain + shift
            up, down = both_sigmoids(both(i, LANE) + peep * n + bias)
            f[b, i, :, cols] = up
            g[b, i, :, cols] = down
            cand[b, i, :, cols] = cd
            rpre[b, i, :, cols] = both(i, 2 * LANE) + rbias
            a = up * lanes(keep[b, i], 2 * LANE)
            return scale * a, a * state + down * cd

        start = jnp.ones((SUB, 2 * LANE), F32), jnp.zeros((SUB, 2 * LANE), F32)
        scale, state = lax.fori_loop(0, steps, one, start, unroll=16)
        ends[b, 0, :, cols] = scale
        ends[b, 1, :, cols] = state

    def stash(k, src, dst):
        return pltpu.make_async_copy(src, dst, outs.at[k])

    norm0(zl)
    own_cot.wait()

    def store_cot(rows, q, v):
        side, at_lanes = q * wide // H, q * wide % H

        @pl.when(zl == side)
        def _():
            cotbuf[zl, rows, at_lanes : at_lanes + wide] = v

        @pl.when(zl != side)
        def _():
            to = pl.ds(pl.multiple_of(rows.start + t, 2 * SUB), 2 * SUB)
            du[to, d + at_lanes : d + at_lanes + wide] = v

    def turn(i, _):
        gather.turn(i)

        @pl.when(i == 3)
        def _():
            permute(du.at[t : 2 * t, 0:d], store_cot)

        @pl.when(i >= 3)
        def _():
            @pl.when(i < parts + 1)
            def _():
                start_load(0, i - 3)

        @pl.when((i >= 4) & (i < parts + 2))
        def _():
            end_load(0, i - 4)
            gates(0, i - 4, zl)

        @pl.when(i == parts + 1)
        def _():
            tokens(1 - zl).wait_recv()
            for k in range(6, 2 * parts):
                gather.begin(k)
            norm0(1 - zl)

        @pl.when(i > parts)
        def _():
            last = i == parts + 2

            def job(k, _):
                m = jnp.where(last, parts - 2 + k // 2, k)
                b = jnp.where(last & (lax.rem(k, 2) == 0), zl, 1 - zl)

                @pl.when(last & (lax.rem(k, 2) == 0))
                def _():
                    end_load(0, m)

                gates(0, m, b)

                @pl.when(jnp.logical_not(last) & (k == 0))
                def _():
                    start_load(0, parts - 2)

                return 0

            @pl.when(last)
            def _():
                start_load(0, parts - 1)

            lax.fori_loop(0, jnp.where(last, 4, parts - 2), job, 0)

        return 0

    lax.fori_loop(2, parts + 3, turn, 0)
    keep_tokx = stash(0, tokbuf.at[zl, :, other], tokx0)
    keep_tokx.start()
    keep_u0, keep_low0 = stash(2, u, u0), stash(3, low, low0)
    gates0 = [stash(4, f, f0), stash(5, g, g0), stash(6, cand, cand0)]
    for copy in [keep_u0, keep_low0] + gates0:
        copy.start()
    chains[0].run(ends, first, False)
    gather.turn(parts + 3)
    keep_u0.wait()
    keep_low0.wait()

    def states0(b):
        def tile(m, _):
            cols = lane_tile(m, 2 * LANE)
            wide = pl.ds(pl.multiple_of(zl * H + m * 2 * LANE, 2 * LANE), 2 * LANE)
            peep = jnp.broadcast_to(vec[0, RPEEP : RPEEP + 1, wide], (SUB, 2 * LANE))

            def one(i, cell):
                before = lanes(keep[b, i], 2 * LANE) * cell
                cell = f[b, i, :, cols] * before + g[b, i, :, cols] * cand[b, i, :, cols]
                gate = jax.nn.sigmoid(rpre[b, i, :, cols] + peep * before)
                np_[b, i, :, cols] = before
                rpre[b, i, :, cols] = gate
                u[b, i, :, cols] = gate * cell + (1.0 - gate) * u[b, i, :, cols]
                return cell

            lax.fori_loop(0, steps, one, first[b, :, cols], unroll=16)
            return 0

        lax.fori_loop(0, parts, tile, 0)

    def local_stats(b):
        def one(q, _):
            v = u[b, pl.ds(q * (LANE // SUB), LANE // SUB)].reshape(LANE, H)
            mu = jnp.mean(v, axis=-1, keepdims=True)
            v = v - mu
            square = jnp.sum(v * v, axis=-1, keepdims=True)
            st_own[b, pl.ds(q, 1), :] = to_row(mu)
            st_own[b, pl.ds(q + t // LANE, 1), :] = to_row(square)
            return 0

        lax.fori_loop(0, t // LANE, one, 0)
        statistics(b, st_got).start()

    def norm1(b):
        half = t // LANE
        statistics(b, st_got).wait_recv()
        m0, m1 = st_own[b, :half], st_got[b, :half]
        gap = m0 - m1
        square = st_own[b, half:] + st_got[b, half:] + gap * gap * (H / 2)
        st_fin[b, :half] = (m0 + m1) * 0.5
        st_fin[b, half:] = lax.rsqrt(square / (2 * H) + epsilon)

        def one(q, _):
            spot = pl.ds(q * (LANE // SUB), LANE // SUB)
            mu = to_column(st_fin[b, pl.ds(q, 1), :])
            rstd = to_column(st_fin[b, pl.ds(q + half, 1), :])
            v = u[b, spot].reshape(LANE, H)
            v = (v - mu) * rstd * vec[1, GAIN : GAIN + 1, own] + vec[1, SHIFT : SHIFT + 1, own]
            low[pl.ds(pl.multiple_of(b * t + q * LANE, LANE), LANE), own] = v.astype(BF16)
            stats[1, 0, b, spot] = spread_rows(mu)
            stats[1, 1, b, spot] = spread_rows(rstd)
            return 0

        lax.fori_loop(0, half, one, 0)
        lows(b, own).start()

    states0(0)
    local_stats(0)
    states0(1)
    keep_p0, keep_r0 = stash(7, np_, p0), stash(8, rpre, r0)
    keep_p0.start()
    keep_r0.start()
    norm1(0)
    local_stats(1)
    gather.turn(parts + 4)
    norm1(1)
    start_load(1, 0)
    keep_u1 = stash(2, u, u1)
    keep_u1.start()
    for copy in gates0 + [keep_r0]:
        copy.wait()

    def job1(k, _):
        b, m = k // parts, lax.rem(k, parts)

        @pl.when(m == 0)
        def _():
            lows(b, other).wait_recv()

        @pl.when(k == parts)
        def _():
            cotangents(zl).start()

        @pl.when((k == 1) | (k == 2))
        def _():
            gather.turn(parts + 4 + k)

        @pl.when(k + 1 < 2 * parts)
        def _():
            start_load(1, lax.rem(k + 1, parts))

        end_load(1, m)
        gates(1, m, b)
        return 0

    lax.fori_loop(0, 2 * parts, job1, 0)
    keep_low1 = stash(3, low, low1)
    keep_low1.start()
    chains[1].run(ends, first, False)
    keep_p0.wait()

    def step_back(b, i, cols, top, peep):
        before, gate, up = np_[b, i, :, cols], rpre[b, i, :, cols], f[b, i, :, cols]
        cell = up * before + g[b, i, :, cols] * cand[b, i, :, cols]
        dz_r = top * (cell - u[b, i, :, cols]) * gate * (1.0 - gate)
        direct = top * gate
        kept = lanes(keep[b, i], 2 * LANE)
        decay = up * kept
        return before, gate, up, dz_r, direct, decay, kept * peep * dz_r + decay * direct

    def turn_round(b):
        def tile(m, _):
            cols = lane_tile(m, 2 * LANE)
            wide = pl.ds(pl.multiple_of(zl * H + m * 2 * LANE, 2 * LANE), 2 * LANE)
            peep = jnp.broadcast_to(vec[1, RPEEP : RPEEP + 1, wide], (SUB, 2 * LANE))
            top = cotbuf[b, :, cols].astype(F32).reshape(steps, SUB, 2 * LANE)
            proj[:, :, 2 * LANE : 4 * LANE] = top

            def one(i, cell):
                before = lanes(keep[b, i], 2 * LANE) * cell
                cell = f[b, i, :, cols] * before + g[b, i, :, cols] * cand[b, i, :, cols]
                gate = jax.nn.sigmoid(rpre[b, i, :, cols] + peep * before)
                np_[b, i, :, cols] = before
                rpre[b, i, :, cols] = gate
                proj[i, :, : 2 * LANE] = gate * cell + (1.0 - gate) * u[b, i, :, cols]
                return cell

            lax.fori_loop(0, steps, one, first[b, :, cols], unroll=16)
            v = proj[:, :, : 2 * LANE].reshape(t, 2 * LANE)
            resbuf[b, :, cols] = v.astype(BF16)

            def back(k, carry):
                scale, q = carry
                i = steps - 1 - k
                _, _, _, _, _, decay, term = step_back(
                    b, i, cols, proj[i, :, 2 * LANE : 4 * LANE], peep
                )
                return scale * decay, decay * q + term

            start = jnp.ones((SUB, 2 * LANE), F32), jnp.zeros((SUB, 2 * LANE), F32)
            scale, q = lax.fori_loop(0, steps, back, start, unroll=16)
            ends[b, 0, :, cols] = scale
            ends[b, 1, :, cols] = q
            return 0

        lax.fori_loop(0, parts, tile, 0)

    def blocks(k, _):
        @pl.when(k == 1)
        def _():
            cotangents(1 - zl).wait_recv()

        turn_round(jnp.where(k == 0, zl, 1 - zl))
        return 0

    lax.fori_loop(0, 2, blocks, 0)
    results().start()
    keep_res = stash(9, resbuf, res1)
    keep_res.start()
    chains[2].run(ends, first, True)

    def down(b):
        def tile(m, _):
            cols = lane_tile(m, 2 * LANE)
            wide = pl.ds(pl.multiple_of(zl * H + m * 2 * LANE, 2 * LANE), 2 * LANE)
            fpeep, rpeep, gain, shift = (
                jnp.broadcast_to(vec[1, k : k + 1, wide], (SUB, 2 * LANE))
                for k in (FPEEP, RPEEP, GAIN, SHIFT)
            )

            def one(k, carry):
                q, s0, s1, s2, s3 = carry
                i = steps - 1 - k
                top = top_of[i]
                before, gate, up, dz_r, direct, decay, term = step_back(b, i, cols, top, rpeep)
                e = direct + q
                low_f = g[b, i, :, cols]
                dz_f = e * (up * low_f) * (before - cand[b, i, :, cols])
                n = (u[b, i, :, cols] - lanes(stats[1, 0, b, i], 2 * LANE)) * lanes(
                    stats[1, 1, b, i], 2 * LANE
                ) * gain + shift
                proj[i, :, : 2 * LANE] = e * low_f
                proj[i, :, 2 * LANE : 4 * LANE] = dz_f
                proj[i, :, 4 * LANE :] = dz_r
                cand[b, i, :, cols] = dz_f * fpeep
                rpre[b, i, :, cols] = top * (1.0 - gate)
                return (
                    decay * q + term,
                    s0 + dz_f * n,
                    s1 + dz_r * before,
                    s2 + dz_f,
                    s3 + dz_r,
                )

            top_of[...] = cotbuf[b, :, cols].astype(F32).reshape(steps, SUB, 2 * LANE)
            zero = jnp.zeros((SUB, 2 * LANE), F32)
            carry = lax.fori_loop(0, steps, one, (first[b, :, cols], zero, zero, zero, zero), unroll=16)
            for k in range(4):
                sums[b, k, :, cols] = carry[k + 1]
            for h in range(2):
                for k in range(3):
                    v = proj[:, :, k * 2 * LANE + h * LANE : k * 2 * LANE + (h + 1) * LANE]
                    to = pl.ds(pl.multiple_of((2 * m + h) * HALF + k * LANE, LANE), LANE)
                    du[rows_of(b), to] = v.reshape(t, LANE).astype(BF16)
            return 0

        lax.fori_loop(0, parts, tile, 0)

    keep_low1.wait()
    cotangents(zl).wait_send()

    def last(b):
        yield stash(3, du.at[rows_of(b)], du1.at[rows_of(b)])
        yield stash(4, cand.at[b], dn1.at[b])
        yield stash(5, rpre.at[b], dhr1.at[b])

    down(0)
    for copy in last(0):
        copy.start()
    down(1)
    for copy in last(0):
        copy.wait()
    for copy in last(1):
        copy.start()
    gather.finish()
    for stage in range(4):
        for copy in vcopies(stage, False):
            copy.wait_send()
    for copy in list(last(1)) + [keep_u1, keep_res, keep_tokx]:
        copy.wait()
    results().wait_recv()
    results().wait_send()
    tokens(zl).wait_send()
    keeps(zl).wait_send()
    for b in range(2):
        statistics(b, st_got).wait_send()
        lows(b, own).wait_send()


def call_forward(seq, row, tok, cot, keep, rows, weight):
    t, d = tok.shape
    layers, per, _ = weight.shape
    Y = row // 2
    X = Y
    Z = seq // X
    H = d // 2
    parts = H // WIDE
    steps = t // SUB
    act, stat = arr(2, steps, SUB, H), arr(2, steps, SUB, LANE)
    half = arr(2 * t, d, dtype=BF16)
    vmem = pl.BlockSpec(memory_space=pltpu.VMEM)
    hbm = pl.BlockSpec(memory_space=pl.ANY)
    count = Z + 2 * X - 2
    dma = pltpu.SemaphoreType.DMA
    big = pltpu.VMEM((2, steps, SUB, H), F32)
    st = pltpu.VMEM((2, 8, LANE), F32)
    return pl.pallas_call(
        lambda *refs: forward_all(seq, row, *refs),
        in_specs=[hbm, hbm] + [vmem] * (1 + len(rows)) + [hbm],
        out_specs=[hbm, vmem, vmem, vmem] + [hbm] * 15 + [vmem],
        out_shape=[
            arr(layers, parts, 2, Z, X, Y, 2, per, HALF, dtype=BF16),
            arr(2, 8, d),
            stat,
            arr(2, 2, 2, steps, SUB, LANE),
        ]
        + [act] * 6
        + [half, half, act, act, act, arr(2 * t, 3 * H, dtype=BF16), arr(2, t, H, dtype=BF16), arr(t // 2, H, dtype=BF16), arr(t, H, dtype=BF16)]
        + [arr(2, 4, SUB, H)],
        scratch_shapes=[
            pltpu.VMEM((4, t, LANE), F32),
            pltpu.VMEM((layers, per, 3 * d), BF16),
            pltpu.VMEM((layers, 2, parts, 2, per, HALF), BF16),
            pltpu.VMEM((2, t, d), BF16),
            pltpu.VMEM((2, t, H), BF16),
            pltpu.VMEM((2, 8, LANE), F32),
            pltpu.VMEM((Z, X, Y, 2, 16, LANE), BF16),
            big, big, big, big, big, big,
            pltpu.VMEM((2 * t, d), BF16),
            pltpu.VMEM((2, Z, X, Y, 2, per, 2 * HALF), BF16),
            pltpu.VMEM((steps, SUB, 2 * HALF), F32),
            pltpu.VMEM((2 * t, 3 * H), BF16),
            pltpu.VMEM((2, t, H), BF16),
            pltpu.VMEM((steps, SUB, 2 * LANE), F32),
            pltpu.VMEM((2, 2, SUB, H), F32),
            pltpu.VMEM((2, SUB, H), F32),
            pltpu.VMEM((3, Z // 2, X, 2, 2, H), F32),
            st, st, st,
            dma((2, 2 * parts, count)),
            dma((2, 2 * parts, count)),
            dma((2, 2 * parts)),
            dma((count,)),
            dma((count,)),
            dma((2, 2)),
            dma((8,)),
            dma((8,)),
            dma((3, Z // 2 * X)),
            dma((3, Z // 2 * X)),
            dma((11,)),
        ],
        compiler_params=pltpu.CompilerParams(
            collective_id=0, has_side_effects=True, vmem_limit_bytes=62 << 20
        ),
        name="forward_all",
    )(tok, cot, keep, *rows, weight)


def wrap(a, b):
    return a % b if isinstance(a, int) else lax.rem(a, b)


class Scatter:
    lag = (0, 1, 3, 5, 7)
    sends = (2, 4, 4, 4)
    slots = (2, 6, 6, 6)
    kept = (1, 3, 3, 3)

    def __init__(self, pos, count, low, du, out, keep, send, recv, done, snd, rcv, outs):
        self.pos, self.count, self.low, self.du, self.out = pos, count, low, du, out
        self.keep, self.send, self.recv, self.done = keep, send, recv, done
        self.snd, self.rcv, self.outs = snd, rcv, outs
        n = pos.X - 1
        self.base = (0, 1, 1 + n, 1 + 2 * n)

    def axis(self, stage, h):
        return ("c", ("x", "y")[h], ("y", "x")[h], "z")[stage]

    def copy(self, g, stage, h, k):
        mine, slot = wrap(g, self.sends[stage]), wrap(g, self.slots[stage])
        sem = self.base[stage] + k - 1
        to = self.pos.device(self.pos.moved(self.axis(stage, h), k))
        return remote(
            self.send[stage].at[mine, k - 1], self.recv[stage].at[slot, k - 1],
            self.snd.at[mine, sem], self.rcv.at[slot, sem], to,
        )

    def each(self, stage, h):
        return self.pos.others(self.axis(stage, h))

    def ready(self, g, stage, h):
        def wait():
            for k in self.each(stage, h):
                self.copy(g, stage, h, k).wait_send()

        if isinstance(g, int):
            if g >= self.sends[stage]:
                wait()
        else:
            pl.when(g >= self.sends[stage])(wait)

    def start(self, g, stage, h):
        for k in self.each(stage, h):
            self.copy(g, stage, h, k).start()

    def arrive(self, g, stage, h):
        for k in self.each(stage, h):
            self.copy(g, stage, h, k).wait_recv()

    def stage0(self, g, h):
        pos, low, t = self.pos, self.low, self.low.shape[0]
        rows = low.shape[1] // pos.Z
        slot = wrap(g, 2)
        q = wrap(g, self.count)
        cols = pl.ds(q * HALF if isinstance(q, int) else pl.multiple_of(q * HALF, LANE), HALF)
        self.ready(g, 0, h)
        first = pos.at["c"] == 0

        def one(z, _):
            lhs = low[:, pl.ds(pl.multiple_of(z * rows, LANE), rows)]
            v = lax.dot_general(
                lhs, self.du[:, cols], (((0,), (0,)), ((), ())), preferred_element_type=F32
            )
            v = v.reshape(pos.X, pos.Y, 2, -1, HALF)
            even, odd = v[:, :, 0], v[:, :, 1]
            self.keep[0][z] = jnp.where(first, even, odd)
            self.send[0][slot, 0, z] = jnp.where(first, odd, even).astype(BF16)
            return 0

        lax.fori_loop(0, pos.Z, one, 0)
        self.start(g, 0, h)

    def stage1(self, g, h):
        pos, axis = self.pos, self.axis(1, h)
        slot, got, mine = wrap(g, 4), wrap(g, 2), wrap(g, 3)
        self.arrive(g, 0, h)
        self.ready(g, 1, h)
        for k in range(pos.sizes[axis]):
            p = pos.moved(axis, k)[axis]

            def one(z, _):
                where = (z, p) if h == 0 else (z, slice(None), p)
                v = self.keep[0][where] + self.recv[0][(got, 0) + where].astype(F32)
                if k == 0:
                    self.keep[1][mine, z] = v
                else:
                    self.send[1][slot, k - 1, z] = v.astype(BF16)
                return 0

            lax.fori_loop(0, pos.Z, one, 0)
        self.start(g, 1, h)

    def stage2(self, g, h):
        pos, axis = self.pos, self.axis(2, h)
        slot, got, mine = wrap(g, 4), wrap(g, 6), wrap(g, 3)
        self.arrive(g, 1, h)
        self.ready(g, 2, h)
        for k in range(pos.sizes[axis]):
            p = pos.moved(axis, k)[axis]
            v = self.keep[1][mine, :, p]
            for e in self.each(1, h):
                v = v + self.recv[1][got, e - 1, :, p].astype(F32)
            if k == 0:
                self.keep[2][mine] = v
            else:
                self.send[2][slot, k - 1] = v.astype(BF16)
        self.start(g, 2, h)

    def stage3(self, g, h):
        pos = self.pos
        slot, got, mine = wrap(g, 4), wrap(g, 6), wrap(g, 3)
        self.arrive(g, 2, h)
        self.ready(g, 3, h)
        for k in range(pos.Z):
            p = pos.moved("z", k)["z"]
            v = self.keep[2][mine, p]
            for e in self.each(2, h):
                v = v + self.recv[2][got, e - 1, p].astype(F32)
            if k == 0:
                self.keep[3][mine] = v
            else:
                self.send[3][slot, k - 1] = v.astype(BF16)
        self.start(g, 3, h)

    def result(self, l, q, half, e):
        d = self.out.shape[-1] // 3
        at = e * d + half * (d // 2) + q * LANE
        return pltpu.make_async_copy(
            self.done.at[half, wrap(q, 4), :, e * LANE : (e + 1) * LANE],
            self.out.at[l, :, pl.ds(pl.multiple_of(at, LANE), LANE)],
            self.outs.at[half, wrap(q, 4), e],
        )

    def stage4(self, g, h, l):
        pos = self.pos
        got, mine, q = wrap(g, 6), wrap(g, 3), wrap(g, self.count)
        self.arrive(g, 3, h)
        own, other = self.keep[3][mine], None
        for k in range(1, pos.Z):
            v = self.recv[3][got, k - 1].astype(F32)
            if k % 2 == 0:
                own = own + v
            else:
                other = v if other is None else other + v
        if isinstance(q, int):
            if q >= 4:
                self.stored(l, q - 4)
        else:
            pl.when(q >= 4)(lambda: self.stored(l, q - 4))
        self.done[pos.zl, wrap(q, 4)] = own
        self.done[1 - pos.zl, wrap(q, 4)] = other
        for half in (pos.zl, 1 - pos.zl):
            for e in range(3):
                self.result(l, q, half, e).start()

    def stored(self, l, q):
        for half in (self.pos.zl, 1 - self.pos.zl):
            for e in range(3):
                self.result(l, q, half, e).wait()

    def turn(self, run, l, pair, e, enters=True):
        first = run * self.count

        def stage(s, f):
            g = first + 2 * pair + e - self.lag[s]
            h = (e - self.lag[s]) % 2
            if isinstance(g, int):
                if first <= g < first + self.count:
                    f(g, h)
            elif s:
                pl.when(g >= first)(lambda: f(g, h))
            else:
                f(g, h)

        stage(1, self.stage1)
        if enters:
            stage(0, self.stage0)
        stage(2, self.stage2)
        stage(3, self.stage3)
        stage(4, lambda g, h: self.stage4(g, h, l))

    def written(self, l):
        for q in range(self.count - 4, self.count):
            self.stored(l, q)

    def finish(self, total):
        for stage in range(4):
            for g in range(total - self.sends[stage], total):
                for k in self.each(stage, g % 2):
                    self.copy(g, stage, g % 2, k).wait_send()


def backward_all(
    seq, row, w_all, vec, keep, stats_all, f0, g0, cand0, p0, r0, u0, low0, low1, u1, dhr1, dn1, du1,
    res1, resx, tok, sums1,
    grad, input_grad, result, vo0, vo1, vo2, vo3, vo4, vo5,
    stats, wbuf, du, low, dn, dnsend, dnrecv, hsend, hrecv, tokx, u, dhr, stream, proj,
    keep0, send0, recv0, keep1, send1, recv1, keep2, send2, recv2, keep3, send3, recv3, done,
    ends, first, table, b_own, b_got, b_fin, sums, sumsx, vbuf, vr0, vr1, vr2, vr3,
    snd, rcv, gouts, psnd, prcv, csnd, crcv, vsnd, vrcv, ins, ssem, wsem,
):
    pos = Place(seq, row)
    at, zl = pos.at, pos.zl
    z, x, y, c = (at[k] for k in "zxyc")
    t2, H3 = du.shape
    t, H = t2 // 2, H3 // 3
    d = 2 * H
    steps = t // SUB
    parts = H // WIDE
    partner = pos.device(dict(at, z=z + 1 - 2 * zl))
    own = pl.ds(pl.multiple_of(zl * H, H), H)
    other = pl.ds(pl.multiple_of((1 - zl) * H, H), H)
    rows_of = lambda b: pl.ds(pl.multiple_of(b * t, t), t)

    def load(k, src, dst):
        return pltpu.make_async_copy(src, dst, ins.at[k])

    def weights(l, half):
        zs = pl.ds(half * (pos.Z // 2), pos.Z // 2)
        for m in range(parts):
            for h in range(2):
                q = 2 * m + h
                yield pltpu.make_async_copy(
                    w_all.at[l, m, h, zs],
                    wbuf.at[:, :, :, :, :, q * HALF : (q + 1) * HALF],
                    wsem.at[q],
                )

    def begin(copies):
        for copy in copies:
            copy.start()

    def end(copies):
        for copy in copies:
            copy.wait()

    get_du, get_low, get_dn = load(0, du1, du), load(1, low1, low), load(2, dn1, dn)
    get_u, get_dhr = load(3, u1, u), load(4, dhr1, dhr)
    get_stats = load(6, stats_all.at[1], stats)
    get_du.start()
    begin(weights(1, 1 - zl))
    pos.barrier(seq)
    scatter = Scatter(
        pos, 2 * parts, low, du, grad, (keep0, keep1, keep2, keep3), (send0, send1, send2, send3),
        (recv0, recv1, recv2, recv3), done, snd, rcv, gouts,
    )
    chain = Chain(pos, table, csnd, crcv)

    def pair(k, src, dst):
        return remote(src, dst, psnd.at[k], prcv.at[k], partner)

    def partial_sums(b):
        return pair(b, dnsend.at[b], dnrecv.at[b])

    def statistics(b):
        return pair(2 + b, b_own.at[b], b_got.at[b])

    def carried():
        return pair(4, hsend, hrecv)

    def results(cols):
        rows = pl.ds(t // 2, t // 2)
        return pair(5, res1.at[1 - zl, rows], result.at[rows, cols])

    own_result = load(5, res1.at[zl], result.at[:, own])
    own_result.start()
    got_result = load(8, resx, result.at[pl.ds(0, t // 2), other])
    got_result.start()
    results(own).start()
    across = (((1,), (1,)), ((), ()))

    n = t2 // parts
    blocks = t // n

    def product(b, k):
        rows = pl.ds(pl.multiple_of(b * t + k * n, n), n)
        return lax.dot_general(
            du[rows, :], wbuf[...].reshape(H, H3), across, preferred_element_type=F32
        )

    def of_block(k):
        return pl.ds(pl.multiple_of(k * (n // SUB), n // SUB), n // SUB)

    def theirs(q, b, more=None):
        def one(k, _):
            v = product(b, k)
            if more is not None:
                v = v + more[of_block(k)].reshape(n, H)
            dnsend[q, pl.ds(pl.multiple_of(k * n, n), n), :] = v.astype(BF16)
            return 0

        lax.fori_loop(0, blocks, one, 0)
        partial_sums(q).start()

    def ours(to, b, k, fresh=False):
        v = product(b, k).reshape(n // SUB, SUB, H)
        if fresh:
            dn[to, of_block(k)] = v
        else:
            dn[to, of_block(k)] += v

    half = t // LANE

    def norm_sums(l, b):
        partial_sums(b).wait_recv()

        def one(q, _):
            spot = pl.ds(q * (LANE // SUB), LANE // SUB)
            rows = pl.ds(pl.multiple_of(q * LANE, LANE), LANE)
            v = dn[b, spot].reshape(LANE, H) + dnrecv[b, rows, :].astype(F32)
            dn[b, spot] = v.reshape(LANE // SUB, SUB, H)
            xhat = hat(l, b, spot)
            sums[l, 0] += jnp.sum((v * xhat).reshape(LANE // SUB, SUB, H), axis=0)
            sums[l, 1] += jnp.sum(v.reshape(LANE // SUB, SUB, H), axis=0)
            v = v * vec[l, GAIN : GAIN + 1, own]
            b_own[b, pl.ds(q, 1), :] = to_row(jnp.sum(v, axis=-1, keepdims=True))
            b_own[b, pl.ds(q + half, 1), :] = to_row(jnp.sum(v * xhat, axis=-1, keepdims=True))
            return 0

        lax.fori_loop(0, half, one, 0)
        statistics(b).start()

    def hat(l, b, spot):
        mu = stats[0, b, spot].reshape(LANE, LANE)[:, :1]
        rstd = stats[1, b, spot].reshape(LANE, LANE)[:, :1]
        return (u[b, spot].reshape(LANE, H) - mu) * rstd

    def norm_back(l, b):
        statistics(b).wait_recv()
        b_fin[...] = (b_own[b] + b_got[b]) * (1.0 / d)

        def one(q, _):
            spot = pl.ds(q * (LANE // SUB), LANE // SUB)
            xhat = hat(l, b, spot)
            rstd = stats[1, b, spot].reshape(LANE, LANE)[:, :1]
            m0 = to_column(b_fin[pl.ds(q, 1), :])
            m1 = to_column(b_fin[pl.ds(q + half, 1), :])
            v = dn[b, spot].reshape(LANE, H) * vec[l, GAIN : GAIN + 1, own]
            v = dhr[b, spot].reshape(LANE, H) + rstd * (v - m0 - xhat * m1)
            dhr[b, spot] = v.reshape(LANE // SUB, SUB, H)
            return 0

        lax.fori_loop(0, half, one, 0)

    def norm_last():
        for q in range(2):
            partial_sums(q).wait_recv()
        carried().wait_recv()
        get_tok.wait()
        piece = 4
        n = piece * SUB

        def one(k, _):
            spot = pl.ds(k * piece, piece)
            rows = pl.ds(pl.multiple_of(k * n, n), n)
            mu = stats[0, zl, spot].reshape(n, LANE)[:, :1]
            rstd = stats[1, zl, spot].reshape(n, LANE)[:, :1]
            scaled, hats = [], []
            m0 = m1 = 0.0
            for q, part in enumerate((zl, 1 - zl)):
                x = u[zl, spot].reshape(n, H) if q == 0 else tokx[rows, :].astype(F32)
                xhat = (x - mu) * rstd
                v = dn[part, spot].reshape(n, H) + dnrecv[q, rows, :].astype(F32)
                total = sums.at[0] if q == 0 else sumsx
                total[0] += jnp.sum((v * xhat).reshape(piece, SUB, H), axis=0)
                total[1] += jnp.sum(v.reshape(piece, SUB, H), axis=0)
                v = v * vec[0, GAIN : GAIN + 1, own if q == 0 else other]
                m0 += jnp.sum(v, axis=-1, keepdims=True)
                m1 += jnp.sum(v * xhat, axis=-1, keepdims=True)
                scaled.append(v)
                hats.append(xhat)
            m0, m1 = m0 * (1.0 / d), m1 * (1.0 / d)
            for q in range(2):
                v = rstd * (scaled[q] - m0 - hats[q] * m1)
                if q == 0:
                    v = v + dhr[zl, spot].reshape(n, H)
                else:
                    v = v + hrecv[rows, :].astype(F32)
                dnsend[q, rows, :] = v.astype(BF16)
            return 0

        lax.fori_loop(0, steps // piece, one, 0)

    units = 2 * parts
    sources = (f0, g0, cand0, p0, r0)

    def fetch(k):
        slot = lax.rem(k, 2)
        b, m = jnp.where(k < parts, 1 - zl, zl), lax.rem(k, parts)
        for j, src in enumerate(sources):
            yield pltpu.make_async_copy(
                src.at[b, :, :, lane_tile(m, WIDE)], stream.at[slot, j], ssem.at[slot, j]
            )

    def tiles(work, between=None):
        begin(fetch(0))

        def one(k, _):
            @pl.when(k + 1 < units)
            def _():
                begin(fetch(k + 1))

            end(fetch(k))
            b, m = jnp.where(k < parts, 1 - zl, zl), lax.rem(k, parts)
            cols = lane_tile(m, WIDE)
            wide = pl.ds(pl.multiple_of(zl * H + m * WIDE, WIDE), WIDE)
            work(lax.rem(k, 2), b, m, cols, wide)
            if between is not None:
                between(k)
            return 0

        lax.fori_loop(0, units, one, 0)

    def step_back(slot, b, i, cols, peep):
        up, down, cd, before, gate = (stream[slot, j, i] for j in range(5))
        cell = up * before + down * cd
        top = dhr[b, i, :, cols]
        dz_r = top * (cell - u[b, i, :, cols]) * gate * (1.0 - gate)
        direct = top * gate
        kept = lanes(keep[b, i], WIDE)
        decay = up * kept
        term = kept * peep * dz_r + decay * direct
        return up, down, cd, before, gate, top, dz_r, direct, decay, term

    def row_wide(l, k, wide):
        return jnp.broadcast_to(vec[l, k : k + 1, wide], (SUB, WIDE))

    def ends_work(slot, b, m, cols, wide):
        peep = row_wide(0, RPEEP, wide)

        def one(k, carry):
            scale, q = carry
            i = steps - 1 - k
            terms = step_back(slot, b, i, cols, peep)
            gate, top, decay, term = terms[4], terms[5], terms[-2], terms[-1]
            proj[i, :, :WIDE] = top * (1.0 - gate)
            return scale * decay, decay * q + term

        start = jnp.ones((SUB, WIDE), F32), jnp.zeros((SUB, WIDE), F32)
        scale, q = lax.fori_loop(0, steps, one, start, unroll=16)
        ends[b, 0, :, cols] = scale
        ends[b, 1, :, cols] = q

        @pl.when(b != zl)
        def _():
            hsend[:, cols] = proj[:, :, :WIDE].reshape(t, WIDE).astype(BF16)

    def send_carried(k):
        pl.when(k == parts - 1)(lambda: carried().start())

    def down_work(slot, b, m, cols, wide):
        fpeep, rpeep, gain, shift = (row_wide(0, k, wide) for k in (FPEEP, RPEEP, GAIN, SHIFT))

        def one(k, carry):
            q, s0, s1, s2, s3 = carry
            i = steps - 1 - k
            up, low_f, cd, before, gate, top, dz_r, direct, decay, term = step_back(
                slot, b, i, cols, rpeep
            )
            e = direct + q
            dz_f = e * (up * low_f) * (before - cd)
            n = (u[b, i, :, cols] - lanes(stats[0, b, i], WIDE)) * lanes(
                stats[1, b, i], WIDE
            ) * gain + shift
            proj[i, :, :WIDE] = e * low_f
            proj[i, :, WIDE : 2 * WIDE] = dz_f
            proj[i, :, 2 * WIDE :] = dz_r
            dn[b, i, :, cols] = dz_f * fpeep
            dhr[b, i, :, cols] = top * (1.0 - gate)
            return (
                decay * q + term,
                s0 + dz_f * n,
                s1 + dz_r * before,
                s2 + dz_f,
                s3 + dz_r,
            )

        zero = jnp.zeros((SUB, WIDE), F32)
        carry = lax.fori_loop(0, steps, one, (first[b, :, cols], zero, zero, zero, zero), unroll=16)
        for k in range(4):
            sums[0, 2 + k, :, cols] += carry[k + 1]
        for h in range(2):
            for k in range(3):
                v = proj[:, :, k * WIDE + h * LANE : k * WIDE + (h + 1) * LANE]
                to = pl.ds(pl.multiple_of((2 * m + h) * HALF + k * LANE, LANE), LANE)
                du[rows_of(b), to] = v.reshape(t, LANE).astype(BF16)

    def late(run, l, k):
        scatter.turn(run, l, parts + k // 2, k % 2, False)

    sums[...] = jnp.zeros_like(sums)
    sumsx[...] = jnp.zeros_like(sumsx)
    sums[1, 2:6] = sums1[0] + sums1[1]
    get_du.wait()
    end(weights(1, 1 - zl))
    begin([get_low, get_dn])
    for b in range(2):
        theirs(b, b)
    begin(weights(1, zl))
    begin([get_u, get_dhr, get_stats])
    get_low.wait()
    get_dn.wait()

    def last_layer(k, _):
        scatter.turn(0, 1, k, 0)

        @pl.when(k == 0)
        def _():
            end(weights(1, zl))

        ours(k // blocks, k // blocks, lax.rem(k, blocks))
        scatter.turn(0, 1, k, 1)
        return 0

    lax.fori_loop(0, parts, last_layer, 0)
    get_low = load(1, low0, low)
    get_low.start()
    get_u.wait()
    get_dhr.wait()
    get_stats.wait()
    begin(weights(0, 1 - zl))
    norm_sums(1, 0)
    norm_sums(1, 1)
    late(0, 1, 0)
    norm_back(1, 0)
    norm_back(1, 1)
    get_u, get_stats = load(3, u0, u), load(6, stats_all.at[0], stats)
    get_tok = load(7, tok, tokx)
    begin([get_u, get_stats, get_tok])
    late(0, 1, 1)
    get_u.wait()
    get_stats.wait()
    late(0, 1, 2)
    tiles(ends_work, send_carried)
    late(0, 1, 3)
    chain.run(ends, first, True)
    for k in range(4, 7):
        late(0, 1, k)
    for b in range(2):
        partial_sums(b).wait_send()
        statistics(b).wait_send()
    end(weights(0, 1 - zl))

    def between(k):
        @pl.when(k == parts - 1)
        def _():
            theirs(0, 1 - zl)
            begin(weights(0, zl))

        for e in range(2):
            pl.when(k == parts + e)(lambda: scatter.turn(1, 0, 0, e))

    scatter.written(1)
    get_low.wait()
    tiles(down_work, between)
    end(weights(0, zl))
    theirs(1, 1 - zl, dn.at[1 - zl])

    def first_layer(k, _):
        scatter.turn(1, 0, k, 0)

        @pl.when(k == 1)
        def _():
            ours(zl, zl, 0)
            ours(zl, zl, 1)
            begin(weights(0, 1 - zl))

        @pl.when(k == 2)
        def _():
            end(weights(0, 1 - zl))

        @pl.when(k > 1)
        def _():
            ours(1 - zl, zl, k - 2, True)

        scatter.turn(1, 0, k, 1)
        return 0

    lax.fori_loop(1, parts, first_layer, 0)
    late(1, 0, 0)
    late(1, 0, 1)
    for b in range(2):
        partial_sums(b).wait_send()
    norm_last()
    out_own = load(0, dnsend.at[0], input_grad.at[:, own])
    out_other = load(1, dnsend.at[1], input_grad.at[:, other])
    begin([out_own, out_other])
    late(1, 0, 2)
    late(1, 0, 3)

    vbuf[...] = jnp.zeros_like(vbuf)
    per = d // (seq * row)
    total = [jnp.sum(sums[l], axis=1) for l in range(2)]
    totalx = jnp.sum(sumsx[...], axis=1)
    blank = jnp.zeros((6, LANE - per), F32) if per < LANE else None
    for i in range(H // per):
        spot = (zl * (pos.Z // 2) + i // (2 * pos.Y * pos.X), i // (2 * pos.Y) % pos.X, i // 2 % pos.Y, i % 2)
        for l in range(2):
            piece = total[l][:, i * per : (i + 1) * per]
            vbuf[spot + (slice(l * 8, l * 8 + 6),)] = jnp.concatenate([piece, blank], axis=-1)
        away = (lax.rem(spot[0] + pos.Z // 2, pos.Z),) + spot[1:]
        piece = totalx[:, i * per : (i + 1) * per]
        vbuf[away + (slice(0, 2),)] = jnp.concatenate([piece, blank[:2]], axis=-1)
    every = slice(None)

    def vspot(stage, who):
        if stage == 0:
            return (every, every, every, who["c"])
        if stage == 1:
            return (every, who["x"], every, c)
        if stage == 2:
            return (every, x, who["y"], c)
        return (who["z"], x, y, c)

    vrecv = (vr0, vr1, vr2, vr3)

    def vcopy(stage, k):
        axis = "cxyz"[stage]
        to = pos.moved(axis, k)
        sem = scatter.base[stage] + k - 1
        return remote(
            vbuf.at[vspot(stage, to)], vrecv[stage].at[k - 1], vsnd.at[sem], vrcv.at[sem],
            pos.device(to),
        )

    def vstart(stage):
        for k in pos.others("cxyz"[stage]):
            vcopy(stage, k).start()

    def vtake(stage):
        for k in pos.others("cxyz"[stage]):
            vcopy(stage, k).wait_recv()
            vbuf[vspot(stage, at)] += vrecv[stage][k - 1]

    vstart(0)
    late(1, 0, 4)
    vtake(0)
    vstart(1)
    late(1, 0, 5)
    vtake(1)
    vstart(2)
    late(1, 0, 6)
    vtake(2)
    vstart(3)
    vtake(3)
    mine = vbuf[z, x, y, c]
    for k, out in enumerate((vo0, vo1, vo2, vo3, vo4, vo5)):
        out[...] = jnp.concatenate([mine[l * 8 + k : l * 8 + k + 1, :per] for l in range(2)], axis=0)
    for stage in range(4):
        for k in pos.others("cxyz"[stage]):
            vcopy(stage, k).wait_send()
    scatter.written(0)
    scatter.finish(2 * scatter.count)
    carried().wait_send()
    end([out_own, out_other])
    own_result.wait()
    got_result.wait()
    results(own).wait_send()
    results(other).wait_recv()


def call_backward(seq, row, t, d, given):
    w_all = given[0]
    layers, parts, _, Z, X, Y, _, per, _ = w_all.shape
    H = d // 2
    steps = t // SUB
    vmem = pl.BlockSpec(memory_space=pltpu.VMEM)
    hbm = pl.BlockSpec(memory_space=pl.ANY)
    dma = pltpu.SemaphoreType.DMA
    big = pltpu.VMEM((2, steps, SUB, H), F32)
    half, quarter = pltpu.VMEM((2, t, H), BF16), pltpu.VMEM((t, H), BF16)
    st = pltpu.VMEM((2, 8, LANE), F32)
    count = 1 + 2 * (X - 1) + Z - 1
    chunk = (Z, X, Y, per, HALF)

    def buf(*shape, dtype=BF16):
        return pltpu.VMEM(shape, dtype)

    return pl.pallas_call(
        lambda *refs: backward_all(seq, row, *refs),
        in_specs=[hbm, vmem, vmem] + [hbm] * 16 + [vmem],
        out_specs=[hbm, hbm, hbm] + [vmem] * 6,
        out_shape=[arr(layers, per, 3 * d)] + [arr(t, d, dtype=BF16)] * 2 + [arr(layers, per)] * 6,
        scratch_shapes=[
            buf(2, 2, steps, SUB, LANE, dtype=F32),
            buf(Z // 2, X, Y, 2, per, 3 * H),
            buf(2 * t, 3 * H),
            buf(2 * t, d),
            big, half, half, quarter, quarter, quarter, big, big,
            buf(2, 5, steps, SUB, WIDE, dtype=F32),
            buf(steps, SUB, 3 * WIDE, dtype=F32),
            buf(*chunk, dtype=F32), buf(2, 1, *chunk), buf(2, 1, *chunk),
            buf(3, Z, Y, per, HALF, dtype=F32), buf(4, X - 1, Z, Y, per, HALF),
            buf(6, X - 1, Z, Y, per, HALF),
            buf(3, Z, per, HALF, dtype=F32), buf(4, Y - 1, Z, per, HALF),
            buf(6, Y - 1, Z, per, HALF),
            buf(3, per, HALF, dtype=F32), buf(4, Z - 1, per, HALF), buf(6, Z - 1, per, HALF),
            buf(2, 4, per, HALF, dtype=F32),
            buf(2, 2, SUB, H, dtype=F32),
            buf(2, SUB, H, dtype=F32),
            buf(Z // 2, X, 2, 2, H, dtype=F32),
            st, st, buf(8, LANE, dtype=F32),
            buf(2, 6, SUB, H, dtype=F32),
            buf(2, SUB, H, dtype=F32),
            buf(Z, X, Y, 2, 16, LANE, dtype=F32),
            buf(1, Z, X, Y, 16, LANE, dtype=F32),
            buf(X - 1, Z, Y, 16, LANE, dtype=F32),
            buf(Y - 1, Z, 16, LANE, dtype=F32),
            buf(Z - 1, 16, LANE, dtype=F32),
            dma((4, count)), dma((6, count)),
            dma((2, 4, 3)),
            dma((6,)), dma((6,)),
            dma((Z // 2 * X,)), dma((Z // 2 * X,)),
            dma((count,)), dma((count,)),
            dma((9,)),
            dma((2, 5)),
            dma((2 * parts,)),
        ],
        compiler_params=pltpu.CompilerParams(
            collective_id=1, has_side_effects=True, vmem_limit_bytes=63 << 20
        ),
        name="backward_all",
    )(*given)


def body(tokens, resets, cotangent, weight, *rows):
    _, t, d = tokens.shape
    layers = weight.shape[0]
    steps = t // SUB
    seq, row = lax.axis_size("seq"), lax.axis_size("row")

    def restored(v):
        return v.reshape(steps, SUB, d).transpose(1, 0, 2).reshape(1, t, d)

    out = call_forward(
        seq, row, tokens[0], cotangent[0], resets, rows, weight
    )
    grad, input_grad, result, *vectors = call_backward(seq, row, t, d, out)
    return (restored(result), restored(input_grad), grad) + tuple(vectors)


def solution(mesh):
    tokens = P("row", "seq", None)
    rows = P(None, ("seq", "row"))
    weight = P(None, ("seq", "row"), None)
    return jax.shard_map(
        body,
        mesh=mesh,
        in_specs=(tokens, P("row", "seq"), tokens, weight) + (rows,) * 6,
        out_specs=(tokens, tokens, weight) + (rows,) * 6,
        check_vma=False,
    )
```

```python
import jax
import jax.numpy as jnp
from jax import lax
from jax.experimental import pallas as pl
from jax.experimental.pallas import tpu as pltpu
from jax.sharding import PartitionSpec as P

epsilon = 1e-05
SUB = 8
WIDE = 256
F32 = jnp.float32
BF16 = jnp.bfloat16
GAIN, SHIFT, FPEEP, RPEEP, FBIAS, RBIAS = range(6)


def both_sigmoids(z):
    tail = jnp.exp(-jnp.abs(z))
    big = 1.0 / (1.0 + tail)
    small = tail * big
    up = z >= 0
    return jnp.where(up, big, small), jnp.where(up, small, big)


def lanes(value, width):
    return jnp.concatenate([value] * (width // value.shape[-1]), axis=-1)


def arr(*shape, dtype=F32):
    return jax.ShapeDtypeStruct(shape, dtype)


MESH = pl.DeviceIdType.MESH
HALF = 384
LANE = 128


class Place:
    def __init__(self, seq, row):
        self.Y = row // 2
        self.X = self.Y
        self.Z = seq // self.X
        self.C = 2
        self.sizes = dict(z=self.Z, x=self.X, y=self.Y, c=self.C)
        s, r = lax.axis_index("seq"), lax.axis_index("row")
        self.at = dict(z=s // self.X, x=s % self.X, y=r // 2, c=r % 2)
        self.zl = lax.rem(self.at["z"], 2)

    def moved(self, axis, k):
        size = self.sizes[axis]
        return dict(self.at, **{axis: lax.rem(self.at[axis] + k, size)})

    def device(self, at):
        return {"seq": at["z"] * self.X + at["x"], "row": at["y"] * 2 + at["c"]}

    def others(self, axis):
        return range(1, self.sizes[axis])

    def barrier(self, seq):
        sem = pltpu.get_barrier_semaphore()
        count = 0
        s, r = lax.axis_index("seq"), lax.axis_index("row")
        for k in range(1, seq):
            pl.semaphore_signal(
                sem, inc=1, device_id={"seq": lax.rem(s + k, seq), "row": r}, device_id_type=MESH
            )
            count += 1
        for axis in ("y", "c"):
            for k in self.others(axis):
                pl.semaphore_signal(
                    sem, inc=1, device_id=self.device(self.moved(axis, k)), device_id_type=MESH
                )
                count += 1
        pl.semaphore_wait(sem, count)


def remote(src, dst, send, recv, to):
    return pltpu.make_async_remote_copy(
        src_ref=src, dst_ref=dst, send_sem=send, recv_sem=recv, device_id=to, device_id_type=MESH
    )


def total_of(scale, state, backward):
    order = range(SUB - 1, -1, -1) if backward else range(SUB)
    whole_scale, whole_state = None, None
    for k in order:
        a, b = scale[k : k + 1], state[k : k + 1]
        if whole_scale is None:
            whole_scale, whole_state = a, b
        else:
            whole_scale, whole_state = a * whole_scale, a * whole_state + b
    return jnp.concatenate([whole_scale, whole_state], axis=0)


class Gather:
    def __init__(self, pos, parts, w_own, w_all, snd, rcv, loc):
        self.pos, self.parts = pos, parts
        self.w_own, self.w_all, self.snd, self.rcv, self.loc = w_own, w_all, snd, rcv, loc
        z, x, y = pos.Z - 1, pos.X - 1, pos.Y - 1
        self.base = (0, z, z + max(x, y), z + 2 * max(x, y))

    def axis(self, stage, h):
        return ("z", ("y", "x")[h], ("x", "y")[h], "c")[stage]

    def region(self, ref, head, stage, h, who):
        every = slice(None)
        spot = [who["z"], who["x"], who["y"], who["c"]]
        if stage >= 1:
            spot[0] = every
        if stage >= 2:
            spot[2 if h == 0 else 1] = every
        if stage >= 3:
            spot[1] = spot[2] = every
        return ref.at[head + tuple(spot)]

    def copies(self, g, stage, h, arriving):
        pos, axis = self.pos, self.axis(stage, h)
        l, m = g // self.parts, lax.rem(g, self.parts)
        size = pos.sizes[axis]
        for k in pos.others(axis):
            sem = self.base[stage] + k - 1
            to = pos.moved(axis, k)
            who = pos.moved(axis, size - k) if arriving else pos.at
            mine = self.region(self.w_all, (l, m, h), stage, h, who)
            src = mine
            if stage == 0 and not arriving:
                src = self.w_own.at[l, lax.rem(to["z"], 2), m, h]
            yield remote(src, mine, self.snd.at[h, g, sem], self.rcv.at[h, g, sem], pos.device(to))

    def local(self, g, h):
        at = self.pos.at
        l, m = g // self.parts, lax.rem(g, self.parts)
        return pltpu.make_async_copy(
            self.w_own.at[l, self.pos.zl, m, h],
            self.w_all.at[l, m, h, at["z"], at["x"], at["y"], at["c"]],
            self.loc.at[h, g],
        )

    def begin(self, g):
        for h in range(2):
            self.local(g, h).start()
            for copy in self.copies(g, 0, h, False):
                copy.start()

    def advance(self, g, stage):
        for h in range(2):
            if stage == 1:
                self.local(g, h).wait()
            for copy in self.copies(g, stage - 1, h, True):
                copy.wait_recv()
            if stage < 4:
                for copy in self.copies(g, stage, h, False):
                    copy.start()

    def turn(self, i):
        total = 2 * self.parts

        @pl.when(i < 2)
        def _():
            self.begin(i + 4)

        for stage in range(1, 5):
            g = i - (stage - 1)

            @pl.when((g >= 0) & (g < total))
            def _():
                self.advance(g, stage)

    def finish(self):
        def one(g, _):
            for h in range(2):
                for stage in range(4):
                    for copy in self.copies(g, stage, h, False):
                        copy.wait_send()
            return 0

        lax.fori_loop(0, 2 * self.parts, one, 0)


class Chain:
    def __init__(self, pos, table, snd, rcv):
        self.pos, self.table, self.snd, self.rcv = pos, table, snd, rcv

    def run(self, ends, first, backward):
        pos, table = self.pos, self.table
        zh, x = pos.at["z"] // 2, pos.at["x"]
        r = lax.axis_index("row")
        for b in range(2):
            table[zh, x, b] = total_of(ends[b, 0], ends[b, 1], backward)
        moves = [(i, j) for i in range(pos.Z // 2) for j in range(pos.X) if i or j]

        def copy(k, sign):
            i, j = moves[k]
            there = lax.rem(zh + i, pos.Z // 2), lax.rem(x + j, pos.X)
            back = lax.rem(zh + pos.Z // 2 - i, pos.Z // 2), lax.rem(x + pos.X - j, pos.X)
            spot = (zh, x) if sign > 0 else back
            to = {"seq": (2 * there[0] + pos.zl) * pos.X + there[1], "row": r}
            return remote(table.at[spot], table.at[spot], self.snd.at[k], self.rcv.at[k], to)

        for k in range(len(moves)):
            copy(k, 1).start()
        for k in range(len(moves)):
            copy(k, -1).wait_recv()
        for k in range(len(moves)):
            copy(k, 1).wait_send()
        blocks = [(i, b, j) for i in range(pos.Z // 2) for b in range(2) for j in range(pos.X)]
        if backward:
            blocks = blocks[::-1]
        value = jnp.zeros_like(table[0, 0, 0, 0:1])
        mine = [value, value]
        for i, b, j in blocks:
            here = (i == zh) & (j == x)
            mine[b] = jnp.where(here, value, mine[b])
            value = table[i, j, b, 0:1] * value + table[i, j, b, 1:2]
        for b in range(2):
            value = mine[b]
            for k in range(SUB - 1, -1, -1) if backward else range(SUB):
                first[b, k : k + 1] = value
                value = ends[b, 0, k : k + 1] * value + ends[b, 1, k : k + 1]


def diagonal():
    return lax.broadcasted_iota(jnp.int32, (LANE, LANE), 0) == lax.broadcasted_iota(
        jnp.int32, (LANE, LANE), 1
    )


def to_row(column):
    spread = jnp.broadcast_to(column, (LANE, LANE))
    return jnp.sum(jnp.where(diagonal(), spread, 0.0), axis=0, keepdims=True)


def to_column(line):
    spread = jnp.broadcast_to(line, (LANE, LANE))
    return jnp.sum(jnp.where(diagonal(), spread, 0.0), axis=1, keepdims=True)


def spread_rows(column):
    return jnp.broadcast_to(column, (LANE, LANE)).reshape(LANE // SUB, SUB, LANE)


def lane_tile(m, width):
    return pl.ds(pl.multiple_of(m * width, width), width)


def forward_all(
    seq, row, tok, cot, resets, gain_in, shift_in, fpeep_in, rpeep_in, fbias_in, rbias_in, weight,
    w_all, vec, keep, stats, f0, g0, cand0, p0, r0, u0, low0, low1, u1, dhr1, dn1, du1, res1, resx, tokx0,
    sums, nat, w_nat, w_own, tokbuf, cotbuf, keepc, vall, u, np_, f, g, cand, rpre, low, wbuf, proj, du, resbuf, top_of, ends,
    first, tables, st_own, st_got, st_fin,
    gsnd, grcv, gloc, vsnd, vrcv, wsem, psnd, prcv, csnd, crcv, outs,
):
    pos = Place(seq, row)
    at, zl = pos.at, pos.zl
    z, x, y, c = (at[k] for k in "zxyc")
    _, t, d = tokbuf.shape
    steps, H = u.shape[1], u.shape[3]
    parts = w_own.shape[2]
    partner = pos.device(dict(at, z=z + 1 - 2 * zl))
    own = pl.ds(pl.multiple_of(zl * H, H), H)
    other = pl.ds(pl.multiple_of((1 - zl) * H, H), H)
    rows_of = lambda b: pl.ds(pl.multiple_of(b * t, t), t)
    get_weight = pltpu.make_async_copy(weight, w_nat, outs.at[10])
    get_weight.start()
    pos.barrier(seq)
    get_weight.wait()
    for l in range(2):
        for p in range(2):
            for m in range(parts):
                for h in range(2):
                    for e in range(3):
                        start = e * d + p * H + (2 * m + h) * LANE
                        w_own[l, p, m, h, :, e * LANE : (e + 1) * LANE] = w_nat[
                            l, :, start : start + LANE
                        ]

    gather = Gather(pos, parts, w_own, w_all, gsnd, grcv, gloc)
    chains = [Chain(pos, tables.at[k], csnd.at[k], crcv.at[k]) for k in range(3)]

    def pair(k, src, dst):
        return remote(src, dst, psnd.at[k], prcv.at[k], partner)

    def tokens(b):
        return pair(0, tokbuf.at[b], tokbuf.at[b])

    def cotangents(b):
        return pair(1, du.at[t : 2 * t, d : d + H], cotbuf.at[b])

    def permute(src, store):
        group = nat.shape[0]
        for q in range(d // LANE // group):
            for k in range(group):
                at_lanes = (q * group + k) * LANE
                nat[k] = src[:, at_lanes : at_lanes + LANE].astype(F32)

            def one(k, _):
                rows = [
                    jnp.concatenate(
                        [nat[e, pl.ds(2 * k + j, SUB, stride=steps), :] for e in range(group)], axis=-1
                    )
                    for j in range(2)
                ]
                spot = pl.ds(pl.multiple_of(2 * SUB * k, 2 * SUB), 2 * SUB)
                store(spot, q, jnp.concatenate(rows, axis=0).astype(BF16))
                return 0

            lax.fori_loop(0, steps // 2, one, 0, unroll=4)

    def keeps(b):
        return pair(2, keepc.at[b], keepc.at[b])

    def statistics(b, to):
        return pair(3 + b, st_own.at[b], to.at[b])

    def lows(b, cols):
        return pair(5 + b, low.at[rows_of(b), cols], low.at[rows_of(b), cols])

    def results():
        return pair(7, resbuf.at[1 - zl, pl.ds(0, t // 2)], resx)

    def vcopies(stage, arriving):
        axis = gather.axis(stage, 0)
        size = pos.sizes[axis]
        for k in pos.others(axis):
            sem = gather.base[stage] + k - 1
            to = pos.moved(axis, k)
            who = pos.moved(axis, size - k) if arriving else at
            mine = gather.region(vall, (), stage, 0, who)
            yield remote(mine, mine, vsnd.at[sem], vrcv.at[sem], pos.device(to))

    def vadvance(stage):
        for copy in vcopies(stage - 1, True):
            copy.wait_recv()
        if stage < 4:
            for copy in vcopies(stage, False):
                copy.start()

    own_tokens = pltpu.make_async_copy(tok, du.at[0:t, 0:d], outs.at[0])
    own_cot = pltpu.make_async_copy(cot, du.at[t : 2 * t, 0:d], outs.at[1])
    given = [
        v[...].astype(F32) for v in (gain_in, shift_in, fpeep_in, rpeep_in, fbias_in, rbias_in)
    ]
    per = given[0].shape[-1]
    blank = jnp.zeros((2, per), F32)
    given = jnp.concatenate(
        [v[l : l + 1] for l in range(2) for v in given + [blank] * 2], axis=0
    )
    given = jnp.concatenate([given, jnp.zeros((16, LANE - per), F32)], axis=-1)
    vall[z, x, y, c] = given.astype(BF16)
    kept = 1.0 - resets[...].astype(F32)
    kept = jnp.concatenate([kept[:, k * steps : (k + 1) * steps] for k in range(SUB)], axis=0)
    keepc[zl] = jnp.concatenate([kept, jnp.zeros((SUB, LANE - steps), F32)], axis=-1)
    own_tokens.start()
    own_cot.start()
    for copy in vcopies(0, False):
        copy.start()
    keeps(zl).start()
    gather.begin(0)
    gather.begin(1)
    gather.begin(2)
    gather.begin(3)
    vadvance(1)
    own_tokens.wait()
    wide = nat.shape[0] * LANE

    def store_tokens(rows, q, v):
        tokbuf[zl, rows, q * wide : (q + 1) * wide] = v

    permute(du.at[0:t, 0:d], store_tokens)
    gather.turn(0)
    vadvance(2)
    vadvance(3)
    gather.turn(1)
    tokens(zl).start()
    vadvance(4)

    per = d // (seq * row)
    for q in range(d // LANE):
        pieces = []
        for e in range(LANE // per):
            i = q * (LANE // per) + e
            spot = (i // (2 * pos.Y * pos.X), i // (2 * pos.Y) % pos.X, i // 2 % pos.Y, i % 2)
            pieces.append(vall[spot][:, :per].astype(F32))
        value = jnp.concatenate(pieces, axis=-1)
        for l in range(2):
            vec[l, :, q * LANE : (q + 1) * LANE] = value[l * 8 : l * 8 + 8]
    keeps(1 - zl).wait_recv()
    for b in range(2):
        kept = keepc[b]
        for i in range(steps):
            keep[b, i] = jnp.broadcast_to(kept[:, i : i + 1], (SUB, LANE))

    def norm0(b):
        piece = 8

        def one(k, _):
            rows = pl.ds(pl.multiple_of(k * piece * SUB, piece * SUB), piece * SUB)
            spot = pl.ds(k * piece, piece)
            v = tokbuf[b, rows, :].astype(F32)
            mu = jnp.mean(v, axis=-1, keepdims=True)
            v = v - mu
            rstd = lax.rsqrt(jnp.mean(v * v, axis=-1, keepdims=True) + epsilon)
            v = v * rstd * vec[0, GAIN : GAIN + 1, :] + vec[0, SHIFT : SHIFT + 1, :]
            at_rows = pl.ds(pl.multiple_of(b * t + k * piece * SUB, piece * SUB), piece * SUB)
            low[at_rows, :] = v.astype(BF16)
            u[b, spot] = tokbuf[b, rows, own].astype(F32).reshape(piece, SUB, H)
            stats[0, 0, b, spot] = jnp.broadcast_to(mu, (piece * SUB, LANE)).reshape(piece, SUB, LANE)
            stats[0, 1, b, spot] = jnp.broadcast_to(rstd, (piece * SUB, LANE)).reshape(
                piece, SUB, LANE
            )
            return 0

        lax.fori_loop(0, steps // piece, one, 0)

    def load(l, m, h):
        slot = lax.rem(m, 2)
        return pltpu.make_async_copy(
            w_all.at[l, m, h],
            wbuf.at[slot, :, :, :, :, :, pl.ds(h * HALF, HALF)],
            wsem.at[slot, h],
        )

    def start_load(l, m):
        for h in range(2):
            load(l, m, h).start()

    def end_load(l, m):
        for h in range(2):
            load(l, m, h).wait()

    def gates(l, m, b):
        w = wbuf[lax.rem(m, 2)].reshape(d, 2 * HALF)
        v = jnp.dot(low[rows_of(b), :], w, preferred_element_type=F32)
        proj[...] = v.reshape(steps, SUB, 2 * HALF)
        cols = lane_tile(m, 2 * LANE)
        wide = pl.ds(pl.multiple_of(zl * H + m * 2 * LANE, 2 * LANE), 2 * LANE)
        peep, bias, rbias, gain, shift = (
            jnp.broadcast_to(vec[l, k : k + 1, wide], (SUB, 2 * LANE))
            for k in (FPEEP, FBIAS, RBIAS, GAIN, SHIFT)
        )

        def both(i, off):
            return jnp.concatenate(
                [proj[i, :, h * HALF + off : h * HALF + off + LANE] for h in range(2)], axis=-1
            )

        def one(i, carry):
            scale, state = carry
            cd = both(i, 0)
            n = (u[b, i, :, cols] - lanes(stats[l, 0, b, i], 2 * LANE)) * lanes(
                stats[l, 1, b, i], 2 * LANE
            ) * gain + shift
            up, down = both_sigmoids(both(i, LANE) + peep * n + bias)
            f[b, i, :, cols] = up
            g[b, i, :, cols] = down
            cand[b, i, :, cols] = cd
            rpre[b, i, :, cols] = both(i, 2 * LANE) + rbias
            a = up * lanes(keep[b, i], 2 * LANE)
            return scale * a, a * state + down * cd

        start = jnp.ones((SUB, 2 * LANE), F32), jnp.zeros((SUB, 2 * LANE), F32)
        scale, state = lax.fori_loop(0, steps, one, start, unroll=16)
        ends[b, 0, :, cols] = scale
        ends[b, 1, :, cols] = state

    def stash(k, src, dst):
        return pltpu.make_async_copy(src, dst, outs.at[k])

    norm0(zl)
    own_cot.wait()

    def store_cot(rows, q, v):
        side, at_lanes = q * wide // H, q * wide % H

        @pl.when(zl == side)
        def _():
            cotbuf[zl, rows, at_lanes : at_lanes + wide] = v

        @pl.when(zl != side)
        def _():
            to = pl.ds(pl.multiple_of(rows.start + t, 2 * SUB), 2 * SUB)
            du[to, d + at_lanes : d + at_lanes + wide] = v

    def turn(i, _):
        gather.turn(i)

        @pl.when(i == 3)
        def _():
            permute(du.at[t : 2 * t, 0:d], store_cot)

        @pl.when(i >= 3)
        def _():
            @pl.when(i < parts + 1)
            def _():
                start_load(0, i - 3)

        @pl.when((i >= 4) & (i < parts + 2))
        def _():
            end_load(0, i - 4)
            gates(0, i - 4, zl)

        @pl.when(i == parts + 1)
        def _():
            tokens(1 - zl).wait_recv()
            for k in range(6, 2 * parts):
                gather.begin(k)
            norm0(1 - zl)

        @pl.when(i > parts)
        def _():
            last = i == parts + 2

            def job(k, _):
                m = jnp.where(last, parts - 2 + k // 2, k)
                b = jnp.where(last & (lax.rem(k, 2) == 0), zl, 1 - zl)

                @pl.when(last & (lax.rem(k, 2) == 0))
                def _():
                    end_load(0, m)

                gates(0, m, b)

                @pl.when(jnp.logical_not(last) & (k == 0))
                def _():
                    start_load(0, parts - 2)

                return 0

            @pl.when(last)
            def _():
                start_load(0, parts - 1)

            lax.fori_loop(0, jnp.where(last, 4, parts - 2), job, 0)

        return 0

    lax.fori_loop(2, parts + 3, turn, 0)
    keep_tokx = stash(0, tokbuf.at[zl, :, other], tokx0)
    keep_tokx.start()
    keep_u0, keep_low0 = stash(2, u, u0), stash(3, low, low0)
    gates0 = [stash(4, f, f0), stash(5, g, g0), stash(6, cand, cand0)]
    for copy in [keep_u0, keep_low0] + gates0:
        copy.start()
    chains[0].run(ends, first, False)
    gather.turn(parts + 3)
    keep_u0.wait()
    keep_low0.wait()

    def states0(b):
        def tile(m, _):
            cols = lane_tile(m, 2 * LANE)
            wide = pl.ds(pl.multiple_of(zl * H + m * 2 * LANE, 2 * LANE), 2 * LANE)
            peep = jnp.broadcast_to(vec[0, RPEEP : RPEEP + 1, wide], (SUB, 2 * LANE))

            def one(i, cell):
                before = lanes(keep[b, i], 2 * LANE) * cell
                cell = f[b, i, :, cols] * before + g[b, i, :, cols] * cand[b, i, :, cols]
                gate = jax.nn.sigmoid(rpre[b, i, :, cols] + peep * before)
                np_[b, i, :, cols] = before
                rpre[b, i, :, cols] = gate
                u[b, i, :, cols] = gate * cell + (1.0 - gate) * u[b, i, :, cols]
                return cell

            lax.fori_loop(0, steps, one, first[b, :, cols], unroll=16)
            return 0

        lax.fori_loop(0, parts, tile, 0)

    def local_stats(b):
        def one(q, _):
            v = u[b, pl.ds(q * (LANE // SUB), LANE // SUB)].reshape(LANE, H)
            mu = jnp.mean(v, axis=-1, keepdims=True)
            v = v - mu
            square = jnp.sum(v * v, axis=-1, keepdims=True)
            st_own[b, pl.ds(q, 1), :] = to_row(mu)
            st_own[b, pl.ds(q + t // LANE, 1), :] = to_row(square)
            return 0

        lax.fori_loop(0, t // LANE, one, 0)
        statistics(b, st_got).start()

    def norm1(b):
        half = t // LANE
        statistics(b, st_got).wait_recv()
        m0, m1 = st_own[b, :half], st_got[b, :half]
        gap = m0 - m1
        square = st_own[b, half:] + st_got[b, half:] + gap * gap * (H / 2)
        st_fin[b, :half] = (m0 + m1) * 0.5
        st_fin[b, half:] = lax.rsqrt(square / (2 * H) + epsilon)

        def one(q, _):
            spot = pl.ds(q * (LANE // SUB), LANE // SUB)
            mu = to_column(st_fin[b, pl.ds(q, 1), :])
            rstd = to_column(st_fin[b, pl.ds(q + half, 1), :])
            v = u[b, spot].reshape(LANE, H)
            v = (v - mu) * rstd * vec[1, GAIN : GAIN + 1, own] + vec[1, SHIFT : SHIFT + 1, own]
            low[pl.ds(pl.multiple_of(b * t + q * LANE, LANE), LANE), own] = v.astype(BF16)
            stats[1, 0, b, spot] = spread_rows(mu)
            stats[1, 1, b, spot] = spread_rows(rstd)
            return 0

        lax.fori_loop(0, half, one, 0)
        lows(b, own).start()

    states0(0)
    local_stats(0)
    states0(1)
    keep_p0, keep_r0 = stash(7, np_, p0), stash(8, rpre, r0)
    keep_p0.start()
    keep_r0.start()
    norm1(0)
    local_stats(1)
    gather.turn(parts + 4)
    norm1(1)
    start_load(1, 0)
    keep_u1 = stash(2, u, u1)
    keep_u1.start()
    for copy in gates0 + [keep_r0]:
        copy.wait()

    def job1(k, _):
        b, m = k // parts, lax.rem(k, parts)

        @pl.when(m == 0)
        def _():
            lows(b, other).wait_recv()

        @pl.when(k == parts)
        def _():
            cotangents(zl).start()

        @pl.when((k == 1) | (k == 2))
        def _():
            gather.turn(parts + 4 + k)

        @pl.when(k + 1 < 2 * parts)
        def _():
            start_load(1, lax.rem(k + 1, parts))

        end_load(1, m)
        gates(1, m, b)
        return 0

    lax.fori_loop(0, 2 * parts, job1, 0)
    keep_low1 = stash(3, low, low1)
    keep_low1.start()
    chains[1].run(ends, first, False)
    keep_p0.wait()

    def step_back(b, i, cols, top, peep):
        before, gate, up = np_[b, i, :, cols], rpre[b, i, :, cols], f[b, i, :, cols]
        cell = up * before + g[b, i, :, cols] * cand[b, i, :, cols]
        dz_r = top * (cell - u[b, i, :, cols]) * gate * (1.0 - gate)
        direct = top * gate
        kept = lanes(keep[b, i], 2 * LANE)
        decay = up * kept
        return before, gate, up, dz_r, direct, decay, kept * peep * dz_r + decay * direct

    def turn_round(b):
        def tile(m, _):
            cols = lane_tile(m, 2 * LANE)
            wide = pl.ds(pl.multiple_of(zl * H + m * 2 * LANE, 2 * LANE), 2 * LANE)
            peep = jnp.broadcast_to(vec[1, RPEEP : RPEEP + 1, wide], (SUB, 2 * LANE))
            top = cotbuf[b, :, cols].astype(F32).reshape(steps, SUB, 2 * LANE)
            proj[:, :, 2 * LANE : 4 * LANE] = top

            def one(i, cell):
                before = lanes(keep[b, i], 2 * LANE) * cell
                cell = f[b, i, :, cols] * before + g[b, i, :, cols] * cand[b, i, :, cols]
                gate = jax.nn.sigmoid(rpre[b, i, :, cols] + peep * before)
                np_[b, i, :, cols] = before
                rpre[b, i, :, cols] = gate
                proj[i, :, : 2 * LANE] = gate * cell + (1.0 - gate) * u[b, i, :, cols]
                return cell

            lax.fori_loop(0, steps, one, first[b, :, cols], unroll=16)
            v = proj[:, :, : 2 * LANE].reshape(t, 2 * LANE)
            resbuf[b, :, cols] = v.astype(BF16)

            def back(k, carry):
                scale, q = carry
                i = steps - 1 - k
                _, _, _, _, _, decay, term = step_back(
                    b, i, cols, proj[i, :, 2 * LANE : 4 * LANE], peep
                )
                return scale * decay, decay * q + term

            start = jnp.ones((SUB, 2 * LANE), F32), jnp.zeros((SUB, 2 * LANE), F32)
            scale, q = lax.fori_loop(0, steps, back, start, unroll=16)
            ends[b, 0, :, cols] = scale
            ends[b, 1, :, cols] = q
            return 0

        lax.fori_loop(0, parts, tile, 0)

    def blocks(k, _):
        @pl.when(k == 1)
        def _():
            cotangents(1 - zl).wait_recv()

        turn_round(jnp.where(k == 0, zl, 1 - zl))
        return 0

    lax.fori_loop(0, 2, blocks, 0)
    results().start()
    keep_res = stash(9, resbuf, res1)
    keep_res.start()
    chains[2].run(ends, first, True)

    def down(b):
        def tile(m, _):
            cols = lane_tile(m, 2 * LANE)
            wide = pl.ds(pl.multiple_of(zl * H + m * 2 * LANE, 2 * LANE), 2 * LANE)
            fpeep, rpeep, gain, shift = (
                jnp.broadcast_to(vec[1, k : k + 1, wide], (SUB, 2 * LANE))
                for k in (FPEEP, RPEEP, GAIN, SHIFT)
            )

            def one(k, carry):
                q, s0, s1, s2, s3 = carry
                i = steps - 1 - k
                top = top_of[i]
                before, gate, up, dz_r, direct, decay, term = step_back(b, i, cols, top, rpeep)
                e = direct + q
                low_f = g[b, i, :, cols]
                dz_f = e * (up * low_f) * (before - cand[b, i, :, cols])
                n = (u[b, i, :, cols] - lanes(stats[1, 0, b, i], 2 * LANE)) * lanes(
                    stats[1, 1, b, i], 2 * LANE
                ) * gain + shift
                proj[i, :, : 2 * LANE] = e * low_f
                proj[i, :, 2 * LANE : 4 * LANE] = dz_f
                proj[i, :, 4 * LANE :] = dz_r
                cand[b, i, :, cols] = dz_f * fpeep
                rpre[b, i, :, cols] = top * (1.0 - gate)
                return (
                    decay * q + term,
                    s0 + dz_f * n,
                    s1 + dz_r * before,
                    s2 + dz_f,
                    s3 + dz_r,
                )

            top_of[...] = cotbuf[b, :, cols].astype(F32).reshape(steps, SUB, 2 * LANE)
            zero = jnp.zeros((SUB, 2 * LANE), F32)
            carry = lax.fori_loop(0, steps, one, (first[b, :, cols], zero, zero, zero, zero), unroll=16)
            for k in range(4):
                sums[b, k, :, cols] = carry[k + 1]
            for h in range(2):
                for k in range(3):
                    v = proj[:, :, k * 2 * LANE + h * LANE : k * 2 * LANE + (h + 1) * LANE]
                    to = pl.ds(pl.multiple_of((2 * m + h) * HALF + k * LANE, LANE), LANE)
                    du[rows_of(b), to] = v.reshape(t, LANE).astype(BF16)
            return 0

        lax.fori_loop(0, parts, tile, 0)

    keep_low1.wait()
    cotangents(zl).wait_send()

    def last(b):
        yield stash(3, du.at[rows_of(b)], du1.at[rows_of(b)])
        yield stash(4, cand.at[b], dn1.at[b])
        yield stash(5, rpre.at[b], dhr1.at[b])

    down(0)
    for copy in last(0):
        copy.start()
    down(1)
    for copy in last(0):
        copy.wait()
    for copy in last(1):
        copy.start()
    gather.finish()
    for stage in range(4):
        for copy in vcopies(stage, False):
            copy.wait_send()
    for copy in list(last(1)) + [keep_u1, keep_res, keep_tokx]:
        copy.wait()
    results().wait_recv()
    results().wait_send()
    tokens(zl).wait_send()
    keeps(zl).wait_send()
    for b in range(2):
        statistics(b, st_got).wait_send()
        lows(b, own).wait_send()


def call_forward(seq, row, tok, cot, keep, rows, weight):
    t, d = tok.shape
    layers, per, _ = weight.shape
    Y = row // 2
    X = Y
    Z = seq // X
    H = d // 2
    parts = H // WIDE
    steps = t // SUB
    act, stat = arr(2, steps, SUB, H), arr(2, steps, SUB, LANE)
    half = arr(2 * t, d, dtype=BF16)
    vmem = pl.BlockSpec(memory_space=pltpu.VMEM)
    hbm = pl.BlockSpec(memory_space=pl.ANY)
    count = Z + 2 * X - 2
    dma = pltpu.SemaphoreType.DMA
    big = pltpu.VMEM((2, steps, SUB, H), F32)
    st = pltpu.VMEM((2, 8, LANE), F32)
    return pl.pallas_call(
        lambda *refs: forward_all(seq, row, *refs),
        in_specs=[hbm, hbm] + [vmem] * (1 + len(rows)) + [hbm],
        out_specs=[hbm, vmem, vmem, vmem] + [hbm] * 15 + [vmem],
        out_shape=[
            arr(layers, parts, 2, Z, X, Y, 2, per, HALF, dtype=BF16),
            arr(2, 8, d),
            stat,
            arr(2, 2, 2, steps, SUB, LANE),
        ]
        + [act] * 6
        + [half, half, act, act, act, arr(2 * t, 3 * H, dtype=BF16), arr(2, t, H, dtype=BF16), arr(t // 2, H, dtype=BF16), arr(t, H, dtype=BF16)]
        + [arr(2, 4, SUB, H)],
        scratch_shapes=[
            pltpu.VMEM((4, t, LANE), F32),
            pltpu.VMEM((layers, per, 3 * d), BF16),
            pltpu.VMEM((layers, 2, parts, 2, per, HALF), BF16),
            pltpu.VMEM((2, t, d), BF16),
            pltpu.VMEM((2, t, H), BF16),
            pltpu.VMEM((2, 8, LANE), F32),
            pltpu.VMEM((Z, X, Y, 2, 16, LANE), BF16),
            big, big, big, big, big, big,
            pltpu.VMEM((2 * t, d), BF16),
            pltpu.VMEM((2, Z, X, Y, 2, per, 2 * HALF), BF16),
            pltpu.VMEM((steps, SUB, 2 * HALF), F32),
            pltpu.VMEM((2 * t, 3 * H), BF16),
            pltpu.VMEM((2, t, H), BF16),
            pltpu.VMEM((steps, SUB, 2 * LANE), F32),
            pltpu.VMEM((2, 2, SUB, H), F32),
            pltpu.VMEM((2, SUB, H), F32),
            pltpu.VMEM((3, Z // 2, X, 2, 2, H), F32),
            st, st, st,
            dma((2, 2 * parts, count)),
            dma((2, 2 * parts, count)),
            dma((2, 2 * parts)),
            dma((count,)),
            dma((count,)),
            dma((2, 2)),
            dma((8,)),
            dma((8,)),
            dma((3, Z // 2 * X)),
            dma((3, Z // 2 * X)),
            dma((11,)),
        ],
        compiler_params=pltpu.CompilerParams(
            collective_id=0, has_side_effects=True, vmem_limit_bytes=62 << 20
        ),
        name="forward_all",
    )(tok, cot, keep, *rows, weight)


def wrap(a, b):
    return a % b if isinstance(a, int) else lax.rem(a, b)


class Scatter:
    lag = (0, 1, 3, 5, 7)
    sends = (2, 4, 4, 4)
    slots = (2, 6, 6, 6)
    kept = (1, 3, 3, 3)

    def __init__(self, pos, count, low, du, out, keep, send, recv, done, snd, rcv, outs):
        self.pos, self.count, self.low, self.du, self.out = pos, count, low, du, out
        self.keep, self.send, self.recv, self.done = keep, send, recv, done
        self.snd, self.rcv, self.outs = snd, rcv, outs
        n = pos.X - 1
        self.base = (0, 1, 1 + n, 1 + 2 * n)

    def axis(self, stage, h):
        return ("c", ("x", "y")[h], ("y", "x")[h], "z")[stage]

    def copy(self, g, stage, h, k):
        mine, slot = wrap(g, self.sends[stage]), wrap(g, self.slots[stage])
        sem = self.base[stage] + k - 1
        to = self.pos.device(self.pos.moved(self.axis(stage, h), k))
        return remote(
            self.send[stage].at[mine, k - 1], self.recv[stage].at[slot, k - 1],
            self.snd.at[mine, sem], self.rcv.at[slot, sem], to,
        )

    def each(self, stage, h):
        return self.pos.others(self.axis(stage, h))

    def ready(self, g, stage, h):
        def wait():
            for k in self.each(stage, h):
                self.copy(g, stage, h, k).wait_send()

        if isinstance(g, int):
            if g >= self.sends[stage]:
                wait()
        else:
            pl.when(g >= self.sends[stage])(wait)

    def start(self, g, stage, h):
        for k in self.each(stage, h):
            self.copy(g, stage, h, k).start()

    def arrive(self, g, stage, h):
        for k in self.each(stage, h):
            self.copy(g, stage, h, k).wait_recv()

    def stage0(self, g, h):
        pos, low, t = self.pos, self.low, self.low.shape[0]
        rows = low.shape[1] // pos.Z
        slot = wrap(g, 2)
        q = wrap(g, self.count)
        cols = pl.ds(q * HALF if isinstance(q, int) else pl.multiple_of(q * HALF, LANE), HALF)
        self.ready(g, 0, h)
        first = pos.at["c"] == 0

        def one(z, _):
            lhs = low[:, pl.ds(pl.multiple_of(z * rows, LANE), rows)]
            v = lax.dot_general(
                lhs, self.du[:, cols], (((0,), (0,)), ((), ())), preferred_element_type=F32
            )
            v = v.reshape(pos.X, pos.Y, 2, -1, HALF)
            even, odd = v[:, :, 0], v[:, :, 1]
            self.keep[0][z] = jnp.where(first, even, odd)
            self.send[0][slot, 0, z] = jnp.where(first, odd, even).astype(BF16)
            return 0

        lax.fori_loop(0, pos.Z, one, 0)
        self.start(g, 0, h)

    def stage1(self, g, h):
        pos, axis = self.pos, self.axis(1, h)
        slot, got, mine = wrap(g, 4), wrap(g, 2), wrap(g, 3)
        self.arrive(g, 0, h)
        self.ready(g, 1, h)
        for k in range(pos.sizes[axis]):
            p = pos.moved(axis, k)[axis]

            def one(z, _):
                where = (z, p) if h == 0 else (z, slice(None), p)
                v = self.keep[0][where] + self.recv[0][(got, 0) + where].astype(F32)
                if k == 0:
                    self.keep[1][mine, z] = v
                else:
                    self.send[1][slot, k - 1, z] = v.astype(BF16)
                return 0

            lax.fori_loop(0, pos.Z, one, 0)
        self.start(g, 1, h)

    def stage2(self, g, h):
        pos, axis = self.pos, self.axis(2, h)
        slot, got, mine = wrap(g, 4), wrap(g, 6), wrap(g, 3)
        self.arrive(g, 1, h)
        self.ready(g, 2, h)
        for k in range(pos.sizes[axis]):
            p = pos.moved(axis, k)[axis]
            v = self.keep[1][mine, :, p]
            for e in self.each(1, h):
                v = v + self.recv[1][got, e - 1, :, p].astype(F32)
            if k == 0:
                self.keep[2][mine] = v
            else:
                self.send[2][slot, k - 1] = v.astype(BF16)
        self.start(g, 2, h)

    def stage3(self, g, h):
        pos = self.pos
        slot, got, mine = wrap(g, 4), wrap(g, 6), wrap(g, 3)
        self.arrive(g, 2, h)
        self.ready(g, 3, h)
        for k in range(pos.Z):
            p = pos.moved("z", k)["z"]
            v = self.keep[2][mine, p]
            for e in self.each(2, h):
                v = v + self.recv[2][got, e - 1, p].astype(F32)
            if k == 0:
                self.keep[3][mine] = v
            else:
                self.send[3][slot, k - 1] = v.astype(BF16)
        self.start(g, 3, h)

    def result(self, l, q, half, e):
        d = self.out.shape[-1] // 3
        at = e * d + half * (d // 2) + q * LANE
        return pltpu.make_async_copy(
            self.done.at[half, wrap(q, 4), :, e * LANE : (e + 1) * LANE],
            self.out.at[l, :, pl.ds(pl.multiple_of(at, LANE), LANE)],
            self.outs.at[half, wrap(q, 4), e],
        )

    def stage4(self, g, h, l):
        pos = self.pos
        got, mine, q = wrap(g, 6), wrap(g, 3), wrap(g, self.count)
        self.arrive(g, 3, h)
        own, other = self.keep[3][mine], None
        for k in range(1, pos.Z):
            v = self.recv[3][got, k - 1].astype(F32)
            if k % 2 == 0:
                own = own + v
            else:
                other = v if other is None else other + v
        if isinstance(q, int):
            if q >= 4:
                self.stored(l, q - 4)
        else:
            pl.when(q >= 4)(lambda: self.stored(l, q - 4))
        self.done[pos.zl, wrap(q, 4)] = own
        self.done[1 - pos.zl, wrap(q, 4)] = other
        for half in (pos.zl, 1 - pos.zl):
            for e in range(3):
                self.result(l, q, half, e).start()

    def stored(self, l, q):
        for half in (self.pos.zl, 1 - self.pos.zl):
            for e in range(3):
                self.result(l, q, half, e).wait()

    def turn(self, run, l, pair, e, enters=True):
        first = run * self.count

        def stage(s, f):
            g = first + 2 * pair + e - self.lag[s]
            h = (e - self.lag[s]) % 2
            if isinstance(g, int):
                if first <= g < first + self.count:
                    f(g, h)
            elif s:
                pl.when(g >= first)(lambda: f(g, h))
            else:
                f(g, h)

        stage(1, self.stage1)
        if enters:
            stage(0, self.stage0)
        stage(2, self.stage2)
        stage(3, self.stage3)
        stage(4, lambda g, h: self.stage4(g, h, l))

    def written(self, l):
        for q in range(self.count - 4, self.count):
            self.stored(l, q)

    def finish(self, total):
        for stage in range(4):
            for g in range(total - self.sends[stage], total):
                for k in self.each(stage, g % 2):
                    self.copy(g, stage, g % 2, k).wait_send()


def backward_all(
    seq, row, w_all, vec, keep, stats_all, f0, g0, cand0, p0, r0, u0, low0, low1, u1, dhr1, dn1, du1,
    res1, resx, tok, sums1,
    grad, input_grad, result, vo0, vo1, vo2, vo3, vo4, vo5,
    stats, wbuf, du, low, dn, dnsend, dnrecv, hsend, hrecv, tokx, u, dhr, stream, proj,
    keep0, send0, recv0, keep1, send1, recv1, keep2, send2, recv2, keep3, send3, recv3, done,
    ends, first, table, b_own, b_got, b_fin, sums, sumsx, vbuf, vr0, vr1, vr2, vr3,
    snd, rcv, gouts, psnd, prcv, csnd, crcv, vsnd, vrcv, ins, ssem, wsem,
):
    pos = Place(seq, row)
    at, zl = pos.at, pos.zl
    z, x, y, c = (at[k] for k in "zxyc")
    t2, H3 = du.shape
    t, H = t2 // 2, H3 // 3
    d = 2 * H
    steps = t // SUB
    parts = H // WIDE
    partner = pos.device(dict(at, z=z + 1 - 2 * zl))
    own = pl.ds(pl.multiple_of(zl * H, H), H)
    other = pl.ds(pl.multiple_of((1 - zl) * H, H), H)
    rows_of = lambda b: pl.ds(pl.multiple_of(b * t, t), t)

    def load(k, src, dst):
        return pltpu.make_async_copy(src, dst, ins.at[k])

    def weights(l, half):
        zs = pl.ds(half * (pos.Z // 2), pos.Z // 2)
        for m in range(parts):
            for h in range(2):
                q = 2 * m + h
                yield pltpu.make_async_copy(
                    w_all.at[l, m, h, zs],
                    wbuf.at[:, :, :, :, :, q * HALF : (q + 1) * HALF],
                    wsem.at[q],
                )

    def begin(copies):
        for copy in copies:
            copy.start()

    def end(copies):
        for copy in copies:
            copy.wait()

    get_du, get_low, get_dn = load(0, du1, du), load(1, low1, low), load(2, dn1, dn)
    get_u, get_dhr = load(3, u1, u), load(4, dhr1, dhr)
    get_stats = load(6, stats_all.at[1], stats)
    get_du.start()
    begin(weights(1, 1 - zl))
    pos.barrier(seq)
    scatter = Scatter(
        pos, 2 * parts, low, du, grad, (keep0, keep1, keep2, keep3), (send0, send1, send2, send3),
        (recv0, recv1, recv2, recv3), done, snd, rcv, gouts,
    )
    chain = Chain(pos, table, csnd, crcv)

    def pair(k, src, dst):
        return remote(src, dst, psnd.at[k], prcv.at[k], partner)

    def partial_sums(b):
        return pair(b, dnsend.at[b], dnrecv.at[b])

    def statistics(b):
        return pair(2 + b, b_own.at[b], b_got.at[b])

    def carried():
        return pair(4, hsend, hrecv)

    def results(cols):
        rows = pl.ds(t // 2, t // 2)
        return pair(5, res1.at[1 - zl, rows], result.at[rows, cols])

    own_result = load(5, res1.at[zl], result.at[:, own])
    own_result.start()
    got_result = load(8, resx, result.at[pl.ds(0, t // 2), other])
    got_result.start()
    across = (((1,), (1,)), ((), ()))

    n = t2 // parts
    blocks = t // n

    def product(b, k):
        rows = pl.ds(pl.multiple_of(b * t + k * n, n), n)
        return lax.dot_general(
            du[rows, :], wbuf[...].reshape(H, H3), across, preferred_element_type=F32
        )

    def of_block(k):
        return pl.ds(pl.multiple_of(k * (n // SUB), n // SUB), n // SUB)

    def theirs(q, b, more=None):
        def one(k, _):
            v = product(b, k)
            if more is not None:
                v = v + more[of_block(k)].reshape(n, H)
            dnsend[q, pl.ds(pl.multiple_of(k * n, n), n), :] = v.astype(BF16)
            return 0

        lax.fori_loop(0, blocks, one, 0)
        partial_sums(q).start()

    def ours(to, b, k, fresh=False):
        v = product(b, k).reshape(n // SUB, SUB, H)
        if fresh:
            dn[to, of_block(k)] = v
        else:
            dn[to, of_block(k)] += v

    half = t // LANE

    def norm_sums(l, b):
        partial_sums(b).wait_recv()

        def one(q, _):
            spot = pl.ds(q * (LANE // SUB), LANE // SUB)
            rows = pl.ds(pl.multiple_of(q * LANE, LANE), LANE)
            v = dn[b, spot].reshape(LANE, H) + dnrecv[b, rows, :].astype(F32)
            dn[b, spot] = v.reshape(LANE // SUB, SUB, H)
            xhat = hat(l, b, spot)
            sums[l, 0] += jnp.sum((v * xhat).reshape(LANE // SUB, SUB, H), axis=0)
            sums[l, 1] += jnp.sum(v.reshape(LANE // SUB, SUB, H), axis=0)
            v = v * vec[l, GAIN : GAIN + 1, own]
            b_own[b, pl.ds(q, 1), :] = to_row(jnp.sum(v, axis=-1, keepdims=True))
            b_own[b, pl.ds(q + half, 1), :] = to_row(jnp.sum(v * xhat, axis=-1, keepdims=True))
            return 0

        lax.fori_loop(0, half, one, 0)
        statistics(b).start()

    def hat(l, b, spot):
        mu = stats[0, b, spot].reshape(LANE, LANE)[:, :1]
        rstd = stats[1, b, spot].reshape(LANE, LANE)[:, :1]
        return (u[b, spot].reshape(LANE, H) - mu) * rstd

    def norm_back(l, b):
        statistics(b).wait_recv()
        b_fin[...] = (b_own[b] + b_got[b]) * (1.0 / d)

        def one(q, _):
            spot = pl.ds(q * (LANE // SUB), LANE // SUB)
            xhat = hat(l, b, spot)
            rstd = stats[1, b, spot].reshape(LANE, LANE)[:, :1]
            m0 = to_column(b_fin[pl.ds(q, 1), :])
            m1 = to_column(b_fin[pl.ds(q + half, 1), :])
            v = dn[b, spot].reshape(LANE, H) * vec[l, GAIN : GAIN + 1, own]
            v = dhr[b, spot].reshape(LANE, H) + rstd * (v - m0 - xhat * m1)
            dhr[b, spot] = v.reshape(LANE // SUB, SUB, H)
            return 0

        lax.fori_loop(0, half, one, 0)

    def norm_last():
        for q in range(2):
            partial_sums(q).wait_recv()
        carried().wait_recv()
        get_tok.wait()
        piece = 4
        n = piece * SUB

        def one(k, _):
            spot = pl.ds(k * piece, piece)
            rows = pl.ds(pl.multiple_of(k * n, n), n)
            mu = stats[0, zl, spot].reshape(n, LANE)[:, :1]
            rstd = stats[1, zl, spot].reshape(n, LANE)[:, :1]
            scaled, hats = [], []
            m0 = m1 = 0.0
            for q, part in enumerate((zl, 1 - zl)):
                x = u[zl, spot].reshape(n, H) if q == 0 else tokx[rows, :].astype(F32)
                xhat = (x - mu) * rstd
                v = dn[part, spot].reshape(n, H) + dnrecv[q, rows, :].astype(F32)
                total = sums.at[0] if q == 0 else sumsx
                total[0] += jnp.sum((v * xhat).reshape(piece, SUB, H), axis=0)
                total[1] += jnp.sum(v.reshape(piece, SUB, H), axis=0)
                v = v * vec[0, GAIN : GAIN + 1, own if q == 0 else other]
                m0 += jnp.sum(v, axis=-1, keepdims=True)
                m1 += jnp.sum(v * xhat, axis=-1, keepdims=True)
                scaled.append(v)
                hats.append(xhat)
            m0, m1 = m0 * (1.0 / d), m1 * (1.0 / d)
            for q in range(2):
                v = rstd * (scaled[q] - m0 - hats[q] * m1)
                if q == 0:
                    v = v + dhr[zl, spot].reshape(n, H)
                else:
                    v = v + hrecv[rows, :].astype(F32)
                dnsend[q, rows, :] = v.astype(BF16)
            return 0

        lax.fori_loop(0, steps // piece, one, 0)

    units = 2 * parts
    sources = (f0, g0, cand0, p0, r0)

    def fetch(k):
        slot = lax.rem(k, 2)
        b, m = jnp.where(k < parts, 1 - zl, zl), lax.rem(k, parts)
        for j, src in enumerate(sources):
            yield pltpu.make_async_copy(
                src.at[b, :, :, lane_tile(m, WIDE)], stream.at[slot, j], ssem.at[slot, j]
            )

    def tiles(work, between=None):
        begin(fetch(0))

        def one(k, _):
            @pl.when(k + 1 < units)
            def _():
                begin(fetch(k + 1))

            end(fetch(k))
            b, m = jnp.where(k < parts, 1 - zl, zl), lax.rem(k, parts)
            cols = lane_tile(m, WIDE)
            wide = pl.ds(pl.multiple_of(zl * H + m * WIDE, WIDE), WIDE)
            work(lax.rem(k, 2), b, m, cols, wide)
            if between is not None:
                between(k)
            return 0

        lax.fori_loop(0, units, one, 0)

    def step_back(slot, b, i, cols, peep):
        up, down, cd, before, gate = (stream[slot, j, i] for j in range(5))
        cell = up * before + down * cd
        top = dhr[b, i, :, cols]
        dz_r = top * (cell - u[b, i, :, cols]) * gate * (1.0 - gate)
        direct = top * gate
        kept = lanes(keep[b, i], WIDE)
        decay = up * kept
        term = kept * peep * dz_r + decay * direct
        return up, down, cd, before, gate, top, dz_r, direct, decay, term

    def row_wide(l, k, wide):
        return jnp.broadcast_to(vec[l, k : k + 1, wide], (SUB, WIDE))

    def ends_work(slot, b, m, cols, wide):
        peep = row_wide(0, RPEEP, wide)

        def one(k, carry):
            scale, q = carry
            i = steps - 1 - k
            terms = step_back(slot, b, i, cols, peep)
            gate, top, decay, term = terms[4], terms[5], terms[-2], terms[-1]
            proj[i, :, :WIDE] = top * (1.0 - gate)
            return scale * decay, decay * q + term

        start = jnp.ones((SUB, WIDE), F32), jnp.zeros((SUB, WIDE), F32)
        scale, q = lax.fori_loop(0, steps, one, start, unroll=16)
        ends[b, 0, :, cols] = scale
        ends[b, 1, :, cols] = q

        @pl.when(b != zl)
        def _():
            hsend[:, cols] = proj[:, :, :WIDE].reshape(t, WIDE).astype(BF16)

    def send_carried(k):
        pl.when(k == parts - 1)(lambda: carried().start())

    def down_work(slot, b, m, cols, wide):
        fpeep, rpeep, gain, shift = (row_wide(0, k, wide) for k in (FPEEP, RPEEP, GAIN, SHIFT))

        def one(k, carry):
            q, s0, s1, s2, s3 = carry
            i = steps - 1 - k
            up, low_f, cd, before, gate, top, dz_r, direct, decay, term = step_back(
                slot, b, i, cols, rpeep
            )
            e = direct + q
            dz_f = e * (up * low_f) * (before - cd)
            n = (u[b, i, :, cols] - lanes(stats[0, b, i], WIDE)) * lanes(
                stats[1, b, i], WIDE
            ) * gain + shift
            proj[i, :, :WIDE] = e * low_f
            proj[i, :, WIDE : 2 * WIDE] = dz_f
            proj[i, :, 2 * WIDE :] = dz_r
            dn[b, i, :, cols] = dz_f * fpeep
            dhr[b, i, :, cols] = top * (1.0 - gate)
            return (
                decay * q + term,
                s0 + dz_f * n,
                s1 + dz_r * before,
                s2 + dz_f,
                s3 + dz_r,
            )

        zero = jnp.zeros((SUB, WIDE), F32)
        carry = lax.fori_loop(0, steps, one, (first[b, :, cols], zero, zero, zero, zero), unroll=16)
        for k in range(4):
            sums[0, 2 + k, :, cols] += carry[k + 1]
        for h in range(2):
            for k in range(3):
                v = proj[:, :, k * WIDE + h * LANE : k * WIDE + (h + 1) * LANE]
                to = pl.ds(pl.multiple_of((2 * m + h) * HALF + k * LANE, LANE), LANE)
                du[rows_of(b), to] = v.reshape(t, LANE).astype(BF16)

    def late(run, l, k):
        scatter.turn(run, l, parts + k // 2, k % 2, False)

    sums[...] = jnp.zeros_like(sums)
    sumsx[...] = jnp.zeros_like(sumsx)
    sums[1, 2:6] = sums1[0] + sums1[1]
    get_du.wait()
    end(weights(1, 1 - zl))
    begin([get_low, get_dn])
    for b in range(2):
        theirs(b, b)
    begin(weights(1, zl))
    begin([get_u, get_dhr, get_stats])
    get_low.wait()
    get_dn.wait()

    def last_layer(k, _):
        scatter.turn(0, 1, k, 0)

        @pl.when(k == 0)
        def _():
            end(weights(1, zl))

        ours(k // blocks, k // blocks, lax.rem(k, blocks))
        scatter.turn(0, 1, k, 1)
        return 0

    lax.fori_loop(0, parts, last_layer, 0)
    get_low = load(1, low0, low)
    get_low.start()
    get_u.wait()
    get_dhr.wait()
    get_stats.wait()
    begin(weights(0, 1 - zl))
    norm_sums(1, 0)
    norm_sums(1, 1)
    late(0, 1, 0)
    norm_back(1, 0)
    norm_back(1, 1)
    results(own).start()
    get_u, get_stats = load(3, u0, u), load(6, stats_all.at[0], stats)
    get_tok = load(7, tok, tokx)
    begin([get_u, get_stats, get_tok])
    late(0, 1, 1)
    get_u.wait()
    get_stats.wait()
    late(0, 1, 2)
    tiles(ends_work, send_carried)
    late(0, 1, 3)
    chain.run(ends, first, True)
    for b in range(2):
        partial_sums(b).wait_send()
        statistics(b).wait_send()
    end(weights(0, 1 - zl))

    def between(k):
        @pl.when(k == parts - 1)
        def _():
            theirs(0, 1 - zl)
            begin(weights(0, zl))

        for e in range(3):
            pl.when(k == e)(lambda: late(0, 1, 4 + e))
        for e in range(2):
            pl.when(k == parts + e)(lambda: scatter.turn(1, 0, 0, e))

    get_low.wait()
    tiles(down_work, between)
    scatter.written(1)
    end(weights(0, zl))
    theirs(1, 1 - zl, dn.at[1 - zl])

    def first_layer(k, _):
        scatter.turn(1, 0, k, 0)

        @pl.when(k == 1)
        def _():
            ours(zl, zl, 0)
            ours(zl, zl, 1)
            begin(weights(0, 1 - zl))

        @pl.when(k == 2)
        def _():
            end(weights(0, 1 - zl))

        @pl.when(k > 1)
        def _():
            ours(1 - zl, zl, k - 2, True)

        scatter.turn(1, 0, k, 1)
        return 0

    lax.fori_loop(1, parts, first_layer, 0)
    late(1, 0, 0)
    late(1, 0, 1)
    for b in range(2):
        partial_sums(b).wait_send()
    norm_last()
    out_own = load(0, dnsend.at[0], input_grad.at[:, own])
    out_other = load(1, dnsend.at[1], input_grad.at[:, other])
    begin([out_own, out_other])
    late(1, 0, 2)
    late(1, 0, 3)

    vbuf[...] = jnp.zeros_like(vbuf)
    per = d // (seq * row)
    total = [jnp.sum(sums[l], axis=1) for l in range(2)]
    totalx = jnp.sum(sumsx[...], axis=1)
    blank = jnp.zeros((6, LANE - per), F32) if per < LANE else None
    for i in range(H // per):
        spot = (zl * (pos.Z // 2) + i // (2 * pos.Y * pos.X), i // (2 * pos.Y) % pos.X, i // 2 % pos.Y, i % 2)
        for l in range(2):
            piece = total[l][:, i * per : (i + 1) * per]
            vbuf[spot + (slice(l * 8, l * 8 + 6),)] = jnp.concatenate([piece, blank], axis=-1)
        away = (lax.rem(spot[0] + pos.Z // 2, pos.Z),) + spot[1:]
        piece = totalx[:, i * per : (i + 1) * per]
        vbuf[away + (slice(0, 2),)] = jnp.concatenate([piece, blank[:2]], axis=-1)
    every = slice(None)

    def vspot(stage, who):
        if stage == 0:
            return (every, every, every, who["c"])
        if stage == 1:
            return (every, who["x"], every, c)
        if stage == 2:
            return (every, x, who["y"], c)
        return (who["z"], x, y, c)

    vrecv = (vr0, vr1, vr2, vr3)

    def vcopy(stage, k):
        axis = "cxyz"[stage]
        to = pos.moved(axis, k)
        sem = scatter.base[stage] + k - 1
        return remote(
            vbuf.at[vspot(stage, to)], vrecv[stage].at[k - 1], vsnd.at[sem], vrcv.at[sem],
            pos.device(to),
        )

    def vstart(stage):
        for k in pos.others("cxyz"[stage]):
            vcopy(stage, k).start()

    def vtake(stage):
        for k in pos.others("cxyz"[stage]):
            vcopy(stage, k).wait_recv()
            vbuf[vspot(stage, at)] += vrecv[stage][k - 1]

    vstart(0)
    late(1, 0, 4)
    vtake(0)
    vstart(1)
    late(1, 0, 5)
    vtake(1)
    vstart(2)
    late(1, 0, 6)
    vtake(2)
    vstart(3)
    vtake(3)
    mine = vbuf[z, x, y, c]
    for k, out in enumerate((vo0, vo1, vo2, vo3, vo4, vo5)):
        out[...] = jnp.concatenate([mine[l * 8 + k : l * 8 + k + 1, :per] for l in range(2)], axis=0)
    for stage in range(4):
        for k in pos.others("cxyz"[stage]):
            vcopy(stage, k).wait_send()
    scatter.written(0)
    scatter.finish(2 * scatter.count)
    carried().wait_send()
    end([out_own, out_other])
    own_result.wait()
    got_result.wait()
    results(own).wait_send()
    results(other).wait_recv()


def call_backward(seq, row, t, d, given):
    w_all = given[0]
    layers, parts, _, Z, X, Y, _, per, _ = w_all.shape
    H = d // 2
    steps = t // SUB
    vmem = pl.BlockSpec(memory_space=pltpu.VMEM)
    hbm = pl.BlockSpec(memory_space=pl.ANY)
    dma = pltpu.SemaphoreType.DMA
    big = pltpu.VMEM((2, steps, SUB, H), F32)
    half, quarter = pltpu.VMEM((2, t, H), BF16), pltpu.VMEM((t, H), BF16)
    st = pltpu.VMEM((2, 8, LANE), F32)
    count = 1 + 2 * (X - 1) + Z - 1
    chunk = (Z, X, Y, per, HALF)

    def buf(*shape, dtype=BF16):
        return pltpu.VMEM(shape, dtype)

    return pl.pallas_call(
        lambda *refs: backward_all(seq, row, *refs),
        in_specs=[hbm, vmem, vmem] + [hbm] * 16 + [vmem],
        out_specs=[hbm, hbm, hbm] + [vmem] * 6,
        out_shape=[arr(layers, per, 3 * d)] + [arr(t, d, dtype=BF16)] * 2 + [arr(layers, per)] * 6,
        scratch_shapes=[
            buf(2, 2, steps, SUB, LANE, dtype=F32),
            buf(Z // 2, X, Y, 2, per, 3 * H),
            buf(2 * t, 3 * H),
            buf(2 * t, d),
            big, half, half, quarter, quarter, quarter, big, big,
            buf(2, 5, steps, SUB, WIDE, dtype=F32),
            buf(steps, SUB, 3 * WIDE, dtype=F32),
            buf(*chunk, dtype=F32), buf(2, 1, *chunk), buf(2, 1, *chunk),
            buf(3, Z, Y, per, HALF, dtype=F32), buf(4, X - 1, Z, Y, per, HALF),
            buf(6, X - 1, Z, Y, per, HALF),
            buf(3, Z, per, HALF, dtype=F32), buf(4, Y - 1, Z, per, HALF),
            buf(6, Y - 1, Z, per, HALF),
            buf(3, per, HALF, dtype=F32), buf(4, Z - 1, per, HALF), buf(6, Z - 1, per, HALF),
            buf(2, 4, per, HALF, dtype=F32),
            buf(2, 2, SUB, H, dtype=F32),
            buf(2, SUB, H, dtype=F32),
            buf(Z // 2, X, 2, 2, H, dtype=F32),
            st, st, buf(8, LANE, dtype=F32),
            buf(2, 6, SUB, H, dtype=F32),
            buf(2, SUB, H, dtype=F32),
            buf(Z, X, Y, 2, 16, LANE, dtype=F32),
            buf(1, Z, X, Y, 16, LANE, dtype=F32),
            buf(X - 1, Z, Y, 16, LANE, dtype=F32),
            buf(Y - 1, Z, 16, LANE, dtype=F32),
            buf(Z - 1, 16, LANE, dtype=F32),
            dma((4, count)), dma((6, count)),
            dma((2, 4, 3)),
            dma((6,)), dma((6,)),
            dma((Z // 2 * X,)), dma((Z // 2 * X,)),
            dma((count,)), dma((count,)),
            dma((9,)),
            dma((2, 5)),
            dma((2 * parts,)),
        ],
        compiler_params=pltpu.CompilerParams(
            collective_id=1, has_side_effects=True, vmem_limit_bytes=63 << 20
        ),
        name="backward_all",
    )(*given)


def body(tokens, resets, cotangent, weight, *rows):
    _, t, d = tokens.shape
    layers = weight.shape[0]
    steps = t // SUB
    seq, row = lax.axis_size("seq"), lax.axis_size("row")

    def restored(v):
        return v.reshape(steps, SUB, d).transpose(1, 0, 2).reshape(1, t, d)

    out = call_forward(
        seq, row, tokens[0], cotangent[0], resets, rows, weight
    )
    grad, input_grad, result, *vectors = call_backward(seq, row, t, d, out)
    return (restored(result), restored(input_grad), grad) + tuple(vectors)


def solution(mesh):
    tokens = P("row", "seq", None)
    rows = P(None, ("seq", "row"))
    weight = P(None, ("seq", "row"), None)
    return jax.shard_map(
        body,
        mesh=mesh,
        in_specs=(tokens, P("row", "seq"), tokens, weight) + (rows,) * 6,
        out_specs=(tokens, tokens, weight) + (rows,) * 6,
        check_vma=False,
    )
```

```python
import jax
import jax.numpy as jnp
from jax import lax
from jax.experimental import pallas as pl
from jax.experimental.pallas import tpu as pltpu
from jax.sharding import PartitionSpec as P

epsilon = 1e-05
SUB = 8
WIDE = 256
F32 = jnp.float32
BF16 = jnp.bfloat16
GAIN, SHIFT, FPEEP, RPEEP, FBIAS, RBIAS = range(6)


def both_sigmoids(z):
    tail = jnp.exp(-jnp.abs(z))
    big = 1.0 / (1.0 + tail)
    small = tail * big
    up = z >= 0
    return jnp.where(up, big, small), jnp.where(up, small, big)


def lanes(value, width):
    return jnp.concatenate([value] * (width // value.shape[-1]), axis=-1)


def arr(*shape, dtype=F32):
    return jax.ShapeDtypeStruct(shape, dtype)


MESH = pl.DeviceIdType.MESH
HALF = 384
LANE = 128


class Place:
    def __init__(self, seq, row):
        self.Y = row // 2
        self.X = self.Y
        self.Z = seq // self.X
        self.C = 2
        self.sizes = dict(z=self.Z, x=self.X, y=self.Y, c=self.C)
        s, r = lax.axis_index("seq"), lax.axis_index("row")
        self.at = dict(z=s // self.X, x=s % self.X, y=r // 2, c=r % 2)
        self.zl = lax.rem(self.at["z"], 2)

    def moved(self, axis, k):
        size = self.sizes[axis]
        return dict(self.at, **{axis: lax.rem(self.at[axis] + k, size)})

    def device(self, at):
        return {"seq": at["z"] * self.X + at["x"], "row": at["y"] * 2 + at["c"]}

    def others(self, axis):
        return range(1, self.sizes[axis])

    def barrier(self, seq):
        sem = pltpu.get_barrier_semaphore()
        count = 0
        s, r = lax.axis_index("seq"), lax.axis_index("row")
        for k in range(1, seq):
            pl.semaphore_signal(
                sem, inc=1, device_id={"seq": lax.rem(s + k, seq), "row": r}, device_id_type=MESH
            )
            count += 1
        for axis in ("y", "c"):
            for k in self.others(axis):
                pl.semaphore_signal(
                    sem, inc=1, device_id=self.device(self.moved(axis, k)), device_id_type=MESH
                )
                count += 1
        pl.semaphore_wait(sem, count)


def remote(src, dst, send, recv, to):
    return pltpu.make_async_remote_copy(
        src_ref=src, dst_ref=dst, send_sem=send, recv_sem=recv, device_id=to, device_id_type=MESH
    )


def total_of(scale, state, backward):
    order = range(SUB - 1, -1, -1) if backward else range(SUB)
    whole_scale, whole_state = None, None
    for k in order:
        a, b = scale[k : k + 1], state[k : k + 1]
        if whole_scale is None:
            whole_scale, whole_state = a, b
        else:
            whole_scale, whole_state = a * whole_scale, a * whole_state + b
    return jnp.concatenate([whole_scale, whole_state], axis=0)


class Gather:
    def __init__(self, pos, parts, w_own, w_all, snd, rcv, loc):
        self.pos, self.parts = pos, parts
        self.w_own, self.w_all, self.snd, self.rcv, self.loc = w_own, w_all, snd, rcv, loc
        z, x, y = pos.Z - 1, pos.X - 1, pos.Y - 1
        self.base = (0, z, z + max(x, y), z + 2 * max(x, y))

    def axis(self, stage, h):
        return ("z", ("y", "x")[h], ("x", "y")[h], "c")[stage]

    def region(self, ref, head, stage, h, who):
        every = slice(None)
        spot = [who["z"], who["x"], who["y"], who["c"]]
        if stage >= 1:
            spot[0] = every
        if stage >= 2:
            spot[2 if h == 0 else 1] = every
        if stage >= 3:
            spot[1] = spot[2] = every
        return ref.at[head + tuple(spot)]

    def copies(self, g, stage, h, arriving):
        pos, axis = self.pos, self.axis(stage, h)
        l, m = g // self.parts, lax.rem(g, self.parts)
        size = pos.sizes[axis]
        for k in pos.others(axis):
            sem = self.base[stage] + k - 1
            to = pos.moved(axis, k)
            who = pos.moved(axis, size - k) if arriving else pos.at
            mine = self.region(self.w_all, (l, m, h), stage, h, who)
            src = mine
            if stage == 0 and not arriving:
                src = self.w_own.at[l, lax.rem(to["z"], 2), m, h]
            yield remote(src, mine, self.snd.at[h, g, sem], self.rcv.at[h, g, sem], pos.device(to))

    def local(self, g, h):
        at = self.pos.at
        l, m = g // self.parts, lax.rem(g, self.parts)
        return pltpu.make_async_copy(
            self.w_own.at[l, self.pos.zl, m, h],
            self.w_all.at[l, m, h, at["z"], at["x"], at["y"], at["c"]],
            self.loc.at[h, g],
        )

    def begin(self, g):
        for h in range(2):
            self.local(g, h).start()
            for copy in self.copies(g, 0, h, False):
                copy.start()

    def advance(self, g, stage):
        for h in range(2):
            if stage == 1:
                self.local(g, h).wait()
            for copy in self.copies(g, stage - 1, h, True):
                copy.wait_recv()
            if stage < 4:
                for copy in self.copies(g, stage, h, False):
                    copy.start()

    def turn(self, i):
        total = 2 * self.parts

        @pl.when(i < 2)
        def _():
            self.begin(i + 4)

        for stage in range(1, 5):
            g = i - (stage - 1)

            @pl.when((g >= 0) & (g < total))
            def _():
                self.advance(g, stage)

    def finish(self):
        def one(g, _):
            for h in range(2):
                for stage in range(4):
                    for copy in self.copies(g, stage, h, False):
                        copy.wait_send()
            return 0

        lax.fori_loop(0, 2 * self.parts, one, 0)


class Chain:
    def __init__(self, pos, table, snd, rcv):
        self.pos, self.table, self.snd, self.rcv = pos, table, snd, rcv

    def run(self, ends, first, backward):
        pos, table = self.pos, self.table
        zh, x = pos.at["z"] // 2, pos.at["x"]
        r = lax.axis_index("row")
        for b in range(2):
            table[zh, x, b] = total_of(ends[b, 0], ends[b, 1], backward)
        moves = [(i, j) for i in range(pos.Z // 2) for j in range(pos.X) if i or j]

        def copy(k, sign):
            i, j = moves[k]
            there = lax.rem(zh + i, pos.Z // 2), lax.rem(x + j, pos.X)
            back = lax.rem(zh + pos.Z // 2 - i, pos.Z // 2), lax.rem(x + pos.X - j, pos.X)
            spot = (zh, x) if sign > 0 else back
            to = {"seq": (2 * there[0] + pos.zl) * pos.X + there[1], "row": r}
            return remote(table.at[spot], table.at[spot], self.snd.at[k], self.rcv.at[k], to)

        for k in range(len(moves)):
            copy(k, 1).start()
        for k in range(len(moves)):
            copy(k, -1).wait_recv()
        for k in range(len(moves)):
            copy(k, 1).wait_send()
        blocks = [(i, b, j) for i in range(pos.Z // 2) for b in range(2) for j in range(pos.X)]
        if backward:
            blocks = blocks[::-1]
        value = jnp.zeros_like(table[0, 0, 0, 0:1])
        mine = [value, value]
        for i, b, j in blocks:
            here = (i == zh) & (j == x)
            mine[b] = jnp.where(here, value, mine[b])
            value = table[i, j, b, 0:1] * value + table[i, j, b, 1:2]
        for b in range(2):
            value = mine[b]
            for k in range(SUB - 1, -1, -1) if backward else range(SUB):
                first[b, k : k + 1] = value
                value = ends[b, 0, k : k + 1] * value + ends[b, 1, k : k + 1]


def diagonal():
    return lax.broadcasted_iota(jnp.int32, (LANE, LANE), 0) == lax.broadcasted_iota(
        jnp.int32, (LANE, LANE), 1
    )


def to_row(column):
    spread = jnp.broadcast_to(column, (LANE, LANE))
    return jnp.sum(jnp.where(diagonal(), spread, 0.0), axis=0, keepdims=True)


def to_column(line):
    spread = jnp.broadcast_to(line, (LANE, LANE))
    return jnp.sum(jnp.where(diagonal(), spread, 0.0), axis=1, keepdims=True)


def spread_rows(column):
    return jnp.broadcast_to(column, (LANE, LANE)).reshape(LANE // SUB, SUB, LANE)


def lane_tile(m, width):
    return pl.ds(pl.multiple_of(m * width, width), width)


def forward_all(
    seq, row, tok, cot, resets, gain_in, shift_in, fpeep_in, rpeep_in, fbias_in, rbias_in, weight,
    w_all, vec, keep, stats, f0, g0, cand0, p0, r0, u0, low0, low1, u1, dhr1, dn1, du1, res1, resx, tokx0,
    sums, nat, w_nat, w_own, tokbuf, cotbuf, keepc, vall, u, np_, f, g, cand, rpre, low, wbuf, proj, du, resbuf, top_of, ends,
    first, tables, st_own, st_got, st_fin,
    gsnd, grcv, gloc, vsnd, vrcv, wsem, psnd, prcv, csnd, crcv, outs,
):
    pos = Place(seq, row)
    at, zl = pos.at, pos.zl
    z, x, y, c = (at[k] for k in "zxyc")
    _, t, d = tokbuf.shape
    steps, H = u.shape[1], u.shape[3]
    parts = w_own.shape[2]
    partner = pos.device(dict(at, z=z + 1 - 2 * zl))
    own = pl.ds(pl.multiple_of(zl * H, H), H)
    other = pl.ds(pl.multiple_of((1 - zl) * H, H), H)
    rows_of = lambda b: pl.ds(pl.multiple_of(b * t, t), t)
    get_weight = pltpu.make_async_copy(weight, w_nat, outs.at[10])
    get_weight.start()
    pos.barrier(seq)
    get_weight.wait()
    for l in range(2):
        for p in range(2):
            for m in range(parts):
                for h in range(2):
                    for e in range(3):
                        start = e * d + p * H + (2 * m + h) * LANE
                        w_own[l, p, m, h, :, e * LANE : (e + 1) * LANE] = w_nat[
                            l, :, start : start + LANE
                        ]

    gather = Gather(pos, parts, w_own, w_all, gsnd, grcv, gloc)
    chains = [Chain(pos, tables.at[k], csnd.at[k], crcv.at[k]) for k in range(3)]

    def pair(k, src, dst):
        return remote(src, dst, psnd.at[k], prcv.at[k], partner)

    def tokens(b):
        return pair(0, tokbuf.at[b], tokbuf.at[b])

    def cotangents(b):
        return pair(1, du.at[t : 2 * t, d : d + H], cotbuf.at[b])

    def permute(src, store):
        group = nat.shape[0]
        for q in range(d // LANE // group):
            for k in range(group):
                at_lanes = (q * group + k) * LANE
                nat[k] = src[:, at_lanes : at_lanes + LANE].astype(F32)

            def one(k, _):
                rows = [
                    jnp.concatenate(
                        [nat[e, pl.ds(2 * k + j, SUB, stride=steps), :] for e in range(group)], axis=-1
                    )
                    for j in range(2)
                ]
                spot = pl.ds(pl.multiple_of(2 * SUB * k, 2 * SUB), 2 * SUB)
                store(spot, q, jnp.concatenate(rows, axis=0).astype(BF16))
                return 0

            lax.fori_loop(0, steps // 2, one, 0, unroll=4)

    def keeps(b):
        return pair(2, keepc.at[b], keepc.at[b])

    def statistics(b, to):
        return pair(3 + b, st_own.at[b], to.at[b])

    def lows(b, cols):
        return pair(5 + b, low.at[rows_of(b), cols], low.at[rows_of(b), cols])

    def results():
        return pair(7, resbuf.at[1 - zl, pl.ds(0, t // 2)], resx)

    def vcopies(stage, arriving):
        axis = gather.axis(stage, 0)
        size = pos.sizes[axis]
        for k in pos.others(axis):
            sem = gather.base[stage] + k - 1
            to = pos.moved(axis, k)
            who = pos.moved(axis, size - k) if arriving else at
            mine = gather.region(vall, (), stage, 0, who)
            yield remote(mine, mine, vsnd.at[sem], vrcv.at[sem], pos.device(to))

    def vadvance(stage):
        for copy in vcopies(stage - 1, True):
            copy.wait_recv()
        if stage < 4:
            for copy in vcopies(stage, False):
                copy.start()

    own_tokens = pltpu.make_async_copy(tok, du.at[0:t, 0:d], outs.at[0])
    own_cot = pltpu.make_async_copy(cot, du.at[t : 2 * t, 0:d], outs.at[1])
    given = [
        v[...].astype(F32) for v in (gain_in, shift_in, fpeep_in, rpeep_in, fbias_in, rbias_in)
    ]
    per = given[0].shape[-1]
    blank = jnp.zeros((2, per), F32)
    given = jnp.concatenate(
        [v[l : l + 1] for l in range(2) for v in given + [blank] * 2], axis=0
    )
    given = jnp.concatenate([given, jnp.zeros((16, LANE - per), F32)], axis=-1)
    vall[z, x, y, c] = given.astype(BF16)
    kept = 1.0 - resets[...].astype(F32)
    kept = jnp.concatenate([kept[:, k * steps : (k + 1) * steps] for k in range(SUB)], axis=0)
    keepc[zl] = jnp.concatenate([kept, jnp.zeros((SUB, LANE - steps), F32)], axis=-1)
    own_tokens.start()
    own_cot.start()
    for copy in vcopies(0, False):
        copy.start()
    keeps(zl).start()
    gather.begin(0)
    gather.begin(1)
    gather.begin(2)
    gather.begin(3)
    vadvance(1)
    own_tokens.wait()
    wide = nat.shape[0] * LANE

    def store_tokens(rows, q, v):
        tokbuf[zl, rows, q * wide : (q + 1) * wide] = v

    permute(du.at[0:t, 0:d], store_tokens)
    gather.turn(0)
    vadvance(2)
    vadvance(3)
    gather.turn(1)
    tokens(zl).start()
    vadvance(4)

    per = d // (seq * row)
    for q in range(d // LANE):
        pieces = []
        for e in range(LANE // per):
            i = q * (LANE // per) + e
            spot = (i // (2 * pos.Y * pos.X), i // (2 * pos.Y) % pos.X, i // 2 % pos.Y, i % 2)
            pieces.append(vall[spot][:, :per].astype(F32))
        value = jnp.concatenate(pieces, axis=-1)
        for l in range(2):
            vec[l, :, q * LANE : (q + 1) * LANE] = value[l * 8 : l * 8 + 8]
    keeps(1 - zl).wait_recv()
    for b in range(2):
        kept = keepc[b]
        for i in range(steps):
            keep[b, i] = jnp.broadcast_to(kept[:, i : i + 1], (SUB, LANE))

    def norm0(b):
        piece = 8

        def one(k, _):
            rows = pl.ds(pl.multiple_of(k * piece * SUB, piece * SUB), piece * SUB)
            spot = pl.ds(k * piece, piece)
            v = tokbuf[b, rows, :].astype(F32)
            mu = jnp.mean(v, axis=-1, keepdims=True)
            v = v - mu
            rstd = lax.rsqrt(jnp.mean(v * v, axis=-1, keepdims=True) + epsilon)
            v = v * rstd * vec[0, GAIN : GAIN + 1, :] + vec[0, SHIFT : SHIFT + 1, :]
            at_rows = pl.ds(pl.multiple_of(b * t + k * piece * SUB, piece * SUB), piece * SUB)
            low[at_rows, :] = v.astype(BF16)
            u[b, spot] = tokbuf[b, rows, own].astype(F32).reshape(piece, SUB, H)
            stats[0, 0, b, spot] = jnp.broadcast_to(mu, (piece * SUB, LANE)).reshape(piece, SUB, LANE)
            stats[0, 1, b, spot] = jnp.broadcast_to(rstd, (piece * SUB, LANE)).reshape(
                piece, SUB, LANE
            )
            return 0

        lax.fori_loop(0, steps // piece, one, 0)

    def load(l, m, h):
        slot = lax.rem(m, 2)
        return pltpu.make_async_copy(
            w_all.at[l, m, h],
            wbuf.at[slot, :, :, :, :, :, pl.ds(h * HALF, HALF)],
            wsem.at[slot, h],
        )

    def start_load(l, m):
        for h in range(2):
            load(l, m, h).start()

    def end_load(l, m):
        for h in range(2):
            load(l, m, h).wait()

    def gates(l, m, b):
        w = wbuf[lax.rem(m, 2)].reshape(d, 2 * HALF)
        v = jnp.dot(low[rows_of(b), :], w, preferred_element_type=F32)
        proj[...] = v.reshape(steps, SUB, 2 * HALF)
        cols = lane_tile(m, 2 * LANE)
        wide = pl.ds(pl.multiple_of(zl * H + m * 2 * LANE, 2 * LANE), 2 * LANE)
        peep, bias, rbias, gain, shift = (
            jnp.broadcast_to(vec[l, k : k + 1, wide], (SUB, 2 * LANE))
            for k in (FPEEP, FBIAS, RBIAS, GAIN, SHIFT)
        )

        def both(i, off):
            return jnp.concatenate(
                [proj[i, :, h * HALF + off : h * HALF + off + LANE] for h in range(2)], axis=-1
            )

        def one(i, carry):
            scale, state = carry
            cd = both(i, 0)
            n = (u[b, i, :, cols] - lanes(stats[l, 0, b, i], 2 * LANE)) * lanes(
                stats[l, 1, b, i], 2 * LANE
            ) * gain + shift
            up, down = both_sigmoids(both(i, LANE) + peep * n + bias)
            f[b, i, :, cols] = up
            g[b, i, :, cols] = down
            cand[b, i, :, cols] = cd
            rpre[b, i, :, cols] = both(i, 2 * LANE) + rbias
            a = up * lanes(keep[b, i], 2 * LANE)
            return scale * a, a * state + down * cd

        start = jnp.ones((SUB, 2 * LANE), F32), jnp.zeros((SUB, 2 * LANE), F32)
        scale, state = lax.fori_loop(0, steps, one, start, unroll=16)
        ends[b, 0, :, cols] = scale
        ends[b, 1, :, cols] = state

    def stash(k, src, dst):
        return pltpu.make_async_copy(src, dst, outs.at[k])

    norm0(zl)
    own_cot.wait()

    def store_cot(rows, q, v):
        side, at_lanes = q * wide // H, q * wide % H

        @pl.when(zl == side)
        def _():
            cotbuf[zl, rows, at_lanes : at_lanes + wide] = v

        @pl.when(zl != side)
        def _():
            to = pl.ds(pl.multiple_of(rows.start + t, 2 * SUB), 2 * SUB)
            du[to, d + at_lanes : d + at_lanes + wide] = v

    def turn(i, _):
        gather.turn(i)

        @pl.when(i == 3)
        def _():
            permute(du.at[t : 2 * t, 0:d], store_cot)

        @pl.when(i >= 3)
        def _():
            @pl.when(i < parts + 1)
            def _():
                start_load(0, i - 3)

        @pl.when((i >= 4) & (i < parts + 2))
        def _():
            end_load(0, i - 4)
            gates(0, i - 4, zl)

        @pl.when(i == parts + 1)
        def _():
            tokens(1 - zl).wait_recv()
            for k in range(6, 2 * parts):
                gather.begin(k)
            norm0(1 - zl)

        @pl.when(i > parts)
        def _():
            last = i == parts + 2

            def job(k, _):
                m = jnp.where(last, parts - 2 + k // 2, k)
                b = jnp.where(last & (lax.rem(k, 2) == 0), zl, 1 - zl)

                @pl.when(last & (lax.rem(k, 2) == 0))
                def _():
                    end_load(0, m)

                gates(0, m, b)

                @pl.when(jnp.logical_not(last) & (k == 0))
                def _():
                    start_load(0, parts - 2)

                return 0

            @pl.when(last)
            def _():
                start_load(0, parts - 1)

            lax.fori_loop(0, jnp.where(last, 4, parts - 2), job, 0)

        return 0

    lax.fori_loop(2, parts + 3, turn, 0)
    keep_tokx = stash(0, tokbuf.at[zl, :, other], tokx0)
    keep_tokx.start()
    keep_u0, keep_low0 = stash(2, u, u0), stash(3, low, low0)
    gates0 = [stash(4, f, f0), stash(5, g, g0), stash(6, cand, cand0)]
    for copy in [keep_u0, keep_low0] + gates0:
        copy.start()
    chains[0].run(ends, first, False)
    gather.turn(parts + 3)
    keep_u0.wait()
    keep_low0.wait()

    def states0(b):
        def tile(m, _):
            cols = lane_tile(m, 2 * LANE)
            wide = pl.ds(pl.multiple_of(zl * H + m * 2 * LANE, 2 * LANE), 2 * LANE)
            peep = jnp.broadcast_to(vec[0, RPEEP : RPEEP + 1, wide], (SUB, 2 * LANE))

            def one(i, cell):
                before = lanes(keep[b, i], 2 * LANE) * cell
                cell = f[b, i, :, cols] * before + g[b, i, :, cols] * cand[b, i, :, cols]
                gate = jax.nn.sigmoid(rpre[b, i, :, cols] + peep * before)
                np_[b, i, :, cols] = before
                rpre[b, i, :, cols] = gate
                u[b, i, :, cols] = gate * cell + (1.0 - gate) * u[b, i, :, cols]
                return cell

            lax.fori_loop(0, steps, one, first[b, :, cols], unroll=16)
            return 0

        lax.fori_loop(0, parts, tile, 0)

    def local_stats(b):
        def one(q, _):
            v = u[b, pl.ds(q * (LANE // SUB), LANE // SUB)].reshape(LANE, H)
            mu = jnp.mean(v, axis=-1, keepdims=True)
            v = v - mu
            square = jnp.sum(v * v, axis=-1, keepdims=True)
            st_own[b, pl.ds(q, 1), :] = to_row(mu)
            st_own[b, pl.ds(q + t // LANE, 1), :] = to_row(square)
            return 0

        lax.fori_loop(0, t // LANE, one, 0)
        statistics(b, st_got).start()

    def norm1(b):
        half = t // LANE
        statistics(b, st_got).wait_recv()
        m0, m1 = st_own[b, :half], st_got[b, :half]
        gap = m0 - m1
        square = st_own[b, half:] + st_got[b, half:] + gap * gap * (H / 2)
        st_fin[b, :half] = (m0 + m1) * 0.5
        st_fin[b, half:] = lax.rsqrt(square / (2 * H) + epsilon)

        def one(q, _):
            spot = pl.ds(q * (LANE // SUB), LANE // SUB)
            mu = to_column(st_fin[b, pl.ds(q, 1), :])
            rstd = to_column(st_fin[b, pl.ds(q + half, 1), :])
            v = u[b, spot].reshape(LANE, H)
            v = (v - mu) * rstd * vec[1, GAIN : GAIN + 1, own] + vec[1, SHIFT : SHIFT + 1, own]
            low[pl.ds(pl.multiple_of(b * t + q * LANE, LANE), LANE), own] = v.astype(BF16)
            stats[1, 0, b, spot] = spread_rows(mu)
            stats[1, 1, b, spot] = spread_rows(rstd)
            return 0

        lax.fori_loop(0, half, one, 0)
        lows(b, own).start()

    states0(0)
    local_stats(0)
    states0(1)
    keep_p0, keep_r0 = stash(7, np_, p0), stash(8, rpre, r0)
    keep_p0.start()
    keep_r0.start()
    norm1(0)
    local_stats(1)
    gather.turn(parts + 4)
    norm1(1)
    start_load(1, 0)
    keep_u1 = stash(2, u, u1)
    keep_u1.start()
    for copy in gates0 + [keep_r0]:
        copy.wait()

    def job1(k, _):
        b, m = k // parts, lax.rem(k, parts)

        @pl.when(m == 0)
        def _():
            lows(b, other).wait_recv()

        @pl.when(k == parts)
        def _():
            cotangents(zl).start()

        @pl.when((k == 1) | (k == 2))
        def _():
            gather.turn(parts + 4 + k)

        @pl.when(k + 1 < 2 * parts)
        def _():
            start_load(1, lax.rem(k + 1, parts))

        end_load(1, m)
        gates(1, m, b)
        return 0

    lax.fori_loop(0, 2 * parts, job1, 0)
    keep_low1 = stash(3, low, low1)
    keep_low1.start()
    chains[1].run(ends, first, False)
    keep_p0.wait()

    def step_back(b, i, cols, top, peep):
        before, gate, up = np_[b, i, :, cols], rpre[b, i, :, cols], f[b, i, :, cols]
        cell = up * before + g[b, i, :, cols] * cand[b, i, :, cols]
        dz_r = top * (cell - u[b, i, :, cols]) * gate * (1.0 - gate)
        direct = top * gate
        kept = lanes(keep[b, i], 2 * LANE)
        decay = up * kept
        return before, gate, up, dz_r, direct, decay, kept * peep * dz_r + decay * direct

    def turn_round(b):
        def tile(m, _):
            cols = lane_tile(m, 2 * LANE)
            wide = pl.ds(pl.multiple_of(zl * H + m * 2 * LANE, 2 * LANE), 2 * LANE)
            peep = jnp.broadcast_to(vec[1, RPEEP : RPEEP + 1, wide], (SUB, 2 * LANE))
            top = cotbuf[b, :, cols].astype(F32).reshape(steps, SUB, 2 * LANE)
            proj[:, :, 2 * LANE : 4 * LANE] = top

            def one(i, cell):
                before = lanes(keep[b, i], 2 * LANE) * cell
                cell = f[b, i, :, cols] * before + g[b, i, :, cols] * cand[b, i, :, cols]
                gate = jax.nn.sigmoid(rpre[b, i, :, cols] + peep * before)
                np_[b, i, :, cols] = before
                rpre[b, i, :, cols] = gate
                proj[i, :, : 2 * LANE] = gate * cell + (1.0 - gate) * u[b, i, :, cols]
                return cell

            lax.fori_loop(0, steps, one, first[b, :, cols], unroll=16)
            v = proj[:, :, : 2 * LANE].reshape(t, 2 * LANE)
            resbuf[b, :, cols] = v.astype(BF16)

            def back(k, carry):
                scale, q = carry
                i = steps - 1 - k
                _, _, _, _, _, decay, term = step_back(
                    b, i, cols, proj[i, :, 2 * LANE : 4 * LANE], peep
                )
                return scale * decay, decay * q + term

            start = jnp.ones((SUB, 2 * LANE), F32), jnp.zeros((SUB, 2 * LANE), F32)
            scale, q = lax.fori_loop(0, steps, back, start, unroll=16)
            ends[b, 0, :, cols] = scale
            ends[b, 1, :, cols] = q
            return 0

        lax.fori_loop(0, parts, tile, 0)

    def blocks(k, _):
        @pl.when(k == 1)
        def _():
            cotangents(1 - zl).wait_recv()

        turn_round(jnp.where(k == 0, zl, 1 - zl))
        return 0

    lax.fori_loop(0, 2, blocks, 0)
    results().start()
    keep_res = stash(9, resbuf, res1)
    keep_res.start()
    chains[2].run(ends, first, True)

    def down(b):
        def tile(m, _):
            cols = lane_tile(m, 2 * LANE)
            wide = pl.ds(pl.multiple_of(zl * H + m * 2 * LANE, 2 * LANE), 2 * LANE)
            fpeep, rpeep, gain, shift = (
                jnp.broadcast_to(vec[1, k : k + 1, wide], (SUB, 2 * LANE))
                for k in (FPEEP, RPEEP, GAIN, SHIFT)
            )

            def one(k, carry):
                q, s0, s1, s2, s3 = carry
                i = steps - 1 - k
                top = top_of[i]
                before, gate, up, dz_r, direct, decay, term = step_back(b, i, cols, top, rpeep)
                e = direct + q
                low_f = g[b, i, :, cols]
                dz_f = e * (up * low_f) * (before - cand[b, i, :, cols])
                n = (u[b, i, :, cols] - lanes(stats[1, 0, b, i], 2 * LANE)) * lanes(
                    stats[1, 1, b, i], 2 * LANE
                ) * gain + shift
                proj[i, :, : 2 * LANE] = e * low_f
                proj[i, :, 2 * LANE : 4 * LANE] = dz_f
                proj[i, :, 4 * LANE :] = dz_r
                cand[b, i, :, cols] = dz_f * fpeep
                rpre[b, i, :, cols] = top * (1.0 - gate)
                return (
                    decay * q + term,
                    s0 + dz_f * n,
                    s1 + dz_r * before,
                    s2 + dz_f,
                    s3 + dz_r,
                )

            top_of[...] = cotbuf[b, :, cols].astype(F32).reshape(steps, SUB, 2 * LANE)
            zero = jnp.zeros((SUB, 2 * LANE), F32)
            carry = lax.fori_loop(0, steps, one, (first[b, :, cols], zero, zero, zero, zero), unroll=16)
            for k in range(4):
                sums[b, k, :, cols] = carry[k + 1]
            for h in range(2):
                for k in range(3):
                    v = proj[:, :, k * 2 * LANE + h * LANE : k * 2 * LANE + (h + 1) * LANE]
                    to = pl.ds(pl.multiple_of((2 * m + h) * HALF + k * LANE, LANE), LANE)
                    du[rows_of(b), to] = v.reshape(t, LANE).astype(BF16)
            return 0

        lax.fori_loop(0, parts, tile, 0)

    keep_low1.wait()
    cotangents(zl).wait_send()

    def last(b):
        yield stash(3, du.at[rows_of(b)], du1.at[rows_of(b)])
        yield stash(4, cand.at[b], dn1.at[b])
        yield stash(5, rpre.at[b], dhr1.at[b])

    down(0)
    for copy in last(0):
        copy.start()
    down(1)
    for copy in last(0):
        copy.wait()
    for copy in last(1):
        copy.start()
    gather.finish()
    for stage in range(4):
        for copy in vcopies(stage, False):
            copy.wait_send()
    for copy in list(last(1)) + [keep_u1, keep_res, keep_tokx]:
        copy.wait()
    results().wait_recv()
    results().wait_send()
    tokens(zl).wait_send()
    keeps(zl).wait_send()
    for b in range(2):
        statistics(b, st_got).wait_send()
        lows(b, own).wait_send()


def call_forward(seq, row, tok, cot, keep, rows, weight):
    t, d = tok.shape
    layers, per, _ = weight.shape
    Y = row // 2
    X = Y
    Z = seq // X
    H = d // 2
    parts = H // WIDE
    steps = t // SUB
    act, stat = arr(2, steps, SUB, H), arr(2, steps, SUB, LANE)
    half = arr(2 * t, d, dtype=BF16)
    vmem = pl.BlockSpec(memory_space=pltpu.VMEM)
    hbm = pl.BlockSpec(memory_space=pl.ANY)
    count = Z + 2 * X - 2
    dma = pltpu.SemaphoreType.DMA
    big = pltpu.VMEM((2, steps, SUB, H), F32)
    st = pltpu.VMEM((2, 8, LANE), F32)
    return pl.pallas_call(
        lambda *refs: forward_all(seq, row, *refs),
        in_specs=[hbm, hbm] + [vmem] * (1 + len(rows)) + [hbm],
        out_specs=[hbm, vmem, vmem, vmem] + [hbm] * 15 + [vmem],
        out_shape=[
            arr(layers, parts, 2, Z, X, Y, 2, per, HALF, dtype=BF16),
            arr(2, 8, d),
            stat,
            arr(2, 2, 2, steps, SUB, LANE),
        ]
        + [act] * 6
        + [half, half, act, act, act, arr(2 * t, 3 * H, dtype=BF16), arr(2, t, H, dtype=BF16), arr(t // 2, H, dtype=BF16), arr(t, H, dtype=BF16)]
        + [arr(2, 4, SUB, H)],
        scratch_shapes=[
            pltpu.VMEM((4, t, LANE), F32),
            pltpu.VMEM((layers, per, 3 * d), BF16),
            pltpu.VMEM((layers, 2, parts, 2, per, HALF), BF16),
            pltpu.VMEM((2, t, d), BF16),
            pltpu.VMEM((2, t, H), BF16),
            pltpu.VMEM((2, 8, LANE), F32),
            pltpu.VMEM((Z, X, Y, 2, 16, LANE), BF16),
            big, big, big, big, big, big,
            pltpu.VMEM((2 * t, d), BF16),
            pltpu.VMEM((2, Z, X, Y, 2, per, 2 * HALF), BF16),
            pltpu.VMEM((steps, SUB, 2 * HALF), F32),
            pltpu.VMEM((2 * t, 3 * H), BF16),
            pltpu.VMEM((2, t, H), BF16),
            pltpu.VMEM((steps, SUB, 2 * LANE), F32),
            pltpu.VMEM((2, 2, SUB, H), F32),
            pltpu.VMEM((2, SUB, H), F32),
            pltpu.VMEM((3, Z // 2, X, 2, 2, H), F32),
            st, st, st,
            dma((2, 2 * parts, count)),
            dma((2, 2 * parts, count)),
            dma((2, 2 * parts)),
            dma((count,)),
            dma((count,)),
            dma((2, 2)),
            dma((8,)),
            dma((8,)),
            dma((3, Z // 2 * X)),
            dma((3, Z // 2 * X)),
            dma((11,)),
        ],
        compiler_params=pltpu.CompilerParams(
            collective_id=0, has_side_effects=True, vmem_limit_bytes=62 << 20
        ),
        name="forward_all",
    )(tok, cot, keep, *rows, weight)


def wrap(a, b):
    return a % b if isinstance(a, int) else lax.rem(a, b)


class Scatter:
    lag = (0, 1, 3, 5, 7)
    sends = (2, 4, 4, 4)
    slots = (2, 6, 6, 6)
    kept = (1, 3, 3, 3)

    def __init__(self, pos, count, low, du, out, keep, send, recv, done, snd, rcv, outs):
        self.pos, self.count, self.low, self.du, self.out = pos, count, low, du, out
        self.keep, self.send, self.recv, self.done = keep, send, recv, done
        self.snd, self.rcv, self.outs = snd, rcv, outs
        n = pos.X - 1
        self.base = (0, 1, 1 + n, 1 + 2 * n)

    def axis(self, stage, h):
        return ("c", ("x", "y")[h], ("y", "x")[h], "z")[stage]

    def copy(self, g, stage, h, k):
        mine, slot = wrap(g, self.sends[stage]), wrap(g, self.slots[stage])
        sem = self.base[stage] + k - 1
        to = self.pos.device(self.pos.moved(self.axis(stage, h), k))
        return remote(
            self.send[stage].at[mine, k - 1], self.recv[stage].at[slot, k - 1],
            self.snd.at[mine, sem], self.rcv.at[slot, sem], to,
        )

    def each(self, stage, h):
        return self.pos.others(self.axis(stage, h))

    def ready(self, g, stage, h):
        def wait():
            for k in self.each(stage, h):
                self.copy(g, stage, h, k).wait_send()

        if isinstance(g, int):
            if g >= self.sends[stage]:
                wait()
        else:
            pl.when(g >= self.sends[stage])(wait)

    def start(self, g, stage, h):
        for k in self.each(stage, h):
            self.copy(g, stage, h, k).start()

    def arrive(self, g, stage, h):
        for k in self.each(stage, h):
            self.copy(g, stage, h, k).wait_recv()

    def stage0(self, g, h):
        pos, low, t = self.pos, self.low, self.low.shape[0]
        rows = low.shape[1] // pos.Z
        slot = wrap(g, 2)
        q = wrap(g, self.count)
        cols = pl.ds(q * HALF if isinstance(q, int) else pl.multiple_of(q * HALF, LANE), HALF)
        self.ready(g, 0, h)
        first = pos.at["c"] == 0

        def one(z, _):
            lhs = low[:, pl.ds(pl.multiple_of(z * rows, LANE), rows)]
            v = lax.dot_general(
                lhs, self.du[:, cols], (((0,), (0,)), ((), ())), preferred_element_type=F32
            )
            v = v.reshape(pos.X, pos.Y, 2, -1, HALF)
            even, odd = v[:, :, 0], v[:, :, 1]
            self.keep[0][z] = jnp.where(first, even, odd)
            self.send[0][slot, 0, z] = jnp.where(first, odd, even).astype(BF16)
            return 0

        lax.fori_loop(0, pos.Z, one, 0)
        self.start(g, 0, h)

    def stage1(self, g, h):
        pos, axis = self.pos, self.axis(1, h)
        slot, got, mine = wrap(g, 4), wrap(g, 2), wrap(g, 3)
        self.arrive(g, 0, h)
        self.ready(g, 1, h)
        for k in range(pos.sizes[axis]):
            p = pos.moved(axis, k)[axis]

            def one(z, _):
                where = (z, p) if h == 0 else (z, slice(None), p)
                v = self.keep[0][where] + self.recv[0][(got, 0) + where].astype(F32)
                if k == 0:
                    self.keep[1][mine, z] = v
                else:
                    self.send[1][slot, k - 1, z] = v.astype(BF16)
                return 0

            lax.fori_loop(0, pos.Z, one, 0)
        self.start(g, 1, h)

    def stage2(self, g, h):
        pos, axis = self.pos, self.axis(2, h)
        slot, got, mine = wrap(g, 4), wrap(g, 6), wrap(g, 3)
        self.arrive(g, 1, h)
        self.ready(g, 2, h)
        for k in range(pos.sizes[axis]):
            p = pos.moved(axis, k)[axis]
            v = self.keep[1][mine, :, p]
            for e in self.each(1, h):
                v = v + self.recv[1][got, e - 1, :, p].astype(F32)
            if k == 0:
                self.keep[2][mine] = v
            else:
                self.send[2][slot, k - 1] = v.astype(BF16)
        self.start(g, 2, h)

    def stage3(self, g, h):
        pos = self.pos
        slot, got, mine = wrap(g, 4), wrap(g, 6), wrap(g, 3)
        self.arrive(g, 2, h)
        self.ready(g, 3, h)
        for k in range(pos.Z):
            p = pos.moved("z", k)["z"]
            v = self.keep[2][mine, p]
            for e in self.each(2, h):
                v = v + self.recv[2][got, e - 1, p].astype(F32)
            if k == 0:
                self.keep[3][mine] = v
            else:
                self.send[3][slot, k - 1] = v.astype(BF16)
        self.start(g, 3, h)

    def result(self, l, q, half, e):
        d = self.out.shape[-1] // 3
        at = e * d + half * (d // 2) + q * LANE
        return pltpu.make_async_copy(
            self.done.at[half, wrap(q, 4), :, e * LANE : (e + 1) * LANE],
            self.out.at[l, :, pl.ds(pl.multiple_of(at, LANE), LANE)],
            self.outs.at[half, wrap(q, 4), e],
        )

    def stage4(self, g, h, l):
        pos = self.pos
        got, mine, q = wrap(g, 6), wrap(g, 3), wrap(g, self.count)
        self.arrive(g, 3, h)
        own, other = self.keep[3][mine], None
        for k in range(1, pos.Z):
            v = self.recv[3][got, k - 1].astype(F32)
            if k % 2 == 0:
                own = own + v
            else:
                other = v if other is None else other + v
        if isinstance(q, int):
            if q >= 4:
                self.stored(l, q - 4)
        else:
            pl.when(q >= 4)(lambda: self.stored(l, q - 4))
        self.done[pos.zl, wrap(q, 4)] = own
        self.done[1 - pos.zl, wrap(q, 4)] = other
        for half in (pos.zl, 1 - pos.zl):
            for e in range(3):
                self.result(l, q, half, e).start()

    def stored(self, l, q):
        for half in (self.pos.zl, 1 - self.pos.zl):
            for e in range(3):
                self.result(l, q, half, e).wait()

    def turn(self, run, l, pair, e, enters=True):
        first = run * self.count

        def stage(s, f):
            g = first + 2 * pair + e - self.lag[s]
            h = (e - self.lag[s]) % 2
            if isinstance(g, int):
                if first <= g < first + self.count:
                    f(g, h)
            elif s:
                pl.when(g >= first)(lambda: f(g, h))
            else:
                f(g, h)

        stage(1, self.stage1)
        if enters:
            stage(0, self.stage0)
        stage(2, self.stage2)
        stage(3, self.stage3)
        stage(4, lambda g, h: self.stage4(g, h, l))

    def written(self, l):
        for q in range(self.count - 4, self.count):
            self.stored(l, q)

    def finish(self, total):
        for stage in range(4):
            for g in range(total - self.sends[stage], total):
                for k in self.each(stage, g % 2):
                    self.copy(g, stage, g % 2, k).wait_send()


def backward_all(
    seq, row, w_all, vec, keep, stats_all, f0, g0, cand0, p0, r0, u0, low0, low1, u1, dhr1, dn1, du1,
    res1, resx, tok, sums1,
    grad, input_grad, result, vo0, vo1, vo2, vo3, vo4, vo5,
    stats, wbuf, du, low, dn, dnsend, dnrecv, hsend, hrecv, tokx, u, dhr, stream, proj,
    keep0, send0, recv0, keep1, send1, recv1, keep2, send2, recv2, keep3, send3, recv3, done,
    ends, first, table, b_own, b_got, b_fin, sums, sumsx, vbuf, vr0, vr1, vr2, vr3,
    snd, rcv, gouts, psnd, prcv, csnd, crcv, vsnd, vrcv, ins, ssem, wsem,
):
    pos = Place(seq, row)
    at, zl = pos.at, pos.zl
    z, x, y, c = (at[k] for k in "zxyc")
    t2, H3 = du.shape
    t, H = t2 // 2, H3 // 3
    d = 2 * H
    steps = t // SUB
    parts = H // WIDE
    partner = pos.device(dict(at, z=z + 1 - 2 * zl))
    own = pl.ds(pl.multiple_of(zl * H, H), H)
    other = pl.ds(pl.multiple_of((1 - zl) * H, H), H)
    rows_of = lambda b: pl.ds(pl.multiple_of(b * t, t), t)

    def load(k, src, dst):
        return pltpu.make_async_copy(src, dst, ins.at[k])

    def weights(l, half):
        zs = pl.ds(half * (pos.Z // 2), pos.Z // 2)
        for m in range(parts):
            for h in range(2):
                q = 2 * m + h
                yield pltpu.make_async_copy(
                    w_all.at[l, m, h, zs],
                    wbuf.at[:, :, :, :, :, q * HALF : (q + 1) * HALF],
                    wsem.at[q],
                )

    def begin(copies):
        for copy in copies:
            copy.start()

    def end(copies):
        for copy in copies:
            copy.wait()

    get_du, get_low, get_dn = load(0, du1, du), load(1, low1, low), load(2, dn1, dn)
    get_u, get_dhr = load(3, u1, u), load(4, dhr1, dhr)
    get_stats = load(6, stats_all.at[1], stats)
    get_du.start()
    begin(weights(1, 1 - zl))
    pos.barrier(seq)
    scatter = Scatter(
        pos, 2 * parts, low, du, grad, (keep0, keep1, keep2, keep3), (send0, send1, send2, send3),
        (recv0, recv1, recv2, recv3), done, snd, rcv, gouts,
    )
    chain = Chain(pos, table, csnd, crcv)

    def pair(k, src, dst):
        return remote(src, dst, psnd.at[k], prcv.at[k], partner)

    def partial_sums(b):
        return pair(b, dnsend.at[b], dnrecv.at[b])

    def statistics(b):
        return pair(2 + b, b_own.at[b], b_got.at[b])

    def carried():
        return pair(4, hsend, hrecv)

    def results(cols):
        rows = pl.ds(t // 2, t // 2)
        return pair(5, res1.at[1 - zl, rows], result.at[rows, cols])

    own_result = load(5, res1.at[zl], result.at[:, own])
    own_result.start()
    got_result = load(8, resx, result.at[pl.ds(0, t // 2), other])
    got_result.start()
    across = (((1,), (1,)), ((), ()))

    n = t2 // parts
    blocks = t // n

    def product(b, k):
        rows = pl.ds(pl.multiple_of(b * t + k * n, n), n)
        return lax.dot_general(
            du[rows, :], wbuf[...].reshape(H, H3), across, preferred_element_type=F32
        )

    def of_block(k):
        return pl.ds(pl.multiple_of(k * (n // SUB), n // SUB), n // SUB)

    def theirs(q, b, more=None):
        def one(k, _):
            v = product(b, k)
            if more is not None:
                v = v + more[of_block(k)].reshape(n, H)
            dnsend[q, pl.ds(pl.multiple_of(k * n, n), n), :] = v.astype(BF16)
            return 0

        lax.fori_loop(0, blocks, one, 0)
        partial_sums(q).start()

    def ours(to, b, k, fresh=False):
        v = product(b, k).reshape(n // SUB, SUB, H)
        if fresh:
            dn[to, of_block(k)] = v
        else:
            dn[to, of_block(k)] += v

    half = t // LANE

    def norm_sums(l, b):
        partial_sums(b).wait_recv()

        def one(q, _):
            spot = pl.ds(q * (LANE // SUB), LANE // SUB)
            rows = pl.ds(pl.multiple_of(q * LANE, LANE), LANE)
            v = dn[b, spot].reshape(LANE, H) + dnrecv[b, rows, :].astype(F32)
            dn[b, spot] = v.reshape(LANE // SUB, SUB, H)
            xhat = hat(l, b, spot)
            sums[l, 0] += jnp.sum((v * xhat).reshape(LANE // SUB, SUB, H), axis=0)
            sums[l, 1] += jnp.sum(v.reshape(LANE // SUB, SUB, H), axis=0)
            v = v * vec[l, GAIN : GAIN + 1, own]
            b_own[b, pl.ds(q, 1), :] = to_row(jnp.sum(v, axis=-1, keepdims=True))
            b_own[b, pl.ds(q + half, 1), :] = to_row(jnp.sum(v * xhat, axis=-1, keepdims=True))
            return 0

        lax.fori_loop(0, half, one, 0)
        statistics(b).start()

    def hat(l, b, spot):
        mu = stats[0, b, spot].reshape(LANE, LANE)[:, :1]
        rstd = stats[1, b, spot].reshape(LANE, LANE)[:, :1]
        return (u[b, spot].reshape(LANE, H) - mu) * rstd

    def norm_back(l, b):
        statistics(b).wait_recv()
        b_fin[...] = (b_own[b] + b_got[b]) * (1.0 / d)

        def one(q, _):
            spot = pl.ds(q * (LANE // SUB), LANE // SUB)
            xhat = hat(l, b, spot)
            rstd = stats[1, b, spot].reshape(LANE, LANE)[:, :1]
            m0 = to_column(b_fin[pl.ds(q, 1), :])
            m1 = to_column(b_fin[pl.ds(q + half, 1), :])
            v = dn[b, spot].reshape(LANE, H) * vec[l, GAIN : GAIN + 1, own]
            v = dhr[b, spot].reshape(LANE, H) + rstd * (v - m0 - xhat * m1)
            dhr[b, spot] = v.reshape(LANE // SUB, SUB, H)
            return 0

        lax.fori_loop(0, half, one, 0)

    def norm_last():
        for q in range(2):
            partial_sums(q).wait_recv()
        carried().wait_recv()
        get_tok.wait()
        piece = 4
        n = piece * SUB

        def one(k, _):
            spot = pl.ds(k * piece, piece)
            rows = pl.ds(pl.multiple_of(k * n, n), n)
            mu = stats[0, zl, spot].reshape(n, LANE)[:, :1]
            rstd = stats[1, zl, spot].reshape(n, LANE)[:, :1]
            scaled, hats = [], []
            m0 = m1 = 0.0
            for q, part in enumerate((zl, 1 - zl)):
                x = u[zl, spot].reshape(n, H) if q == 0 else tokx[rows, :].astype(F32)
                xhat = (x - mu) * rstd
                v = dn[part, spot].reshape(n, H) + dnrecv[q, rows, :].astype(F32)
                total = sums.at[0] if q == 0 else sumsx
                total[0] += jnp.sum((v * xhat).reshape(piece, SUB, H), axis=0)
                total[1] += jnp.sum(v.reshape(piece, SUB, H), axis=0)
                v = v * vec[0, GAIN : GAIN + 1, own if q == 0 else other]
                m0 += jnp.sum(v, axis=-1, keepdims=True)
                m1 += jnp.sum(v * xhat, axis=-1, keepdims=True)
                scaled.append(v)
                hats.append(xhat)
            m0, m1 = m0 * (1.0 / d), m1 * (1.0 / d)
            for q in range(2):
                v = rstd * (scaled[q] - m0 - hats[q] * m1)
                if q == 0:
                    v = v + dhr[zl, spot].reshape(n, H)
                else:
                    v = v + hrecv[rows, :].astype(F32)
                dnsend[q, rows, :] = v.astype(BF16)
            return 0

        lax.fori_loop(0, steps // piece, one, 0)

    units = 2 * parts
    sources = (f0, g0, cand0, p0, r0)

    def fetch(k):
        slot = lax.rem(k, 2)
        b, m = jnp.where(k < parts, 1 - zl, zl), lax.rem(k, parts)
        for j, src in enumerate(sources):
            yield pltpu.make_async_copy(
                src.at[b, :, :, lane_tile(m, WIDE)], stream.at[slot, j], ssem.at[slot, j]
            )

    def tiles(work, between=None):
        begin(fetch(0))

        def one(k, _):
            @pl.when(k + 1 < units)
            def _():
                begin(fetch(k + 1))

            end(fetch(k))
            b, m = jnp.where(k < parts, 1 - zl, zl), lax.rem(k, parts)
            cols = lane_tile(m, WIDE)
            wide = pl.ds(pl.multiple_of(zl * H + m * WIDE, WIDE), WIDE)
            work(lax.rem(k, 2), b, m, cols, wide)
            if between is not None:
                between(k)
            return 0

        lax.fori_loop(0, units, one, 0)

    def step_back(slot, b, i, cols, peep):
        up, down, cd, before, gate = (stream[slot, j, i] for j in range(5))
        cell = up * before + down * cd
        top = dhr[b, i, :, cols]
        dz_r = top * (cell - u[b, i, :, cols]) * gate * (1.0 - gate)
        direct = top * gate
        kept = lanes(keep[b, i], WIDE)
        decay = up * kept
        term = kept * peep * dz_r + decay * direct
        return up, down, cd, before, gate, top, dz_r, direct, decay, term

    def row_wide(l, k, wide):
        return jnp.broadcast_to(vec[l, k : k + 1, wide], (SUB, WIDE))

    def ends_work(slot, b, m, cols, wide):
        peep = row_wide(0, RPEEP, wide)

        def one(k, carry):
            scale, q = carry
            i = steps - 1 - k
            terms = step_back(slot, b, i, cols, peep)
            gate, top, decay, term = terms[4], terms[5], terms[-2], terms[-1]
            proj[i, :, :WIDE] = top * (1.0 - gate)
            return scale * decay, decay * q + term

        start = jnp.ones((SUB, WIDE), F32), jnp.zeros((SUB, WIDE), F32)
        scale, q = lax.fori_loop(0, steps, one, start, unroll=16)
        ends[b, 0, :, cols] = scale
        ends[b, 1, :, cols] = q

        @pl.when(b != zl)
        def _():
            hsend[:, cols] = proj[:, :, :WIDE].reshape(t, WIDE).astype(BF16)

    def send_carried(k):
        pl.when(k == parts - 1)(lambda: carried().start())
        pl.when(k == 1)(lambda: late(0, 1, 2))
        pl.when(k == parts + 1)(lambda: late(0, 1, 3))

    def down_work(slot, b, m, cols, wide):
        fpeep, rpeep, gain, shift = (row_wide(0, k, wide) for k in (FPEEP, RPEEP, GAIN, SHIFT))

        def one(k, carry):
            q, s0, s1, s2, s3 = carry
            i = steps - 1 - k
            up, low_f, cd, before, gate, top, dz_r, direct, decay, term = step_back(
                slot, b, i, cols, rpeep
            )
            e = direct + q
            dz_f = e * (up * low_f) * (before - cd)
            n = (u[b, i, :, cols] - lanes(stats[0, b, i], WIDE)) * lanes(
                stats[1, b, i], WIDE
            ) * gain + shift
            proj[i, :, :WIDE] = e * low_f
            proj[i, :, WIDE : 2 * WIDE] = dz_f
            proj[i, :, 2 * WIDE :] = dz_r
            dn[b, i, :, cols] = dz_f * fpeep
            dhr[b, i, :, cols] = top * (1.0 - gate)
            return (
                decay * q + term,
                s0 + dz_f * n,
                s1 + dz_r * before,
                s2 + dz_f,
                s3 + dz_r,
            )

        zero = jnp.zeros((SUB, WIDE), F32)
        carry = lax.fori_loop(0, steps, one, (first[b, :, cols], zero, zero, zero, zero), unroll=16)
        for k in range(4):
            sums[0, 2 + k, :, cols] += carry[k + 1]
        for h in range(2):
            for k in range(3):
                v = proj[:, :, k * WIDE + h * LANE : k * WIDE + (h + 1) * LANE]
                to = pl.ds(pl.multiple_of((2 * m + h) * HALF + k * LANE, LANE), LANE)
                du[rows_of(b), to] = v.reshape(t, LANE).astype(BF16)

    def late(run, l, k):
        scatter.turn(run, l, parts + k // 2, k % 2, False)

    sums[...] = jnp.zeros_like(sums)
    sumsx[...] = jnp.zeros_like(sumsx)
    sums[1, 2:6] = sums1[0] + sums1[1]
    get_du.wait()
    end(weights(1, 1 - zl))
    begin([get_low, get_dn])
    for b in range(2):
        theirs(b, b)
    begin(weights(1, zl))
    begin([get_u, get_dhr, get_stats])
    get_low.wait()
    get_dn.wait()

    def last_layer(k, _):
        scatter.turn(0, 1, k, 0)

        @pl.when(k == 0)
        def _():
            end(weights(1, zl))

        ours(k // blocks, k // blocks, lax.rem(k, blocks))
        scatter.turn(0, 1, k, 1)
        return 0

    lax.fori_loop(0, parts, last_layer, 0)
    get_low = load(1, low0, low)
    get_low.start()
    get_u.wait()
    get_dhr.wait()
    get_stats.wait()
    begin(weights(0, 1 - zl))
    norm_sums(1, 0)
    norm_sums(1, 1)
    late(0, 1, 0)
    norm_back(1, 0)
    norm_back(1, 1)
    results(own).start()
    get_u, get_stats = load(3, u0, u), load(6, stats_all.at[0], stats)
    get_tok = load(7, tok, tokx)
    begin([get_u, get_stats, get_tok])
    late(0, 1, 1)
    get_u.wait()
    get_stats.wait()
    tiles(ends_work, send_carried)
    chain.run(ends, first, True)
    for b in range(2):
        partial_sums(b).wait_send()
        statistics(b).wait_send()
    end(weights(0, 1 - zl))

    def between(k):
        @pl.when(k == parts - 1)
        def _():
            theirs(0, 1 - zl)
            begin(weights(0, zl))

        for e in range(3):
            pl.when(k == e)(lambda: late(0, 1, 4 + e))
        for e in range(2):
            pl.when(k == parts + e)(lambda: scatter.turn(1, 0, 0, e))

    get_low.wait()
    tiles(down_work, between)
    scatter.written(1)
    end(weights(0, zl))
    theirs(1, 1 - zl, dn.at[1 - zl])

    def first_layer(k, _):
        scatter.turn(1, 0, k, 0)

        @pl.when(k == 1)
        def _():
            ours(zl, zl, 0)
            ours(zl, zl, 1)
            begin(weights(0, 1 - zl))

        @pl.when(k == 2)
        def _():
            end(weights(0, 1 - zl))

        @pl.when(k > 1)
        def _():
            ours(1 - zl, zl, k - 2, True)

        scatter.turn(1, 0, k, 1)
        return 0

    lax.fori_loop(1, parts, first_layer, 0)
    late(1, 0, 0)
    late(1, 0, 1)
    for b in range(2):
        partial_sums(b).wait_send()
    norm_last()
    out_own = load(0, dnsend.at[0], input_grad.at[:, own])
    out_other = load(1, dnsend.at[1], input_grad.at[:, other])
    begin([out_own, out_other])
    late(1, 0, 2)
    late(1, 0, 3)

    vbuf[...] = jnp.zeros_like(vbuf)
    per = d // (seq * row)
    total = [jnp.sum(sums[l], axis=1) for l in range(2)]
    totalx = jnp.sum(sumsx[...], axis=1)
    blank = jnp.zeros((6, LANE - per), F32) if per < LANE else None
    for i in range(H // per):
        spot = (zl * (pos.Z // 2) + i // (2 * pos.Y * pos.X), i // (2 * pos.Y) % pos.X, i // 2 % pos.Y, i % 2)
        for l in range(2):
            piece = total[l][:, i * per : (i + 1) * per]
            vbuf[spot + (slice(l * 8, l * 8 + 6),)] = jnp.concatenate([piece, blank], axis=-1)
        away = (lax.rem(spot[0] + pos.Z // 2, pos.Z),) + spot[1:]
        piece = totalx[:, i * per : (i + 1) * per]
        vbuf[away + (slice(0, 2),)] = jnp.concatenate([piece, blank[:2]], axis=-1)
    every = slice(None)

    def vspot(stage, who):
        if stage == 0:
            return (every, every, every, who["c"])
        if stage == 1:
            return (every, who["x"], every, c)
        if stage == 2:
            return (every, x, who["y"], c)
        return (who["z"], x, y, c)

    vrecv = (vr0, vr1, vr2, vr3)

    def vcopy(stage, k):
        axis = "cxyz"[stage]
        to = pos.moved(axis, k)
        sem = scatter.base[stage] + k - 1
        return remote(
            vbuf.at[vspot(stage, to)], vrecv[stage].at[k - 1], vsnd.at[sem], vrcv.at[sem],
            pos.device(to),
        )

    def vstart(stage):
        for k in pos.others("cxyz"[stage]):
            vcopy(stage, k).start()

    def vtake(stage):
        for k in pos.others("cxyz"[stage]):
            vcopy(stage, k).wait_recv()
            vbuf[vspot(stage, at)] += vrecv[stage][k - 1]

    vstart(0)
    late(1, 0, 4)
    vtake(0)
    vstart(1)
    late(1, 0, 5)
    vtake(1)
    vstart(2)
    late(1, 0, 6)
    vtake(2)
    vstart(3)
    vtake(3)
    mine = vbuf[z, x, y, c]
    for k, out in enumerate((vo0, vo1, vo2, vo3, vo4, vo5)):
        out[...] = jnp.concatenate([mine[l * 8 + k : l * 8 + k + 1, :per] for l in range(2)], axis=0)
    for stage in range(4):
        for k in pos.others("cxyz"[stage]):
            vcopy(stage, k).wait_send()
    scatter.written(0)
    scatter.finish(2 * scatter.count)
    carried().wait_send()
    end([out_own, out_other])
    own_result.wait()
    got_result.wait()
    results(own).wait_send()
    results(other).wait_recv()


def call_backward(seq, row, t, d, given):
    w_all = given[0]
    layers, parts, _, Z, X, Y, _, per, _ = w_all.shape
    H = d // 2
    steps = t // SUB
    vmem = pl.BlockSpec(memory_space=pltpu.VMEM)
    hbm = pl.BlockSpec(memory_space=pl.ANY)
    dma = pltpu.SemaphoreType.DMA
    big = pltpu.VMEM((2, steps, SUB, H), F32)
    half, quarter = pltpu.VMEM((2, t, H), BF16), pltpu.VMEM((t, H), BF16)
    st = pltpu.VMEM((2, 8, LANE), F32)
    count = 1 + 2 * (X - 1) + Z - 1
    chunk = (Z, X, Y, per, HALF)

    def buf(*shape, dtype=BF16):
        return pltpu.VMEM(shape, dtype)

    return pl.pallas_call(
        lambda *refs: backward_all(seq, row, *refs),
        in_specs=[hbm, vmem, vmem] + [hbm] * 16 + [vmem],
        out_specs=[hbm, hbm, hbm] + [vmem] * 6,
        out_shape=[arr(layers, per, 3 * d)] + [arr(t, d, dtype=BF16)] * 2 + [arr(layers, per)] * 6,
        scratch_shapes=[
            buf(2, 2, steps, SUB, LANE, dtype=F32),
            buf(Z // 2, X, Y, 2, per, 3 * H),
            buf(2 * t, 3 * H),
            buf(2 * t, d),
            big, half, half, quarter, quarter, quarter, big, big,
            buf(2, 5, steps, SUB, WIDE, dtype=F32),
            buf(steps, SUB, 3 * WIDE, dtype=F32),
            buf(*chunk, dtype=F32), buf(2, 1, *chunk), buf(2, 1, *chunk),
            buf(3, Z, Y, per, HALF, dtype=F32), buf(4, X - 1, Z, Y, per, HALF),
            buf(6, X - 1, Z, Y, per, HALF),
            buf(3, Z, per, HALF, dtype=F32), buf(4, Y - 1, Z, per, HALF),
            buf(6, Y - 1, Z, per, HALF),
            buf(3, per, HALF, dtype=F32), buf(4, Z - 1, per, HALF), buf(6, Z - 1, per, HALF),
            buf(2, 4, per, HALF, dtype=F32),
            buf(2, 2, SUB, H, dtype=F32),
            buf(2, SUB, H, dtype=F32),
            buf(Z // 2, X, 2, 2, H, dtype=F32),
            st, st, buf(8, LANE, dtype=F32),
            buf(2, 6, SUB, H, dtype=F32),
            buf(2, SUB, H, dtype=F32),
            buf(Z, X, Y, 2, 16, LANE, dtype=F32),
            buf(1, Z, X, Y, 16, LANE, dtype=F32),
            buf(X - 1, Z, Y, 16, LANE, dtype=F32),
            buf(Y - 1, Z, 16, LANE, dtype=F32),
            buf(Z - 1, 16, LANE, dtype=F32),
            dma((4, count)), dma((6, count)),
            dma((2, 4, 3)),
            dma((6,)), dma((6,)),
            dma((Z // 2 * X,)), dma((Z // 2 * X,)),
            dma((count,)), dma((count,)),
            dma((9,)),
            dma((2, 5)),
            dma((2 * parts,)),
        ],
        compiler_params=pltpu.CompilerParams(
            collective_id=1, has_side_effects=True, vmem_limit_bytes=63 << 20
        ),
        name="backward_all",
    )(*given)


def body(tokens, resets, cotangent, weight, *rows):
    _, t, d = tokens.shape
    layers = weight.shape[0]
    steps = t // SUB
    seq, row = lax.axis_size("seq"), lax.axis_size("row")

    def restored(v):
        return v.reshape(steps, SUB, d).transpose(1, 0, 2).reshape(1, t, d)

    out = call_forward(
        seq, row, tokens[0], cotangent[0], resets, rows, weight
    )
    grad, input_grad, result, *vectors = call_backward(seq, row, t, d, out)
    return (restored(result), restored(input_grad), grad) + tuple(vectors)


def solution(mesh):
    tokens = P("row", "seq", None)
    rows = P(None, ("seq", "row"))
    weight = P(None, ("seq", "row"), None)
    return jax.shard_map(
        body,
        mesh=mesh,
        in_specs=(tokens, P("row", "seq"), tokens, weight) + (rows,) * 6,
        out_specs=(tokens, tokens, weight) + (rows,) * 6,
        check_vma=False,
    )
```
